32 devices in a mesh: ctx: 4 (over y, core), uly: 8 (over z, x).
Axes of the slice: x: 2, y: 2, z: 4, core: 2. Of those that a mesh axis runs over, the one named last changes fastest.
Arguments:
- queries: bfloat16 [3072, 4096], P(('ctx', 'uly')), may hold values from -6 to 6
- keys: bfloat16 [3072, 4096], P(('ctx', 'uly')), may hold values from -6 to 6
- values: bfloat16 [3072, 4096], P(('ctx', 'uly')), may hold values from -6 to 6
- doc_ids: int32 [3072], P(('ctx', 'uly')), may hold values from 0 to 7, never falling along the last dimension, each value on 1 to 1536 neighbouring positions
- decay_rate: float32 [64], P('uly'), may hold values from 6.510417e-05 to 0.05
- norm_gain: float32 [4096], replicated, may hold values from 0.1 to 1.9
Outputs:
- attended: bfloat16 [3072, 4096], P(('ctx', 'uly'))
The draws below stay inside these ranges and needn't reach their ends.
Inputs may be any that keep to these rules, and one draw needn't show every extreme that they name: doc_ids never fall along the sequence; every document has 1 to 1536 tokens and one has exactly that many.
All inputs are finite; a program needn't handle non-finite values.
Results may differ from the reference program's by a relative error of at most 0.0034.
Values may be sent and summed in bfloat16 or wider, within the bound.
No kernel may reach another device: no remote copies, remote signals or barrier semaphores. Data moves between devices by JAX's collectives and lax.ppermute only.
A program may use at most 64 MiB of HBM per device.

```python
import math
import jax
import jax.numpy as jnp
import numpy as np
from jax import lax

H = 64
HD = 64
BLK = 256
L_CTX = 768
TOKENS = 3072
DOCS = 8


def levels(own_key, extent, cuts, smallest, top_value):
    loudness, own = 1.0, jax.random.fold_in(own_key, 6)
    for dim, blocks in cuts:
        steps = jnp.exp(jax.random.uniform(jax.random.fold_in(own, dim), (blocks,), jnp.float32, smallest / len(cuts), top_value / len(cuts)))
        loudness = loudness * jnp.repeat(steps, extent[dim] // blocks).reshape([-1 if axis == dim else 1 for axis in range(len(extent))])
    return loudness


def split_up(count, total, reach, slope):
    portions = [(1 << 20) // math.isqrt(grade ** slope) + 1 for grade in range(2, count + 1)]
    rest, holding = total - reach - (count - 1), [1] * (count - 1)
    while rest > 0:
        free = [i for i in range(count - 1) if holding[i] < reach]
        pool, left = sum([portions[i] for i in free]), rest
        for i in free:
            extra = min(reach - holding[i], max(1, left * portions[i] // pool), rest)
            holding[i] = holding[i] + extra
            rest = rest - extra
    return np.array([reach] + holding)


def ragged(stream_key, count, total, limit, lean):
    if count == 2:
        one = jax.random.randint(stream_key, (), max(1, total - limit), min(limit, total - 1) + 1)
        return jnp.stack([one, total - one])
    tallies = jnp.asarray(split_up(count, total, limit, lean), jnp.int32)
    pairs = (count - 1) // 2
    giver, taker = tallies[1:1 + 2 * pairs:2], tallies[2:2 + 2 * pairs:2]
    slack = jnp.minimum(giver - 1, limit - taker)
    passed = jax.random.randint(jax.random.fold_in(stream_key, 1), (pairs,), 0, 1 << 20) % (slack + 1)
    tallies = tallies.at[1:1 + 2 * pairs:2].set(giver - passed).at[2:2 + 2 * pairs:2].set(taker + passed)
    return tallies[jax.random.permutation(jax.random.fold_in(stream_key, 2), count)]


def gaussian(own_key, extent, scale, bound, cuts=(), held_as=jnp.bfloat16):
    values = scale * jax.random.normal(own_key, extent, jnp.float32)
    if cuts:
        values = values * levels(own_key, extent, cuts, -0.22, 0.18)
    return jnp.clip(values, -bound, bound).astype(held_as)


def setup_inputs(seed: int = 0) -> dict:
    key_of = jax.random.split(jax.random.key(seed), 7)
    queries = gaussian(key_of[0], (TOKENS, H * HD), 1.0, 6.0, ((0, 32),))
    keys = gaussian(key_of[1], (TOKENS, H * HD), 1.0, 6.0, ((0, 32),))
    values = gaussian(key_of[2], (TOKENS, H * HD), 1.0, 6.0, ((0, 32),))
    doc_ids = jnp.searchsorted(jnp.cumsum(ragged(key_of[3], DOCS, TOKENS, 2 * L_CTX, 2)), jnp.arange(TOKENS), side="right").astype(jnp.int32)
    decay_rate = jnp.clip(jnp.exp(math.log(0.05) - 6.64379 * jax.random.uniform(key_of[4], (H,), jnp.float32) ** levels(key_of[4], (H,), ((0, 8),), -0.2, 0.2)), 6.510417006211355e-05, 0.05)
    norm_gain = jnp.clip(1.0 + 0.18 * jax.random.normal(key_of[5], (H * HD,), jnp.float32), 0.1, 1.9)
    return dict(queries=queries, keys=keys, values=values, doc_ids=doc_ids, decay_rate=decay_rate, norm_gain=norm_gain)


def state_pass(keys3, values3, ids, rate, blk, start_state, start_last):
    length, heads, width = keys3.shape
    count = length // blk
    kblocks = keys3.reshape(count, blk, heads, width)
    vblocks = values3.reshape(count, blk, heads, width)
    iblocks = ids.reshape(count, blk)
    position = jnp.arange(blk).astype(jnp.float32)

    def advance(carry, pieces):
        state, last = carry
        kblock, vblock, iblock = pieces
        endid = iblock[blk - 1]
        keep = jnp.where(endid == last, jnp.exp(-rate * blk), jnp.float32(0.0))
        weights = jnp.where((iblock == endid)[None, :], jnp.exp(-rate[:, None] * (blk - 1 - position)[None, :]), jnp.float32(0.0))
        scaled = kblock.astype(jnp.float32) * jnp.transpose(weights)[:, :, None]
        fresh = jnp.einsum('shd,she->hde', scaled, vblock.astype(jnp.float32), precision=lax.Precision.HIGHEST)
        return ((keep[:, None, None] * state + fresh, endid), (state, last))
    final, entries = lax.scan(advance, (start_state, start_last), (kblocks, vblocks, iblocks))
    return (final, entries)

def block_output(qblock, kblock, vblock, iblock, state, last, rate):
    blk = qblock.shape[0]
    position = jnp.arange(blk).astype(jnp.float32)
    q32 = qblock.astype(jnp.float32)
    scores = jnp.einsum('thd,shd->hts', q32, kblock.astype(jnp.float32))
    diff = position[:, None] - position[None, :]
    mask = (diff >= 0) & (iblock[:, None] == iblock[None, :])
    weight = jnp.where(mask[None], jnp.exp(-rate[:, None, None] * jnp.maximum(diff, 0.0)[None]), jnp.float32(0.0))
    probs = (scores * weight).astype(jnp.bfloat16)
    intra = jnp.einsum('hts,shd->thd', probs.astype(jnp.float32), vblock.astype(jnp.float32))
    factor = jnp.exp(-rate[None, :] * (position + 1.0)[:, None]) * (iblock == last).astype(jnp.float32)[:, None]
    inter = jnp.einsum('thd,hde->the', q32, state, precision=lax.Precision.HIGHEST) * factor[:, :, None]
    return intra + inter

def all_outputs(q3, k3, v3, ids, rate, blk, entries):
    length, heads, width = q3.shape
    count = length // blk
    states, lasts = entries

    def one(pieces):
        qblock, kblock, vblock, iblock, state, last = pieces
        return block_output(qblock, kblock, vblock, iblock, state, last, rate)
    out = lax.map(one, (q3.reshape(count, blk, heads, width), k3.reshape(count, blk, heads, width), v3.reshape(count, blk, heads, width), ids.reshape(count, blk), states, lasts))
    return out.reshape(length, heads, width)

def token_norm(raw, gain):
    flat = raw.reshape(raw.shape[0], raw.shape[1] * raw.shape[2])
    meansq = lax.optimization_barrier(jnp.mean(flat * flat, axis=1, keepdims=True))
    return (flat * lax.rsqrt(meansq + 1e-06) * gain[None, :]).astype(jnp.bfloat16)

def reference(queries, keys, values, doc_ids, decay_rate, norm_gain):
    q3 = queries.reshape(TOKENS, H, HD)
    k3 = keys.reshape(TOKENS, H, HD)
    v3 = values.reshape(TOKENS, H, HD)
    zero_state = jnp.zeros((H, HD, HD), jnp.float32)
    final, entries = state_pass(k3, v3, doc_ids, decay_rate, BLK, zero_state, jnp.int32(-1))
    raw = all_outputs(q3, k3, v3, doc_ids, decay_rate, BLK, entries)
    return token_norm(raw, norm_gain)
```

```python
import functools

import jax
import jax.numpy as jnp
from jax import lax
from jax.experimental import pallas as pl
from jax.experimental.pallas import tpu as pltpu
from jax.sharding import PartitionSpec as P

HD = 64
LANES = 2 * HD
NEVER = 1e9
BOTH_LAST = (((1,), (1,)), ((), ()))
BOTH_FIRST = (((0,), (0,)), ((), ()))


def rate_of(facts, head, here):
    return facts[head // here, head % here]


def pair_rate(facts, pair, here):
    lane = lax.broadcasted_iota(jnp.int32, (1, LANES), 1)
    return jnp.where(lane < HD, rate_of(facts, 2 * pair, here), rate_of(facts, 2 * pair + 1, here))


def ends_kernel(here, pairs, facts, idcol, k_ref, v_ref, out_ref):
    tokens = k_ref.shape[0]
    first = pl.program_id(0) * pairs
    lane = lax.broadcasted_iota(jnp.int32, (HD, LANES), 1)
    place = lax.broadcasted_iota(jnp.int32, (tokens, LANES), 0)
    ids = idcol[...]
    age = jnp.where(ids == ids[tokens - 1 :, :], (tokens - 1 - place).astype(jnp.float32), NEVER)
    for j in range(pairs):
        rate = pair_rate(facts, first + j, here)
        columns = slice(j * LANES, (j + 1) * LANES)
        weighted = k_ref[:, columns].astype(jnp.float32) * jnp.exp(-rate * age)
        high = weighted.astype(jnp.bfloat16)
        low = (weighted - high.astype(jnp.float32)).astype(jnp.bfloat16)
        v = v_ref[:, columns]
        both = lax.dot_general(high, v, BOTH_FIRST, preferred_element_type=jnp.float32)
        both += lax.dot_general(low, v, BOTH_FIRST, preferred_element_type=jnp.float32)
        out_ref[j * HD : (j + 1) * HD, :] = jnp.where(lane < HD, both[:HD], both[HD:]).astype(
            jnp.bfloat16
        )


def inner_kernel(here, pairs, facts, idcol, idrow, q_ref, k_ref, v_ref, out_ref):
    tokens = k_ref.shape[0]
    first = pl.program_id(0) * pairs
    lane = lax.broadcasted_iota(jnp.int32, (tokens, LANES), 1)
    t = lax.broadcasted_iota(jnp.int32, (tokens, tokens), 0)
    s = lax.broadcasted_iota(jnp.int32, (tokens, tokens), 1)
    seen = (t >= s) & (idcol[:, :tokens] == idrow[...])
    age = jnp.where(seen, (t - s).astype(jnp.float32), NEVER)
    for j in range(pairs):
        columns = slice(j * LANES, (j + 1) * LANES)
        q = q_ref[:, columns]
        zero = jnp.zeros_like(q)
        stacked = jnp.concatenate([jnp.where(lane < HD, q, zero), jnp.where(lane < HD, zero, q)], 0)
        scores = lax.dot_general(
            stacked, k_ref[:, columns], BOTH_LAST, preferred_element_type=jnp.float32
        )
        head = 2 * (first + j)
        weight = jnp.concatenate(
            [
                jnp.exp(-rate_of(facts, head, here) * age),
                jnp.exp(-rate_of(facts, head + 1, here) * age),
            ],
            0,
        )
        probs = (scores * weight).astype(jnp.bfloat16)
        got = jnp.dot(probs, v_ref[:, columns], preferred_element_type=jnp.float32)
        out_ref[:, columns] = jnp.where(lane < HD, got[:tokens], got[tokens:])


def scan_kernel(here, tokens, rows, facts, in_ref, out_ref):
    count = in_ref.shape[0]
    me = lax.axis_index("ctx") * lax.axis_size("uly") + lax.axis_index("uly")
    rate = pair_rate(facts, (me * rows) // HD, here)
    decay = jnp.exp(-rate * float(tokens))
    out_ref[0] = jnp.zeros(out_ref.shape[1:], out_ref.dtype)

    def step(i, state):
        linked = facts[i, here] == facts[jnp.maximum(i - 1, 0), here]
        state = in_ref[i].astype(jnp.float32) + jnp.where(linked, decay, 0.0) * state
        out_ref[i + 1] = state.astype(out_ref.dtype)
        return state

    lax.fori_loop(0, count - 1, step, jnp.zeros(in_ref.shape[1:], jnp.float32), unroll=min(count - 1, 31))


def norm_kernel(here, pairs, facts, idcol, q_ref, s_ref, inner_ref, gain, out_ref, raw):
    tokens = q_ref.shape[0]
    step = pl.program_id(0)
    first = step * pairs
    me = lax.axis_index("ctx") * lax.axis_size("uly") + lax.axis_index("uly")
    before = jnp.where(me > 0, facts[jnp.maximum(me - 1, 0), here], -1.0)
    lane = lax.broadcasted_iota(jnp.int32, (HD, LANES), 1)
    place = lax.broadcasted_iota(jnp.int32, (tokens, LANES), 0)
    age = jnp.where(idcol[...].astype(jnp.float32) == before, (place + 1).astype(jnp.float32), NEVER)
    for j in range(pairs):
        columns = slice(j * LANES, (j + 1) * LANES)
        state = s_ref[j * HD : (j + 1) * HD, :]
        zero = jnp.zeros_like(state)
        square = jnp.concatenate(
            [jnp.where(lane < HD, state, zero), jnp.where(lane < HD, zero, state)], 0
        )
        outer = jnp.dot(q_ref[:, columns], square, preferred_element_type=jnp.float32)
        rate = pair_rate(facts, first + j, here)
        raw[step, :, columns] = inner_ref[:, columns] + outer * jnp.exp(-rate * age)

    @pl.when(step == pl.num_programs(0) - 1)
    def _():
        parts, _, width = raw.shape
        total = jnp.zeros((tokens, LANES), jnp.float32)
        for part in range(parts):
            for j in range(width // LANES):
                value = raw[part, :, j * LANES : (j + 1) * LANES]
                total += value * value
        mean = jnp.sum(total, axis=1, keepdims=True) / float(parts * width)
        scale = jnp.broadcast_to(lax.rsqrt(mean + 1e-06), (tokens, LANES))
        for part in range(parts):
            for j in range(width // LANES):
                at = part * width + j * LANES
                value = raw[part, :, j * LANES : (j + 1) * LANES]
                out_ref[:, at : at + LANES] = (value * scale * gain[:, at : at + LANES]).astype(
                    jnp.bfloat16
                )


def local(queries, keys, values, doc_ids, decay_rate, norm_gain):
    tokens, width = queries.shape
    here = decay_rate.shape[0]
    axes = ("ctx", "uly")
    count = lax.axis_size("ctx") * lax.axis_size("uly")
    all_pairs = width // LANES
    steps = 4
    pairs = all_pairs // steps
    rows = all_pairs * HD // count

    own = jnp.concatenate([decay_rate, doc_ids[tokens - 1 :].astype(jnp.float32)])
    facts = lax.all_to_all(
        jnp.broadcast_to(own[None, :], (count, here + 1)), axes, split_axis=0, concat_axis=0, tiled=True
    )
    idcol = jnp.broadcast_to(doc_ids[:, None], (tokens, LANES))
    idrow = doc_ids[None, :]

    smem = pl.BlockSpec(memory_space=pltpu.SMEM)
    whole = lambda shape: pl.BlockSpec(shape, lambda i: (0,) * len(shape))
    part = pl.BlockSpec((tokens, pairs * LANES), lambda i: (0, i))
    state_part = pl.BlockSpec((pairs * HD, LANES), lambda i: (i, 0))
    params = pltpu.CompilerParams(vmem_limit_bytes=32 * 1024 * 1024)

    ends = pl.pallas_call(
        functools.partial(ends_kernel, here, pairs),
        grid=(steps,),
        in_specs=[smem, whole((tokens, LANES)), part, part],
        out_specs=state_part,
        out_shape=jax.ShapeDtypeStruct((all_pairs * HD, LANES), jnp.bfloat16),
        compiler_params=params,
        cost_estimate=pl.CostEstimate(flops=200_000_000, bytes_accessed=2_200_000, transcendentals=0),
        name="ends",
    )(facts, idcol, keys, values)
    pieces = lax.all_to_all(
        ends.reshape(count, rows, LANES), axes, split_axis=0, concat_axis=0, tiled=True
    )
    inner = pl.pallas_call(
        functools.partial(inner_kernel, here, pairs),
        grid=(steps,),
        in_specs=[smem, whole((tokens, LANES)), whole((1, tokens)), part, part, part],
        out_specs=part,
        out_shape=jax.ShapeDtypeStruct((tokens, width), jnp.float32),
        compiler_params=params,
        cost_estimate=pl.CostEstimate(
            flops=8_000_000_000, bytes_accessed=4_000_000, transcendentals=600_000
        ),
        name="inner",
    )(facts, idcol, idrow, queries, keys, values)
    before = pl.pallas_call(
        functools.partial(scan_kernel, here, tokens, rows),
        in_specs=[smem, pl.BlockSpec(memory_space=pltpu.VMEM)],
        out_specs=pl.BlockSpec(memory_space=pltpu.VMEM),
        out_shape=jax.ShapeDtypeStruct((count, rows, LANES), jnp.bfloat16),
        compiler_params=params,
        name="scan",
    )(facts, pieces)
    states = lax.all_to_all(before, axes, split_axis=0, concat_axis=0, tiled=True)
    return pl.pallas_call(
        functools.partial(norm_kernel, here, pairs),
        grid=(steps,),
        in_specs=[smem, whole((tokens, LANES)), part, state_part, part, whole((1, width))],
        out_specs=whole((tokens, width)),
        out_shape=jax.ShapeDtypeStruct((tokens, width), jnp.bfloat16),
        scratch_shapes=[pltpu.VMEM((steps, tokens, pairs * LANES), jnp.float32)],
        compiler_params=params,
        name="norm",
    )(facts, idcol, queries, states.reshape(all_pairs * HD, LANES), inner, norm_gain[None, :])


def solution(mesh):
    in_specs = (
        P(("ctx", "uly"), None),
        P(("ctx", "uly"), None),
        P(("ctx", "uly"), None),
        P(("ctx", "uly")),
        P("uly"),
        P(),
    )
    out_specs = P(("ctx", "uly"), None)
    return jax.shard_map(local, mesh=mesh, in_specs=in_specs, out_specs=out_specs, check_vma=False)
```

```python
import functools

import jax
import jax.numpy as jnp
from jax import lax
from jax.experimental import pallas as pl
from jax.experimental.pallas import tpu as pltpu
from jax.sharding import PartitionSpec as P

HD = 64
LANES = 2 * HD
NEVER = 1e9
BOTH_LAST = (((1,), (1,)), ((), ()))
BOTH_FIRST = (((0,), (0,)), ((), ()))


def rate_of(facts, head, here):
    return facts[head // here, head % here]


def pair_rate(facts, pair, here):
    lane = lax.broadcasted_iota(jnp.int32, (1, LANES), 1)
    return jnp.where(lane < HD, rate_of(facts, 2 * pair, here), rate_of(facts, 2 * pair + 1, here))


def facts_kernel(rates, ids, out_ref):
    lane = lax.broadcasted_iota(jnp.int32, out_ref.shape, 1)
    here = rates.shape[0]
    row = jnp.where(lane == here, ids[ids.shape[0] - 1].astype(jnp.float32), 0.0)
    for j in range(here):
        row = jnp.where(lane == j, rates[j], row)
    out_ref[...] = row


def turn_kernel(ids, k_ref, turned, idrow, idcol):
    tokens, width = k_ref.shape
    fill = jnp.full((1, LANES - tokens), -1.0, jnp.float32)
    row = jnp.concatenate([ids[...].astype(jnp.float32), fill], 1)
    idrow[...] = jnp.broadcast_to(row, idrow.shape)
    idcol[...] = jnp.transpose(jnp.broadcast_to(row, (LANES, LANES)))[:tokens]
    blank = jnp.zeros((LANES - tokens, LANES), jnp.float32)
    for j in range(width // LANES):
        columns = slice(j * LANES, (j + 1) * LANES)
        block = jnp.concatenate([k_ref[:, columns].astype(jnp.float32), blank], 0)
        turned[columns, :] = jnp.transpose(block)


def ends_kernel(here, facts, idrow, turned, v_ref, out_ref):
    tokens, width = v_ref.shape
    lane = lax.broadcasted_iota(jnp.int32, (HD, LANES), 1)
    place = lax.broadcasted_iota(jnp.int32, idrow.shape, 1)
    ids = idrow[...]
    last = ids[:, tokens - 1 : tokens]
    age = jnp.where(ids == last, (tokens - 1 - place).astype(jnp.float32), NEVER)
    blank = jnp.zeros((LANES - tokens, LANES), jnp.bfloat16)
    for j in range(width // LANES):
        weighted = []
        for head in (2 * j, 2 * j + 1):
            weight = jnp.exp(-rate_of(facts, head, here) * age)
            keys = turned[head * HD : (head + 1) * HD, :].reshape(HD // 8, 8, LANES)
            weighted.append((keys * weight[None]).reshape(HD, LANES))
        weighted = jnp.concatenate(weighted, 0)
        high = weighted.astype(jnp.bfloat16)
        low = (weighted - high.astype(jnp.float32)).astype(jnp.bfloat16)
        v = v_ref[:, j * LANES : (j + 1) * LANES]
        both = jnp.dot(
            jnp.concatenate([high, low], 1),
            jnp.concatenate([v, blank, v, blank], 0),
            preferred_element_type=jnp.float32,
        )
        out_ref[j * HD : (j + 1) * HD, :] = jnp.where(lane < HD, both[:HD], both[HD:]).astype(
            jnp.bfloat16
        )


def inner_kernel(here, pairs, facts, idcol, idrow, q_ref, k_ref, v_ref, out_ref):
    tokens = k_ref.shape[0]
    first = pl.program_id(0) * pairs
    lane = lax.broadcasted_iota(jnp.int32, (tokens, LANES), 1)
    t = lax.broadcasted_iota(jnp.int32, (tokens, tokens), 0)
    s = lax.broadcasted_iota(jnp.int32, (tokens, tokens), 1)
    seen = (t >= s) & (idcol[:, :tokens] == idrow[:1, :tokens])
    age = jnp.where(seen, (t - s).astype(jnp.float32), NEVER)
    for j in range(pairs):
        columns = slice(j * LANES, (j + 1) * LANES)
        q = q_ref[:, columns]
        zero = jnp.zeros_like(q)
        stacked = jnp.concatenate([jnp.where(lane < HD, q, zero), jnp.where(lane < HD, zero, q)], 0)
        scores = lax.dot_general(
            stacked, k_ref[:, columns], BOTH_LAST, preferred_element_type=jnp.float32
        )
        head = 2 * (first + j)
        weight = jnp.concatenate(
            [
                jnp.exp(-rate_of(facts, head, here) * age),
                jnp.exp(-rate_of(facts, head + 1, here) * age),
            ],
            0,
        )
        probs = (scores * weight).astype(jnp.bfloat16)
        got = jnp.dot(probs, v_ref[:, columns], preferred_element_type=jnp.float32)
        out_ref[:, columns] = jnp.where(lane < HD, got[:tokens], got[tokens:])


def scan_kernel(here, tokens, rows, facts, in_ref, out_ref):
    count = in_ref.shape[0]
    me = lax.axis_index("ctx") * lax.axis_size("uly") + lax.axis_index("uly")
    rate = pair_rate(facts, (me * rows) // HD, here)
    decay = jnp.exp(-rate * float(tokens))
    out_ref[0] = jnp.zeros(out_ref.shape[1:], out_ref.dtype)

    def step(i, state):
        linked = facts[i, here] == facts[jnp.maximum(i - 1, 0), here]
        state = in_ref[i].astype(jnp.float32) + jnp.where(linked, decay, 0.0) * state
        out_ref[i + 1] = state.astype(out_ref.dtype)
        return state

    lax.fori_loop(0, count - 1, step, jnp.zeros(in_ref.shape[1:], jnp.float32), unroll=min(count - 1, 31))


def norm_kernel(here, facts, idcol, q_ref, s_ref, inner_ref, gain, out_ref, raw):
    tokens, width = q_ref.shape
    me = lax.axis_index("ctx") * lax.axis_size("uly") + lax.axis_index("uly")
    before = jnp.where(me > 0, facts[jnp.maximum(me - 1, 0), here], -1.0)
    lane = lax.broadcasted_iota(jnp.int32, (HD, LANES), 1)
    place = lax.broadcasted_iota(jnp.int32, (tokens, LANES), 0)
    age = jnp.where(idcol[...] == before, (place + 1).astype(jnp.float32), NEVER)
    total = jnp.zeros((tokens, LANES), jnp.float32)
    for j in range(width // LANES):
        columns = slice(j * LANES, (j + 1) * LANES)
        state = s_ref[j * HD : (j + 1) * HD, :]
        zero = jnp.zeros_like(state)
        square = jnp.concatenate(
            [jnp.where(lane < HD, state, zero), jnp.where(lane < HD, zero, state)], 0
        )
        outer = jnp.dot(q_ref[:, columns], square, preferred_element_type=jnp.float32)
        rate = pair_rate(facts, j, here)
        value = inner_ref[:, columns] + outer * jnp.exp(-rate * age)
        total += value * value
        raw[:, columns] = value
    mean = jnp.sum(total, axis=1, keepdims=True) / float(width)
    scale = jnp.broadcast_to(lax.rsqrt(mean + 1e-06), (tokens, LANES))
    for j in range(width // LANES):
        columns = slice(j * LANES, (j + 1) * LANES)
        out_ref[:, columns] = (raw[:, columns] * scale * gain[:, columns]).astype(jnp.bfloat16)


def local(queries, keys, values, doc_ids, decay_rate, norm_gain):
    tokens, width = queries.shape
    here = decay_rate.shape[0]
    axes = ("ctx", "uly")
    count = lax.axis_size("ctx") * lax.axis_size("uly")
    all_pairs = width // LANES
    steps = 4
    pairs = all_pairs // steps
    rows = all_pairs * HD // count

    smem = pl.BlockSpec(memory_space=pltpu.SMEM)
    vmem = pl.BlockSpec(memory_space=pltpu.VMEM)
    whole = lambda shape: pl.BlockSpec(shape, lambda i: (0,) * len(shape))
    part = pl.BlockSpec((tokens, pairs * LANES), lambda i: (0, i))
    params = pltpu.CompilerParams(vmem_limit_bytes=32 * 1024 * 1024)

    own = pl.pallas_call(
        facts_kernel,
        in_specs=[smem, smem],
        out_specs=vmem,
        out_shape=jax.ShapeDtypeStruct((count, LANES), jnp.float32),
        compiler_params=params,
        name="facts",
    )(decay_rate, doc_ids)
    facts = lax.all_to_all(own, axes, split_axis=0, concat_axis=0, tiled=True)
    turned, idrow, idcol = pl.pallas_call(
        turn_kernel,
        in_specs=[vmem, vmem],
        out_specs=[vmem, vmem, vmem],
        out_shape=[
            jax.ShapeDtypeStruct((width, LANES), jnp.float32),
            jax.ShapeDtypeStruct((8, LANES), jnp.float32),
            jax.ShapeDtypeStruct((tokens, LANES), jnp.float32),
        ],
        compiler_params=params,
        cost_estimate=pl.CostEstimate(flops=0, bytes_accessed=12_000_000, transcendentals=0),
        name="turn",
    )(doc_ids[None, :], keys)
    ends = pl.pallas_call(
        functools.partial(ends_kernel, here),
        in_specs=[smem, vmem, vmem, vmem],
        out_specs=vmem,
        out_shape=jax.ShapeDtypeStruct((all_pairs * HD, LANES), jnp.bfloat16),
        compiler_params=params,
        name="ends",
    )(facts, idrow, turned, values)
    pieces = lax.all_to_all(
        ends.reshape(count, rows, LANES), axes, split_axis=0, concat_axis=0, tiled=True
    )
    inner = pl.pallas_call(
        functools.partial(inner_kernel, here, pairs),
        grid=(steps,),
        in_specs=[smem, whole((tokens, LANES)), whole((8, LANES)), part, part, part],
        out_specs=part,
        out_shape=jax.ShapeDtypeStruct((tokens, width), jnp.float32),
        compiler_params=params,
        cost_estimate=pl.CostEstimate(
            flops=8_000_000_000, bytes_accessed=4_000_000, transcendentals=600_000
        ),
        name="inner",
    )(facts, idcol, idrow, queries, keys, values)
    before = pl.pallas_call(
        functools.partial(scan_kernel, here, tokens, rows),
        in_specs=[smem, vmem],
        out_specs=vmem,
        out_shape=jax.ShapeDtypeStruct((count, rows, LANES), jnp.bfloat16),
        compiler_params=params,
        name="scan",
    )(facts, pieces)
    states = lax.all_to_all(before, axes, split_axis=0, concat_axis=0, tiled=True)
    return pl.pallas_call(
        functools.partial(norm_kernel, here),
        in_specs=[smem, vmem, vmem, vmem, vmem, vmem],
        out_specs=vmem,
        out_shape=jax.ShapeDtypeStruct((tokens, width), jnp.bfloat16),
        scratch_shapes=[pltpu.VMEM((tokens, width), jnp.float32)],
        compiler_params=params,
        name="norm",
    )(facts, idcol, queries, states.reshape(all_pairs * HD, LANES), inner, norm_gain[None, :])


def solution(mesh):
    in_specs = (
        P(("ctx", "uly"), None),
        P(("ctx", "uly"), None),
        P(("ctx", "uly"), None),
        P(("ctx", "uly")),
        P("uly"),
        P(),
    )
    out_specs = P(("ctx", "uly"), None)
    return jax.shard_map(local, mesh=mesh, in_specs=in_specs, out_specs=out_specs, check_vma=False)
```

```python
import functools

import jax
import jax.numpy as jnp
from jax import lax
from jax.experimental import pallas as pl
from jax.experimental.pallas import tpu as pltpu
from jax.sharding import PartitionSpec as P

HD = 64
LANES = 2 * HD
NEVER = 1e9
BOTH_LAST = (((1,), (1,)), ((), ()))


def rate_of(facts, head, here):
    return facts[pl.ds(head // here, 1), head % here : head % here + 1]


def pair_rate(facts, pair, here):
    lane = lax.broadcasted_iota(jnp.int32, (1, LANES), 1)
    rates = []
    for head in (2 * pair, 2 * pair + 1):
        row = facts[pl.ds(lax.div(head, here), 1), :]
        rates.append(
            jnp.sum(jnp.where(lane == lax.rem(head, here), row, 0.0), axis=1, keepdims=True)
        )
    return jnp.where(lane < HD, rates[0], rates[1])


def turn_kernel(ids, k_ref, v_ref, turned, filled, idrow, idcol):
    tokens, width = k_ref.shape
    fill = jnp.full((1, LANES - tokens), -1.0, jnp.float32)
    row = jnp.concatenate([ids[...].astype(jnp.float32), fill], 1)
    idrow[...] = jnp.broadcast_to(row, idrow.shape)
    idcol[...] = jnp.transpose(jnp.broadcast_to(row, (LANES, LANES)))[:tokens]
    filled[:tokens, :] = v_ref[...]
    filled[tokens:, :] = jnp.zeros((LANES - tokens, width), filled.dtype)
    blank = jnp.zeros((LANES - tokens, LANES), jnp.float32)
    for j in range(width // LANES):
        columns = slice(j * LANES, (j + 1) * LANES)
        block = jnp.concatenate([k_ref[:, columns].astype(jnp.float32), blank], 0)
        turned[columns, :] = jnp.transpose(block)


def ends_kernel(here, tokens, facts, idrow, turned, v_ref, out_ref):
    width = v_ref.shape[1]
    lane = lax.broadcasted_iota(jnp.int32, (HD, LANES), 1)
    place = lax.broadcasted_iota(jnp.int32, idrow.shape, 1)
    ids = idrow[...]
    last = ids[:, tokens - 1 : tokens]
    age = jnp.where(ids == last, (tokens - 1 - place).astype(jnp.float32), NEVER)
    for j in range(width // LANES):
        weighted = []
        for head in (2 * j, 2 * j + 1):
            weight = jnp.exp(-rate_of(facts, head, here) * age)
            keys = turned[head * HD : (head + 1) * HD, :].reshape(HD // 8, 8, LANES)
            weighted.append((keys * weight[None]).reshape(HD, LANES))
        weighted = jnp.concatenate(weighted, 0)
        high = weighted.astype(jnp.bfloat16)
        low = (weighted - high.astype(jnp.float32)).astype(jnp.bfloat16)
        v = v_ref[:, j * LANES : (j + 1) * LANES]
        both = jnp.dot(
            jnp.concatenate([high, low], 1),
            jnp.concatenate([v, v], 0),
            preferred_element_type=jnp.float32,
        )
        out_ref[j * HD : (j + 1) * HD, :] = jnp.where(lane < HD, both[:HD], both[HD:]).astype(
            jnp.bfloat16
        )


def inner_kernel(
    here, pairs, rows, facts, idcol, idrow, q_ref, k_ref, v_ref, out_ref, fade_ref, link_ref
):
    tokens = k_ref.shape[0]
    step = pl.program_id(0)
    first = step * pairs
    me = lax.axis_index("ctx") * lax.axis_size("uly") + lax.axis_index("uly")

    @pl.when(step == 0)
    def _():
        last = facts[:, LANES - 1 :]
        earlier = jnp.concatenate([last[:1], last[:-1]], 0)
        decay = jnp.exp(-pair_rate(facts, lax.div(me * rows, HD), here) * float(tokens))
        link_ref[...] = jnp.where(last == earlier, decay, 0.0)

    lane = lax.broadcasted_iota(jnp.int32, (tokens, LANES), 1)
    place = lax.broadcasted_iota(jnp.int32, (tokens, LANES), 0)
    t = lax.broadcasted_iota(jnp.int32, (tokens, tokens), 0)
    s = lax.broadcasted_iota(jnp.int32, (tokens, tokens), 1)
    seen = (t >= s) & (idcol[:, :tokens] == idrow[:1, :tokens])
    age = jnp.where(seen, (t - s).astype(jnp.float32), NEVER)
    before = jnp.where(me > 0, facts[pl.ds(jnp.maximum(me - 1, 0), 1), LANES - 1 :], -1.0)
    since = jnp.where(idcol[...] == before, (place + 1).astype(jnp.float32), NEVER)
    for j in range(pairs):
        columns = slice(j * LANES, (j + 1) * LANES)
        q = q_ref[:, columns]
        zero = jnp.zeros_like(q)
        stacked = jnp.concatenate([jnp.where(lane < HD, q, zero), jnp.where(lane < HD, zero, q)], 0)
        scores = lax.dot_general(
            stacked, k_ref[:, columns], BOTH_LAST, preferred_element_type=jnp.float32
        )
        rates = [
            facts[
                pl.ds(lax.div(2 * (first + j) + one, here), 1),
                (2 * j + one) % here : (2 * j + one) % here + 1,
            ]
            for one in (0, 1)
        ]
        weight = jnp.concatenate([jnp.exp(-rate * age) for rate in rates], 0)
        probs = (scores * weight).astype(jnp.bfloat16)
        got = jnp.dot(probs, v_ref[:, columns], preferred_element_type=jnp.float32)
        out_ref[:, columns] = jnp.where(lane < HD, got[:tokens], got[tokens:])
        fade_ref[:, columns] = jnp.exp(-jnp.where(lane < HD, rates[0], rates[1]) * since)


def scan_kernel(link, in_ref, out_ref):
    count = in_ref.shape[0]
    out_ref[0] = jnp.zeros(out_ref.shape[1:], out_ref.dtype)

    def step(i, state):
        state = in_ref[i].astype(jnp.float32) + link[pl.ds(i, 1), :] * state
        out_ref[i + 1] = state.astype(out_ref.dtype)
        return state

    zero = jnp.zeros(in_ref.shape[1:], jnp.float32)
    lax.fori_loop(0, count - 1, step, zero, unroll=min(count - 1, 31))


def norm_kernel(q_ref, s_ref, inner_ref, fade_ref, gain, out_ref, raw, done, sems):
    tokens, width = q_ref.shape
    lane = lax.broadcasted_iota(jnp.int32, (HD, LANES), 1)
    zero = jnp.zeros((HD, LANES), s_ref.dtype)
    total = jnp.zeros((tokens, LANES), jnp.float32)
    for j in range(0, width // LANES, 2):
        square = []
        for one in (0, 1):
            state = s_ref[(j + one) * HD : (j + one + 1) * HD, :]
            for half in (jnp.where(lane < HD, state, zero), jnp.where(lane < HD, zero, state)):
                square.append(jnp.concatenate([zero, half] if one else [half, zero], 1))
        columns = slice(j * LANES, (j + 2) * LANES)
        outer = jnp.dot(
            q_ref[:, columns], jnp.concatenate(square, 0), preferred_element_type=jnp.float32
        )
        value = inner_ref[:, columns] + outer * fade_ref[:, columns]
        total += value[:, :LANES] * value[:, :LANES] + value[:, LANES:] * value[:, LANES:]
        raw[:, columns] = value
    mean = jnp.sum(total, axis=1, keepdims=True) / float(width)
    scale = jnp.broadcast_to(lax.rsqrt(mean + 1e-06), (tokens, LANES))
    parts = sems.shape[0]
    share = width // parts
    copies = []
    for part in range(parts):
        for at in range(part * share, (part + 1) * share, LANES):
            columns = slice(at, at + LANES)
            done[:, columns] = (raw[:, columns] * scale * gain[:, columns]).astype(jnp.bfloat16)
        columns = slice(part * share, (part + 1) * share)
        copies.append(
            pltpu.make_async_copy(done.at[:, columns], out_ref.at[:, columns], sems.at[part])
        )
        copies[-1].start()
    for copy in copies:
        copy.wait()


def local(queries, keys, values, doc_ids, decay_rate, norm_gain):
    tokens, width = queries.shape
    here = decay_rate.shape[0]
    axes = ("ctx", "uly")
    count = lax.axis_size("ctx") * lax.axis_size("uly")
    all_pairs = width // LANES
    steps = 4
    pairs = all_pairs // steps
    rows = all_pairs * HD // count

    vmem = pl.BlockSpec(memory_space=pltpu.VMEM)
    whole = lambda shape: pl.BlockSpec(shape, lambda i: (0,) * len(shape))
    part = pl.BlockSpec((tokens, pairs * LANES), lambda i: (0, i))
    params = pltpu.CompilerParams(vmem_limit_bytes=32 * 1024 * 1024)
    shape = jax.ShapeDtypeStruct

    own = jnp.pad(decay_rate, (0, LANES - here)) + jnp.pad(
        doc_ids.astype(jnp.float32), (LANES - tokens, 0)
    )
    facts = lax.all_to_all(
        jnp.broadcast_to(own[None, :], (count, LANES)), axes, split_axis=0, concat_axis=0, tiled=True
    )
    turned, filled, idrow, idcol = pl.pallas_call(
        turn_kernel,
        in_specs=[vmem] * 3,
        out_specs=[vmem] * 4,
        out_shape=[
            shape((width, LANES), jnp.float32),
            shape((LANES, width), jnp.bfloat16),
            shape((8, LANES), jnp.float32),
            shape((tokens, LANES), jnp.float32),
        ],
        compiler_params=params,
        cost_estimate=pl.CostEstimate(flops=0, bytes_accessed=12_000_000, transcendentals=0),
        name="turn",
    )(doc_ids[None, :], keys, values)
    ends = pl.pallas_call(
        functools.partial(ends_kernel, here, tokens),
        in_specs=[vmem] * 4,
        out_specs=vmem,
        out_shape=shape((all_pairs * HD, LANES), jnp.bfloat16),
        compiler_params=params,
        name="ends",
    )(facts, idrow, turned, filled)
    pieces = lax.all_to_all(
        ends.reshape(count, rows, LANES), axes, split_axis=0, concat_axis=0, tiled=True
    )
    inner, fade, link = pl.pallas_call(
        functools.partial(inner_kernel, here, pairs, rows),
        grid=(steps,),
        in_specs=[whole((count, LANES)), whole((tokens, LANES)), whole((8, LANES)), part, part, part],
        out_specs=[part, part, whole((count, LANES))],
        out_shape=[
            shape((tokens, width), jnp.float32),
            shape((tokens, width), jnp.float32),
            shape((count, LANES), jnp.float32),
        ],
        compiler_params=params,
        cost_estimate=pl.CostEstimate(
            flops=8_000_000_000, bytes_accessed=4_000_000, transcendentals=600_000
        ),
        name="inner",
    )(facts, idcol, idrow, queries, keys, values)
    before = pl.pallas_call(
        scan_kernel,
        in_specs=[vmem] * 2,
        out_specs=vmem,
        out_shape=shape((count, rows, LANES), jnp.bfloat16),
        compiler_params=params,
        name="scan",
    )(link, pieces)
    states = lax.all_to_all(before, axes, split_axis=0, concat_axis=0, tiled=True)
    return pl.pallas_call(
        norm_kernel,
        in_specs=[vmem] * 5,
        out_specs=pl.BlockSpec(memory_space=pl.ANY),
        out_shape=shape((tokens, width), jnp.bfloat16),
        scratch_shapes=[
            pltpu.VMEM((tokens, width), jnp.float32),
            pltpu.VMEM((tokens, width), jnp.bfloat16),
            pltpu.SemaphoreType.DMA((4,)),
        ],
        compiler_params=params,
        name="norm",
    )(queries, states.reshape(all_pairs * HD, LANES), inner, fade, norm_gain[None, :])


def solution(mesh):
    in_specs = (
        P(("ctx", "uly"), None),
        P(("ctx", "uly"), None),
        P(("ctx", "uly"), None),
        P(("ctx", "uly")),
        P("uly"),
        P(),
    )
    out_specs = P(("ctx", "uly"), None)
    return jax.shard_map(local, mesh=mesh, in_specs=in_specs, out_specs=out_specs, check_vma=False)
```

```python
import functools

import jax
import jax.numpy as jnp
from jax import lax
from jax.experimental import pallas as pl
from jax.experimental.pallas import tpu as pltpu
from jax.sharding import PartitionSpec as P

HD = 64
LANES = 2 * HD
NEVER = 1e9
BOTH_LAST = (((1,), (1,)), ((), ()))


def rate_of(facts, head, here):
    return facts[pl.ds(head // here, 1), head % here : head % here + 1]


def pair_rate(facts, pair, here):
    place = lax.broadcasted_iota(jnp.int32, (1, here), 1)
    lane = lax.broadcasted_iota(jnp.int32, (1, LANES), 1)
    rates = []
    for head in (2 * pair, 2 * pair + 1):
        row = facts[pl.ds(lax.div(head, here), 1), :]
        rates.append(
            jnp.sum(jnp.where(place == lax.rem(head, here), row, 0.0), axis=1, keepdims=True)
        )
    return jnp.where(lane < HD, rates[0], rates[1])


def turn_kernel(ids, k_ref, v_ref, turned, filled, idrow, idcol):
    tokens, width = k_ref.shape
    fill = jnp.full((1, LANES - tokens), -1.0, jnp.float32)
    row = jnp.concatenate([ids[...].astype(jnp.float32), fill], 1)
    idrow[...] = jnp.broadcast_to(row, idrow.shape)
    idcol[...] = jnp.transpose(jnp.broadcast_to(row, (LANES, LANES)))[:tokens]
    filled[:tokens, :] = v_ref[...]
    filled[tokens:, :] = jnp.zeros((LANES - tokens, width), filled.dtype)
    blank = jnp.zeros((LANES - tokens, LANES), jnp.float32)
    for j in range(width // LANES):
        columns = slice(j * LANES, (j + 1) * LANES)
        block = jnp.concatenate([k_ref[:, columns].astype(jnp.float32), blank], 0)
        turned[columns, :] = jnp.transpose(block)


def ends_kernel(here, tokens, rows, facts, idrow, turned, v_ref, out_ref):
    width = v_ref.shape[1]
    lane = lax.broadcasted_iota(jnp.int32, (HD, LANES), 1)
    place = lax.broadcasted_iota(jnp.int32, idrow.shape, 1)
    ids = idrow[...]
    last = ids[:, tokens - 1 : tokens]
    age = jnp.where(ids == last, (tokens - 1 - place).astype(jnp.float32), NEVER)
    for j in range(width // LANES):
        weighted = []
        for head in (2 * j, 2 * j + 1):
            weight = jnp.exp(-rate_of(facts, head, here) * age)
            keys = turned[head * HD : (head + 1) * HD, :].reshape(HD // 8, 8, LANES)
            weighted.append((keys * weight[None]).reshape(HD, LANES))
        weighted = jnp.concatenate(weighted, 0)
        high = weighted.astype(jnp.bfloat16)
        low = (weighted - high.astype(jnp.float32)).astype(jnp.bfloat16)
        v = v_ref[:, j * LANES : (j + 1) * LANES]
        both = jnp.dot(
            jnp.concatenate([high, low], 1),
            jnp.concatenate([v, v], 0),
            preferred_element_type=jnp.float32,
        )
        state = jnp.where(lane < HD, both[:HD], both[HD:])
        share = min(rows, HD)
        for at in range(0, HD, share):
            owner, start = divmod(j * HD + at, rows)
            out_ref[owner, start : start + share, :] = state[at : at + share].astype(jnp.bfloat16)
    mark = jnp.broadcast_to(last, (out_ref.shape[1] - rows, LANES)).astype(jnp.bfloat16)
    for owner in range(out_ref.shape[0]):
        out_ref[owner, rows:, :] = mark


def inner_kernel(
    here, pairs, rows, chunks, facts, idcol, idrow, earlier, q_ref, k_ref, v_ref,
    out_ref, fade_ref, one_ref, half_ref
):
    tokens = k_ref.shape[0]
    step = pl.program_id(0)
    first = step * pairs
    ctx, uly = lax.axis_index("ctx"), lax.axis_index("uly")

    @pl.when(step == 0)
    def _():
        owner = ctx * chunks + lax.rem(uly, chunks)
        share = min(rows, HD)
        for at in range(0, rows, share):
            rate = pair_rate(facts, lax.div(owner * rows + at, HD), here)
            for ref, length in ((one_ref, tokens), (half_ref, tokens * chunks)):
                ref[at : at + share, :] = jnp.broadcast_to(
                    jnp.exp(-rate * float(length)), (share, LANES)
                )

    lane = lax.broadcasted_iota(jnp.int32, (tokens, LANES), 1)
    place = lax.broadcasted_iota(jnp.int32, (tokens, LANES), 0)
    t = lax.broadcasted_iota(jnp.int32, (tokens, tokens), 0)
    s = lax.broadcasted_iota(jnp.int32, (tokens, tokens), 1)
    seen = (t >= s) & (idcol[:, :tokens] == idrow[:1, :tokens])
    age = jnp.where(seen, (t - s).astype(jnp.float32), NEVER)
    before = jnp.where(ctx + uly > 0, earlier[:1, tokens - 1 : tokens], -1.0)
    since = jnp.where(idcol[...] == before, (place + 1).astype(jnp.float32), NEVER)
    for j in range(pairs):
        columns = slice(j * LANES, (j + 1) * LANES)
        q = q_ref[:, columns]
        zero = jnp.zeros_like(q)
        stacked = jnp.concatenate([jnp.where(lane < HD, q, zero), jnp.where(lane < HD, zero, q)], 0)
        scores = lax.dot_general(
            stacked, k_ref[:, columns], BOTH_LAST, preferred_element_type=jnp.float32
        )
        rates = [
            facts[
                pl.ds(lax.div(2 * (first + j) + one, here), 1),
                (2 * j + one) % here : (2 * j + one) % here + 1,
            ]
            for one in (0, 1)
        ]
        weight = jnp.concatenate([jnp.exp(-rate * age) for rate in rates], 0)
        probs = (scores * weight).astype(jnp.bfloat16)
        got = jnp.dot(probs, v_ref[:, columns], preferred_element_type=jnp.float32)
        out_ref[:, columns] = jnp.where(lane < HD, got[:tokens], got[tokens:])
        fade_ref[:, columns] = jnp.exp(-jnp.where(lane < HD, rates[0], rates[1]) * since)


def few(count):
    return count if count <= 8 else 1


def half_kernel(chunks, one, in_ref, out_ref):
    count, rows = in_ref.shape[0], one.shape[0]

    def slice_end(c, _):
        start = c * chunks

        def step(j, carry):
            state, last = carry
            piece = in_ref[start + j]
            own = piece[rows : rows + 1].astype(jnp.float32)
            linked = jnp.where(own == last, one[...], 0.0)
            return (piece[:rows].astype(jnp.float32) + linked * state, own)

        piece = in_ref[start]
        begin = (piece[:rows].astype(jnp.float32), piece[rows : rows + 1].astype(jnp.float32))
        state, _ = lax.fori_loop(1, chunks, step, begin, unroll=few(chunks - 1))
        out_ref[c, :rows, :] = state.astype(out_ref.dtype)
        out_ref[c, rows:, :] = in_ref[start + chunks - 1][rows:]
        return 0

    lax.fori_loop(0, count // chunks, slice_end, 0, unroll=few(count // chunks))


def scan_kernel(chunks, one, half, in_ref, other, out_ref):
    count, rows = in_ref.shape[0], one.shape[0]
    later = lax.axis_index("uly") >= chunks

    def over_other(state, last, c, wanted):
        piece = other[c]
        own = piece[rows : rows + 1].astype(jnp.float32)
        linked = jnp.where(own == last, half[...], 0.0)
        moved = piece[:rows].astype(jnp.float32) + linked * state
        return jnp.where(wanted, moved, state), jnp.where(wanted, own, last)

    def over_slice(c, carry):
        carry = over_other(*carry, c, later)

        def step(j, carry):
            state, last = carry
            at = c * chunks + j
            out_ref[at] = state.astype(out_ref.dtype)
            piece = in_ref[at]
            own = piece[rows : rows + 1].astype(jnp.float32)
            linked = jnp.where(own == last, one[...], 0.0)
            return (piece[:rows].astype(jnp.float32) + linked * state, own)

        carry = lax.fori_loop(0, chunks, step, carry, unroll=few(chunks))
        return over_other(*carry, c, jnp.logical_not(later))

    begin = (jnp.zeros((rows, LANES), jnp.float32), jnp.full((1, LANES), -1.0, jnp.float32))
    lax.fori_loop(0, count // chunks, over_slice, begin, unroll=few(count // chunks))


def norm_kernel(q_ref, s_ref, inner_ref, fade_ref, gain, out_ref, raw, done, sems):
    tokens, width = q_ref.shape
    lane = lax.broadcasted_iota(jnp.int32, (HD, LANES), 1)
    zero = jnp.zeros((HD, LANES), s_ref.dtype)
    total = jnp.zeros((tokens, LANES), jnp.float32)
    for j in range(0, width // LANES, 2):
        square = []
        for one in (0, 1):
            state = s_ref[(j + one) * HD : (j + one + 1) * HD, :]
            for half in (jnp.where(lane < HD, state, zero), jnp.where(lane < HD, zero, state)):
                square.append(jnp.concatenate([zero, half] if one else [half, zero], 1))
        columns = slice(j * LANES, (j + 2) * LANES)
        outer = jnp.dot(
            q_ref[:, columns], jnp.concatenate(square, 0), preferred_element_type=jnp.float32
        )
        value = inner_ref[:, columns] + outer * fade_ref[:, columns]
        total += value[:, :LANES] * value[:, :LANES] + value[:, LANES:] * value[:, LANES:]
        raw[:, columns] = value
    mean = jnp.sum(total, axis=1, keepdims=True) / float(width)
    scale = jnp.broadcast_to(lax.rsqrt(mean + 1e-06), (tokens, LANES))
    parts = sems.shape[0]
    share = width // parts
    copies = []
    for part in range(parts):
        for at in range(part * share, (part + 1) * share, LANES):
            columns = slice(at, at + LANES)
            done[:, columns] = (raw[:, columns] * scale * gain[:, columns]).astype(jnp.bfloat16)
        columns = slice(part * share, (part + 1) * share)
        copies.append(
            pltpu.make_async_copy(done.at[:, columns], out_ref.at[:, columns], sems.at[part])
        )
        copies[-1].start()
    for copy in copies:
        copy.wait()


def local(queries, keys, values, doc_ids, decay_rate, norm_gain):
    tokens, width = queries.shape
    here = decay_rate.shape[0]
    axes = ("ctx", "uly")
    slices, members = lax.axis_size("ctx"), lax.axis_size("uly")
    chunks = members // 2
    group = slices * chunks
    all_pairs = width // LANES
    steps = 4
    pairs = all_pairs // steps
    rows = all_pairs * HD // group
    groups = [
        [c * members + half * chunks + u for c in range(slices) for u in range(chunks)]
        for half in (0, 1)
    ]
    device = lambda c, u: c * members + u
    swap = [
        (device(c, u), device(c, (u + chunks) % members))
        for c in range(slices)
        for u in range(members)
    ]
    forward = [(i, i + 1) for i in range(slices * members - 1)]

    vmem = pl.BlockSpec(memory_space=pltpu.VMEM)
    whole = lambda shape: pl.BlockSpec(shape, lambda i: (0,) * len(shape))
    part = pl.BlockSpec((tokens, pairs * LANES), lambda i: (0, i))
    params = pltpu.CompilerParams(vmem_limit_bytes=32 * 1024 * 1024)
    shape = jax.ShapeDtypeStruct

    facts = lax.all_to_all(
        jnp.broadcast_to(decay_rate[None, :], (members, here)),
        "uly", split_axis=0, concat_axis=0, tiled=True,
    )
    turned, filled, idrow, idcol = pl.pallas_call(
        turn_kernel,
        in_specs=[vmem] * 3,
        out_specs=[vmem] * 4,
        out_shape=[
            shape((width, LANES), jnp.float32),
            shape((LANES, width), jnp.bfloat16),
            shape((8, LANES), jnp.float32),
            shape((tokens, LANES), jnp.float32),
        ],
        compiler_params=params,
        cost_estimate=pl.CostEstimate(flops=0, bytes_accessed=12_000_000, transcendentals=0),
        name="turn",
    )(doc_ids[None, :], keys, values)
    earlier = lax.ppermute(idrow, axes, forward)
    ends = pl.pallas_call(
        functools.partial(ends_kernel, here, tokens, rows),
        in_specs=[vmem] * 4,
        out_specs=vmem,
        out_shape=shape((group, rows + 8, LANES), jnp.bfloat16),
        compiler_params=params,
        name="ends",
    )(facts, idrow, turned, filled)
    pieces = lax.all_to_all(
        ends, axes, split_axis=0, concat_axis=0, axis_index_groups=groups, tiled=True
    )
    inner, fade, one, half = pl.pallas_call(
        functools.partial(inner_kernel, here, pairs, rows, chunks),
        grid=(steps,),
        in_specs=[
            whole((members, here)), whole((tokens, LANES)), whole((8, LANES)), whole((8, LANES)),
            part, part, part,
        ],
        out_specs=[part, part, whole((rows, LANES)), whole((rows, LANES))],
        out_shape=[
            shape((tokens, width), jnp.float32),
            shape((tokens, width), jnp.float32),
            shape((rows, LANES), jnp.float32),
            shape((rows, LANES), jnp.float32),
        ],
        compiler_params=params,
        cost_estimate=pl.CostEstimate(
            flops=8_000_000_000, bytes_accessed=4_000_000, transcendentals=600_000
        ),
        name="inner",
    )(facts, idcol, idrow, earlier, queries, keys, values)
    halves = pl.pallas_call(
        functools.partial(half_kernel, chunks),
        in_specs=[vmem] * 2,
        out_specs=vmem,
        out_shape=shape((slices, rows + 8, LANES), jnp.bfloat16),
        compiler_params=params,
        name="half",
    )(one, pieces)
    other = lax.ppermute(halves, axes, swap)
    before = pl.pallas_call(
        functools.partial(scan_kernel, chunks),
        in_specs=[vmem] * 4,
        out_specs=vmem,
        out_shape=shape((group, rows, LANES), jnp.bfloat16),
        compiler_params=params,
        name="scan",
    )(one, half, pieces, other)
    states = lax.all_to_all(
        before, axes, split_axis=0, concat_axis=0, axis_index_groups=groups, tiled=True
    )
    return pl.pallas_call(
        norm_kernel,
        in_specs=[vmem] * 5,
        out_specs=pl.BlockSpec(memory_space=pl.ANY),
        out_shape=shape((tokens, width), jnp.bfloat16),
        scratch_shapes=[
            pltpu.VMEM((tokens, width), jnp.float32),
            pltpu.VMEM((tokens, width), jnp.bfloat16),
            pltpu.SemaphoreType.DMA((4,)),
        ],
        compiler_params=params,
        name="norm",
    )(queries, states.reshape(all_pairs * HD, LANES), inner, fade, norm_gain[None, :])


def solution(mesh):
    in_specs = (
        P(("ctx", "uly"), None),
        P(("ctx", "uly"), None),
        P(("ctx", "uly"), None),
        P(("ctx", "uly")),
        P("uly"),
        P(),
    )
    out_specs = P(("ctx", "uly"), None)
    return jax.shard_map(local, mesh=mesh, in_specs=in_specs, out_specs=out_specs, check_vma=False)
```

```python
import functools

import jax
import jax.numpy as jnp
from jax import lax
from jax.experimental import pallas as pl
from jax.experimental.pallas import tpu as pltpu
from jax.sharding import PartitionSpec as P

HD = 64
LANES = 2 * HD
NEVER = 1e9


def rate_of(facts, head, here):
    return facts[pl.ds(head // here, 1), head % here : head % here + 1]


def pair_rate(facts, pair, here):
    place = lax.broadcasted_iota(jnp.int32, (1, here), 1)
    lane = lax.broadcasted_iota(jnp.int32, (1, LANES), 1)
    rates = []
    for head in (2 * pair, 2 * pair + 1):
        row = facts[pl.ds(lax.div(head, here), 1), :]
        rates.append(
            jnp.sum(jnp.where(place == lax.rem(head, here), row, 0.0), axis=1, keepdims=True)
        )
    return jnp.where(lane < HD, rates[0], rates[1])


def turn_kernel(ids, k_ref, v_ref, turned, filled, idrow, idcol, ids_here, keys, sems):
    tokens, width = k_ref.shape
    parts = sems.shape[0] - 2
    share = width // parts
    copies = [pltpu.make_async_copy(ids, ids_here, sems.at[parts])]
    for part in range(parts):
        columns = slice(part * share, (part + 1) * share)
        copies.append(
            pltpu.make_async_copy(k_ref.at[:, columns], keys.at[:, columns], sems.at[part])
        )
    copies.append(pltpu.make_async_copy(v_ref, filled.at[:tokens, :], sems.at[parts + 1]))
    for copy in copies:
        copy.start()
    filled[tokens:, :] = jnp.zeros((LANES - tokens, width), filled.dtype)
    copies[0].wait()
    fill = jnp.full((1, LANES - tokens), -1.0, jnp.float32)
    row = jnp.concatenate([ids_here[...].astype(jnp.float32), fill], 1)
    idrow[...] = jnp.broadcast_to(row, idrow.shape)
    idcol[...] = jnp.transpose(jnp.broadcast_to(row, (LANES, LANES)))[:tokens]
    blank = jnp.zeros((LANES - tokens, LANES), jnp.float32)
    for part in range(parts):
        copies[part + 1].wait()
        for at in range(part * share, (part + 1) * share, LANES):
            columns = slice(at, at + LANES)
            block = jnp.concatenate([keys[:, columns].astype(jnp.float32), blank], 0)
            turned[columns, :] = jnp.transpose(block)
    copies[-1].wait()


def ends_kernel(here, tokens, rows, facts, idrow, turned, v_ref, out_ref):
    width = v_ref.shape[1]
    lane = lax.broadcasted_iota(jnp.int32, (HD, LANES), 1)
    place = lax.broadcasted_iota(jnp.int32, idrow.shape, 1)
    ids = idrow[...]
    last = ids[:, tokens - 1 : tokens]
    age = jnp.where(ids == last, (tokens - 1 - place).astype(jnp.float32), NEVER)
    for j in range(width // LANES):
        weighted = []
        for head in (2 * j, 2 * j + 1):
            weight = jnp.exp(-rate_of(facts, head, here) * age)
            keys = turned[head * HD : (head + 1) * HD, :].reshape(HD // 8, 8, LANES)
            weighted.append((keys * weight[None]).reshape(HD, LANES))
        weighted = jnp.concatenate(weighted, 0)
        high = weighted.astype(jnp.bfloat16)
        low = (weighted - high.astype(jnp.float32)).astype(jnp.bfloat16)
        v = v_ref[:, j * LANES : (j + 1) * LANES]
        both = jnp.dot(
            jnp.concatenate([high, low], 1),
            jnp.concatenate([v, v], 0),
            preferred_element_type=jnp.float32,
        )
        state = jnp.where(lane < HD, both[:HD], both[HD:])
        share = min(rows, HD)
        for at in range(0, HD, share):
            owner, start = divmod(j * HD + at, rows)
            out_ref[owner, start : start + share, :] = state[at : at + share].astype(jnp.bfloat16)
    mark = jnp.broadcast_to(last, (out_ref.shape[1] - rows, LANES)).astype(jnp.bfloat16)
    for owner in range(out_ref.shape[0]):
        out_ref[owner, rows:, :] = mark


def inner_kernel(
    here, rows, chunks, facts, idcol, idrow, q_ref, turned, v_ref, out_ref, one_ref, half_ref, rates_ref
):
    tokens, width = q_ref.shape
    owner = lax.axis_index("ctx") * chunks + lax.rem(lax.axis_index("uly"), chunks)
    share = min(rows, HD)
    for at in range(0, rows, share):
        rate = pair_rate(facts, lax.div(owner * rows + at, HD), here)
        for ref, length in ((one_ref, tokens), (half_ref, tokens * chunks)):
            ref[at : at + share, :] = jnp.broadcast_to(
                jnp.exp(-rate * float(length)), (share, LANES)
            )
    lane = lax.broadcasted_iota(jnp.int32, (tokens, LANES), 1)
    t = lax.broadcasted_iota(jnp.int32, (tokens, LANES), 0)
    seen = (t >= lane) & (idcol[...] == idrow[:1, :])
    age = jnp.where(seen, (t - lane).astype(jnp.float32), NEVER)
    for j in range(width // LANES):
        columns = slice(j * LANES, (j + 1) * LANES)
        q = q_ref[:, columns]
        zero = jnp.zeros_like(q)
        stacked = jnp.concatenate([jnp.where(lane < HD, q, zero), jnp.where(lane < HD, zero, q)], 0)
        scores = jnp.dot(
            stacked, turned[columns, :].astype(jnp.bfloat16), preferred_element_type=jnp.float32
        )
        rates = [rate_of(facts, 2 * j + one, here) for one in (0, 1)]
        weight = jnp.concatenate([jnp.exp(-rate * age) for rate in rates], 0)
        probs = (scores * weight).astype(jnp.bfloat16)
        got = jnp.dot(probs, v_ref[:, columns], preferred_element_type=jnp.float32)
        out_ref[:, columns] = jnp.where(lane < HD, got[:tokens], got[tokens:])
        rates_ref[:, columns] = jnp.where(lane[:1] < HD, rates[0], rates[1])


def few(count):
    return count if count <= 8 else 1


def half_kernel(chunks, one, in_ref, out_ref):
    count, rows = in_ref.shape[0], one.shape[0]

    def slice_end(c, _):
        start = c * chunks

        def step(j, carry):
            state, last = carry
            piece = in_ref[start + j]
            own = piece[rows : rows + 1].astype(jnp.float32)
            linked = jnp.where(own == last, one[...], 0.0)
            return (piece[:rows].astype(jnp.float32) + linked * state, own)

        piece = in_ref[start]
        begin = (piece[:rows].astype(jnp.float32), piece[rows : rows + 1].astype(jnp.float32))
        state, _ = lax.fori_loop(1, chunks, step, begin, unroll=few(chunks - 1))
        out_ref[c, :rows, :] = state.astype(out_ref.dtype)
        out_ref[c, rows:, :] = in_ref[start + chunks - 1][rows:]
        return 0

    lax.fori_loop(0, count // chunks, slice_end, 0, unroll=few(count // chunks))


def scan_kernel(chunks, one, half, in_ref, other, out_ref):
    count, rows = in_ref.shape[0], one.shape[0]
    marks = (out_ref.shape[1] - rows, LANES)
    later = lax.axis_index("uly") >= chunks

    def over_other(state, last, c, wanted):
        piece = other[c]
        own = piece[rows : rows + 1].astype(jnp.float32)
        linked = jnp.where(own == last, half[...], 0.0)
        moved = piece[:rows].astype(jnp.float32) + linked * state
        return jnp.where(wanted, moved, state), jnp.where(wanted, own, last)

    def over_slice(c, carry):
        carry = over_other(*carry, c, later)

        def step(j, carry):
            state, last = carry
            at = c * chunks + j
            out_ref[at, :rows, :] = state.astype(out_ref.dtype)
            out_ref[at, rows:, :] = jnp.broadcast_to(last, marks).astype(out_ref.dtype)
            piece = in_ref[at]
            own = piece[rows : rows + 1].astype(jnp.float32)
            linked = jnp.where(own == last, one[...], 0.0)
            return (piece[:rows].astype(jnp.float32) + linked * state, own)

        carry = lax.fori_loop(0, chunks, step, carry, unroll=few(chunks))
        return over_other(*carry, c, jnp.logical_not(later))

    begin = (jnp.zeros((rows, LANES), jnp.float32), jnp.full((1, LANES), -1.0, jnp.float32))
    lax.fori_loop(0, count // chunks, over_slice, begin, unroll=few(count // chunks))


def norm_kernel(rows, idcol, rates, q_ref, s_ref, inner_ref, gain, out_ref, raw, done, sems):
    tokens, width = q_ref.shape
    lane = lax.broadcasted_iota(jnp.int32, (HD, LANES), 1)
    place = lax.broadcasted_iota(jnp.int32, (tokens, LANES), 0)
    before = s_ref[0, rows : rows + 8, :].astype(jnp.float32)[:1]
    age = jnp.where(idcol[...] == before, (place + 1).astype(jnp.float32), NEVER)
    zero = jnp.zeros((HD, LANES), s_ref.dtype)
    total = jnp.zeros((tokens, LANES), jnp.float32)
    share = min(rows, HD)
    for j in range(0, width // LANES, 2):
        square = []
        for one in (0, 1):
            state = [
                s_ref[at // rows, at % rows : at % rows + share, :]
                for at in range((j + one) * HD, (j + one + 1) * HD, share)
            ]
            if len(state) > 1:
                state = [jnp.concatenate([s.astype(jnp.float32) for s in state], 0).astype(zero.dtype)]
            state = state[0]
            for half in (jnp.where(lane < HD, state, zero), jnp.where(lane < HD, zero, state)):
                square.append(jnp.concatenate([zero, half] if one else [half, zero], 1))
        columns = slice(j * LANES, (j + 2) * LANES)
        outer = jnp.dot(
            q_ref[:, columns], jnp.concatenate(square, 0), preferred_element_type=jnp.float32
        )
        for one in (0, 1):
            columns = slice((j + one) * LANES, (j + one + 1) * LANES)
            fade = jnp.exp(-rates[:, columns] * age)
            value = inner_ref[:, columns] + outer[:, one * LANES : (one + 1) * LANES] * fade
            total += value * value
            raw[:, columns] = value
    mean = jnp.sum(total, axis=1, keepdims=True) / float(width)
    scale = jnp.broadcast_to(lax.rsqrt(mean + 1e-06), (tokens, LANES))
    parts = sems.shape[0]
    share = width // parts
    copies = []
    for part in range(parts):
        for at in range(part * share, (part + 1) * share, LANES):
            columns = slice(at, at + LANES)
            done[:, columns] = (raw[:, columns] * scale * gain[:, columns]).astype(jnp.bfloat16)
        columns = slice(part * share, (part + 1) * share)
        copies.append(
            pltpu.make_async_copy(done.at[:, columns], out_ref.at[:, columns], sems.at[part])
        )
        copies[-1].start()
    for copy in copies:
        copy.wait()


def local(queries, keys, values, doc_ids, decay_rate, norm_gain):
    tokens, width = queries.shape
    here = decay_rate.shape[0]
    axes = ("ctx", "uly")
    slices, members = lax.axis_size("ctx"), lax.axis_size("uly")
    chunks = members // 2
    group = slices * chunks
    all_pairs = width // LANES
    rows = all_pairs * HD // group
    groups = [
        [c * members + half * chunks + u for c in range(slices) for u in range(chunks)]
        for half in (0, 1)
    ]
    device = lambda c, u: c * members + u
    swap = [
        (device(c, u), device(c, (u + chunks) % members))
        for c in range(slices)
        for u in range(members)
    ]

    vmem = pl.BlockSpec(memory_space=pltpu.VMEM)
    params = pltpu.CompilerParams(vmem_limit_bytes=32 * 1024 * 1024)
    shape = jax.ShapeDtypeStruct

    facts = lax.all_to_all(
        jnp.broadcast_to(decay_rate[None, :], (members, here)),
        "uly", split_axis=0, concat_axis=0, tiled=True,
    )
    turned, filled, idrow, idcol = pl.pallas_call(
        turn_kernel,
        in_specs=[pl.BlockSpec(memory_space=pltpu.HBM)] * 3,
        out_specs=[vmem] * 4,
        out_shape=[
            shape((width, LANES), jnp.float32),
            shape((LANES, width), jnp.bfloat16),
            shape((8, LANES), jnp.float32),
            shape((tokens, LANES), jnp.float32),
        ],
        scratch_shapes=[
            pltpu.VMEM((1, tokens), jnp.int32),
            pltpu.VMEM((tokens, width), jnp.bfloat16),
            pltpu.SemaphoreType.DMA((6,)),
        ],
        compiler_params=params,
        cost_estimate=pl.CostEstimate(flops=0, bytes_accessed=12_000_000, transcendentals=0),
        name="turn",
    )(doc_ids[None, :], keys, values)
    ends = pl.pallas_call(
        functools.partial(ends_kernel, here, tokens, rows),
        in_specs=[vmem] * 4,
        out_specs=vmem,
        out_shape=shape((group, rows + 8, LANES), jnp.bfloat16),
        compiler_params=params,
        name="ends",
    )(facts, idrow, turned, filled)
    pieces = lax.all_to_all(
        ends, axes, split_axis=0, concat_axis=0, axis_index_groups=groups, tiled=True
    )
    inner, one, half, rates = pl.pallas_call(
        functools.partial(inner_kernel, here, rows, chunks),
        in_specs=[vmem] * 6,
        out_specs=[vmem] * 4,
        out_shape=[
            shape((tokens, width), jnp.float32),
            shape((rows, LANES), jnp.float32),
            shape((rows, LANES), jnp.float32),
            shape((1, width), jnp.float32),
        ],
        compiler_params=params,
        cost_estimate=pl.CostEstimate(
            flops=8_000_000_000, bytes_accessed=4_000_000, transcendentals=600_000
        ),
        name="inner",
    )(facts, idcol, idrow, queries, turned, filled)
    halves = pl.pallas_call(
        functools.partial(half_kernel, chunks),
        in_specs=[vmem] * 2,
        out_specs=vmem,
        out_shape=shape((slices, rows + 8, LANES), jnp.bfloat16),
        compiler_params=params,
        name="half",
    )(one, pieces)
    other = lax.ppermute(halves, axes, swap)
    before = pl.pallas_call(
        functools.partial(scan_kernel, chunks),
        in_specs=[vmem] * 4,
        out_specs=vmem,
        out_shape=shape((group, rows + 8, LANES), jnp.bfloat16),
        compiler_params=params,
        name="scan",
    )(one, half, pieces, other)
    states = lax.all_to_all(
        before, axes, split_axis=0, concat_axis=0, axis_index_groups=groups, tiled=True
    )
    return pl.pallas_call(
        functools.partial(norm_kernel, rows),
        in_specs=[vmem] * 6,
        out_specs=pl.BlockSpec(memory_space=pl.ANY),
        out_shape=shape((tokens, width), jnp.bfloat16),
        scratch_shapes=[
            pltpu.VMEM((tokens, width), jnp.float32),
            pltpu.VMEM((tokens, width), jnp.bfloat16),
            pltpu.SemaphoreType.DMA((4,)),
        ],
        compiler_params=params,
        name="norm",
    )(idcol, rates, queries, states, inner, norm_gain[None, :])


def solution(mesh):
    in_specs = (
        P(("ctx", "uly"), None),
        P(("ctx", "uly"), None),
        P(("ctx", "uly"), None),
        P(("ctx", "uly")),
        P("uly"),
        P(),
    )
    out_specs = P(("ctx", "uly"), None)
    return jax.shard_map(local, mesh=mesh, in_specs=in_specs, out_specs=out_specs, check_vma=False)
```

```python
import functools

import jax
import jax.numpy as jnp
from jax import lax
from jax.experimental import pallas as pl
from jax.experimental.pallas import tpu as pltpu
from jax.sharding import PartitionSpec as P

HD = 64
LANES = 2 * HD
NEVER = 1e9


def rate_of(facts, head, here):
    return facts[head // here : head // here + 1, head % here : head % here + 1]


def pair_rate(facts, pair, here):
    lane = lax.broadcasted_iota(jnp.int32, (1, LANES), 1)
    rates = []
    for head in (2 * pair, 2 * pair + 1):
        row = facts[pl.ds(lax.div(head, here), 1), :]
        rates.append(
            jnp.sum(jnp.where(lane == lax.rem(head, here), row, 0.0), axis=1, keepdims=True)
        )
    return jnp.where(lane < HD, rates[0], rates[1])


def pair_kernel(rates, ids, next_rates, next_ids, out_ref):
    here, tokens = rates.shape[1], ids.shape[1]
    me = lax.axis_index("uly")
    place = lax.broadcasted_iota(jnp.int32, out_ref.shape, 0)
    out = jnp.zeros(out_ref.shape, jnp.float32)
    for member, rate, document in ((me, rates, ids), (me ^ 1, next_rates, next_ids)):
        last = document[:, tokens - 1 :].astype(jnp.float32)
        row = jnp.concatenate([rate[...], jnp.broadcast_to(last, (1, LANES - here))], 1)
        out = jnp.where(place == member, row, out)
    out_ref[...] = out


def turn_kernel(ids, k_ref, v_ref, turned, filled, idrow, idcol, ids_here, keys, sems):
    tokens, width = k_ref.shape
    parts = sems.shape[0] - 2
    share = width // parts
    copies = [pltpu.make_async_copy(ids, ids_here, sems.at[parts])]
    for part in range(parts):
        columns = slice(part * share, (part + 1) * share)
        copies.append(
            pltpu.make_async_copy(k_ref.at[:, columns], keys.at[:, columns], sems.at[part])
        )
    copies.append(pltpu.make_async_copy(v_ref, filled.at[:tokens, :], sems.at[parts + 1]))
    for copy in copies:
        copy.start()
    filled[tokens:, :] = jnp.zeros((LANES - tokens, width), filled.dtype)
    copies[0].wait()
    fill = jnp.full((1, LANES - tokens), -1.0, jnp.float32)
    row = jnp.concatenate([ids_here[...].astype(jnp.float32), fill], 1)
    idrow[...] = jnp.broadcast_to(row, idrow.shape)
    idcol[...] = jnp.transpose(jnp.broadcast_to(row, (LANES, LANES)))[:tokens]
    blank = jnp.zeros((LANES - tokens, LANES), jnp.float32)
    for part in range(parts):
        copies[part + 1].wait()
        for at in range(part * share, (part + 1) * share, LANES):
            columns = slice(at, at + LANES)
            block = jnp.concatenate([keys[:, columns].astype(jnp.float32), blank], 0)
            turned[columns, :] = jnp.transpose(block)
    copies[-1].wait()


def ends_kernel(here, tokens, known, found, idrow, turned, v_ref, out_ref):
    width = v_ref.shape[1]
    facts = known[...] + found[...]
    lane = lax.broadcasted_iota(jnp.int32, (HD, LANES), 1)
    place = lax.broadcasted_iota(jnp.int32, idrow.shape, 1)
    ids = idrow[...]
    last = ids[:, tokens - 1 : tokens]
    age = jnp.where(ids == last, (tokens - 1 - place).astype(jnp.float32), NEVER)
    for j in range(width // LANES):
        weighted = []
        for head in (2 * j, 2 * j + 1):
            weight = jnp.exp(-rate_of(facts, head, here) * age)
            keys = turned[head * HD : (head + 1) * HD, :].reshape(HD // 8, 8, LANES)
            weighted.append((keys * weight[None]).reshape(HD, LANES))
        weighted = jnp.concatenate(weighted, 0)
        high = weighted.astype(jnp.bfloat16)
        low = (weighted - high.astype(jnp.float32)).astype(jnp.bfloat16)
        v = v_ref[:, j * LANES : (j + 1) * LANES]
        both = jnp.dot(
            jnp.concatenate([high, low], 1),
            jnp.concatenate([v, v], 0),
            preferred_element_type=jnp.float32,
        )
        out_ref[j * HD : (j + 1) * HD, :] = jnp.where(lane < HD, both[:HD], both[HD:]).astype(
            jnp.bfloat16
        )


def inner_kernel(
    here, known, found, idcol, idrow, q_ref, turned, v_ref, ends, out_ref, facts, rates_ref
):
    tokens, width = q_ref.shape
    facts[...] = known[...] + found[...]
    lane = lax.broadcasted_iota(jnp.int32, (tokens, LANES), 1)
    t = lax.broadcasted_iota(jnp.int32, (tokens, LANES), 0)
    seen = (t >= lane) & (idcol[...] == idrow[:1, :])
    age = jnp.where(seen, (t - lane).astype(jnp.float32), NEVER)
    for j in range(width // LANES):
        columns = slice(j * LANES, (j + 1) * LANES)
        q = q_ref[:, columns]
        zero = jnp.zeros_like(q)
        stacked = jnp.concatenate([jnp.where(lane < HD, q, zero), jnp.where(lane < HD, zero, q)], 0)
        scores = jnp.dot(
            stacked, turned[columns, :].astype(jnp.bfloat16), preferred_element_type=jnp.float32
        )
        rates = [rate_of(facts, 2 * j + one, here) for one in (0, 1)]
        weight = jnp.concatenate([jnp.exp(-rate * age) for rate in rates], 0)
        probs = (scores * weight).astype(jnp.bfloat16)
        got = jnp.dot(probs, v_ref[:, columns], preferred_element_type=jnp.float32)
        out_ref[:, columns] = jnp.where(lane < HD, got[:tokens], got[tokens:])
        rates_ref[:, columns] = jnp.where(lane[:1] < HD, rates[0], rates[1])


def link_kernel(here, tokens, rows, facts, *refs):
    others, (link, before, last) = refs[:-3], refs[-3:]
    members, slices = facts.shape[0], len(others) + 1
    ctx, uly = lax.axis_index("ctx"), lax.axis_index("uly")
    for back, tile in enumerate((facts, *others)):
        at = lax.rem(ctx + slices - back, slices) * members
        last[pl.ds(pl.multiple_of(at, members), members), :] = jnp.broadcast_to(
            tile[:, LANES - 1 :], (members, LANES)
        )
    me = ctx * members + uly
    decay = jnp.exp(-pair_rate(facts, lax.div(me * rows, HD), here) * float(tokens))
    now = last[...]
    then = jnp.concatenate([now[:1], now[:-1]], 0)
    link[...] = jnp.where(now == then, decay, 0.0)
    before[...] = jnp.where(me > 0, last[pl.ds(jnp.maximum(me - 1, 0), 1), :], -1.0)


def scan_kernel(link, in_ref, out_ref):
    count = in_ref.shape[0]
    out_ref[0] = jnp.zeros(out_ref.shape[1:], out_ref.dtype)

    def step(i, state):
        state = in_ref[i].astype(jnp.float32) + link[pl.ds(i, 1), :] * state
        out_ref[i + 1] = state.astype(out_ref.dtype)
        return state

    zero = jnp.zeros(in_ref.shape[1:], jnp.float32)
    lax.fori_loop(0, count - 1, step, zero, unroll=min(count - 1, 31))


def norm_kernel(idcol, before, rates, q_ref, s_ref, inner_ref, gain, out_ref, raw, done, sems):
    tokens, width = q_ref.shape
    lane = lax.broadcasted_iota(jnp.int32, (HD, LANES), 1)
    place = lax.broadcasted_iota(jnp.int32, (tokens, LANES), 0)
    age = jnp.where(idcol[...] == before[...], (place + 1).astype(jnp.float32), NEVER)
    zero = jnp.zeros((HD, LANES), s_ref.dtype)
    total = jnp.zeros((tokens, LANES), jnp.float32)
    for j in range(0, width // LANES, 2):
        square = []
        for one in (0, 1):
            state = s_ref[(j + one) * HD : (j + one + 1) * HD, :]
            for half in (jnp.where(lane < HD, state, zero), jnp.where(lane < HD, zero, state)):
                square.append(jnp.concatenate([zero, half] if one else [half, zero], 1))
        columns = slice(j * LANES, (j + 2) * LANES)
        outer = jnp.dot(
            q_ref[:, columns], jnp.concatenate(square, 0), preferred_element_type=jnp.float32
        )
        for one in (0, 1):
            columns = slice((j + one) * LANES, (j + one + 1) * LANES)
            fade = jnp.exp(-rates[:, columns] * age)
            value = inner_ref[:, columns] + outer[:, one * LANES : (one + 1) * LANES] * fade
            total += value * value
            raw[:, columns] = value
    mean = jnp.sum(total, axis=1, keepdims=True) / float(width)
    scale = jnp.broadcast_to(lax.rsqrt(mean + 1e-06), (tokens, LANES))
    parts = sems.shape[0]
    share = width // parts
    copies = []
    for part in range(parts):
        for at in range(part * share, (part + 1) * share, LANES):
            columns = slice(at, at + LANES)
            done[:, columns] = (raw[:, columns] * scale * gain[:, columns]).astype(jnp.bfloat16)
        columns = slice(part * share, (part + 1) * share)
        copies.append(
            pltpu.make_async_copy(done.at[:, columns], out_ref.at[:, columns], sems.at[part])
        )
        copies[-1].start()
    for copy in copies:
        copy.wait()


def local(queries, keys, values, doc_ids, decay_rate, norm_gain):
    tokens, width = queries.shape
    here = decay_rate.shape[0]
    axes = ("ctx", "uly")
    slices, members = lax.axis_size("ctx"), lax.axis_size("uly")
    count = slices * members
    all_pairs = width // LANES
    rows = all_pairs * HD // count

    vmem = pl.BlockSpec(memory_space=pltpu.VMEM)
    params = pltpu.CompilerParams(vmem_limit_bytes=32 * 1024 * 1024)
    shape = jax.ShapeDtypeStruct
    tile = shape((members, LANES), jnp.float32)

    def swapped(value, reach):
        return lax.ppermute(value, "uly", [(u, u ^ reach) for u in range(members)])

    next_rates, next_ids = swapped(decay_rate, 1), swapped(doc_ids, 1)
    known = pl.pallas_call(
        pair_kernel,
        in_specs=[vmem] * 4,
        out_specs=vmem,
        out_shape=tile,
        compiler_params=params,
        name="pair",
    )(decay_rate[None, :], doc_ids[None, :], next_rates[None, :], next_ids[None, :])
    reach, found = 2, jnp.zeros(tile.shape, tile.dtype)
    while reach < members:
        known = known + found if reach > 2 else known
        found = swapped(known, reach)
        reach *= 2

    turned, filled, idrow, idcol = pl.pallas_call(
        turn_kernel,
        in_specs=[pl.BlockSpec(memory_space=pl.ANY)] * 3,
        out_specs=[vmem] * 4,
        out_shape=[
            shape((width, LANES), jnp.float32),
            shape((LANES, width), jnp.bfloat16),
            shape((8, LANES), jnp.float32),
            shape((tokens, LANES), jnp.float32),
        ],
        scratch_shapes=[
            pltpu.VMEM((1, tokens), jnp.int32),
            pltpu.VMEM((tokens, width), jnp.bfloat16),
            pltpu.SemaphoreType.DMA((6,)),
        ],
        compiler_params=params,
        cost_estimate=pl.CostEstimate(flops=0, bytes_accessed=12_000_000, transcendentals=0),
        name="turn",
    )(doc_ids[None, :], keys, values)
    ends = pl.pallas_call(
        functools.partial(ends_kernel, here, tokens),
        in_specs=[vmem] * 5,
        out_specs=vmem,
        out_shape=shape((all_pairs * HD, LANES), jnp.bfloat16),
        compiler_params=params,
        name="ends",
    )(known, found, idrow, turned, filled)
    pieces = lax.all_to_all(
        ends.reshape(count, rows, LANES), axes, split_axis=0, concat_axis=0, tiled=True
    )
    inner, facts, rates = pl.pallas_call(
        functools.partial(inner_kernel, here),
        in_specs=[vmem] * 7 + [pl.BlockSpec(memory_space=pl.ANY)],
        out_specs=[vmem] * 3,
        out_shape=[shape((tokens, width), jnp.float32), tile, shape((1, width), jnp.float32)],
        compiler_params=params,
        cost_estimate=pl.CostEstimate(
            flops=8_000_000_000, bytes_accessed=4_000_000, transcendentals=600_000
        ),
        name="inner",
    )(known, found, idcol, idrow, queries, turned, filled, ends)
    others = [
        lax.ppermute(facts, "ctx", [(c, (c + ahead) % slices) for c in range(slices)])
        for ahead in range(1, slices)
    ]
    link, before = pl.pallas_call(
        functools.partial(link_kernel, here, tokens, rows),
        in_specs=[vmem] * slices,
        out_specs=[vmem] * 2,
        out_shape=[shape((count, LANES), jnp.float32), shape((1, LANES), jnp.float32)],
        scratch_shapes=[pltpu.VMEM((count, LANES), jnp.float32)],
        compiler_params=params,
        name="link",
    )(facts, *others)
    moved = pl.pallas_call(
        scan_kernel,
        in_specs=[vmem] * 2,
        out_specs=vmem,
        out_shape=shape((count, rows, LANES), jnp.bfloat16),
        compiler_params=params,
        name="scan",
    )(link, pieces)
    states = lax.all_to_all(moved, axes, split_axis=0, concat_axis=0, tiled=True)
    return pl.pallas_call(
        norm_kernel,
        in_specs=[vmem] * 7,
        out_specs=pl.BlockSpec(memory_space=pl.ANY),
        out_shape=shape((tokens, width), jnp.bfloat16),
        scratch_shapes=[
            pltpu.VMEM((tokens, width), jnp.float32),
            pltpu.VMEM((tokens, width), jnp.bfloat16),
            pltpu.SemaphoreType.DMA((4,)),
        ],
        compiler_params=params,
        name="norm",
    )(idcol, before, rates, queries, states.reshape(all_pairs * HD, LANES), inner, norm_gain[None, :])


def solution(mesh):
    in_specs = (
        P(("ctx", "uly"), None),
        P(("ctx", "uly"), None),
        P(("ctx", "uly"), None),
        P(("ctx", "uly")),
        P("uly"),
        P(),
    )
    out_specs = P(("ctx", "uly"), None)
    return jax.shard_map(local, mesh=mesh, in_specs=in_specs, out_specs=out_specs, check_vma=False)
```

```python
import functools

import jax
import jax.numpy as jnp
from jax import lax
from jax.experimental import pallas as pl
from jax.experimental.pallas import tpu as pltpu
from jax.sharding import PartitionSpec as P

HD = 64
LANES = 2 * HD
NEVER = 1e9


def rate_of(facts, head, here):
    return facts[head // here : head // here + 1, head % here : head % here + 1]


def pair_rate(facts, pair, here):
    lane = lax.broadcasted_iota(jnp.int32, (1, LANES), 1)
    rates = []
    for head in (2 * pair, 2 * pair + 1):
        row = facts[pl.ds(lax.div(head, here), 1), :]
        rates.append(
            jnp.sum(jnp.where(lane == lax.rem(head, here), row, 0.0), axis=1, keepdims=True)
        )
    return jnp.where(lane < HD, rates[0], rates[1])


def turn_kernel(row_ref, k_ref, v_ref, turned, filled, idrow, idcol):
    tokens, width = k_ref.shape
    fill = jnp.full((1, LANES - tokens), -1.0, jnp.float32)
    row = jnp.concatenate([row_ref[:, LANES - tokens :], fill], 1)
    idrow[...] = jnp.broadcast_to(row, idrow.shape)
    idcol[...] = jnp.transpose(jnp.broadcast_to(row, (LANES, LANES)))[:tokens]
    filled[:tokens, :] = v_ref[...]
    filled[tokens:, :] = jnp.zeros((LANES - tokens, width), filled.dtype)
    blank = jnp.zeros((LANES - tokens, LANES), jnp.float32)
    for j in range(width // LANES):
        columns = slice(j * LANES, (j + 1) * LANES)
        block = jnp.concatenate([k_ref[:, columns].astype(jnp.float32), blank], 0)
        turned[columns, :] = jnp.transpose(block).astype(turned.dtype)


def ends_kernel(here, tokens, idrow, turned, v_ref, *refs):
    width = v_ref.shape[1]
    rows, (out_ref, facts) = refs[:-2], refs[-2:]
    place = lax.broadcasted_iota(jnp.int32, facts.shape, 0)
    tile = jnp.zeros(facts.shape, jnp.float32)
    for apart, row in enumerate(rows):
        tile = jnp.where(place == lax.axis_index("uly") ^ apart, row[...], tile)
    facts[...] = tile
    lane = lax.broadcasted_iota(jnp.int32, (HD, LANES), 1)
    place = lax.broadcasted_iota(jnp.int32, idrow.shape, 1)
    ids = idrow[...]
    last = ids[:, tokens - 1 : tokens]
    age = jnp.where(ids == last, (tokens - 1 - place).astype(jnp.float32), NEVER)
    for j in range(width // LANES):
        weighted = []
        for head in (2 * j, 2 * j + 1):
            weight = jnp.exp(-rate_of(facts, head, here) * age)
            keys = turned[head * HD : (head + 1) * HD, :].astype(jnp.float32)
            keys = keys.reshape(HD // 8, 8, LANES) * weight[None]
            weighted.append(keys.reshape(HD, LANES))
        weighted = jnp.concatenate(weighted, 0)
        high = weighted.astype(jnp.bfloat16)
        low = (weighted - high.astype(jnp.float32)).astype(jnp.bfloat16)
        v = v_ref[:, j * LANES : (j + 1) * LANES]
        both = jnp.dot(
            jnp.concatenate([high, low], 1),
            jnp.concatenate([v, v], 0),
            preferred_element_type=jnp.float32,
        )
        out_ref[j * HD : (j + 1) * HD, :] = jnp.where(lane < HD, both[:HD], both[HD:]).astype(
            jnp.bfloat16
        )


def inner_kernel(
    here, facts, idcol, idrow, q_ref, turned, v_ref, out_ref, tile_ref, rates_ref
):
    tokens, width = q_ref.shape
    tile_ref[...] = facts[...]
    lane = lax.broadcasted_iota(jnp.int32, (tokens, LANES), 1)
    t = lax.broadcasted_iota(jnp.int32, (tokens, LANES), 0)
    seen = (t >= lane) & (idcol[...] == idrow[:1, :])
    age = jnp.where(seen, (t - lane).astype(jnp.float32), NEVER)
    for j in range(width // LANES):
        columns = slice(j * LANES, (j + 1) * LANES)
        q = q_ref[:, columns]
        zero = jnp.zeros_like(q)
        stacked = jnp.concatenate([jnp.where(lane < HD, q, zero), jnp.where(lane < HD, zero, q)], 0)
        scores = jnp.dot(
            stacked, turned[columns, :], preferred_element_type=jnp.float32
        )
        rates = [rate_of(facts, 2 * j + one, here) for one in (0, 1)]
        weight = jnp.concatenate([jnp.exp(-rate * age) for rate in rates], 0)
        probs = (scores * weight).astype(jnp.bfloat16)
        got = jnp.dot(probs, v_ref[:, columns], preferred_element_type=jnp.float32)
        out_ref[:, columns] = jnp.where(lane < HD, got[:tokens], got[tokens:])
        rates_ref[:, columns] = jnp.where(lane[:1] < HD, rates[0], rates[1])


def link_kernel(here, tokens, rows, facts, *refs):
    others, (link, before, last) = refs[:-3], refs[-3:]
    members, slices = facts.shape[0], len(others) + 1
    ctx, uly = lax.axis_index("ctx"), lax.axis_index("uly")
    for back, tile in enumerate((facts, *others)):
        at = lax.rem(ctx + slices - back, slices) * members
        last[pl.ds(pl.multiple_of(at, members), members), :] = jnp.broadcast_to(
            tile[:, LANES - 1 :], (members, LANES)
        )
    me = ctx * members + uly
    decay = jnp.exp(-pair_rate(facts, lax.div(me * rows, HD), here) * float(tokens))
    now = last[...]
    then = jnp.concatenate([now[:1], now[:-1]], 0)
    link[...] = jnp.where(now == then, decay, 0.0)
    before[...] = jnp.where(me > 0, last[pl.ds(jnp.maximum(me - 1, 0), 1), :], -1.0)


def scan_kernel(link, in_ref, out_ref):
    count = in_ref.shape[0]
    out_ref[0] = jnp.zeros(out_ref.shape[1:], out_ref.dtype)

    def step(i, state):
        state = in_ref[i].astype(jnp.float32) + link[pl.ds(i, 1), :] * state
        out_ref[i + 1] = state.astype(out_ref.dtype)
        return state

    zero = jnp.zeros(in_ref.shape[1:], jnp.float32)
    lax.fori_loop(0, count - 1, step, zero, unroll=min(count - 1, 31))


def norm_kernel(idcol, before, rates, q_ref, s_ref, inner_ref, gain, out_ref, raw, done, sems):
    tokens, width = q_ref.shape
    lane = lax.broadcasted_iota(jnp.int32, (HD, LANES), 1)
    place = lax.broadcasted_iota(jnp.int32, (tokens, LANES), 0)
    age = jnp.where(idcol[...] == before[...], (place + 1).astype(jnp.float32), NEVER)
    zero = jnp.zeros((HD, LANES), s_ref.dtype)
    total = jnp.zeros((tokens, LANES), jnp.float32)
    for j in range(0, width // LANES, 2):
        square = []
        for one in (0, 1):
            state = s_ref[(j + one) * HD : (j + one + 1) * HD, :]
            for half in (jnp.where(lane < HD, state, zero), jnp.where(lane < HD, zero, state)):
                square.append(jnp.concatenate([zero, half] if one else [half, zero], 1))
        columns = slice(j * LANES, (j + 2) * LANES)
        outer = jnp.dot(
            q_ref[:, columns], jnp.concatenate(square, 0), preferred_element_type=jnp.float32
        )
        for one in (0, 1):
            columns = slice((j + one) * LANES, (j + one + 1) * LANES)
            fade = jnp.exp(-rates[:, columns] * age)
            value = inner_ref[:, columns] + outer[:, one * LANES : (one + 1) * LANES] * fade
            total += value * value
            raw[:, columns] = value
    mean = jnp.sum(total, axis=1, keepdims=True) / float(width)
    scale = jnp.broadcast_to(lax.rsqrt(mean + 1e-06), (tokens, LANES))
    parts = sems.shape[0]
    share = width // parts
    copies = []
    for part in range(parts):
        for at in range(part * share, (part + 1) * share, LANES):
            columns = slice(at, at + LANES)
            done[:, columns] = (raw[:, columns] * scale * gain[:, columns]).astype(jnp.bfloat16)
        columns = slice(part * share, (part + 1) * share)
        copies.append(
            pltpu.make_async_copy(done.at[:, columns], out_ref.at[:, columns], sems.at[part])
        )
        copies[-1].start()
    for copy in copies:
        copy.wait()


def local(queries, keys, values, doc_ids, decay_rate, norm_gain):
    tokens, width = queries.shape
    here = decay_rate.shape[0]
    axes = ("ctx", "uly")
    slices, members = lax.axis_size("ctx"), lax.axis_size("uly")
    count = slices * members
    all_pairs = width // LANES
    rows = all_pairs * HD // count

    vmem = pl.BlockSpec(memory_space=pltpu.VMEM)
    params = pltpu.CompilerParams(vmem_limit_bytes=32 * 1024 * 1024)
    shape = jax.ShapeDtypeStruct
    tile = shape((members, LANES), jnp.float32)

    row = jnp.pad(decay_rate, (0, LANES - here)) + jnp.pad(
        doc_ids, (LANES - tokens, 0)
    ).astype(jnp.float32)
    rows_of = [row] + [
        lax.ppermute(row, "uly", [(u, u ^ apart) for u in range(members)])
        for apart in range(1, members)
    ]
    turned, filled, idrow, idcol = pl.pallas_call(
        turn_kernel,
        in_specs=[vmem] * 3,
        out_specs=[vmem] * 4,
        out_shape=[
            shape((width, LANES), jnp.bfloat16),
            shape((LANES, width), jnp.bfloat16),
            shape((8, LANES), jnp.float32),
            shape((tokens, LANES), jnp.float32),
        ],
        compiler_params=params,
        cost_estimate=pl.CostEstimate(flops=0, bytes_accessed=12_000_000, transcendentals=0),
        name="turn",
    )(row[None, :], keys, values)
    ends, facts = pl.pallas_call(
        functools.partial(ends_kernel, here, tokens),
        in_specs=[vmem] * (3 + members),
        out_specs=[vmem] * 2,
        out_shape=[shape((all_pairs * HD, LANES), jnp.bfloat16), tile],
        compiler_params=params,
        name="ends",
    )(idrow, turned, filled, *[found[None, :] for found in rows_of])
    pieces = lax.all_to_all(
        ends.reshape(count, rows, LANES), axes, split_axis=0, concat_axis=0, tiled=True
    )
    inner, slice_facts, rates = pl.pallas_call(
        functools.partial(inner_kernel, here),
        in_specs=[vmem] * 6,
        out_specs=[vmem] * 3,
        out_shape=[shape((tokens, width), jnp.float32), tile, shape((1, width), jnp.float32)],
        compiler_params=params,
        cost_estimate=pl.CostEstimate(
            flops=8_000_000_000, bytes_accessed=4_000_000, transcendentals=600_000
        ),
        name="inner",
    )(facts, idcol, idrow, queries, turned, filled)
    others = [
        lax.ppermute(slice_facts, "ctx", [(c, (c + ahead) % slices) for c in range(slices)])
        for ahead in range(1, slices)
    ]
    link, before = pl.pallas_call(
        functools.partial(link_kernel, here, tokens, rows),
        in_specs=[vmem] * slices,
        out_specs=[vmem] * 2,
        out_shape=[shape((count, LANES), jnp.float32), shape((1, LANES), jnp.float32)],
        scratch_shapes=[pltpu.VMEM((count, LANES), jnp.float32)],
        compiler_params=params,
        name="link",
    )(slice_facts, *others)
    moved = pl.pallas_call(
        scan_kernel,
        in_specs=[vmem] * 2,
        out_specs=vmem,
        out_shape=shape((count, rows, LANES), jnp.bfloat16),
        compiler_params=params,
        name="scan",
    )(link, pieces)
    states = lax.all_to_all(moved, axes, split_axis=0, concat_axis=0, tiled=True)
    return pl.pallas_call(
        norm_kernel,
        in_specs=[vmem] * 7,
        out_specs=pl.BlockSpec(memory_space=pl.ANY),
        out_shape=shape((tokens, width), jnp.bfloat16),
        scratch_shapes=[
            pltpu.VMEM((tokens, width), jnp.float32),
            pltpu.VMEM((tokens, width), jnp.bfloat16),
            pltpu.SemaphoreType.DMA((4,)),
        ],
        compiler_params=params,
        name="norm",
    )(idcol, before, rates, queries, states.reshape(all_pairs * HD, LANES), inner, norm_gain[None, :])


def solution(mesh):
    in_specs = (
        P(("ctx", "uly"), None),
        P(("ctx", "uly"), None),
        P(("ctx", "uly"), None),
        P(("ctx", "uly")),
        P("uly"),
        P(),
    )
    out_specs = P(("ctx", "uly"), None)
    return jax.shard_map(local, mesh=mesh, in_specs=in_specs, out_specs=out_specs, check_vma=False)
```

```python
import functools

import jax
import jax.numpy as jnp
from jax import lax
from jax.experimental import pallas as pl
from jax.experimental.pallas import tpu as pltpu
from jax.sharding import PartitionSpec as P

HD = 64
LANES = 2 * HD
NEVER = 1e9


def rate_of(facts, head, here):
    return facts[head // here : head // here + 1, head % here : head % here + 1]


def pair_rate(facts, pair, here):
    lane = lax.broadcasted_iota(jnp.int32, (1, LANES), 1)
    rates = []
    for head in (2 * pair, 2 * pair + 1):
        row = facts[pl.ds(lax.div(head, here), 1), :]
        rates.append(
            jnp.sum(jnp.where(lane == lax.rem(head, here), row, 0.0), axis=1, keepdims=True)
        )
    return jnp.where(lane < HD, rates[0], rates[1])


def turn_kernel(row_ref, k_ref, v_ref, turned, filled, idrow, idcol):
    tokens, width = k_ref.shape
    fill = jnp.full((1, LANES - tokens), -1.0, jnp.float32)
    row = jnp.concatenate([row_ref[:1, LANES - tokens :], fill], 1)
    idrow[...] = jnp.broadcast_to(row, idrow.shape)
    idcol[...] = jnp.transpose(jnp.broadcast_to(row, (LANES, LANES)))[:tokens]
    filled[:tokens, :] = v_ref[...]
    filled[tokens:, :] = jnp.zeros((LANES - tokens, width), filled.dtype)
    blank = jnp.zeros((LANES - tokens, LANES), jnp.float32)
    for j in range(width // LANES):
        columns = slice(j * LANES, (j + 1) * LANES)
        block = jnp.concatenate([k_ref[:, columns].astype(jnp.float32), blank], 0)
        turned[columns, :] = jnp.transpose(block).astype(turned.dtype)


def ends_kernel(here, tokens, facts, idrow, turned, v_ref, out_ref):
    width = v_ref.shape[1]
    lane = lax.broadcasted_iota(jnp.int32, (HD, LANES), 1)
    place = lax.broadcasted_iota(jnp.int32, idrow.shape, 1)
    ids = idrow[...]
    last = ids[:, tokens - 1 : tokens]
    age = jnp.where(ids == last, (tokens - 1 - place).astype(jnp.float32), NEVER)
    for j in range(width // LANES):
        weighted = []
        for head in (2 * j, 2 * j + 1):
            weight = jnp.exp(-rate_of(facts, head, here) * age)
            keys = turned[head * HD : (head + 1) * HD, :].astype(jnp.float32)
            keys = keys.reshape(HD // 8, 8, LANES) * weight[None]
            weighted.append(keys.reshape(HD, LANES))
        weighted = jnp.concatenate(weighted, 0)
        high = weighted.astype(jnp.bfloat16)
        low = (weighted - high.astype(jnp.float32)).astype(jnp.bfloat16)
        v = v_ref[:, j * LANES : (j + 1) * LANES]
        both = jnp.dot(
            jnp.concatenate([high, low], 1),
            jnp.concatenate([v, v], 0),
            preferred_element_type=jnp.float32,
        )
        out_ref[j * HD : (j + 1) * HD, :] = jnp.where(lane < HD, both[:HD], both[HD:]).astype(
            jnp.bfloat16
        )


def inner_kernel(
    here, facts, idcol, idrow, q_ref, turned, v_ref, out_ref, tile_ref, rates_ref
):
    tokens, width = q_ref.shape
    tile_ref[...] = facts[...]
    lane = lax.broadcasted_iota(jnp.int32, (tokens, LANES), 1)
    t = lax.broadcasted_iota(jnp.int32, (tokens, LANES), 0)
    seen = (t >= lane) & (idcol[...] == idrow[:1, :])
    age = jnp.where(seen, (t - lane).astype(jnp.float32), NEVER)
    for j in range(width // LANES):
        columns = slice(j * LANES, (j + 1) * LANES)
        q = q_ref[:, columns]
        zero = jnp.zeros_like(q)
        stacked = jnp.concatenate([jnp.where(lane < HD, q, zero), jnp.where(lane < HD, zero, q)], 0)
        scores = jnp.dot(
            stacked, turned[columns, :], preferred_element_type=jnp.float32
        )
        rates = [rate_of(facts, 2 * j + one, here) for one in (0, 1)]
        weight = jnp.concatenate([jnp.exp(-rate * age) for rate in rates], 0)
        probs = (scores * weight)[:, :tokens].astype(jnp.bfloat16)
        got = jnp.dot(probs, v_ref[:, columns], preferred_element_type=jnp.float32)
        out_ref[:, columns] = jnp.where(lane < HD, got[:tokens], got[tokens:])
        rates_ref[:, columns] = jnp.where(lane[:1] < HD, rates[0], rates[1])


def link_kernel(here, tokens, rows, facts, *refs):
    others, (link, before, last) = refs[:-3], refs[-3:]
    members, slices = facts.shape[0], len(others) + 1
    ctx, uly = lax.axis_index("ctx"), lax.axis_index("uly")
    for back, tile in enumerate((facts, *others)):
        at = lax.rem(ctx + slices - back, slices) * members
        last[pl.ds(pl.multiple_of(at, members), members), :] = jnp.broadcast_to(
            tile[:, LANES - 1 :], (members, LANES)
        )
    me = ctx * members + uly
    decay = jnp.exp(-pair_rate(facts, lax.div(me * rows, HD), here) * float(tokens))
    now = last[...]
    then = jnp.concatenate([now[:1], now[:-1]], 0)
    link[...] = jnp.where(now == then, decay, 0.0)
    before[...] = jnp.where(me > 0, last[pl.ds(jnp.maximum(me - 1, 0), 1), :], -1.0)


def scan_kernel(link, in_ref, out_ref):
    count = in_ref.shape[0]
    out_ref[0] = jnp.zeros(out_ref.shape[1:], out_ref.dtype)

    def step(i, state):
        state = in_ref[i].astype(jnp.float32) + link[pl.ds(i, 1), :] * state
        out_ref[i + 1] = state.astype(out_ref.dtype)
        return state

    zero = jnp.zeros(in_ref.shape[1:], jnp.float32)
    lax.fori_loop(0, count - 1, step, zero, unroll=min(count - 1, 31))


def norm_kernel(idcol, before, rates, q_ref, s_ref, inner_ref, gain, out_ref, raw, done, sems):
    tokens, width = q_ref.shape
    lane = lax.broadcasted_iota(jnp.int32, (HD, LANES), 1)
    place = lax.broadcasted_iota(jnp.int32, (tokens, LANES), 0)
    age = jnp.where(idcol[...] == before[...], (place + 1).astype(jnp.float32), NEVER)
    zero = jnp.zeros((HD, LANES), s_ref.dtype)
    total = jnp.zeros((tokens, LANES), jnp.float32)
    for j in range(0, width // LANES, 2):
        square = []
        for one in (0, 1):
            state = s_ref[(j + one) * HD : (j + one + 1) * HD, :]
            for half in (jnp.where(lane < HD, state, zero), jnp.where(lane < HD, zero, state)):
                square.append(jnp.concatenate([zero, half] if one else [half, zero], 1))
        columns = slice(j * LANES, (j + 2) * LANES)
        outer = jnp.dot(
            q_ref[:, columns], jnp.concatenate(square, 0), preferred_element_type=jnp.float32
        )
        for one in (0, 1):
            columns = slice((j + one) * LANES, (j + one + 1) * LANES)
            fade = jnp.exp(-rates[:, columns] * age)
            value = inner_ref[:, columns] + outer[:, one * LANES : (one + 1) * LANES] * fade
            total += value * value
            raw[:, columns] = value
    mean = jnp.sum(total, axis=1, keepdims=True) / float(width)
    scale = jnp.broadcast_to(lax.rsqrt(mean + 1e-06), (tokens, LANES))
    parts = sems.shape[0]
    share = width // parts
    copies = []
    for part in range(parts):
        for at in range(part * share, (part + 1) * share, LANES):
            columns = slice(at, at + LANES)
            done[:, columns] = (raw[:, columns] * scale * gain[:, columns]).astype(jnp.bfloat16)
        columns = slice(part * share, (part + 1) * share)
        copies.append(
            pltpu.make_async_copy(done.at[:, columns], out_ref.at[:, columns], sems.at[part])
        )
        copies[-1].start()
    for copy in copies:
        copy.wait()


def local(queries, keys, values, doc_ids, decay_rate, norm_gain):
    tokens, width = queries.shape
    here = decay_rate.shape[0]
    axes = ("ctx", "uly")
    slices, members = lax.axis_size("ctx"), lax.axis_size("uly")
    count = slices * members
    all_pairs = width // LANES
    rows = all_pairs * HD // count

    vmem = pl.BlockSpec(memory_space=pltpu.VMEM)
    params = pltpu.CompilerParams(vmem_limit_bytes=32 * 1024 * 1024)
    shape = jax.ShapeDtypeStruct
    tile = shape((members, LANES), jnp.float32)

    own = jnp.pad(decay_rate, (0, LANES - here)) + jnp.pad(
        doc_ids, (LANES - tokens, 0)
    ).astype(jnp.float32)
    facts = lax.all_to_all(
        jnp.broadcast_to(own[None, :], tile.shape), "uly", split_axis=0, concat_axis=0, tiled=True
    )
    turned, filled, idrow, idcol = pl.pallas_call(
        turn_kernel,
        in_specs=[vmem] * 3,
        out_specs=[vmem] * 4,
        out_shape=[
            shape((width, LANES), jnp.bfloat16),
            shape((LANES, width), jnp.bfloat16),
            shape((8, LANES), jnp.float32),
            shape((tokens, LANES), jnp.float32),
        ],
        compiler_params=params,
        cost_estimate=pl.CostEstimate(flops=0, bytes_accessed=12_000_000, transcendentals=0),
        name="turn",
    )(own[None, :], keys, values)
    ends = pl.pallas_call(
        functools.partial(ends_kernel, here, tokens),
        in_specs=[vmem] * 4,
        out_specs=vmem,
        out_shape=shape((all_pairs * HD, LANES), jnp.bfloat16),
        compiler_params=params,
        name="ends",
    )(facts, idrow, turned, filled)
    pieces = lax.all_to_all(
        ends.reshape(count, rows, LANES), axes, split_axis=0, concat_axis=0, tiled=True
    )
    inner, slice_facts, rates = pl.pallas_call(
        functools.partial(inner_kernel, here),
        in_specs=[vmem] * 6,
        out_specs=[vmem] * 3,
        out_shape=[shape((tokens, width), jnp.float32), tile, shape((1, width), jnp.float32)],
        compiler_params=params,
        cost_estimate=pl.CostEstimate(
            flops=8_000_000_000, bytes_accessed=4_000_000, transcendentals=600_000
        ),
        name="inner",
    )(facts, idcol, idrow, queries, turned, values)
    others = [
        lax.ppermute(slice_facts, "ctx", [(c, (c + ahead) % slices) for c in range(slices)])
        for ahead in range(1, slices)
    ]
    link, before = pl.pallas_call(
        functools.partial(link_kernel, here, tokens, rows),
        in_specs=[vmem] * slices,
        out_specs=[vmem] * 2,
        out_shape=[shape((count, LANES), jnp.float32), shape((1, LANES), jnp.float32)],
        scratch_shapes=[pltpu.VMEM((count, LANES), jnp.float32)],
        compiler_params=params,
        name="link",
    )(slice_facts, *others)
    moved = pl.pallas_call(
        scan_kernel,
        in_specs=[vmem] * 2,
        out_specs=vmem,
        out_shape=shape((count, rows, LANES), jnp.bfloat16),
        compiler_params=params,
        name="scan",
    )(link, pieces)
    states = lax.all_to_all(moved, axes, split_axis=0, concat_axis=0, tiled=True)
    return pl.pallas_call(
        norm_kernel,
        in_specs=[vmem] * 7,
        out_specs=pl.BlockSpec(memory_space=pl.ANY),
        out_shape=shape((tokens, width), jnp.bfloat16),
        scratch_shapes=[
            pltpu.VMEM((tokens, width), jnp.float32),
            pltpu.VMEM((tokens, width), jnp.bfloat16),
            pltpu.SemaphoreType.DMA((4,)),
        ],
        compiler_params=params,
        name="norm",
    )(idcol, before, rates, queries, states.reshape(all_pairs * HD, LANES), inner, norm_gain[None, :])


def solution(mesh):
    in_specs = (
        P(("ctx", "uly"), None),
        P(("ctx", "uly"), None),
        P(("ctx", "uly"), None),
        P(("ctx", "uly")),
        P("uly"),
        P(),
    )
    out_specs = P(("ctx", "uly"), None)
    return jax.shard_map(local, mesh=mesh, in_specs=in_specs, out_specs=out_specs, check_vma=False)
```

```python
import functools

import jax
import jax.numpy as jnp
from jax import lax
from jax.experimental import pallas as pl
from jax.experimental.pallas import tpu as pltpu
from jax.sharding import PartitionSpec as P

HD = 64
LANES = 2 * HD
NEVER = 1e9


def rate_of(facts, head, here):
    return facts[head // here : head // here + 1, head % here : head % here + 1]


def pair_rate(facts, pair, here):
    lane = lax.broadcasted_iota(jnp.int32, (1, LANES), 1)
    rates = []
    for head in (2 * pair, 2 * pair + 1):
        row = facts[pl.ds(lax.div(head, here), 1), :]
        rates.append(
            jnp.sum(jnp.where(lane == lax.rem(head, here), row, 0.0), axis=1, keepdims=True)
        )
    return jnp.where(lane < HD, rates[0], rates[1])


def turn_kernel(row_ref, k_ref, v_ref, turned, filled, idrow, idcol):
    tokens, width = k_ref.shape
    fill = jnp.full((1, LANES - tokens), -1.0, jnp.float32)
    row = jnp.concatenate([row_ref[:1, LANES - tokens :], fill], 1)
    idrow[...] = jnp.broadcast_to(row, idrow.shape)
    idcol[...] = jnp.transpose(jnp.broadcast_to(row, (LANES, LANES)))[:tokens]
    filled[:tokens, :] = v_ref[...]
    filled[tokens:, :] = jnp.zeros((LANES - tokens, width), filled.dtype)
    blank = jnp.zeros((LANES - tokens, LANES), jnp.float32)
    for j in range(width // LANES):
        columns = slice(j * LANES, (j + 1) * LANES)
        block = jnp.concatenate([k_ref[:, columns].astype(jnp.float32), blank], 0)
        turned[columns, :] = jnp.transpose(block).astype(turned.dtype)


def ends_kernel(here, tokens, facts, idrow, turned, v_ref, out_ref):
    width = v_ref.shape[1]
    lane = lax.broadcasted_iota(jnp.int32, (HD, LANES), 1)
    place = lax.broadcasted_iota(jnp.int32, idrow.shape, 1)
    ids = idrow[...]
    last = ids[:, tokens - 1 : tokens]
    age = jnp.where(ids == last, (tokens - 1 - place).astype(jnp.float32), NEVER)
    for j in range(width // LANES):
        weighted = []
        for head in (2 * j, 2 * j + 1):
            weight = jnp.exp(-rate_of(facts, head, here) * age)
            keys = turned[head * HD : (head + 1) * HD, :].astype(jnp.float32)
            keys = keys.reshape(HD // 8, 8, LANES) * weight[None]
            weighted.append(keys.reshape(HD, LANES))
        weighted = jnp.concatenate(weighted, 0)
        high = weighted.astype(jnp.bfloat16)
        low = (weighted - high.astype(jnp.float32)).astype(jnp.bfloat16)
        v = v_ref[:, j * LANES : (j + 1) * LANES]
        both = jnp.dot(
            jnp.concatenate([high, low], 1),
            jnp.concatenate([v, v], 0),
            preferred_element_type=jnp.float32,
        )
        out_ref[j * HD : (j + 1) * HD, :] = jnp.where(lane < HD, both[:HD], both[HD:]).astype(
            jnp.bfloat16
        )


def inner_kernel(
    here, facts, idcol, idrow, q_ref, turned, v_ref, out_ref, tile_ref, rates_ref
):
    tokens, width = q_ref.shape
    tile_ref[...] = facts[...]
    lane = lax.broadcasted_iota(jnp.int32, (tokens, LANES), 1)
    t = lax.broadcasted_iota(jnp.int32, (tokens, LANES), 0)
    seen = (t >= lane) & (idcol[...] == idrow[:1, :])
    age = jnp.where(seen, (t - lane).astype(jnp.float32), NEVER)
    for j in range(width // LANES):
        columns = slice(j * LANES, (j + 1) * LANES)
        q = q_ref[:, columns]
        zero = jnp.zeros_like(q)
        stacked = jnp.concatenate([jnp.where(lane < HD, q, zero), jnp.where(lane < HD, zero, q)], 0)
        scores = jnp.dot(
            stacked, turned[columns, :], preferred_element_type=jnp.float32
        )
        rates = [rate_of(facts, 2 * j + one, here) for one in (0, 1)]
        weight = jnp.concatenate([jnp.exp(-rate * age) for rate in rates], 0)
        probs = (scores * weight)[:, :tokens].astype(jnp.bfloat16)
        got = jnp.dot(probs, v_ref[:, columns], preferred_element_type=jnp.float32)
        out_ref[:, columns] = jnp.where(lane < HD, got[:tokens], got[tokens:])
        rates_ref[:, columns] = jnp.where(lane[:1] < HD, rates[0], rates[1])


def few(count):
    return count if count <= 8 else 1


def link_kernel(here, tokens, chunks, facts, *refs):
    others, (linked, through, one, half, before, last) = refs[:-6], refs[-6:]
    members, slices = facts.shape[0], len(others) + 1
    ctx, uly = lax.axis_index("ctx"), lax.axis_index("uly")
    for back, tile in enumerate((facts, *others)):
        at = lax.rem(ctx + slices - back, slices) * members
        last[pl.ds(pl.multiple_of(at, members), members), :] = jnp.broadcast_to(
            tile[:, LANES - 1 :], (members, LANES)
        )
    me = ctx * members + uly
    now = last[...]
    then = jnp.concatenate([now[:1], now[:-1]], 0)
    end = jnp.concatenate([now[chunks - 1 :], now[: chunks - 1]], 0)
    linked[...] = jnp.where(now == then, 1.0, 0.0)
    through[...] = jnp.where(end == then, 1.0, 0.0)
    before[...] = jnp.where(me > 0, last[pl.ds(jnp.maximum(me - 1, 0), 1), :], -1.0)
    rows = one.shape[0]
    share = min(rows, HD)
    owner = ctx * chunks + lax.rem(uly, chunks)
    for at in range(0, rows, share):
        rate = pair_rate(facts, lax.div(owner * rows + at, HD), here)
        for ref, length in ((one, tokens), (half, tokens * chunks)):
            ref[at : at + share, :] = jnp.broadcast_to(
                jnp.exp(-rate * float(length)), (share, LANES)
            )


def half_kernel(chunks, linked, one, in_ref, out_ref):
    slices = out_ref.shape[0]
    offset = jnp.where(lax.axis_index("uly") >= chunks, chunks, 0)

    def slice_end(c, _):
        def step(j, state):
            keep = linked[pl.ds(c * 2 * chunks + offset + j, 1), :] * one[...]
            return in_ref[c * chunks + j].astype(jnp.float32) + keep * state

        begin = in_ref[c * chunks].astype(jnp.float32)
        state = lax.fori_loop(1, chunks, step, begin, unroll=few(chunks - 1))
        out_ref[c] = state.astype(out_ref.dtype)
        return 0

    lax.fori_loop(0, slices, slice_end, 0, unroll=few(slices))


def scan_kernel(chunks, linked, through, one, half, in_ref, other, out_ref):
    slices = other.shape[0]
    later = lax.axis_index("uly") >= chunks
    offset = jnp.where(later, chunks, 0)

    def over_other(state, c, wanted):
        keep = through[pl.ds(c * 2 * chunks + chunks - offset, 1), :] * half[...]
        return jnp.where(wanted, other[c].astype(jnp.float32) + keep * state, state)

    def over_slice(c, state):
        state = over_other(state, c, later)

        def step(j, state):
            at = c * chunks + j
            out_ref[at] = state.astype(out_ref.dtype)
            keep = linked[pl.ds(c * 2 * chunks + offset + j, 1), :] * one[...]
            return in_ref[at].astype(jnp.float32) + keep * state

        state = lax.fori_loop(0, chunks, step, state, unroll=few(chunks))
        return over_other(state, c, jnp.logical_not(later))

    begin = jnp.zeros(in_ref.shape[1:], jnp.float32)
    lax.fori_loop(0, slices, over_slice, begin, unroll=few(slices))


def norm_kernel(idcol, before, rates, q_ref, s_ref, inner_ref, gain, out_ref, raw, done, sems):
    tokens, width = q_ref.shape
    lane = lax.broadcasted_iota(jnp.int32, (HD, LANES), 1)
    place = lax.broadcasted_iota(jnp.int32, (tokens, LANES), 0)
    age = jnp.where(idcol[...] == before[...], (place + 1).astype(jnp.float32), NEVER)
    zero = jnp.zeros((HD, LANES), s_ref.dtype)
    total = jnp.zeros((tokens, LANES), jnp.float32)
    for j in range(0, width // LANES, 2):
        square = []
        for one in (0, 1):
            state = s_ref[(j + one) * HD : (j + one + 1) * HD, :]
            for half in (jnp.where(lane < HD, state, zero), jnp.where(lane < HD, zero, state)):
                square.append(jnp.concatenate([zero, half] if one else [half, zero], 1))
        columns = slice(j * LANES, (j + 2) * LANES)
        outer = jnp.dot(
            q_ref[:, columns], jnp.concatenate(square, 0), preferred_element_type=jnp.float32
        )
        for one in (0, 1):
            columns = slice((j + one) * LANES, (j + one + 1) * LANES)
            fade = jnp.exp(-rates[:, columns] * age)
            value = inner_ref[:, columns] + outer[:, one * LANES : (one + 1) * LANES] * fade
            total += value * value
            raw[:, columns] = value
    mean = jnp.sum(total, axis=1, keepdims=True) / float(width)
    scale = jnp.broadcast_to(lax.rsqrt(mean + 1e-06), (tokens, LANES))
    parts = sems.shape[0]
    share = width // parts
    copies = []
    for part in range(parts):
        for at in range(part * share, (part + 1) * share, LANES):
            columns = slice(at, at + LANES)
            done[:, columns] = (raw[:, columns] * scale * gain[:, columns]).astype(jnp.bfloat16)
        columns = slice(part * share, (part + 1) * share)
        copies.append(
            pltpu.make_async_copy(done.at[:, columns], out_ref.at[:, columns], sems.at[part])
        )
        copies[-1].start()
    for copy in copies:
        copy.wait()


def local(queries, keys, values, doc_ids, decay_rate, norm_gain):
    tokens, width = queries.shape
    here = decay_rate.shape[0]
    axes = ("ctx", "uly")
    slices, members = lax.axis_size("ctx"), lax.axis_size("uly")
    count = slices * members
    all_pairs = width // LANES
    chunks = members // 2
    group = slices * chunks
    rows = all_pairs * HD // group
    groups = [
        [c * members + half * chunks + u for c in range(slices) for u in range(chunks)]
        for half in (0, 1)
    ]
    swap = [
        (c * members + u, c * members + (u + chunks) % members)
        for c in range(slices)
        for u in range(members)
    ]

    vmem = pl.BlockSpec(memory_space=pltpu.VMEM)
    params = pltpu.CompilerParams(vmem_limit_bytes=32 * 1024 * 1024)
    shape = jax.ShapeDtypeStruct
    tile = shape((members, LANES), jnp.float32)

    own = jnp.pad(decay_rate, (0, LANES - here)) + jnp.pad(
        doc_ids, (LANES - tokens, 0)
    ).astype(jnp.float32)
    facts = lax.all_to_all(
        jnp.broadcast_to(own[None, :], tile.shape), "uly", split_axis=0, concat_axis=0, tiled=True
    )
    turned, filled, idrow, idcol = pl.pallas_call(
        turn_kernel,
        in_specs=[vmem] * 3,
        out_specs=[vmem] * 4,
        out_shape=[
            shape((width, LANES), jnp.bfloat16),
            shape((LANES, width), jnp.bfloat16),
            shape((8, LANES), jnp.float32),
            shape((tokens, LANES), jnp.float32),
        ],
        compiler_params=params,
        cost_estimate=pl.CostEstimate(flops=0, bytes_accessed=12_000_000, transcendentals=0),
        name="turn",
    )(own[None, :], keys, values)
    ends = pl.pallas_call(
        functools.partial(ends_kernel, here, tokens),
        in_specs=[vmem] * 4,
        out_specs=vmem,
        out_shape=shape((all_pairs * HD, LANES), jnp.bfloat16),
        compiler_params=params,
        name="ends",
    )(facts, idrow, turned, filled)
    pieces = lax.all_to_all(
        ends.reshape(group, rows, LANES),
        axes, split_axis=0, concat_axis=0, axis_index_groups=groups, tiled=True,
    )
    inner, slice_facts, rates = pl.pallas_call(
        functools.partial(inner_kernel, here),
        in_specs=[vmem] * 6,
        out_specs=[vmem] * 3,
        out_shape=[shape((tokens, width), jnp.float32), tile, shape((1, width), jnp.float32)],
        compiler_params=params,
        cost_estimate=pl.CostEstimate(
            flops=8_000_000_000, bytes_accessed=4_000_000, transcendentals=600_000
        ),
        name="inner",
    )(facts, idcol, idrow, queries, turned, values)
    others = [
        lax.ppermute(slice_facts, "ctx", [(c, (c + ahead) % slices) for c in range(slices)])
        for ahead in range(1, slices)
    ]
    linked, through, one, half, before = pl.pallas_call(
        functools.partial(link_kernel, here, tokens, chunks),
        in_specs=[vmem] * slices,
        out_specs=[vmem] * 5,
        out_shape=[shape((count, LANES), jnp.float32)] * 2
        + [shape((rows, LANES), jnp.float32)] * 2
        + [shape((1, LANES), jnp.float32)],
        scratch_shapes=[pltpu.VMEM((count, LANES), jnp.float32)],
        compiler_params=params,
        name="link",
    )(slice_facts, *others)
    halves = pl.pallas_call(
        functools.partial(half_kernel, chunks),
        in_specs=[vmem] * 3,
        out_specs=vmem,
        out_shape=shape((slices, rows, LANES), jnp.bfloat16),
        compiler_params=params,
        name="half",
    )(linked, one, pieces)
    other = lax.ppermute(halves, axes, swap)
    moved = pl.pallas_call(
        functools.partial(scan_kernel, chunks),
        in_specs=[vmem] * 6,
        out_specs=vmem,
        out_shape=shape((group, rows, LANES), jnp.bfloat16),
        compiler_params=params,
        name="scan",
    )(linked, through, one, half, pieces, other)
    states = lax.all_to_all(
        moved, axes, split_axis=0, concat_axis=0, axis_index_groups=groups, tiled=True
    )
    return pl.pallas_call(
        norm_kernel,
        in_specs=[vmem] * 7,
        out_specs=pl.BlockSpec(memory_space=pl.ANY),
        out_shape=shape((tokens, width), jnp.bfloat16),
        scratch_shapes=[
            pltpu.VMEM((tokens, width), jnp.float32),
            pltpu.VMEM((tokens, width), jnp.bfloat16),
            pltpu.SemaphoreType.DMA((4,)),
        ],
        compiler_params=params,
        name="norm",
    )(idcol, before, rates, queries, states.reshape(all_pairs * HD, LANES), inner, norm_gain[None, :])


def solution(mesh):
    in_specs = (
        P(("ctx", "uly"), None),
        P(("ctx", "uly"), None),
        P(("ctx", "uly"), None),
        P(("ctx", "uly")),
        P("uly"),
        P(),
    )
    out_specs = P(("ctx", "uly"), None)
    return jax.shard_map(local, mesh=mesh, in_specs=in_specs, out_specs=out_specs, check_vma=False)
```

```python
import functools

import jax
import jax.numpy as jnp
from jax import lax
from jax.experimental import pallas as pl
from jax.experimental.pallas import tpu as pltpu
from jax.sharding import PartitionSpec as P

HD = 64
LANES = 2 * HD
NEVER = 1e9


def rate_of(facts, head, here):
    return facts[head // here : head // here + 1, head % here : head % here + 1]


def pair_rate(facts, pair, here):
    lane = lax.broadcasted_iota(jnp.int32, (1, LANES), 1)
    rates = []
    for head in (2 * pair, 2 * pair + 1):
        row = facts[pl.ds(lax.div(head, here), 1), :]
        rates.append(
            jnp.sum(jnp.where(lane == lax.rem(head, here), row, 0.0), axis=1, keepdims=True)
        )
    return jnp.where(lane < HD, rates[0], rates[1])


def turn_kernel(row_ref, k_ref, v_ref, turned, filled, idrow, idcol):
    tokens, width = k_ref.shape
    fill = jnp.full((1, LANES - tokens), -1.0, jnp.float32)
    row = jnp.concatenate([row_ref[:1, LANES - tokens :], fill], 1)
    idrow[...] = jnp.broadcast_to(row, idrow.shape)
    idcol[...] = jnp.transpose(jnp.broadcast_to(row, (LANES, LANES)))[:tokens]
    filled[:tokens, :] = v_ref[...]
    filled[tokens:, :] = jnp.zeros((LANES - tokens, width), filled.dtype)
    blank = jnp.zeros((LANES - tokens, LANES), jnp.float32)
    for j in range(width // LANES):
        columns = slice(j * LANES, (j + 1) * LANES)
        block = jnp.concatenate([k_ref[:, columns].astype(jnp.float32), blank], 0)
        turned[columns, :] = jnp.transpose(block).astype(turned.dtype)


def ends_kernel(here, tokens, facts, idrow, turned, v_ref, out_ref):
    width = v_ref.shape[1]
    lane = lax.broadcasted_iota(jnp.int32, (HD, LANES), 1)
    place = lax.broadcasted_iota(jnp.int32, idrow.shape, 1)
    ids = idrow[...]
    last = ids[:, tokens - 1 : tokens]
    age = jnp.where(ids == last, (tokens - 1 - place).astype(jnp.float32), NEVER)
    for j in range(width // LANES):
        weighted = []
        for head in (2 * j, 2 * j + 1):
            weight = jnp.exp(-rate_of(facts, head, here) * age)
            keys = turned[head * HD : (head + 1) * HD, :].astype(jnp.float32)
            keys = keys.reshape(HD // 8, 8, LANES) * weight[None]
            weighted.append(keys.reshape(HD, LANES))
        weighted = jnp.concatenate(weighted, 0)
        high = weighted.astype(jnp.bfloat16)
        low = (weighted - high.astype(jnp.float32)).astype(jnp.bfloat16)
        v = v_ref[:, j * LANES : (j + 1) * LANES]
        both = jnp.dot(
            jnp.concatenate([high, low], 1),
            jnp.concatenate([v, v], 0),
            preferred_element_type=jnp.float32,
        )
        out_ref[j * HD : (j + 1) * HD, :] = jnp.where(lane < HD, both[:HD], both[HD:]).astype(
            jnp.bfloat16
        )


def inner_kernel(
    here, facts, idcol, idrow, q_ref, turned, v_ref, after, out_ref, rates_ref
):
    tokens, width = q_ref.shape
    lane = lax.broadcasted_iota(jnp.int32, (tokens, LANES), 1)
    t = lax.broadcasted_iota(jnp.int32, (tokens, LANES), 0)
    seen = (t >= lane) & (idcol[...] == idrow[:1, :])
    age = jnp.where(seen, (t - lane).astype(jnp.float32), NEVER)
    for j in range(width // LANES):
        columns = slice(j * LANES, (j + 1) * LANES)
        q = q_ref[:, columns]
        zero = jnp.zeros_like(q)
        stacked = jnp.concatenate([jnp.where(lane < HD, q, zero), jnp.where(lane < HD, zero, q)], 0)
        scores = jnp.dot(
            stacked, turned[columns, :], preferred_element_type=jnp.float32
        )
        rates = [rate_of(facts, 2 * j + one, here) for one in (0, 1)]
        weight = jnp.concatenate([jnp.exp(-rate * age) for rate in rates], 0)
        probs = (scores * weight)[:, :tokens].astype(jnp.bfloat16)
        got = jnp.dot(probs, v_ref[:, columns], preferred_element_type=jnp.float32)
        out_ref[:, columns] = jnp.where(lane < HD, got[:tokens], got[tokens:])
        rates_ref[:, columns] = jnp.where(lane[:1] < HD, rates[0], rates[1])


def pass_kernel(facts, after, out_ref):
    out_ref[...] = facts[...]


def few(count):
    return count if count <= 8 else 1


def link_kernel(here, tokens, chunks, facts, *refs):
    others, (linked, through, one, half, before, last) = refs[:-6], refs[-6:]
    members, slices = facts.shape[0], len(others) + 1
    ctx, uly = lax.axis_index("ctx"), lax.axis_index("uly")
    for back, tile in enumerate((facts, *others)):
        at = lax.rem(ctx + slices - back, slices) * members
        last[pl.ds(pl.multiple_of(at, members), members), :] = jnp.broadcast_to(
            tile[:, LANES - 1 :], (members, LANES)
        )
    me = ctx * members + uly
    now = last[...]
    then = jnp.concatenate([now[:1], now[:-1]], 0)
    end = jnp.concatenate([now[chunks - 1 :], now[: chunks - 1]], 0)
    linked[...] = jnp.where(now == then, 1.0, 0.0)
    through[...] = jnp.where(end == then, 1.0, 0.0)
    before[...] = jnp.where(me > 0, last[pl.ds(jnp.maximum(me - 1, 0), 1), :], -1.0)
    rows = one.shape[0]
    share = min(rows, HD)
    owner = ctx * chunks + lax.rem(uly, chunks)
    for at in range(0, rows, share):
        rate = pair_rate(facts, lax.div(owner * rows + at, HD), here)
        for ref, length in ((one, tokens), (half, tokens * chunks)):
            ref[at : at + share, :] = jnp.broadcast_to(
                jnp.exp(-rate * float(length)), (share, LANES)
            )


def half_kernel(chunks, linked, one, in_ref, out_ref):
    slices = out_ref.shape[0]
    offset = jnp.where(lax.axis_index("uly") >= chunks, chunks, 0)

    def slice_end(c, _):
        def step(j, state):
            keep = linked[pl.ds(c * 2 * chunks + offset + j, 1), :] * one[...]
            return in_ref[c * chunks + j].astype(jnp.float32) + keep * state

        begin = in_ref[c * chunks].astype(jnp.float32)
        state = lax.fori_loop(1, chunks, step, begin, unroll=few(chunks - 1))
        out_ref[c] = state.astype(out_ref.dtype)
        return 0

    lax.fori_loop(0, slices, slice_end, 0, unroll=few(slices))


def scan_kernel(chunks, linked, through, one, half, in_ref, other, out_ref):
    slices = other.shape[0]
    later = lax.axis_index("uly") >= chunks
    offset = jnp.where(later, chunks, 0)

    def over_other(state, c, wanted):
        keep = through[pl.ds(c * 2 * chunks + chunks - offset, 1), :] * half[...]
        return jnp.where(wanted, other[c].astype(jnp.float32) + keep * state, state)

    def over_slice(c, state):
        state = over_other(state, c, later)

        def step(j, state):
            at = c * chunks + j
            out_ref[at] = state.astype(out_ref.dtype)
            keep = linked[pl.ds(c * 2 * chunks + offset + j, 1), :] * one[...]
            return in_ref[at].astype(jnp.float32) + keep * state

        state = lax.fori_loop(0, chunks, step, state, unroll=few(chunks))
        return over_other(state, c, jnp.logical_not(later))

    begin = jnp.zeros(in_ref.shape[1:], jnp.float32)
    lax.fori_loop(0, slices, over_slice, begin, unroll=few(slices))


def norm_kernel(idcol, before, rates, q_ref, s_ref, inner_ref, gain, out_ref, raw, done, sems):
    tokens, width = q_ref.shape
    lane = lax.broadcasted_iota(jnp.int32, (HD, LANES), 1)
    place = lax.broadcasted_iota(jnp.int32, (tokens, LANES), 0)
    age = jnp.where(idcol[...] == before[...], (place + 1).astype(jnp.float32), NEVER)
    zero = jnp.zeros((HD, LANES), s_ref.dtype)
    total = jnp.zeros((tokens, LANES), jnp.float32)
    for j in range(0, width // LANES, 2):
        square = []
        for one in (0, 1):
            state = s_ref[(j + one) * HD : (j + one + 1) * HD, :]
            for half in (jnp.where(lane < HD, state, zero), jnp.where(lane < HD, zero, state)):
                square.append(jnp.concatenate([zero, half] if one else [half, zero], 1))
        columns = slice(j * LANES, (j + 2) * LANES)
        outer = jnp.dot(
            q_ref[:, columns], jnp.concatenate(square, 0), preferred_element_type=jnp.float32
        )
        for one in (0, 1):
            columns = slice((j + one) * LANES, (j + one + 1) * LANES)
            fade = jnp.exp(-rates[:, columns] * age)
            value = inner_ref[:, columns] + outer[:, one * LANES : (one + 1) * LANES] * fade
            total += value * value
            raw[:, columns] = value
    mean = jnp.sum(total, axis=1, keepdims=True) / float(width)
    scale = jnp.broadcast_to(lax.rsqrt(mean + 1e-06), (tokens, LANES))
    parts = sems.shape[0]
    share = width // parts
    copies = []
    for part in range(parts):
        for at in range(part * share, (part + 1) * share, LANES):
            columns = slice(at, at + LANES)
            done[:, columns] = (raw[:, columns] * scale * gain[:, columns]).astype(jnp.bfloat16)
        columns = slice(part * share, (part + 1) * share)
        copies.append(
            pltpu.make_async_copy(done.at[:, columns], out_ref.at[:, columns], sems.at[part])
        )
        copies[-1].start()
    for copy in copies:
        copy.wait()


def local(queries, keys, values, doc_ids, decay_rate, norm_gain):
    tokens, width = queries.shape
    here = decay_rate.shape[0]
    axes = ("ctx", "uly")
    slices, members = lax.axis_size("ctx"), lax.axis_size("uly")
    count = slices * members
    all_pairs = width // LANES
    chunks = members // 2
    group = slices * chunks
    rows = all_pairs * HD // group
    groups = [
        [c * members + half * chunks + u for c in range(slices) for u in range(chunks)]
        for half in (0, 1)
    ]
    swap = [
        (c * members + u, c * members + (u + chunks) % members)
        for c in range(slices)
        for u in range(members)
    ]

    vmem = pl.BlockSpec(memory_space=pltpu.VMEM)
    params = pltpu.CompilerParams(vmem_limit_bytes=32 * 1024 * 1024)
    shape = jax.ShapeDtypeStruct
    tile = shape((members, LANES), jnp.float32)

    own = jnp.pad(decay_rate, (0, LANES - here)) + jnp.pad(
        doc_ids, (LANES - tokens, 0)
    ).astype(jnp.float32)
    facts = lax.all_to_all(
        jnp.broadcast_to(own[None, :], tile.shape), "uly", split_axis=0, concat_axis=0, tiled=True
    )
    turned, filled, idrow, idcol = pl.pallas_call(
        turn_kernel,
        in_specs=[vmem] * 3,
        out_specs=[vmem] * 4,
        out_shape=[
            shape((width, LANES), jnp.bfloat16),
            shape((LANES, width), jnp.bfloat16),
            shape((8, LANES), jnp.float32),
            shape((tokens, LANES), jnp.float32),
        ],
        compiler_params=params,
        cost_estimate=pl.CostEstimate(flops=0, bytes_accessed=12_000_000, transcendentals=0),
        name="turn",
    )(own[None, :], keys, values)
    ends = pl.pallas_call(
        functools.partial(ends_kernel, here, tokens),
        in_specs=[vmem] * 4,
        out_specs=vmem,
        out_shape=shape((all_pairs * HD, LANES), jnp.bfloat16),
        compiler_params=params,
        name="ends",
    )(facts, idrow, turned, filled)
    pieces = lax.all_to_all(
        ends.reshape(group, rows, LANES),
        axes, split_axis=0, concat_axis=0, axis_index_groups=groups, tiled=True,
    )
    slice_facts = pl.pallas_call(
        pass_kernel,
        in_specs=[vmem, pl.BlockSpec(memory_space=pl.ANY)],
        out_specs=vmem,
        out_shape=tile,
        compiler_params=params,
        name="pass",
    )(facts, ends)
    others = [
        lax.ppermute(slice_facts, "ctx", [(c, (c + ahead) % slices) for c in range(slices)])
        for ahead in range(1, slices)
    ]
    linked, through, one, half, before = pl.pallas_call(
        functools.partial(link_kernel, here, tokens, chunks),
        in_specs=[vmem] * slices,
        out_specs=[vmem] * 5,
        out_shape=[shape((count, LANES), jnp.float32)] * 2
        + [shape((rows, LANES), jnp.float32)] * 2
        + [shape((1, LANES), jnp.float32)],
        scratch_shapes=[pltpu.VMEM((count, LANES), jnp.float32)],
        compiler_params=params,
        name="link",
    )(slice_facts, *others)
    halves = pl.pallas_call(
        functools.partial(half_kernel, chunks),
        in_specs=[vmem] * 3,
        out_specs=vmem,
        out_shape=shape((slices, rows, LANES), jnp.bfloat16),
        compiler_params=params,
        name="half",
    )(linked, one, pieces)
    other = lax.ppermute(halves, axes, swap)
    inner, rates = pl.pallas_call(
        functools.partial(inner_kernel, here),
        in_specs=[vmem] * 6 + [pl.BlockSpec(memory_space=pl.ANY)],
        out_specs=[vmem] * 2,
        out_shape=[shape((tokens, width), jnp.float32), shape((1, width), jnp.float32)],
        compiler_params=params,
        cost_estimate=pl.CostEstimate(
            flops=8_000_000_000, bytes_accessed=4_000_000, transcendentals=600_000
        ),
        name="inner",
    )(facts, idcol, idrow, queries, turned, values, halves)
    moved = pl.pallas_call(
        functools.partial(scan_kernel, chunks),
        in_specs=[vmem] * 6,
        out_specs=vmem,
        out_shape=shape((group, rows, LANES), jnp.bfloat16),
        compiler_params=params,
        name="scan",
    )(linked, through, one, half, pieces, other)
    states = lax.all_to_all(
        moved, axes, split_axis=0, concat_axis=0, axis_index_groups=groups, tiled=True
    )
    return pl.pallas_call(
        norm_kernel,
        in_specs=[vmem] * 7,
        out_specs=pl.BlockSpec(memory_space=pl.ANY),
        out_shape=shape((tokens, width), jnp.bfloat16),
        scratch_shapes=[
            pltpu.VMEM((tokens, width), jnp.float32),
            pltpu.VMEM((tokens, width), jnp.bfloat16),
            pltpu.SemaphoreType.DMA((4,)),
        ],
        compiler_params=params,
        name="norm",
    )(idcol, before, rates, queries, states.reshape(all_pairs * HD, LANES), inner, norm_gain[None, :])


def solution(mesh):
    in_specs = (
        P(("ctx", "uly"), None),
        P(("ctx", "uly"), None),
        P(("ctx", "uly"), None),
        P(("ctx", "uly")),
        P("uly"),
        P(),
    )
    out_specs = P(("ctx", "uly"), None)
    return jax.shard_map(local, mesh=mesh, in_specs=in_specs, out_specs=out_specs, check_vma=False)
```

```python
import functools

import jax
import jax.numpy as jnp
from jax import lax
from jax.experimental import pallas as pl
from jax.experimental.pallas import tpu as pltpu
from jax.sharding import PartitionSpec as P

HD = 64
LANES = 2 * HD
NEVER = 1e9


def rate_of(facts, head, here):
    return facts[head // here : head // here + 1, head % here : head % here + 1]


def pair_rate(facts, pair, here):
    lane = lax.broadcasted_iota(jnp.int32, (1, LANES), 1)
    rates = []
    for head in (2 * pair, 2 * pair + 1):
        row = facts[pl.ds(lax.div(head, here), 1), :]
        rates.append(
            jnp.sum(jnp.where(lane == lax.rem(head, here), row, 0.0), axis=1, keepdims=True)
        )
    return jnp.where(lane < HD, rates[0], rates[1])


def turn_kernel(row_ref, k_ref, v_ref, turned, filled, idrow, idcol):
    tokens, width = k_ref.shape
    fill = jnp.full((1, LANES - tokens), -1.0, jnp.float32)
    row = jnp.concatenate([row_ref[:1, LANES - tokens :], fill], 1)
    idrow[...] = jnp.broadcast_to(row, idrow.shape)
    idcol[...] = jnp.transpose(jnp.broadcast_to(row, (LANES, LANES)))[:tokens]
    filled[:tokens, :] = v_ref[...]
    filled[tokens:, :] = jnp.zeros((LANES - tokens, width), filled.dtype)
    blank = jnp.zeros((LANES - tokens, LANES), jnp.float32)
    for j in range(width // LANES):
        columns = slice(j * LANES, (j + 1) * LANES)
        block = jnp.concatenate([k_ref[:, columns].astype(jnp.float32), blank], 0)
        turned[columns, :] = jnp.transpose(block).astype(turned.dtype)


def ends_kernel(here, tokens, facts, idrow, turned, v_ref, out_ref):
    width = v_ref.shape[1]
    lane = lax.broadcasted_iota(jnp.int32, (HD, LANES), 1)
    place = lax.broadcasted_iota(jnp.int32, idrow.shape, 1)
    ids = idrow[...]
    last = ids[:, tokens - 1 : tokens]
    age = jnp.where(ids == last, (tokens - 1 - place).astype(jnp.float32), NEVER)
    for j in range(width // LANES):
        weighted = []
        for head in (2 * j, 2 * j + 1):
            weight = jnp.exp(-rate_of(facts, head, here) * age)
            keys = turned[head * HD : (head + 1) * HD, :].astype(jnp.float32)
            keys = keys.reshape(HD // 8, 8, LANES) * weight[None]
            weighted.append(keys.reshape(HD, LANES))
        weighted = jnp.concatenate(weighted, 0)
        high = weighted.astype(jnp.bfloat16)
        low = (weighted - high.astype(jnp.float32)).astype(jnp.bfloat16)
        v = v_ref[:, j * LANES : (j + 1) * LANES]
        both = jnp.dot(
            jnp.concatenate([high, low], 1),
            jnp.concatenate([v, v], 0),
            preferred_element_type=jnp.float32,
        )
        out_ref[j * HD : (j + 1) * HD, :] = jnp.where(lane < HD, both[:HD], both[HD:]).astype(
            jnp.bfloat16
        )


def inner_kernel(
    here, facts, idcol, idrow, q_ref, turned, v_ref, after, out_ref, rates_ref
):
    tokens, width = q_ref.shape
    lane = lax.broadcasted_iota(jnp.int32, (tokens, LANES), 1)
    t = lax.broadcasted_iota(jnp.int32, (tokens, LANES), 0)
    seen = (t >= lane) & (idcol[...] == idrow[:1, :])
    age = jnp.where(seen, (t - lane).astype(jnp.float32), NEVER)
    for j in range(width // LANES):
        columns = slice(j * LANES, (j + 1) * LANES)
        q = q_ref[:, columns]
        zero = jnp.zeros_like(q)
        stacked = jnp.concatenate([jnp.where(lane < HD, q, zero), jnp.where(lane < HD, zero, q)], 0)
        scores = jnp.dot(
            stacked, turned[columns, :], preferred_element_type=jnp.float32
        )
        rates = [rate_of(facts, 2 * j + one, here) for one in (0, 1)]
        weight = jnp.concatenate([jnp.exp(-rate * age) for rate in rates], 0)
        probs = (scores * weight)[:, :tokens].astype(jnp.bfloat16)
        got = jnp.dot(probs, v_ref[:, columns], preferred_element_type=jnp.float32)
        out_ref[:, columns] = jnp.where(lane < HD, got[:tokens], got[tokens:])
        rates_ref[:, columns] = jnp.where(lane[:1] < HD, rates[0], rates[1])


def pass_kernel(facts, after, out_ref):
    out_ref[...] = facts[...]


def few(count):
    return count if count <= 8 else 1


def link_kernel(here, tokens, chunks, facts, *refs):
    others, (linked, through, one, half, before, last) = refs[:-6], refs[-6:]
    members, slices = facts.shape[0], len(others) + 1
    ctx, uly = lax.axis_index("ctx"), lax.axis_index("uly")
    for back, tile in enumerate((facts, *others)):
        at = lax.rem(ctx + slices - back, slices) * members
        last[pl.ds(pl.multiple_of(at, members), members), :] = jnp.broadcast_to(
            tile[:, LANES - 1 :], (members, LANES)
        )
    me = ctx * members + uly
    now = last[...]
    then = jnp.concatenate([now[:1], now[:-1]], 0)
    end = jnp.concatenate([now[chunks - 1 :], now[: chunks - 1]], 0)
    linked[...] = jnp.where(now == then, 1.0, 0.0)
    through[...] = jnp.where(end == then, 1.0, 0.0)
    before[...] = jnp.where(me > 0, last[pl.ds(jnp.maximum(me - 1, 0), 1), :], -1.0)
    rows = one.shape[0]
    share = min(rows, HD)
    owner = ctx * chunks + lax.rem(uly, chunks)
    for at in range(0, rows, share):
        rate = pair_rate(facts, lax.div(owner * rows + at, HD), here)
        for ref, length in ((one, tokens), (half, tokens * chunks)):
            ref[at : at + share, :] = jnp.broadcast_to(
                jnp.exp(-rate * float(length)), (share, LANES)
            )


def half_kernel(chunks, linked, one, in_ref, out_ref):
    slices = out_ref.shape[0]
    offset = jnp.where(lax.axis_index("uly") >= chunks, chunks, 0)

    def slice_end(c, _):
        def step(j, state):
            keep = linked[pl.ds(c * 2 * chunks + offset + j, 1), :] * one[...]
            return in_ref[c * chunks + j].astype(jnp.float32) + keep * state

        begin = in_ref[c * chunks].astype(jnp.float32)
        state = lax.fori_loop(1, chunks, step, begin, unroll=few(chunks - 1))
        out_ref[c] = state.astype(out_ref.dtype)
        return 0

    lax.fori_loop(0, slices, slice_end, 0, unroll=few(slices))


def scan_kernel(chunks, linked, through, one, half, in_ref, other, after, out_ref):
    slices = other.shape[0]
    later = lax.axis_index("uly") >= chunks
    offset = jnp.where(later, chunks, 0)

    def over_other(state, c, wanted):
        keep = through[pl.ds(c * 2 * chunks + chunks - offset, 1), :] * half[...]
        return jnp.where(wanted, other[c].astype(jnp.float32) + keep * state, state)

    def over_slice(c, state):
        state = over_other(state, c, later)

        def step(j, state):
            at = c * chunks + j
            out_ref[at] = state.astype(out_ref.dtype)
            keep = linked[pl.ds(c * 2 * chunks + offset + j, 1), :] * one[...]
            return in_ref[at].astype(jnp.float32) + keep * state

        state = lax.fori_loop(0, chunks, step, state, unroll=few(chunks))
        return over_other(state, c, jnp.logical_not(later))

    begin = jnp.zeros(in_ref.shape[1:], jnp.float32)
    lax.fori_loop(0, slices, over_slice, begin, unroll=few(slices))


def norm_kernel(idcol, before, rates, q_ref, s_ref, inner_ref, gain, out_ref, raw, done, sems):
    tokens, width = q_ref.shape
    lane = lax.broadcasted_iota(jnp.int32, (HD, LANES), 1)
    place = lax.broadcasted_iota(jnp.int32, (tokens, LANES), 0)
    age = jnp.where(idcol[...] == before[...], (place + 1).astype(jnp.float32), NEVER)
    zero = jnp.zeros((HD, LANES), s_ref.dtype)
    total = jnp.zeros((tokens, LANES), jnp.float32)
    for j in range(0, width // LANES, 2):
        square = []
        for one in (0, 1):
            state = s_ref[(j + one) * HD : (j + one + 1) * HD, :]
            for half in (jnp.where(lane < HD, state, zero), jnp.where(lane < HD, zero, state)):
                square.append(jnp.concatenate([zero, half] if one else [half, zero], 1))
        columns = slice(j * LANES, (j + 2) * LANES)
        outer = jnp.dot(
            q_ref[:, columns], jnp.concatenate(square, 0), preferred_element_type=jnp.float32
        )
        for one in (0, 1):
            columns = slice((j + one) * LANES, (j + one + 1) * LANES)
            fade = jnp.exp(-rates[:, columns] * age)
            value = inner_ref[:, columns] + outer[:, one * LANES : (one + 1) * LANES] * fade
            total += value * value
            raw[:, columns] = value
    mean = jnp.sum(total, axis=1, keepdims=True) / float(width)
    scale = jnp.broadcast_to(lax.rsqrt(mean + 1e-06), (tokens, LANES))
    parts = sems.shape[0]
    share = width // parts
    copies = []
    for part in range(parts):
        for at in range(part * share, (part + 1) * share, LANES):
            columns = slice(at, at + LANES)
            done[:, columns] = (raw[:, columns] * scale * gain[:, columns]).astype(jnp.bfloat16)
        columns = slice(part * share, (part + 1) * share)
        copies.append(
            pltpu.make_async_copy(done.at[:, columns], out_ref.at[:, columns], sems.at[part])
        )
        copies[-1].start()
    for copy in copies:
        copy.wait()


def local(queries, keys, values, doc_ids, decay_rate, norm_gain):
    tokens, width = queries.shape
    here = decay_rate.shape[0]
    axes = ("ctx", "uly")
    slices, members = lax.axis_size("ctx"), lax.axis_size("uly")
    count = slices * members
    all_pairs = width // LANES
    chunks = members // 2
    group = slices * chunks
    rows = all_pairs * HD // group
    groups = [
        [c * members + half * chunks + u for c in range(slices) for u in range(chunks)]
        for half in (0, 1)
    ]
    swap = [
        (c * members + u, c * members + (u + chunks) % members)
        for c in range(slices)
        for u in range(members)
    ]

    vmem = pl.BlockSpec(memory_space=pltpu.VMEM)
    params = pltpu.CompilerParams(vmem_limit_bytes=32 * 1024 * 1024)
    shape = jax.ShapeDtypeStruct
    tile = shape((members, LANES), jnp.float32)

    own = jnp.pad(decay_rate, (0, LANES - here)) + jnp.pad(
        doc_ids, (LANES - tokens, 0)
    ).astype(jnp.float32)
    facts = lax.all_to_all(
        jnp.broadcast_to(own[None, :], tile.shape), "uly", split_axis=0, concat_axis=0, tiled=True
    )
    turned, filled, idrow, idcol = pl.pallas_call(
        turn_kernel,
        in_specs=[vmem] * 3,
        out_specs=[vmem] * 4,
        out_shape=[
            shape((width, LANES), jnp.bfloat16),
            shape((LANES, width), jnp.bfloat16),
            shape((8, LANES), jnp.float32),
            shape((tokens, LANES), jnp.float32),
        ],
        compiler_params=params,
        cost_estimate=pl.CostEstimate(flops=0, bytes_accessed=12_000_000, transcendentals=0),
        name="turn",
    )(own[None, :], keys, values)
    ends = pl.pallas_call(
        functools.partial(ends_kernel, here, tokens),
        in_specs=[vmem] * 4,
        out_specs=vmem,
        out_shape=shape((all_pairs * HD, LANES), jnp.bfloat16),
        compiler_params=params,
        name="ends",
    )(facts, idrow, turned, filled)
    pieces = lax.all_to_all(
        ends.reshape(group, rows, LANES),
        axes, split_axis=0, concat_axis=0, axis_index_groups=groups, tiled=True,
    )
    slice_facts = pl.pallas_call(
        pass_kernel,
        in_specs=[vmem, pl.BlockSpec(memory_space=pl.ANY)],
        out_specs=vmem,
        out_shape=tile,
        compiler_params=params,
        name="pass",
    )(facts, ends)
    others = [
        lax.ppermute(slice_facts, "ctx", [(c, (c + ahead) % slices) for c in range(slices)])
        for ahead in range(1, slices)
    ]
    linked, through, one, half, before = pl.pallas_call(
        functools.partial(link_kernel, here, tokens, chunks),
        in_specs=[vmem] * slices,
        out_specs=[vmem] * 5,
        out_shape=[shape((count, LANES), jnp.float32)] * 2
        + [shape((rows, LANES), jnp.float32)] * 2
        + [shape((1, LANES), jnp.float32)],
        scratch_shapes=[pltpu.VMEM((count, LANES), jnp.float32)],
        compiler_params=params,
        name="link",
    )(slice_facts, *others)
    halves = pl.pallas_call(
        functools.partial(half_kernel, chunks),
        in_specs=[vmem] * 3,
        out_specs=vmem,
        out_shape=shape((slices, rows, LANES), jnp.bfloat16),
        compiler_params=params,
        name="half",
    )(linked, one, pieces)
    other = lax.ppermute(halves, axes, swap)
    inner, rates = pl.pallas_call(
        functools.partial(inner_kernel, here),
        in_specs=[vmem] * 6 + [pl.BlockSpec(memory_space=pl.ANY)],
        out_specs=[vmem] * 2,
        out_shape=[shape((tokens, width), jnp.float32), shape((1, width), jnp.float32)],
        compiler_params=params,
        cost_estimate=pl.CostEstimate(
            flops=8_000_000_000, bytes_accessed=4_000_000, transcendentals=600_000
        ),
        name="inner",
    )(facts, idcol, idrow, queries, turned, values, halves)
    moved = pl.pallas_call(
        functools.partial(scan_kernel, chunks),
        in_specs=[vmem] * 6 + [pl.BlockSpec(memory_space=pl.ANY)],
        out_specs=vmem,
        out_shape=shape((group, rows, LANES), jnp.bfloat16),
        compiler_params=params,
        name="scan",
    )(linked, through, one, half, pieces, other, rates)
    states = lax.all_to_all(
        moved, axes, split_axis=0, concat_axis=0, axis_index_groups=groups, tiled=True
    )
    return pl.pallas_call(
        norm_kernel,
        in_specs=[vmem] * 7,
        out_specs=pl.BlockSpec(memory_space=pl.ANY),
        out_shape=shape((tokens, width), jnp.bfloat16),
        scratch_shapes=[
            pltpu.VMEM((tokens, width), jnp.float32),
            pltpu.VMEM((tokens, width), jnp.bfloat16),
            pltpu.SemaphoreType.DMA((4,)),
        ],
        compiler_params=params,
        name="norm",
    )(idcol, before, rates, queries, states.reshape(all_pairs * HD, LANES), inner, norm_gain[None, :])


def solution(mesh):
    in_specs = (
        P(("ctx", "uly"), None),
        P(("ctx", "uly"), None),
        P(("ctx", "uly"), None),
        P(("ctx", "uly")),
        P("uly"),
        P(),
    )
    out_specs = P(("ctx", "uly"), None)
    return jax.shard_map(local, mesh=mesh, in_specs=in_specs, out_specs=out_specs, check_vma=False)
```

```python
import functools

import jax
import jax.numpy as jnp
from jax import lax
from jax.experimental import pallas as pl
from jax.experimental.pallas import tpu as pltpu
from jax.sharding import PartitionSpec as P

HD = 64
LANES = 2 * HD
NEVER = 1e9


def rate_of(facts, head, here):
    return facts[head // here : head // here + 1, head % here : head % here + 1]


def pair_rate(facts, pair, here):
    lane = lax.broadcasted_iota(jnp.int32, (1, LANES), 1)
    rates = []
    for head in (2 * pair, 2 * pair + 1):
        row = facts[pl.ds(lax.div(head, here), 1), :]
        rates.append(
            jnp.sum(jnp.where(lane == lax.rem(head, here), row, 0.0), axis=1, keepdims=True)
        )
    return jnp.where(lane < HD, rates[0], rates[1])


def turn_kernel(row_ref, k_ref, v_ref, turned, filled, idrow, idcol):
    tokens, width = k_ref.shape
    fill = jnp.full((1, LANES - tokens), -1.0, jnp.float32)
    row = jnp.concatenate([row_ref[:1, LANES - tokens :], fill], 1)
    idrow[...] = jnp.broadcast_to(row, idrow.shape)
    idcol[...] = jnp.transpose(jnp.broadcast_to(row, (LANES, LANES)))[:tokens]
    filled[:tokens, :] = v_ref[...]
    filled[tokens:, :] = jnp.zeros((LANES - tokens, width), filled.dtype)
    blank = jnp.zeros((LANES - tokens, LANES), jnp.float32)
    for j in range(width // LANES):
        columns = slice(j * LANES, (j + 1) * LANES)
        block = jnp.concatenate([k_ref[:, columns].astype(jnp.float32), blank], 0)
        turned[columns, :] = jnp.transpose(block).astype(turned.dtype)


def ends_kernel(here, tokens, facts, idrow, turned, v_ref, out_ref):
    width = v_ref.shape[1]
    lane = lax.broadcasted_iota(jnp.int32, (HD, LANES), 1)
    place = lax.broadcasted_iota(jnp.int32, idrow.shape, 1)
    ids = idrow[...]
    last = ids[:, tokens - 1 : tokens]
    age = jnp.where(ids == last, (tokens - 1 - place).astype(jnp.float32), NEVER)
    for j in range(width // LANES):
        weighted = []
        for head in (2 * j, 2 * j + 1):
            weight = jnp.exp(-rate_of(facts, head, here) * age)
            keys = turned[head * HD : (head + 1) * HD, :].astype(jnp.float32)
            keys = keys.reshape(HD // 8, 8, LANES) * weight[None]
            weighted.append(keys.reshape(HD, LANES))
        weighted = jnp.concatenate(weighted, 0)
        high = weighted.astype(jnp.bfloat16)
        low = (weighted - high.astype(jnp.float32)).astype(jnp.bfloat16)
        v = v_ref[:, j * LANES : (j + 1) * LANES]
        both = jnp.dot(
            jnp.concatenate([high, low], 1),
            jnp.concatenate([v, v], 0),
            preferred_element_type=jnp.float32,
        )
        out_ref[j * HD : (j + 1) * HD, :] = jnp.where(lane < HD, both[:HD], both[HD:]).astype(
            jnp.bfloat16
        )


def inner_kernel(
    here, facts, idcol, idrow, q_ref, turned, v_ref, after, out_ref, rates_ref
):
    tokens, width = q_ref.shape
    lane = lax.broadcasted_iota(jnp.int32, (tokens, LANES), 1)
    t = lax.broadcasted_iota(jnp.int32, (tokens, LANES), 0)
    seen = (t >= lane) & (idcol[...] == idrow[:1, :])
    age = jnp.where(seen, (t - lane).astype(jnp.float32), NEVER)
    for j in range(width // LANES):
        columns = slice(j * LANES, (j + 1) * LANES)
        q = q_ref[:, columns]
        zero = jnp.zeros_like(q)
        stacked = jnp.concatenate([jnp.where(lane < HD, q, zero), jnp.where(lane < HD, zero, q)], 0)
        scores = jnp.dot(
            stacked, turned[columns, :], preferred_element_type=jnp.float32
        )
        rates = [rate_of(facts, 2 * j + one, here) for one in (0, 1)]
        weight = jnp.concatenate([jnp.exp(-rate * age) for rate in rates], 0)
        probs = (scores * weight)[:, :tokens].astype(jnp.bfloat16)
        got = jnp.dot(probs, v_ref[:, columns], preferred_element_type=jnp.float32)
        out_ref[:, columns] = jnp.where(lane < HD, got[:tokens], got[tokens:])
        rates_ref[:, columns] = jnp.where(lane[:1] < HD, rates[0], rates[1])


def pass_kernel(facts, after, out_ref):
    out_ref[...] = facts[...]


def few(count):
    return count if count <= 8 else 1


def link_kernel(here, tokens, chunks, facts, *refs):
    others, (linked, through, one, half, before, last) = refs[:-6], refs[-6:]
    members, slices = facts.shape[0], len(others) + 1
    ctx, uly = lax.axis_index("ctx"), lax.axis_index("uly")
    for back, tile in enumerate((facts, *others)):
        at = lax.rem(ctx + slices - back, slices) * members
        last[pl.ds(pl.multiple_of(at, members), members), :] = jnp.broadcast_to(
            tile[:, LANES - 1 :], (members, LANES)
        )
    me = ctx * members + uly
    now = last[...]
    then = jnp.concatenate([now[:1], now[:-1]], 0)
    end = jnp.concatenate([now[chunks - 1 :], now[: chunks - 1]], 0)
    linked[...] = jnp.where(now == then, 1.0, 0.0)
    through[...] = jnp.where(end == then, 1.0, 0.0)
    before[...] = jnp.where(me > 0, last[pl.ds(jnp.maximum(me - 1, 0), 1), :], -1.0)
    rows = one.shape[0]
    share = min(rows, HD)
    owner = ctx * chunks + lax.rem(uly, chunks)
    for at in range(0, rows, share):
        rate = pair_rate(facts, lax.div(owner * rows + at, HD), here)
        for ref, length in ((one, tokens), (half, tokens * chunks)):
            ref[at : at + share, :] = jnp.broadcast_to(
                jnp.exp(-rate * float(length)), (share, LANES)
            )


def half_kernel(chunks, linked, one, in_ref, early_ref, final_ref):
    slices = early_ref.shape[0] + 1
    offset = jnp.where(lax.axis_index("uly") >= chunks, chunks, 0)

    def slice_end(c):
        def step(j, state):
            keep = linked[pl.ds(c * 2 * chunks + offset + j, 1), :] * one[...]
            return in_ref[c * chunks + j].astype(jnp.float32) + keep * state

        begin = in_ref[c * chunks].astype(jnp.float32)
        state = lax.fori_loop(1, chunks, step, begin, unroll=few(chunks - 1))
        return state.astype(early_ref.dtype)

    def early(c, _):
        early_ref[c] = slice_end(c)
        return 0

    lax.fori_loop(0, slices - 1, early, 0, unroll=few(slices - 1))
    final_ref[0] = slice_end(slices - 1)


def scan_kernel(
    chunks, linked, through, one, half, in_ref, early, final, after, out_ref
):
    slices = early.shape[0] + 1
    later = lax.axis_index("uly") >= chunks
    offset = jnp.where(later, chunks, 0)

    def over_other(state, c, piece, wanted):
        keep = through[pl.ds(c * 2 * chunks + chunks - offset, 1), :] * half[...]
        return jnp.where(wanted, piece.astype(jnp.float32) + keep * state, state)

    def over_own(state, c):
        def step(j, state):
            at = c * chunks + j
            out_ref[at] = state.astype(out_ref.dtype)
            keep = linked[pl.ds(c * 2 * chunks + offset + j, 1), :] * one[...]
            return in_ref[at].astype(jnp.float32) + keep * state

        return lax.fori_loop(0, chunks, step, state, unroll=few(chunks))

    def over_slice(c, state):
        state = over_own(over_other(state, c, early[c], later), c)
        return over_other(state, c, early[c], jnp.logical_not(later))

    begin = jnp.zeros(in_ref.shape[1:], jnp.float32)
    state = lax.fori_loop(0, slices - 1, over_slice, begin, unroll=few(slices - 1))
    over_own(over_other(state, slices - 1, final[0], later), slices - 1)


def norm_kernel(idcol, before, rates, q_ref, s_ref, inner_ref, gain, out_ref, raw, done, sems):
    tokens, width = q_ref.shape
    lane = lax.broadcasted_iota(jnp.int32, (HD, LANES), 1)
    place = lax.broadcasted_iota(jnp.int32, (tokens, LANES), 0)
    age = jnp.where(idcol[...] == before[...], (place + 1).astype(jnp.float32), NEVER)
    zero = jnp.zeros((HD, LANES), s_ref.dtype)
    total = jnp.zeros((tokens, LANES), jnp.float32)
    for j in range(0, width // LANES, 2):
        square = []
        for one in (0, 1):
            state = s_ref[(j + one) * HD : (j + one + 1) * HD, :]
            for half in (jnp.where(lane < HD, state, zero), jnp.where(lane < HD, zero, state)):
                square.append(jnp.concatenate([zero, half] if one else [half, zero], 1))
        columns = slice(j * LANES, (j + 2) * LANES)
        outer = jnp.dot(
            q_ref[:, columns], jnp.concatenate(square, 0), preferred_element_type=jnp.float32
        )
        for one in (0, 1):
            columns = slice((j + one) * LANES, (j + one + 1) * LANES)
            fade = jnp.exp(-rates[:, columns] * age)
            value = inner_ref[:, columns] + outer[:, one * LANES : (one + 1) * LANES] * fade
            total += value * value
            raw[:, columns] = value
    mean = jnp.sum(total, axis=1, keepdims=True) / float(width)
    scale = jnp.broadcast_to(lax.rsqrt(mean + 1e-06), (tokens, LANES))
    parts = sems.shape[0]
    share = width // parts
    copies = []
    for part in range(parts):
        for at in range(part * share, (part + 1) * share, LANES):
            columns = slice(at, at + LANES)
            done[:, columns] = (raw[:, columns] * scale * gain[:, columns]).astype(jnp.bfloat16)
        columns = slice(part * share, (part + 1) * share)
        copies.append(
            pltpu.make_async_copy(done.at[:, columns], out_ref.at[:, columns], sems.at[part])
        )
        copies[-1].start()
    for copy in copies:
        copy.wait()


def local(queries, keys, values, doc_ids, decay_rate, norm_gain):
    tokens, width = queries.shape
    here = decay_rate.shape[0]
    axes = ("ctx", "uly")
    slices, members = lax.axis_size("ctx"), lax.axis_size("uly")
    count = slices * members
    all_pairs = width // LANES
    chunks = members // 2
    group = slices * chunks
    rows = all_pairs * HD // group
    groups = [
        [c * members + half * chunks + u for c in range(slices) for u in range(chunks)]
        for half in (0, 1)
    ]
    swap = [
        (c * members + u, c * members + (u + chunks) % members)
        for c in range(slices)
        for u in range(members)
    ]

    vmem = pl.BlockSpec(memory_space=pltpu.VMEM)
    params = pltpu.CompilerParams(vmem_limit_bytes=32 * 1024 * 1024)
    shape = jax.ShapeDtypeStruct
    tile = shape((members, LANES), jnp.float32)

    own = jnp.pad(decay_rate, (0, LANES - here)) + jnp.pad(
        doc_ids, (LANES - tokens, 0)
    ).astype(jnp.float32)
    facts = lax.all_to_all(
        jnp.broadcast_to(own[None, :], tile.shape), "uly", split_axis=0, concat_axis=0, tiled=True
    )
    turned, filled, idrow, idcol = pl.pallas_call(
        turn_kernel,
        in_specs=[vmem] * 3,
        out_specs=[vmem] * 4,
        out_shape=[
            shape((width, LANES), jnp.bfloat16),
            shape((LANES, width), jnp.bfloat16),
            shape((8, LANES), jnp.float32),
            shape((tokens, LANES), jnp.float32),
        ],
        compiler_params=params,
        cost_estimate=pl.CostEstimate(flops=0, bytes_accessed=12_000_000, transcendentals=0),
        name="turn",
    )(own[None, :], keys, values)
    ends = pl.pallas_call(
        functools.partial(ends_kernel, here, tokens),
        in_specs=[vmem] * 4,
        out_specs=vmem,
        out_shape=shape((all_pairs * HD, LANES), jnp.bfloat16),
        compiler_params=params,
        name="ends",
    )(facts, idrow, turned, filled)
    pieces = lax.all_to_all(
        ends.reshape(group, rows, LANES),
        axes, split_axis=0, concat_axis=0, axis_index_groups=groups, tiled=True,
    )
    slice_facts = pl.pallas_call(
        pass_kernel,
        in_specs=[vmem, pl.BlockSpec(memory_space=pl.ANY)],
        out_specs=vmem,
        out_shape=tile,
        compiler_params=params,
        name="pass",
    )(facts, ends)
    others = [
        lax.ppermute(slice_facts, "ctx", [(c, (c + ahead) % slices) for c in range(slices)])
        for ahead in range(1, slices)
    ]
    linked, through, one, half, before = pl.pallas_call(
        functools.partial(link_kernel, here, tokens, chunks),
        in_specs=[vmem] * slices,
        out_specs=[vmem] * 5,
        out_shape=[shape((count, LANES), jnp.float32)] * 2
        + [shape((rows, LANES), jnp.float32)] * 2
        + [shape((1, LANES), jnp.float32)],
        scratch_shapes=[pltpu.VMEM((count, LANES), jnp.float32)],
        compiler_params=params,
        name="link",
    )(slice_facts, *others)
    early_ends, final_end = pl.pallas_call(
        functools.partial(half_kernel, chunks),
        in_specs=[vmem] * 3,
        out_specs=[vmem] * 2,
        out_shape=[
            shape((slices - 1, rows, LANES), jnp.bfloat16),
            shape((1, rows, LANES), jnp.bfloat16),
        ],
        compiler_params=params,
        name="half",
    )(linked, one, pieces)
    early = lax.ppermute(early_ends, axes, swap)
    final = lax.ppermute(final_end, axes, [(low, high) for low, high in swap if low < high])
    inner, rates = pl.pallas_call(
        functools.partial(inner_kernel, here),
        in_specs=[vmem] * 6 + [pl.BlockSpec(memory_space=pl.ANY)],
        out_specs=[vmem] * 2,
        out_shape=[shape((tokens, width), jnp.float32), shape((1, width), jnp.float32)],
        compiler_params=params,
        cost_estimate=pl.CostEstimate(
            flops=8_000_000_000, bytes_accessed=4_000_000, transcendentals=600_000
        ),
        name="inner",
    )(facts, idcol, idrow, queries, turned, values, early_ends)
    moved = pl.pallas_call(
        functools.partial(scan_kernel, chunks),
        in_specs=[vmem] * 7 + [pl.BlockSpec(memory_space=pl.ANY)],
        out_specs=vmem,
        out_shape=shape((group, rows, LANES), jnp.bfloat16),
        compiler_params=params,
        name="scan",
    )(linked, through, one, half, pieces, early, final, rates)
    states = lax.all_to_all(
        moved, axes, split_axis=0, concat_axis=0, axis_index_groups=groups, tiled=True
    )
    return pl.pallas_call(
        norm_kernel,
        in_specs=[vmem] * 7,
        out_specs=pl.BlockSpec(memory_space=pl.ANY),
        out_shape=shape((tokens, width), jnp.bfloat16),
        scratch_shapes=[
            pltpu.VMEM((tokens, width), jnp.float32),
            pltpu.VMEM((tokens, width), jnp.bfloat16),
            pltpu.SemaphoreType.DMA((4,)),
        ],
        compiler_params=params,
        name="norm",
    )(idcol, before, rates, queries, states.reshape(all_pairs * HD, LANES), inner, norm_gain[None, :])


def solution(mesh):
    in_specs = (
        P(("ctx", "uly"), None),
        P(("ctx", "uly"), None),
        P(("ctx", "uly"), None),
        P(("ctx", "uly")),
        P("uly"),
        P(),
    )
    out_specs = P(("ctx", "uly"), None)
    return jax.shard_map(local, mesh=mesh, in_specs=in_specs, out_specs=out_specs, check_vma=False)
```

```python
import functools

import jax
import jax.numpy as jnp
from jax import lax
from jax.experimental import pallas as pl
from jax.experimental.pallas import tpu as pltpu
from jax.sharding import PartitionSpec as P

HD = 64
LANES = 2 * HD
NEVER = 1e9


def rate_of(facts, head, here):
    return facts[head // here : head // here + 1, head % here : head % here + 1]


def pair_rate(facts, pair, here):
    lane = lax.broadcasted_iota(jnp.int32, (1, LANES), 1)
    rates = []
    for head in (2 * pair, 2 * pair + 1):
        row = facts[pl.ds(lax.div(head, here), 1), :]
        rates.append(
            jnp.sum(jnp.where(lane == lax.rem(head, here), row, 0.0), axis=1, keepdims=True)
        )
    return jnp.where(lane < HD, rates[0], rates[1])


def turn_kernel(row_ref, k_ref, v_ref, turned, filled, idrow, idcol):
    tokens, width = k_ref.shape
    fill = jnp.full((1, LANES - tokens), -1.0, jnp.float32)
    row = jnp.concatenate([row_ref[:1, LANES - tokens :], fill], 1)
    idrow[...] = jnp.broadcast_to(row, idrow.shape)
    idcol[...] = jnp.transpose(jnp.broadcast_to(row, (LANES, LANES)))[:tokens]
    filled[:tokens, :] = v_ref[...]
    filled[tokens:, :] = jnp.zeros((LANES - tokens, width), filled.dtype)
    blank = jnp.zeros((LANES - tokens, LANES), jnp.float32)
    for j in range(width // LANES):
        columns = slice(j * LANES, (j + 1) * LANES)
        block = jnp.concatenate([k_ref[:, columns].astype(jnp.float32), blank], 0)
        turned[columns, :] = jnp.transpose(block).astype(turned.dtype)


def ends_kernel(here, tokens, facts, idrow, turned, v_ref, out_ref):
    width = v_ref.shape[1]
    lane = lax.broadcasted_iota(jnp.int32, (HD, LANES), 1)
    place = lax.broadcasted_iota(jnp.int32, idrow.shape, 1)
    ids = idrow[...]
    last = ids[:, tokens - 1 : tokens]
    age = jnp.where(ids == last, (tokens - 1 - place).astype(jnp.float32), NEVER)
    for j in range(0, width // LANES, 2):
        weighted = []
        for head in range(2 * j, 2 * j + 4):
            weight = jnp.exp(-rate_of(facts, head, here) * age)
            keys = turned[head * HD : (head + 1) * HD, :].astype(jnp.float32)
            keys = keys.reshape(HD // 8, 8, LANES) * weight[None]
            weighted.append(keys.reshape(HD, LANES))
        weighted = jnp.concatenate(weighted, 0)
        high = weighted.astype(jnp.bfloat16)
        low = (weighted - high.astype(jnp.float32)).astype(jnp.bfloat16)
        v = v_ref[:, j * LANES : (j + 2) * LANES]
        both = jnp.dot(
            jnp.concatenate([high, low], 1),
            jnp.concatenate([v, v], 0),
            preferred_element_type=jnp.float32,
        )
        for one in (0, 1):
            pair = both[one * LANES : (one + 1) * LANES, one * LANES : (one + 1) * LANES]
            out_ref[(j + one) * HD : (j + one + 1) * HD, :] = jnp.where(
                lane < HD, pair[:HD], pair[HD:]
            ).astype(jnp.bfloat16)


def inner_kernel(
    here, facts, idcol, idrow, q_ref, turned, v_ref, after, out_ref, rates_ref
):
    tokens, width = q_ref.shape
    lane = lax.broadcasted_iota(jnp.int32, (tokens, LANES), 1)
    t = lax.broadcasted_iota(jnp.int32, (tokens, LANES), 0)
    seen = (t >= lane) & (idcol[...] == idrow[:1, :])
    age = jnp.where(seen, (t - lane).astype(jnp.float32), NEVER)
    for j in range(width // LANES):
        columns = slice(j * LANES, (j + 1) * LANES)
        q = q_ref[:, columns]
        zero = jnp.zeros_like(q)
        stacked = jnp.concatenate([jnp.where(lane < HD, q, zero), jnp.where(lane < HD, zero, q)], 0)
        scores = jnp.dot(
            stacked, turned[columns, :], preferred_element_type=jnp.float32
        )
        rates = [rate_of(facts, 2 * j + one, here) for one in (0, 1)]
        weight = jnp.concatenate([jnp.exp(-rate * age) for rate in rates], 0)
        probs = (scores * weight)[:, :tokens].astype(jnp.bfloat16)
        got = jnp.dot(probs, v_ref[:, columns], preferred_element_type=jnp.float32)
        out_ref[:, columns] = jnp.where(lane < HD, got[:tokens], got[tokens:])
        rates_ref[:, columns] = jnp.where(lane[:1] < HD, rates[0], rates[1])


def pass_kernel(facts, after, out_ref):
    out_ref[...] = facts[...]


def few(count):
    return count if count <= 8 else 1


def link_kernel(here, tokens, chunks, facts, *refs):
    others, (linked, through, one, half, before, last) = refs[:-6], refs[-6:]
    members, slices = facts.shape[0], len(others) + 1
    ctx, uly = lax.axis_index("ctx"), lax.axis_index("uly")
    for back, tile in enumerate((facts, *others)):
        at = lax.rem(ctx + slices - back, slices) * members
        last[pl.ds(pl.multiple_of(at, members), members), :] = jnp.broadcast_to(
            tile[:, LANES - 1 :], (members, LANES)
        )
    me = ctx * members + uly
    now = last[...]
    then = jnp.concatenate([now[:1], now[:-1]], 0)
    end = jnp.concatenate([now[chunks - 1 :], now[: chunks - 1]], 0)
    linked[...] = jnp.where(now == then, 1.0, 0.0)
    through[...] = jnp.where(end == then, 1.0, 0.0)
    before[...] = jnp.where(me > 0, last[pl.ds(jnp.maximum(me - 1, 0), 1), :], -1.0)
    rows = one.shape[0]
    share = min(rows, HD)
    owner = ctx * chunks + lax.rem(uly, chunks)
    for at in range(0, rows, share):
        rate = pair_rate(facts, lax.div(owner * rows + at, HD), here)
        for ref, length in ((one, tokens), (half, tokens * chunks)):
            ref[at : at + share, :] = jnp.broadcast_to(
                jnp.exp(-rate * float(length)), (share, LANES)
            )


def half_kernel(chunks, linked, one, in_ref, early_ref, final_ref):
    slices = early_ref.shape[0] + 1
    offset = jnp.where(lax.axis_index("uly") >= chunks, chunks, 0)

    def slice_end(c):
        def step(j, state):
            keep = linked[pl.ds(c * 2 * chunks + offset + j, 1), :] * one[...]
            return in_ref[c * chunks + j].astype(jnp.float32) + keep * state

        begin = in_ref[c * chunks].astype(jnp.float32)
        state = lax.fori_loop(1, chunks, step, begin, unroll=few(chunks - 1))
        return state.astype(early_ref.dtype)

    def early(c, _):
        early_ref[c] = slice_end(c)
        return 0

    lax.fori_loop(0, slices - 1, early, 0, unroll=few(slices - 1))
    final_ref[0] = slice_end(slices - 1)


def scan_kernel(
    chunks, linked, through, one, half, in_ref, early, final, after, out_ref
):
    slices = early.shape[0] + 1
    later = lax.axis_index("uly") >= chunks
    offset = jnp.where(later, chunks, 0)

    def over_other(state, c, piece, wanted):
        keep = through[pl.ds(c * 2 * chunks + chunks - offset, 1), :] * half[...]
        return jnp.where(wanted, piece.astype(jnp.float32) + keep * state, state)

    def over_own(state, c):
        def step(j, state):
            at = c * chunks + j
            out_ref[at] = state.astype(out_ref.dtype)
            keep = linked[pl.ds(c * 2 * chunks + offset + j, 1), :] * one[...]
            return in_ref[at].astype(jnp.float32) + keep * state

        return lax.fori_loop(0, chunks, step, state, unroll=few(chunks))

    def over_slice(c, state):
        state = over_own(over_other(state, c, early[c], later), c)
        return over_other(state, c, early[c], jnp.logical_not(later))

    begin = jnp.zeros(in_ref.shape[1:], jnp.float32)
    state = lax.fori_loop(0, slices - 1, over_slice, begin, unroll=few(slices - 1))
    over_own(over_other(state, slices - 1, final[0], later), slices - 1)


def norm_kernel(idcol, before, rates, q_ref, s_ref, inner_ref, gain, out_ref, raw, done, sems):
    tokens, width = q_ref.shape
    lane = lax.broadcasted_iota(jnp.int32, (HD, LANES), 1)
    place = lax.broadcasted_iota(jnp.int32, (tokens, LANES), 0)
    age = jnp.where(idcol[...] == before[...], (place + 1).astype(jnp.float32), NEVER)
    zero = jnp.zeros((HD, LANES), s_ref.dtype)
    total = jnp.zeros((tokens, LANES), jnp.float32)
    for j in range(0, width // LANES, 2):
        square = []
        for one in (0, 1):
            state = s_ref[(j + one) * HD : (j + one + 1) * HD, :]
            for half in (jnp.where(lane < HD, state, zero), jnp.where(lane < HD, zero, state)):
                square.append(jnp.concatenate([zero, half] if one else [half, zero], 1))
        columns = slice(j * LANES, (j + 2) * LANES)
        outer = jnp.dot(
            q_ref[:, columns], jnp.concatenate(square, 0), preferred_element_type=jnp.float32
        )
        for one in (0, 1):
            columns = slice((j + one) * LANES, (j + one + 1) * LANES)
            fade = jnp.exp(-rates[:, columns] * age)
            value = inner_ref[:, columns] + outer[:, one * LANES : (one + 1) * LANES] * fade
            total += value * value
            raw[:, columns] = value
    mean = jnp.sum(total, axis=1, keepdims=True) / float(width)
    scale = jnp.broadcast_to(lax.rsqrt(mean + 1e-06), (tokens, LANES))
    parts = sems.shape[0]
    share = width // parts
    copies = []
    for part in range(parts):
        for at in range(part * share, (part + 1) * share, LANES):
            columns = slice(at, at + LANES)
            done[:, columns] = (raw[:, columns] * scale * gain[:, columns]).astype(jnp.bfloat16)
        columns = slice(part * share, (part + 1) * share)
        copies.append(
            pltpu.make_async_copy(done.at[:, columns], out_ref.at[:, columns], sems.at[part])
        )
        copies[-1].start()
    for copy in copies:
        copy.wait()


def local(queries, keys, values, doc_ids, decay_rate, norm_gain):
    tokens, width = queries.shape
    here = decay_rate.shape[0]
    axes = ("ctx", "uly")
    slices, members = lax.axis_size("ctx"), lax.axis_size("uly")
    count = slices * members
    all_pairs = width // LANES
    chunks = members // 2
    group = slices * chunks
    rows = all_pairs * HD // group
    groups = [
        [c * members + half * chunks + u for c in range(slices) for u in range(chunks)]
        for half in (0, 1)
    ]
    swap = [
        (c * members + u, c * members + (u + chunks) % members)
        for c in range(slices)
        for u in range(members)
    ]

    vmem = pl.BlockSpec(memory_space=pltpu.VMEM)
    params = pltpu.CompilerParams(vmem_limit_bytes=32 * 1024 * 1024)
    shape = jax.ShapeDtypeStruct
    tile = shape((members, LANES), jnp.float32)

    own = jnp.pad(decay_rate, (0, LANES - here)) + jnp.pad(
        doc_ids, (LANES - tokens, 0)
    ).astype(jnp.float32)
    facts = lax.all_to_all(
        jnp.broadcast_to(own[None, :], tile.shape), "uly", split_axis=0, concat_axis=0, tiled=True
    )
    turned, filled, idrow, idcol = pl.pallas_call(
        turn_kernel,
        in_specs=[vmem] * 3,
        out_specs=[vmem] * 4,
        out_shape=[
            shape((width, LANES), jnp.bfloat16),
            shape((LANES, width), jnp.bfloat16),
            shape((8, LANES), jnp.float32),
            shape((tokens, LANES), jnp.float32),
        ],
        compiler_params=params,
        cost_estimate=pl.CostEstimate(flops=0, bytes_accessed=12_000_000, transcendentals=0),
        name="turn",
    )(own[None, :], keys, values)
    ends = pl.pallas_call(
        functools.partial(ends_kernel, here, tokens),
        in_specs=[vmem] * 4,
        out_specs=vmem,
        out_shape=shape((all_pairs * HD, LANES), jnp.bfloat16),
        compiler_params=params,
        name="ends",
    )(facts, idrow, turned, filled)
    pieces = lax.all_to_all(
        ends.reshape(group, rows, LANES),
        axes, split_axis=0, concat_axis=0, axis_index_groups=groups, tiled=True,
    )
    slice_facts = pl.pallas_call(
        pass_kernel,
        in_specs=[vmem, pl.BlockSpec(memory_space=pl.ANY)],
        out_specs=vmem,
        out_shape=tile,
        compiler_params=params,
        name="pass",
    )(facts, ends)
    others = [
        lax.ppermute(slice_facts, "ctx", [(c, (c + ahead) % slices) for c in range(slices)])
        for ahead in range(1, slices)
    ]
    linked, through, one, half, before = pl.pallas_call(
        functools.partial(link_kernel, here, tokens, chunks),
        in_specs=[vmem] * slices,
        out_specs=[vmem] * 5,
        out_shape=[shape((count, LANES), jnp.float32)] * 2
        + [shape((rows, LANES), jnp.float32)] * 2
        + [shape((1, LANES), jnp.float32)],
        scratch_shapes=[pltpu.VMEM((count, LANES), jnp.float32)],
        compiler_params=params,
        name="link",
    )(slice_facts, *others)
    early_ends, final_end = pl.pallas_call(
        functools.partial(half_kernel, chunks),
        in_specs=[vmem] * 3,
        out_specs=[vmem] * 2,
        out_shape=[
            shape((slices - 1, rows, LANES), jnp.bfloat16),
            shape((1, rows, LANES), jnp.bfloat16),
        ],
        compiler_params=params,
        name="half",
    )(linked, one, pieces)
    early = lax.ppermute(early_ends, axes, swap)
    final = lax.ppermute(final_end, axes, [(low, high) for low, high in swap if low < high])
    inner, rates = pl.pallas_call(
        functools.partial(inner_kernel, here),
        in_specs=[vmem] * 6 + [pl.BlockSpec(memory_space=pl.ANY)],
        out_specs=[vmem] * 2,
        out_shape=[shape((tokens, width), jnp.float32), shape((1, width), jnp.float32)],
        compiler_params=params,
        cost_estimate=pl.CostEstimate(
            flops=8_000_000_000, bytes_accessed=4_000_000, transcendentals=600_000
        ),
        name="inner",
    )(facts, idcol, idrow, queries, turned, values, early_ends)
    moved = pl.pallas_call(
        functools.partial(scan_kernel, chunks),
        in_specs=[vmem] * 7 + [pl.BlockSpec(memory_space=pl.ANY)],
        out_specs=vmem,
        out_shape=shape((group, rows, LANES), jnp.bfloat16),
        compiler_params=params,
        name="scan",
    )(linked, through, one, half, pieces, early, final, rates)
    states = lax.all_to_all(
        moved, axes, split_axis=0, concat_axis=0, axis_index_groups=groups, tiled=True
    )
    return pl.pallas_call(
        norm_kernel,
        in_specs=[vmem] * 7,
        out_specs=pl.BlockSpec(memory_space=pl.ANY),
        out_shape=shape((tokens, width), jnp.bfloat16),
        scratch_shapes=[
            pltpu.VMEM((tokens, width), jnp.float32),
            pltpu.VMEM((tokens, width), jnp.bfloat16),
            pltpu.SemaphoreType.DMA((4,)),
        ],
        compiler_params=params,
        name="norm",
    )(idcol, before, rates, queries, states.reshape(all_pairs * HD, LANES), inner, norm_gain[None, :])


def solution(mesh):
    in_specs = (
        P(("ctx", "uly"), None),
        P(("ctx", "uly"), None),
        P(("ctx", "uly"), None),
        P(("ctx", "uly")),
        P("uly"),
        P(),
    )
    out_specs = P(("ctx", "uly"), None)
    return jax.shard_map(local, mesh=mesh, in_specs=in_specs, out_specs=out_specs, check_vma=False)
```

```python
import functools

import jax
import jax.numpy as jnp
from jax import lax
from jax.experimental import pallas as pl
from jax.experimental.pallas import tpu as pltpu
from jax.sharding import PartitionSpec as P

HD = 64
LANES = 2 * HD
NEVER = 1e9


def rate_of(facts, head, here):
    return facts[head // here : head // here + 1, head % here : head % here + 1]


def pair_rate(facts, pair, here):
    lane = lax.broadcasted_iota(jnp.int32, (1, LANES), 1)
    rates = []
    for head in (2 * pair, 2 * pair + 1):
        row = facts[pl.ds(lax.div(head, here), 1), :]
        rates.append(
            jnp.sum(jnp.where(lane == lax.rem(head, here), row, 0.0), axis=1, keepdims=True)
        )
    return jnp.where(lane < HD, rates[0], rates[1])


def turn_kernel(row_ref, k_ref, v_ref, turned, filled, idrow, idcol):
    tokens, width = k_ref.shape
    fill = jnp.full((1, LANES - tokens), -1.0, jnp.float32)
    row = jnp.concatenate([row_ref[:1, LANES - tokens :], fill], 1)
    idrow[...] = jnp.broadcast_to(row, idrow.shape)
    idcol[...] = jnp.transpose(jnp.broadcast_to(row, (LANES, LANES)))[:tokens]
    filled[:tokens, :] = v_ref[...]
    filled[tokens:, :] = jnp.zeros((LANES - tokens, width), filled.dtype)
    blank = jnp.zeros((LANES - tokens, LANES), jnp.float32)
    for j in range(width // LANES):
        columns = slice(j * LANES, (j + 1) * LANES)
        block = jnp.concatenate([k_ref[:, columns].astype(jnp.float32), blank], 0)
        turned[columns, :] = jnp.transpose(block).astype(turned.dtype)


def ends_kernel(here, tokens, facts, idrow, turned, v_ref, out_ref, made, sems):
    width = v_ref.shape[1]
    lane = lax.broadcasted_iota(jnp.int32, (HD, LANES), 1)
    place = lax.broadcasted_iota(jnp.int32, idrow.shape, 1)
    ids = idrow[...]
    last = ids[:, tokens - 1 : tokens]
    age = jnp.where(ids == last, (tokens - 1 - place).astype(jnp.float32), NEVER)
    parts = sems.shape[0]
    share = made.shape[0] // parts
    copies = []
    for j in range(0, width // LANES, 2):
        weighted = []
        for head in range(2 * j, 2 * j + 4):
            weight = jnp.exp(-rate_of(facts, head, here) * age)
            keys = turned[head * HD : (head + 1) * HD, :].astype(jnp.float32)
            keys = keys.reshape(HD // 8, 8, LANES) * weight[None]
            weighted.append(keys.reshape(HD, LANES))
        weighted = jnp.concatenate(weighted, 0)
        high = weighted.astype(jnp.bfloat16)
        low = (weighted - high.astype(jnp.float32)).astype(jnp.bfloat16)
        v = v_ref[:, j * LANES : (j + 2) * LANES]
        both = jnp.dot(
            jnp.concatenate([high, low], 1),
            jnp.concatenate([v, v], 0),
            preferred_element_type=jnp.float32,
        )
        for one in (0, 1):
            pair = both[one * LANES : (one + 1) * LANES, one * LANES : (one + 1) * LANES]
            made[(j + one) * HD : (j + one + 1) * HD, :] = jnp.where(
                lane < HD, pair[:HD], pair[HD:]
            ).astype(jnp.bfloat16)
        if (j + 2) * HD % share == 0:
            part = (j + 2) * HD // share - 1
            rows = slice(part * share, (part + 1) * share)
            copies.append(pltpu.make_async_copy(made.at[rows], out_ref.at[rows], sems.at[part]))
            copies[-1].start()
    for copy in copies:
        copy.wait()


def inner_kernel(
    here, facts, idcol, idrow, q_ref, turned, v_ref, after, out_ref, rates_ref
):
    tokens, width = q_ref.shape
    lane = lax.broadcasted_iota(jnp.int32, (tokens, LANES), 1)
    t = lax.broadcasted_iota(jnp.int32, (tokens, LANES), 0)
    seen = (t >= lane) & (idcol[...] == idrow[:1, :])
    age = jnp.where(seen, (t - lane).astype(jnp.float32), NEVER)
    for j in range(width // LANES):
        columns = slice(j * LANES, (j + 1) * LANES)
        q = q_ref[:, columns]
        zero = jnp.zeros_like(q)
        stacked = jnp.concatenate([jnp.where(lane < HD, q, zero), jnp.where(lane < HD, zero, q)], 0)
        scores = jnp.dot(
            stacked, turned[columns, :], preferred_element_type=jnp.float32
        )
        rates = [rate_of(facts, 2 * j + one, here) for one in (0, 1)]
        weight = jnp.concatenate([jnp.exp(-rate * age) for rate in rates], 0)
        probs = (scores * weight)[:, :tokens].astype(jnp.bfloat16)
        got = jnp.dot(probs, v_ref[:, columns], preferred_element_type=jnp.float32)
        out_ref[:, columns] = jnp.where(lane < HD, got[:tokens], got[tokens:])
        rates_ref[:, columns] = jnp.where(lane[:1] < HD, rates[0], rates[1])


def pass_kernel(facts, after, out_ref):
    out_ref[...] = facts[...]


def few(count):
    return count if count <= 8 else 1


def link_kernel(here, tokens, chunks, facts, *refs):
    others, (linked, through, one, half, before, last) = refs[:-6], refs[-6:]
    members, slices = facts.shape[0], len(others) + 1
    ctx, uly = lax.axis_index("ctx"), lax.axis_index("uly")
    for back, tile in enumerate((facts, *others)):
        at = lax.rem(ctx + slices - back, slices) * members
        last[pl.ds(pl.multiple_of(at, members), members), :] = jnp.broadcast_to(
            tile[:, LANES - 1 :], (members, LANES)
        )
    me = ctx * members + uly
    now = last[...]
    then = jnp.concatenate([now[:1], now[:-1]], 0)
    end = jnp.concatenate([now[chunks - 1 :], now[: chunks - 1]], 0)
    linked[...] = jnp.where(now == then, 1.0, 0.0)
    through[...] = jnp.where(end == then, 1.0, 0.0)
    before[...] = jnp.where(me > 0, last[pl.ds(jnp.maximum(me - 1, 0), 1), :], -1.0)
    rows = one.shape[0]
    share = min(rows, HD)
    owner = ctx * chunks + lax.rem(uly, chunks)
    for at in range(0, rows, share):
        rate = pair_rate(facts, lax.div(owner * rows + at, HD), here)
        for ref, length in ((one, tokens), (half, tokens * chunks)):
            ref[at : at + share, :] = jnp.broadcast_to(
                jnp.exp(-rate * float(length)), (share, LANES)
            )


def half_kernel(chunks, linked, one, in_ref, early_ref, final_ref):
    slices = early_ref.shape[0] + 1
    offset = jnp.where(lax.axis_index("uly") >= chunks, chunks, 0)

    def slice_end(c):
        def step(j, state):
            keep = linked[pl.ds(c * 2 * chunks + offset + j, 1), :] * one[...]
            return in_ref[c * chunks + j].astype(jnp.float32) + keep * state

        begin = in_ref[c * chunks].astype(jnp.float32)
        state = lax.fori_loop(1, chunks, step, begin, unroll=few(chunks - 1))
        return state.astype(early_ref.dtype)

    def early(c, _):
        early_ref[c] = slice_end(c)
        return 0

    lax.fori_loop(0, slices - 1, early, 0, unroll=few(slices - 1))
    final_ref[0] = slice_end(slices - 1)


def scan_kernel(
    chunks, linked, through, one, half, in_ref, early, final, after, out_ref
):
    slices = early.shape[0] + 1
    later = lax.axis_index("uly") >= chunks
    offset = jnp.where(later, chunks, 0)

    def over_other(state, c, piece, wanted):
        keep = through[pl.ds(c * 2 * chunks + chunks - offset, 1), :] * half[...]
        return jnp.where(wanted, piece.astype(jnp.float32) + keep * state, state)

    def over_own(state, c):
        def step(j, state):
            at = c * chunks + j
            out_ref[at] = state.astype(out_ref.dtype)
            keep = linked[pl.ds(c * 2 * chunks + offset + j, 1), :] * one[...]
            return in_ref[at].astype(jnp.float32) + keep * state

        return lax.fori_loop(0, chunks, step, state, unroll=few(chunks))

    def over_slice(c, state):
        state = over_own(over_other(state, c, early[c], later), c)
        return over_other(state, c, early[c], jnp.logical_not(later))

    begin = jnp.zeros(in_ref.shape[1:], jnp.float32)
    state = lax.fori_loop(0, slices - 1, over_slice, begin, unroll=few(slices - 1))
    over_own(over_other(state, slices - 1, final[0], later), slices - 1)


def norm_kernel(idcol, before, rates, q_ref, s_ref, inner_ref, gain, out_ref, raw, done, sems):
    tokens, width = q_ref.shape
    lane = lax.broadcasted_iota(jnp.int32, (HD, LANES), 1)
    place = lax.broadcasted_iota(jnp.int32, (tokens, LANES), 0)
    age = jnp.where(idcol[...] == before[...], (place + 1).astype(jnp.float32), NEVER)
    zero = jnp.zeros((HD, LANES), s_ref.dtype)
    total = jnp.zeros((tokens, LANES), jnp.float32)
    for j in range(0, width // LANES, 2):
        square = []
        for one in (0, 1):
            state = s_ref[(j + one) * HD : (j + one + 1) * HD, :]
            for half in (jnp.where(lane < HD, state, zero), jnp.where(lane < HD, zero, state)):
                square.append(jnp.concatenate([zero, half] if one else [half, zero], 1))
        columns = slice(j * LANES, (j + 2) * LANES)
        outer = jnp.dot(
            q_ref[:, columns], jnp.concatenate(square, 0), preferred_element_type=jnp.float32
        )
        for one in (0, 1):
            columns = slice((j + one) * LANES, (j + one + 1) * LANES)
            fade = jnp.exp(-rates[:, columns] * age)
            value = inner_ref[:, columns] + outer[:, one * LANES : (one + 1) * LANES] * fade
            total += value * value
            raw[:, columns] = value
    mean = jnp.sum(total, axis=1, keepdims=True) / float(width)
    scale = jnp.broadcast_to(lax.rsqrt(mean + 1e-06), (tokens, LANES))
    parts = sems.shape[0]
    share = width // parts
    copies = []
    for part in range(parts):
        for at in range(part * share, (part + 1) * share, LANES):
            columns = slice(at, at + LANES)
            done[:, columns] = (raw[:, columns] * scale * gain[:, columns]).astype(jnp.bfloat16)
        columns = slice(part * share, (part + 1) * share)
        copies.append(
            pltpu.make_async_copy(done.at[:, columns], out_ref.at[:, columns], sems.at[part])
        )
        copies[-1].start()
    for copy in copies:
        copy.wait()


def local(queries, keys, values, doc_ids, decay_rate, norm_gain):
    tokens, width = queries.shape
    here = decay_rate.shape[0]
    axes = ("ctx", "uly")
    slices, members = lax.axis_size("ctx"), lax.axis_size("uly")
    count = slices * members
    all_pairs = width // LANES
    chunks = members // 2
    group = slices * chunks
    rows = all_pairs * HD // group
    groups = [
        [c * members + half * chunks + u for c in range(slices) for u in range(chunks)]
        for half in (0, 1)
    ]
    swap = [
        (c * members + u, c * members + (u + chunks) % members)
        for c in range(slices)
        for u in range(members)
    ]

    vmem = pl.BlockSpec(memory_space=pltpu.VMEM)
    params = pltpu.CompilerParams(vmem_limit_bytes=32 * 1024 * 1024)
    shape = jax.ShapeDtypeStruct
    tile = shape((members, LANES), jnp.float32)

    own = jnp.pad(decay_rate, (0, LANES - here)) + jnp.pad(
        doc_ids, (LANES - tokens, 0)
    ).astype(jnp.float32)
    facts = lax.all_to_all(
        jnp.broadcast_to(own[None, :], tile.shape), "uly", split_axis=0, concat_axis=0, tiled=True
    )
    turned, filled, idrow, idcol = pl.pallas_call(
        turn_kernel,
        in_specs=[vmem] * 3,
        out_specs=[vmem] * 4,
        out_shape=[
            shape((width, LANES), jnp.bfloat16),
            shape((LANES, width), jnp.bfloat16),
            shape((8, LANES), jnp.float32),
            shape((tokens, LANES), jnp.float32),
        ],
        compiler_params=params,
        cost_estimate=pl.CostEstimate(flops=0, bytes_accessed=12_000_000, transcendentals=0),
        name="turn",
    )(own[None, :], keys, values)
    ends = pl.pallas_call(
        functools.partial(ends_kernel, here, tokens),
        in_specs=[vmem] * 4,
        out_specs=pl.BlockSpec(memory_space=pl.ANY),
        out_shape=shape((all_pairs * HD, LANES), jnp.bfloat16),
        scratch_shapes=[
            pltpu.VMEM((all_pairs * HD, LANES), jnp.bfloat16),
            pltpu.SemaphoreType.DMA((8,)),
        ],
        compiler_params=params,
        name="ends",
    )(facts, idrow, turned, filled)
    pieces = lax.all_to_all(
        ends.reshape(group, rows, LANES),
        axes, split_axis=0, concat_axis=0, axis_index_groups=groups, tiled=True,
    )
    slice_facts = pl.pallas_call(
        pass_kernel,
        in_specs=[vmem, pl.BlockSpec(memory_space=pl.ANY)],
        out_specs=vmem,
        out_shape=tile,
        compiler_params=params,
        name="pass",
    )(facts, ends)
    others = [
        lax.ppermute(slice_facts, "ctx", [(c, (c + ahead) % slices) for c in range(slices)])
        for ahead in range(1, slices)
    ]
    linked, through, one, half, before = pl.pallas_call(
        functools.partial(link_kernel, here, tokens, chunks),
        in_specs=[vmem] * slices,
        out_specs=[vmem] * 5,
        out_shape=[shape((count, LANES), jnp.float32)] * 2
        + [shape((rows, LANES), jnp.float32)] * 2
        + [shape((1, LANES), jnp.float32)],
        scratch_shapes=[pltpu.VMEM((count, LANES), jnp.float32)],
        compiler_params=params,
        name="link",
    )(slice_facts, *others)
    early_ends, final_end = pl.pallas_call(
        functools.partial(half_kernel, chunks),
        in_specs=[vmem] * 3,
        out_specs=[vmem] * 2,
        out_shape=[
            shape((slices - 1, rows, LANES), jnp.bfloat16),
            shape((1, rows, LANES), jnp.bfloat16),
        ],
        compiler_params=params,
        name="half",
    )(linked, one, pieces)
    early = lax.ppermute(early_ends, axes, swap)
    final = lax.ppermute(final_end, axes, [(low, high) for low, high in swap if low < high])
    inner, rates = pl.pallas_call(
        functools.partial(inner_kernel, here),
        in_specs=[vmem] * 6 + [pl.BlockSpec(memory_space=pl.ANY)],
        out_specs=[vmem] * 2,
        out_shape=[shape((tokens, width), jnp.float32), shape((1, width), jnp.float32)],
        compiler_params=params,
        cost_estimate=pl.CostEstimate(
            flops=8_000_000_000, bytes_accessed=4_000_000, transcendentals=600_000
        ),
        name="inner",
    )(facts, idcol, idrow, queries, turned, values, early_ends)
    moved = pl.pallas_call(
        functools.partial(scan_kernel, chunks),
        in_specs=[vmem] * 7 + [pl.BlockSpec(memory_space=pl.ANY)],
        out_specs=vmem,
        out_shape=shape((group, rows, LANES), jnp.bfloat16),
        compiler_params=params,
        name="scan",
    )(linked, through, one, half, pieces, early, final, rates)
    states = lax.all_to_all(
        moved, axes, split_axis=0, concat_axis=0, axis_index_groups=groups, tiled=True
    )
    return pl.pallas_call(
        norm_kernel,
        in_specs=[vmem] * 7,
        out_specs=pl.BlockSpec(memory_space=pl.ANY),
        out_shape=shape((tokens, width), jnp.bfloat16),
        scratch_shapes=[
            pltpu.VMEM((tokens, width), jnp.float32),
            pltpu.VMEM((tokens, width), jnp.bfloat16),
            pltpu.SemaphoreType.DMA((16,)),
        ],
        compiler_params=params,
        name="norm",
    )(idcol, before, rates, queries, states.reshape(all_pairs * HD, LANES), inner, norm_gain[None, :])


def solution(mesh):
    in_specs = (
        P(("ctx", "uly"), None),
        P(("ctx", "uly"), None),
        P(("ctx", "uly"), None),
        P(("ctx", "uly")),
        P("uly"),
        P(),
    )
    out_specs = P(("ctx", "uly"), None)
    return jax.shard_map(local, mesh=mesh, in_specs=in_specs, out_specs=out_specs, check_vma=False)
```

```python
import functools

import jax
import jax.numpy as jnp
from jax import lax
from jax.experimental import pallas as pl
from jax.experimental.pallas import tpu as pltpu
from jax.sharding import PartitionSpec as P

HD = 64
LANES = 2 * HD
NEVER = 1e9


def rate_of(facts, head, here):
    return facts[head // here : head // here + 1, head % here : head % here + 1]


def pair_rate(facts, pair, here):
    lane = lax.broadcasted_iota(jnp.int32, (1, LANES), 1)
    rates = []
    for head in (2 * pair, 2 * pair + 1):
        row = facts[pl.ds(lax.div(head, here), 1), :]
        rates.append(
            jnp.sum(jnp.where(lane == lax.rem(head, here), row, 0.0), axis=1, keepdims=True)
        )
    return jnp.where(lane < HD, rates[0], rates[1])


def turn_kernel(row_ref, k_ref, v_ref, turned, filled, idrow, idcol):
    tokens, width = k_ref.shape
    fill = jnp.full((1, LANES - tokens), -1.0, jnp.float32)
    row = jnp.concatenate([row_ref[:1, LANES - tokens :], fill], 1)
    idrow[...] = jnp.broadcast_to(row, idrow.shape)
    idcol[...] = jnp.transpose(jnp.broadcast_to(row, (LANES, LANES)))[:tokens]
    filled[:tokens, :] = v_ref[...]
    filled[tokens:, :] = jnp.zeros((LANES - tokens, width), filled.dtype)
    blank = jnp.zeros((LANES - tokens, LANES), jnp.float32)
    for j in range(width // LANES):
        columns = slice(j * LANES, (j + 1) * LANES)
        block = jnp.concatenate([k_ref[:, columns].astype(jnp.float32), blank], 0)
        turned[columns, :] = jnp.transpose(block).astype(turned.dtype)


def ends_kernel(here, tokens, facts, idrow, turned, v_ref, out_ref, made, sems):
    width = v_ref.shape[1]
    lane = lax.broadcasted_iota(jnp.int32, (HD, LANES), 1)
    place = lax.broadcasted_iota(jnp.int32, idrow.shape, 1)
    ids = idrow[...]
    last = ids[:, tokens - 1 : tokens]
    age = jnp.where(ids == last, (tokens - 1 - place).astype(jnp.float32), NEVER)
    parts = sems.shape[0]
    share = made.shape[0] // parts
    copies = []
    for j in range(0, width // LANES, 2):
        weighted = []
        for head in range(2 * j, 2 * j + 4):
            weight = jnp.exp(-rate_of(facts, head, here) * age)
            keys = turned[head * HD : (head + 1) * HD, :].astype(jnp.float32)
            keys = keys.reshape(HD // 8, 8, LANES) * weight[None]
            weighted.append(keys.reshape(HD, LANES))
        weighted = jnp.concatenate(weighted, 0)
        high = weighted.astype(jnp.bfloat16)
        low = (weighted - high.astype(jnp.float32)).astype(jnp.bfloat16)
        v = v_ref[:, j * LANES : (j + 2) * LANES]
        both = jnp.dot(
            jnp.concatenate([high, low], 1),
            jnp.concatenate([v, v], 0),
            preferred_element_type=jnp.float32,
        )
        for one in (0, 1):
            pair = both[one * LANES : (one + 1) * LANES, one * LANES : (one + 1) * LANES]
            made[(j + one) * HD : (j + one + 1) * HD, :] = jnp.where(
                lane < HD, pair[:HD], pair[HD:]
            ).astype(jnp.bfloat16)
        if (j + 2) * HD % share == 0:
            part = (j + 2) * HD // share - 1
            rows = slice(part * share, (part + 1) * share)
            copies.append(pltpu.make_async_copy(made.at[rows], out_ref.at[rows], sems.at[part]))
            copies[-1].start(priority=part % 2)
    for copy in copies:
        copy.wait()


def inner_kernel(
    here, facts, idcol, idrow, q_ref, turned, v_ref, after, out_ref, rates_ref
):
    tokens, width = q_ref.shape
    lane = lax.broadcasted_iota(jnp.int32, (tokens, LANES), 1)
    t = lax.broadcasted_iota(jnp.int32, (tokens, LANES), 0)
    seen = (t >= lane) & (idcol[...] == idrow[:1, :])
    age = jnp.where(seen, (t - lane).astype(jnp.float32), NEVER)
    for j in range(width // LANES):
        columns = slice(j * LANES, (j + 1) * LANES)
        q = q_ref[:, columns]
        zero = jnp.zeros_like(q)
        stacked = jnp.concatenate([jnp.where(lane < HD, q, zero), jnp.where(lane < HD, zero, q)], 0)
        scores = jnp.dot(
            stacked, turned[columns, :], preferred_element_type=jnp.float32
        )
        rates = [rate_of(facts, 2 * j + one, here) for one in (0, 1)]
        weight = jnp.concatenate([jnp.exp(-rate * age) for rate in rates], 0)
        probs = (scores * weight)[:, :tokens].astype(jnp.bfloat16)
        got = jnp.dot(probs, v_ref[:, columns], preferred_element_type=jnp.float32)
        out_ref[:, columns] = jnp.where(lane < HD, got[:tokens], got[tokens:])
        rates_ref[:, columns] = jnp.where(lane[:1] < HD, rates[0], rates[1])


def pass_kernel(facts, after, out_ref):
    out_ref[...] = facts[...]


def few(count):
    return count if count <= 8 else 1


def link_kernel(here, tokens, chunks, facts, *refs):
    others, (linked, through, one, half, before, last) = refs[:-6], refs[-6:]
    members, slices = facts.shape[0], len(others) + 1
    ctx, uly = lax.axis_index("ctx"), lax.axis_index("uly")
    for back, tile in enumerate((facts, *others)):
        at = lax.rem(ctx + slices - back, slices) * members
        last[pl.ds(pl.multiple_of(at, members), members), :] = jnp.broadcast_to(
            tile[:, LANES - 1 :], (members, LANES)
        )
    me = ctx * members + uly
    now = last[...]
    then = jnp.concatenate([now[:1], now[:-1]], 0)
    end = jnp.concatenate([now[chunks - 1 :], now[: chunks - 1]], 0)
    linked[...] = jnp.where(now == then, 1.0, 0.0)
    through[...] = jnp.where(end == then, 1.0, 0.0)
    before[...] = jnp.where(me > 0, last[pl.ds(jnp.maximum(me - 1, 0), 1), :], -1.0)
    rows = one.shape[0]
    share = min(rows, HD)
    owner = ctx * chunks + lax.rem(uly, chunks)
    for at in range(0, rows, share):
        rate = pair_rate(facts, lax.div(owner * rows + at, HD), here)
        for ref, length in ((one, tokens), (half, tokens * chunks)):
            ref[at : at + share, :] = jnp.broadcast_to(
                jnp.exp(-rate * float(length)), (share, LANES)
            )


def half_kernel(chunks, linked, one, in_ref, early_ref, final_ref):
    slices = early_ref.shape[0] + 1
    offset = jnp.where(lax.axis_index("uly") >= chunks, chunks, 0)

    def slice_end(c):
        def step(j, state):
            keep = linked[pl.ds(c * 2 * chunks + offset + j, 1), :] * one[...]
            return in_ref[c * chunks + j].astype(jnp.float32) + keep * state

        begin = in_ref[c * chunks].astype(jnp.float32)
        state = lax.fori_loop(1, chunks, step, begin, unroll=few(chunks - 1))
        return state.astype(early_ref.dtype)

    def early(c, _):
        early_ref[c] = slice_end(c)
        return 0

    lax.fori_loop(0, slices - 1, early, 0, unroll=few(slices - 1))
    final_ref[0] = slice_end(slices - 1)


def scan_kernel(
    chunks, linked, through, one, half, in_ref, early, final, after, out_ref
):
    slices = early.shape[0] + 1
    later = lax.axis_index("uly") >= chunks
    offset = jnp.where(later, chunks, 0)

    def over_other(state, c, piece, wanted):
        keep = through[pl.ds(c * 2 * chunks + chunks - offset, 1), :] * half[...]
        return jnp.where(wanted, piece.astype(jnp.float32) + keep * state, state)

    def over_own(state, c):
        def step(j, state):
            at = c * chunks + j
            out_ref[at] = state.astype(out_ref.dtype)
            keep = linked[pl.ds(c * 2 * chunks + offset + j, 1), :] * one[...]
            return in_ref[at].astype(jnp.float32) + keep * state

        return lax.fori_loop(0, chunks, step, state, unroll=few(chunks))

    def over_slice(c, state):
        state = over_own(over_other(state, c, early[c], later), c)
        return over_other(state, c, early[c], jnp.logical_not(later))

    begin = jnp.zeros(in_ref.shape[1:], jnp.float32)
    state = lax.fori_loop(0, slices - 1, over_slice, begin, unroll=few(slices - 1))
    over_own(over_other(state, slices - 1, final[0], later), slices - 1)


def norm_kernel(idcol, before, rates, q_ref, s_ref, inner_ref, gain, out_ref, raw, done, sems):
    tokens, width = q_ref.shape
    lane = lax.broadcasted_iota(jnp.int32, (HD, LANES), 1)
    place = lax.broadcasted_iota(jnp.int32, (tokens, LANES), 0)
    age = jnp.where(idcol[...] == before[...], (place + 1).astype(jnp.float32), NEVER)
    zero = jnp.zeros((HD, LANES), s_ref.dtype)
    total = jnp.zeros((tokens, LANES), jnp.float32)
    for j in range(0, width // LANES, 2):
        square = []
        for one in (0, 1):
            state = s_ref[(j + one) * HD : (j + one + 1) * HD, :]
            for half in (jnp.where(lane < HD, state, zero), jnp.where(lane < HD, zero, state)):
                square.append(jnp.concatenate([zero, half] if one else [half, zero], 1))
        columns = slice(j * LANES, (j + 2) * LANES)
        outer = jnp.dot(
            q_ref[:, columns], jnp.concatenate(square, 0), preferred_element_type=jnp.float32
        )
        for one in (0, 1):
            columns = slice((j + one) * LANES, (j + one + 1) * LANES)
            fade = jnp.exp(-rates[:, columns] * age)
            value = inner_ref[:, columns] + outer[:, one * LANES : (one + 1) * LANES] * fade
            total += value * value
            raw[:, columns] = value
    mean = jnp.sum(total, axis=1, keepdims=True) / float(width)
    scale = jnp.broadcast_to(lax.rsqrt(mean + 1e-06), (tokens, LANES))
    parts = sems.shape[0]
    share = width // parts
    copies = []
    for part in range(parts):
        for at in range(part * share, (part + 1) * share, LANES):
            columns = slice(at, at + LANES)
            done[:, columns] = (raw[:, columns] * scale * gain[:, columns]).astype(jnp.bfloat16)
        columns = slice(part * share, (part + 1) * share)
        copies.append(
            pltpu.make_async_copy(done.at[:, columns], out_ref.at[:, columns], sems.at[part])
        )
        copies[-1].start(priority=part % 2)
    for copy in copies:
        copy.wait()


def local(queries, keys, values, doc_ids, decay_rate, norm_gain):
    tokens, width = queries.shape
    here = decay_rate.shape[0]
    axes = ("ctx", "uly")
    slices, members = lax.axis_size("ctx"), lax.axis_size("uly")
    count = slices * members
    all_pairs = width // LANES
    chunks = members // 2
    group = slices * chunks
    rows = all_pairs * HD // group
    groups = [
        [c * members + half * chunks + u for c in range(slices) for u in range(chunks)]
        for half in (0, 1)
    ]
    swap = [
        (c * members + u, c * members + (u + chunks) % members)
        for c in range(slices)
        for u in range(members)
    ]

    vmem = pl.BlockSpec(memory_space=pltpu.VMEM)
    params = pltpu.CompilerParams(vmem_limit_bytes=32 * 1024 * 1024)
    shape = jax.ShapeDtypeStruct
    tile = shape((members, LANES), jnp.float32)

    own = jnp.pad(decay_rate, (0, LANES - here)) + jnp.pad(
        doc_ids, (LANES - tokens, 0)
    ).astype(jnp.float32)
    facts = lax.all_to_all(
        jnp.broadcast_to(own[None, :], tile.shape), "uly", split_axis=0, concat_axis=0, tiled=True
    )
    turned, filled, idrow, idcol = pl.pallas_call(
        turn_kernel,
        in_specs=[vmem] * 3,
        out_specs=[vmem] * 4,
        out_shape=[
            shape((width, LANES), jnp.bfloat16),
            shape((LANES, width), jnp.bfloat16),
            shape((8, LANES), jnp.float32),
            shape((tokens, LANES), jnp.float32),
        ],
        compiler_params=params,
        cost_estimate=pl.CostEstimate(flops=0, bytes_accessed=12_000_000, transcendentals=0),
        name="turn",
    )(own[None, :], keys, values)
    ends = pl.pallas_call(
        functools.partial(ends_kernel, here, tokens),
        in_specs=[vmem] * 4,
        out_specs=pl.BlockSpec(memory_space=pl.ANY),
        out_shape=shape((all_pairs * HD, LANES), jnp.bfloat16),
        scratch_shapes=[
            pltpu.VMEM((all_pairs * HD, LANES), jnp.bfloat16),
            pltpu.SemaphoreType.DMA((8,)),
        ],
        compiler_params=params,
        name="ends",
    )(facts, idrow, turned, filled)
    pieces = lax.all_to_all(
        ends.reshape(group, rows, LANES),
        axes, split_axis=0, concat_axis=0, axis_index_groups=groups, tiled=True,
    )
    slice_facts = pl.pallas_call(
        pass_kernel,
        in_specs=[vmem, pl.BlockSpec(memory_space=pl.ANY)],
        out_specs=vmem,
        out_shape=tile,
        compiler_params=params,
        name="pass",
    )(facts, ends)
    others = [
        lax.ppermute(slice_facts, "ctx", [(c, (c + ahead) % slices) for c in range(slices)])
        for ahead in range(1, slices)
    ]
    linked, through, one, half, before = pl.pallas_call(
        functools.partial(link_kernel, here, tokens, chunks),
        in_specs=[vmem] * slices,
        out_specs=[vmem] * 5,
        out_shape=[shape((count, LANES), jnp.float32)] * 2
        + [shape((rows, LANES), jnp.float32)] * 2
        + [shape((1, LANES), jnp.float32)],
        scratch_shapes=[pltpu.VMEM((count, LANES), jnp.float32)],
        compiler_params=params,
        name="link",
    )(slice_facts, *others)
    early_ends, final_end = pl.pallas_call(
        functools.partial(half_kernel, chunks),
        in_specs=[vmem] * 3,
        out_specs=[vmem] * 2,
        out_shape=[
            shape((slices - 1, rows, LANES), jnp.bfloat16),
            shape((1, rows, LANES), jnp.bfloat16),
        ],
        compiler_params=params,
        name="half",
    )(linked, one, pieces)
    early = lax.ppermute(early_ends, axes, swap)
    final = lax.ppermute(final_end, axes, [(low, high) for low, high in swap if low < high])
    inner, rates = pl.pallas_call(
        functools.partial(inner_kernel, here),
        in_specs=[vmem] * 6 + [pl.BlockSpec(memory_space=pl.ANY)],
        out_specs=[vmem] * 2,
        out_shape=[shape((tokens, width), jnp.float32), shape((1, width), jnp.float32)],
        compiler_params=params,
        cost_estimate=pl.CostEstimate(
            flops=8_000_000_000, bytes_accessed=4_000_000, transcendentals=600_000
        ),
        name="inner",
    )(facts, idcol, idrow, queries, turned, values, early_ends)
    moved = pl.pallas_call(
        functools.partial(scan_kernel, chunks),
        in_specs=[vmem] * 7 + [pl.BlockSpec(memory_space=pl.ANY)],
        out_specs=vmem,
        out_shape=shape((group, rows, LANES), jnp.bfloat16),
        compiler_params=params,
        name="scan",
    )(linked, through, one, half, pieces, early, final, rates)
    states = lax.all_to_all(
        moved, axes, split_axis=0, concat_axis=0, axis_index_groups=groups, tiled=True
    )
    return pl.pallas_call(
        norm_kernel,
        in_specs=[vmem] * 7,
        out_specs=pl.BlockSpec(memory_space=pl.ANY),
        out_shape=shape((tokens, width), jnp.bfloat16),
        scratch_shapes=[
            pltpu.VMEM((tokens, width), jnp.float32),
            pltpu.VMEM((tokens, width), jnp.bfloat16),
            pltpu.SemaphoreType.DMA((16,)),
        ],
        compiler_params=params,
        name="norm",
    )(idcol, before, rates, queries, states.reshape(all_pairs * HD, LANES), inner, norm_gain[None, :])


def solution(mesh):
    in_specs = (
        P(("ctx", "uly"), None),
        P(("ctx", "uly"), None),
        P(("ctx", "uly"), None),
        P(("ctx", "uly")),
        P("uly"),
        P(),
    )
    out_specs = P(("ctx", "uly"), None)
    return jax.shard_map(local, mesh=mesh, in_specs=in_specs, out_specs=out_specs, check_vma=False)
```

```python
import functools

import jax
import jax.numpy as jnp
from jax import lax
from jax.experimental import pallas as pl
from jax.experimental.pallas import tpu as pltpu
from jax.sharding import PartitionSpec as P

HD = 64
LANES = 2 * HD
NEVER = 1e9


def rate_of(facts, head, here):
    return facts[head // here : head // here + 1, head % here : head % here + 1]


def pair_rate(facts, pair, here):
    lane = lax.broadcasted_iota(jnp.int32, (1, LANES), 1)
    rates = []
    for head in (2 * pair, 2 * pair + 1):
        row = facts[pl.ds(lax.div(head, here), 1), :]
        rates.append(
            jnp.sum(jnp.where(lane == lax.rem(head, here), row, 0.0), axis=1, keepdims=True)
        )
    return jnp.where(lane < HD, rates[0], rates[1])


def turn_kernel(row_ref, k_ref, v_ref, turned, filled, idrow, idcol):
    tokens, width = k_ref.shape
    fill = jnp.full((1, LANES - tokens), -1.0, jnp.float32)
    row = jnp.concatenate([row_ref[:1, LANES - tokens :], fill], 1)
    idrow[...] = jnp.broadcast_to(row, idrow.shape)
    idcol[...] = jnp.transpose(jnp.broadcast_to(row, (LANES, LANES)))[:tokens]
    filled[:tokens, :] = v_ref[...]
    filled[tokens:, :] = jnp.zeros((LANES - tokens, width), filled.dtype)
    blank = jnp.zeros((LANES - tokens, LANES), jnp.float32)
    for j in range(width // LANES):
        columns = slice(j * LANES, (j + 1) * LANES)
        block = jnp.concatenate([k_ref[:, columns].astype(jnp.float32), blank], 0)
        turned[columns, :] = jnp.transpose(block).astype(turned.dtype)


def ends_kernel(here, tokens, facts, idrow, turned, v_ref, out_ref, made, sems):
    width = v_ref.shape[1]
    lane = lax.broadcasted_iota(jnp.int32, (HD, LANES), 1)
    place = lax.broadcasted_iota(jnp.int32, idrow.shape, 1)
    ids = idrow[...]
    last = ids[:, tokens - 1 : tokens]
    age = jnp.where(ids == last, (tokens - 1 - place).astype(jnp.float32), NEVER)
    parts = sems.shape[0]
    wide = width // parts
    tall = made.shape[0] // parts

    def copy_of(part):
        rows = pl.ds(pl.multiple_of(part * tall, tall), tall)
        return pltpu.make_async_copy(made.at[rows], out_ref.at[rows], sems.at[part])

    def make(part, _):
        for quad in range(wide // (2 * LANES)):
            weighted = []
            for head in range(4 * quad, 4 * quad + 4):
                row = part * (wide // HD // here) + head // here
                rate = facts[pl.ds(row, 1), head % here : head % here + 1]
                weight = jnp.exp(-rate * age)
                at = pl.multiple_of(part * wide + head * HD, HD)
                keys = turned[pl.ds(at, HD), :].astype(jnp.float32)
                keys = keys.reshape(HD // 8, 8, LANES) * weight[None]
                weighted.append(keys.reshape(HD, LANES))
            weighted = jnp.concatenate(weighted, 0)
            high = weighted.astype(jnp.bfloat16)
            low = (weighted - high.astype(jnp.float32)).astype(jnp.bfloat16)
            at = pl.multiple_of(part * wide + quad * 2 * LANES, 2 * LANES)
            v = v_ref[:, pl.ds(at, 2 * LANES)]
            both = jnp.dot(
                jnp.concatenate([high, low], 1),
                jnp.concatenate([v, v], 0),
                preferred_element_type=jnp.float32,
            )
            for one in (0, 1):
                pair = both[one * LANES : (one + 1) * LANES, one * LANES : (one + 1) * LANES]
                at = pl.multiple_of(part * tall + (2 * quad + one) * HD, HD)
                made[pl.ds(at, HD), :] = jnp.where(lane < HD, pair[:HD], pair[HD:]).astype(
                    jnp.bfloat16
                )
        copy_of(part).start()
        return 0

    lax.fori_loop(0, parts, make, 0)

    def finish(part, _):
        copy_of(part).wait()
        return 0

    lax.fori_loop(0, parts, finish, 0)


def inner_kernel(
    here, facts, idcol, idrow, q_ref, turned, v_ref, after, out_ref, rates_ref
):
    tokens, width = q_ref.shape
    lane = lax.broadcasted_iota(jnp.int32, (tokens, LANES), 1)
    t = lax.broadcasted_iota(jnp.int32, (tokens, LANES), 0)
    seen = (t >= lane) & (idcol[...] == idrow[:1, :])
    age = jnp.where(seen, (t - lane).astype(jnp.float32), NEVER)
    for j in range(width // LANES):
        columns = slice(j * LANES, (j + 1) * LANES)
        q = q_ref[:, columns]
        zero = jnp.zeros_like(q)
        stacked = jnp.concatenate([jnp.where(lane < HD, q, zero), jnp.where(lane < HD, zero, q)], 0)
        scores = jnp.dot(
            stacked, turned[columns, :], preferred_element_type=jnp.float32
        )
        rates = [rate_of(facts, 2 * j + one, here) for one in (0, 1)]
        weight = jnp.concatenate([jnp.exp(-rate * age) for rate in rates], 0)
        probs = (scores * weight)[:, :tokens].astype(jnp.bfloat16)
        got = jnp.dot(probs, v_ref[:, columns], preferred_element_type=jnp.float32)
        out_ref[:, columns] = jnp.where(lane < HD, got[:tokens], got[tokens:])
        rates_ref[:, columns] = jnp.where(lane[:1] < HD, rates[0], rates[1])


def pass_kernel(facts, after, out_ref):
    out_ref[...] = facts[...]


def few(count):
    return count if count <= 8 else 1


def link_kernel(here, tokens, chunks, facts, *refs):
    others, (linked, through, one, half, before, last) = refs[:-6], refs[-6:]
    members, slices = facts.shape[0], len(others) + 1
    ctx, uly = lax.axis_index("ctx"), lax.axis_index("uly")
    for back, tile in enumerate((facts, *others)):
        at = lax.rem(ctx + slices - back, slices) * members
        last[pl.ds(pl.multiple_of(at, members), members), :] = jnp.broadcast_to(
            tile[:, LANES - 1 :], (members, LANES)
        )
    me = ctx * members + uly
    now = last[...]
    then = jnp.concatenate([now[:1], now[:-1]], 0)
    end = jnp.concatenate([now[chunks - 1 :], now[: chunks - 1]], 0)
    linked[...] = jnp.where(now == then, 1.0, 0.0)
    through[...] = jnp.where(end == then, 1.0, 0.0)
    before[...] = jnp.where(me > 0, last[pl.ds(jnp.maximum(me - 1, 0), 1), :], -1.0)
    rows = one.shape[0]
    share = min(rows, HD)
    owner = ctx * chunks + lax.rem(uly, chunks)
    for at in range(0, rows, share):
        rate = pair_rate(facts, lax.div(owner * rows + at, HD), here)
        for ref, length in ((one, tokens), (half, tokens * chunks)):
            ref[at : at + share, :] = jnp.broadcast_to(
                jnp.exp(-rate * float(length)), (share, LANES)
            )


def half_kernel(chunks, linked, one, in_ref, early_ref, final_ref):
    slices = early_ref.shape[0] + 1
    offset = jnp.where(lax.axis_index("uly") >= chunks, chunks, 0)

    def slice_end(c):
        def step(j, state):
            keep = linked[pl.ds(c * 2 * chunks + offset + j, 1), :] * one[...]
            return in_ref[c * chunks + j].astype(jnp.float32) + keep * state

        begin = in_ref[c * chunks].astype(jnp.float32)
        state = lax.fori_loop(1, chunks, step, begin, unroll=few(chunks - 1))
        return state.astype(early_ref.dtype)

    def early(c, _):
        early_ref[c] = slice_end(c)
        return 0

    lax.fori_loop(0, slices - 1, early, 0, unroll=few(slices - 1))
    final_ref[0] = slice_end(slices - 1)


def scan_kernel(
    chunks, linked, through, one, half, in_ref, early, final, after, out_ref
):
    slices = early.shape[0] + 1
    later = lax.axis_index("uly") >= chunks
    offset = jnp.where(later, chunks, 0)

    def over_other(state, c, piece, wanted):
        keep = through[pl.ds(c * 2 * chunks + chunks - offset, 1), :] * half[...]
        return jnp.where(wanted, piece.astype(jnp.float32) + keep * state, state)

    def over_own(state, c):
        def step(j, state):
            at = c * chunks + j
            out_ref[at] = state.astype(out_ref.dtype)
            keep = linked[pl.ds(c * 2 * chunks + offset + j, 1), :] * one[...]
            return in_ref[at].astype(jnp.float32) + keep * state

        return lax.fori_loop(0, chunks, step, state, unroll=few(chunks))

    def over_slice(c, state):
        state = over_own(over_other(state, c, early[c], later), c)
        return over_other(state, c, early[c], jnp.logical_not(later))

    begin = jnp.zeros(in_ref.shape[1:], jnp.float32)
    state = lax.fori_loop(0, slices - 1, over_slice, begin, unroll=few(slices - 1))
    over_own(over_other(state, slices - 1, final[0], later), slices - 1)


def norm_kernel(idcol, before, rates, q_ref, s_ref, inner_ref, gain, out_ref, raw, done, sems):
    tokens, width = q_ref.shape
    lane = lax.broadcasted_iota(jnp.int32, (HD, LANES), 1)
    place = lax.broadcasted_iota(jnp.int32, (tokens, LANES), 0)
    age = jnp.where(idcol[...] == before[...], (place + 1).astype(jnp.float32), NEVER)
    zero = jnp.zeros((HD, LANES), s_ref.dtype)

    def join(quad, total):
        square = []
        for one in (0, 1):
            at = pl.multiple_of((2 * quad + one) * HD, HD)
            state = s_ref[pl.ds(at, HD), :]
            for half in (jnp.where(lane < HD, state, zero), jnp.where(lane < HD, zero, state)):
                square.append(jnp.concatenate([zero, half] if one else [half, zero], 1))
        columns = pl.ds(pl.multiple_of(quad * 2 * LANES, 2 * LANES), 2 * LANES)
        outer = jnp.dot(
            q_ref[:, columns], jnp.concatenate(square, 0), preferred_element_type=jnp.float32
        )
        for one in (0, 1):
            columns = pl.ds(pl.multiple_of((2 * quad + one) * LANES, LANES), LANES)
            fade = jnp.exp(-rates[:, columns] * age)
            value = inner_ref[:, columns] + outer[:, one * LANES : (one + 1) * LANES] * fade
            total += value * value
            raw[:, columns] = value
        return total

    total = jnp.zeros((tokens, LANES), jnp.float32)
    total = lax.fori_loop(0, width // (2 * LANES), join, total, unroll=2)
    mean = jnp.sum(total, axis=1, keepdims=True) / float(width)
    scale = jnp.broadcast_to(lax.rsqrt(mean + 1e-06), (tokens, LANES))
    parts = sems.shape[0]
    share = width // parts

    def copy_of(part):
        columns = pl.ds(pl.multiple_of(part * share, share), share)
        return pltpu.make_async_copy(done.at[:, columns], out_ref.at[:, columns], sems.at[part])

    def send(part, _):
        for at in range(0, share, LANES):
            columns = pl.ds(pl.multiple_of(part * share + at, LANES), LANES)
            done[:, columns] = (raw[:, columns] * scale * gain[:, columns]).astype(jnp.bfloat16)
        copy_of(part).start()
        return 0

    lax.fori_loop(0, parts, send, 0, unroll=2)

    def finish(part, _):
        copy_of(part).wait()
        return 0

    lax.fori_loop(0, parts, finish, 0)


def local(queries, keys, values, doc_ids, decay_rate, norm_gain):
    tokens, width = queries.shape
    here = decay_rate.shape[0]
    axes = ("ctx", "uly")
    slices, members = lax.axis_size("ctx"), lax.axis_size("uly")
    count = slices * members
    all_pairs = width // LANES
    chunks = members // 2
    group = slices * chunks
    rows = all_pairs * HD // group
    groups = [
        [c * members + half * chunks + u for c in range(slices) for u in range(chunks)]
        for half in (0, 1)
    ]
    swap = [
        (c * members + u, c * members + (u + chunks) % members)
        for c in range(slices)
        for u in range(members)
    ]

    vmem = pl.BlockSpec(memory_space=pltpu.VMEM)
    params = pltpu.CompilerParams(vmem_limit_bytes=32 * 1024 * 1024)
    shape = jax.ShapeDtypeStruct
    tile = shape((members, LANES), jnp.float32)

    own = jnp.pad(decay_rate, (0, LANES - here)) + jnp.pad(
        doc_ids, (LANES - tokens, 0)
    ).astype(jnp.float32)
    facts = lax.all_to_all(
        jnp.broadcast_to(own[None, :], tile.shape), "uly", split_axis=0, concat_axis=0, tiled=True
    )
    turned, filled, idrow, idcol = pl.pallas_call(
        turn_kernel,
        in_specs=[vmem] * 3,
        out_specs=[vmem] * 4,
        out_shape=[
            shape((width, LANES), jnp.bfloat16),
            shape((LANES, width), jnp.bfloat16),
            shape((8, LANES), jnp.float32),
            shape((tokens, LANES), jnp.float32),
        ],
        compiler_params=params,
        cost_estimate=pl.CostEstimate(flops=0, bytes_accessed=12_000_000, transcendentals=0),
        name="turn",
    )(own[None, :], keys, values)
    ends = pl.pallas_call(
        functools.partial(ends_kernel, here, tokens),
        in_specs=[vmem] * 4,
        out_specs=pl.BlockSpec(memory_space=pl.ANY),
        out_shape=shape((all_pairs * HD, LANES), jnp.bfloat16),
        scratch_shapes=[
            pltpu.VMEM((all_pairs * HD, LANES), jnp.bfloat16),
            pltpu.SemaphoreType.DMA((8,)),
        ],
        compiler_params=params,
        name="ends",
    )(facts, idrow, turned, filled)
    pieces = lax.all_to_all(
        ends.reshape(group, rows, LANES),
        axes, split_axis=0, concat_axis=0, axis_index_groups=groups, tiled=True,
    )
    slice_facts = pl.pallas_call(
        pass_kernel,
        in_specs=[vmem, pl.BlockSpec(memory_space=pl.ANY)],
        out_specs=vmem,
        out_shape=tile,
        compiler_params=params,
        name="pass",
    )(facts, ends)
    others = [
        lax.ppermute(slice_facts, "ctx", [(c, (c + ahead) % slices) for c in range(slices)])
        for ahead in range(1, slices)
    ]
    linked, through, one, half, before = pl.pallas_call(
        functools.partial(link_kernel, here, tokens, chunks),
        in_specs=[vmem] * slices,
        out_specs=[vmem] * 5,
        out_shape=[shape((count, LANES), jnp.float32)] * 2
        + [shape((rows, LANES), jnp.float32)] * 2
        + [shape((1, LANES), jnp.float32)],
        scratch_shapes=[pltpu.VMEM((count, LANES), jnp.float32)],
        compiler_params=params,
        name="link",
    )(slice_facts, *others)
    early_ends, final_end = pl.pallas_call(
        functools.partial(half_kernel, chunks),
        in_specs=[vmem] * 3,
        out_specs=[vmem] * 2,
        out_shape=[
            shape((slices - 1, rows, LANES), jnp.bfloat16),
            shape((1, rows, LANES), jnp.bfloat16),
        ],
        compiler_params=params,
        name="half",
    )(linked, one, pieces)
    early = lax.ppermute(early_ends, axes, swap)
    final = lax.ppermute(final_end, axes, [(low, high) for low, high in swap if low < high])
    inner, rates = pl.pallas_call(
        functools.partial(inner_kernel, here),
        in_specs=[vmem] * 6 + [pl.BlockSpec(memory_space=pl.ANY)],
        out_specs=[vmem] * 2,
        out_shape=[shape((tokens, width), jnp.float32), shape((1, width), jnp.float32)],
        compiler_params=params,
        cost_estimate=pl.CostEstimate(
            flops=8_000_000_000, bytes_accessed=4_000_000, transcendentals=600_000
        ),
        name="inner",
    )(facts, idcol, idrow, queries, turned, values, early_ends)
    moved = pl.pallas_call(
        functools.partial(scan_kernel, chunks),
        in_specs=[vmem] * 7 + [pl.BlockSpec(memory_space=pl.ANY)],
        out_specs=vmem,
        out_shape=shape((group, rows, LANES), jnp.bfloat16),
        compiler_params=params,
        name="scan",
    )(linked, through, one, half, pieces, early, final, rates)
    states = lax.all_to_all(
        moved, axes, split_axis=0, concat_axis=0, axis_index_groups=groups, tiled=True
    )
    return pl.pallas_call(
        norm_kernel,
        in_specs=[vmem] * 7,
        out_specs=pl.BlockSpec(memory_space=pl.ANY),
        out_shape=shape((tokens, width), jnp.bfloat16),
        scratch_shapes=[
            pltpu.VMEM((tokens, width), jnp.float32),
            pltpu.VMEM((tokens, width), jnp.bfloat16),
            pltpu.SemaphoreType.DMA((8,)),
        ],
        compiler_params=params,
        name="norm",
    )(idcol, before, rates, queries, states.reshape(all_pairs * HD, LANES), inner, norm_gain[None, :])


def solution(mesh):
    in_specs = (
        P(("ctx", "uly"), None),
        P(("ctx", "uly"), None),
        P(("ctx", "uly"), None),
        P(("ctx", "uly")),
        P("uly"),
        P(),
    )
    out_specs = P(("ctx", "uly"), None)
    return jax.shard_map(local, mesh=mesh, in_specs=in_specs, out_specs=out_specs, check_vma=False)
```

```python
import functools

import jax
import jax.numpy as jnp
from jax import lax
from jax.experimental import pallas as pl
from jax.experimental.pallas import tpu as pltpu
from jax.sharding import PartitionSpec as P

HD = 64
LANES = 2 * HD
NEVER = 1e9


def rate_of(facts, head, here):
    return facts[head // here : head // here + 1, head % here : head % here + 1]


def pair_rate(facts, pair, here):
    lane = lax.broadcasted_iota(jnp.int32, (1, LANES), 1)
    rates = []
    for head in (2 * pair, 2 * pair + 1):
        row = facts[pl.ds(lax.div(head, here), 1), :]
        rates.append(
            jnp.sum(jnp.where(lane == lax.rem(head, here), row, 0.0), axis=1, keepdims=True)
        )
    return jnp.where(lane < HD, rates[0], rates[1])


def turn_kernel(row_ref, k_ref, v_ref, turned, filled, idrow, idcol):
    tokens, width = k_ref.shape
    fill = jnp.full((1, LANES - tokens), -1.0, jnp.float32)
    row = jnp.concatenate([row_ref[:1, LANES - tokens :], fill], 1)
    idrow[...] = jnp.broadcast_to(row, idrow.shape)
    idcol[...] = jnp.transpose(jnp.broadcast_to(row, (LANES, LANES)))[:tokens]
    filled[:tokens, :] = v_ref[...]
    filled[tokens:, :] = jnp.zeros((LANES - tokens, width), filled.dtype)
    blank = jnp.zeros((LANES - tokens, LANES), jnp.float32)
    for j in range(width // LANES):
        columns = slice(j * LANES, (j + 1) * LANES)
        block = jnp.concatenate([k_ref[:, columns].astype(jnp.float32), blank], 0)
        turned[columns, :] = jnp.transpose(block).astype(turned.dtype)


def ends_kernel(here, tokens, facts, idrow, turned, v_ref, out_ref, made, sems):
    width = v_ref.shape[1]
    lane = lax.broadcasted_iota(jnp.int32, (HD, LANES), 1)
    place = lax.broadcasted_iota(jnp.int32, idrow.shape, 1)
    ids = idrow[...]
    last = ids[:, tokens - 1 : tokens]
    age = jnp.where(ids == last, (tokens - 1 - place).astype(jnp.float32), NEVER)
    parts = sems.shape[0]
    share = made.shape[0] // parts
    copies = []
    for j in range(0, width // LANES, 2):
        weighted = []
        for head in range(2 * j, 2 * j + 4):
            weight = jnp.exp(-rate_of(facts, head, here) * age)
            keys = turned[head * HD : (head + 1) * HD, :].astype(jnp.float32)
            keys = keys.reshape(HD // 8, 8, LANES) * weight[None]
            weighted.append(keys.reshape(HD, LANES))
        weighted = jnp.concatenate(weighted, 0)
        high = weighted.astype(jnp.bfloat16)
        low = (weighted - high.astype(jnp.float32)).astype(jnp.bfloat16)
        v = v_ref[:, j * LANES : (j + 2) * LANES]
        both = jnp.dot(
            jnp.concatenate([high, low], 1),
            jnp.concatenate([v, v], 0),
            preferred_element_type=jnp.float32,
        )
        for one in (0, 1):
            pair = both[one * LANES : (one + 1) * LANES, one * LANES : (one + 1) * LANES]
            made[(j + one) * HD : (j + one + 1) * HD, :] = jnp.where(
                lane < HD, pair[:HD], pair[HD:]
            ).astype(jnp.bfloat16)
        if (j + 2) * HD % share == 0:
            part = (j + 2) * HD // share - 1
            rows = slice(part * share, (part + 1) * share)
            copies.append(pltpu.make_async_copy(made.at[rows], out_ref.at[rows], sems.at[part]))
            copies[-1].start()
    for copy in copies:
        copy.wait()


def inner_kernel(
    here, facts, idcol, idrow, q_ref, turned, v_ref, after, out_ref, rates_ref
):
    tokens, width = q_ref.shape
    lane = lax.broadcasted_iota(jnp.int32, (tokens, LANES), 1)
    t = lax.broadcasted_iota(jnp.int32, (tokens, LANES), 0)
    seen = (t >= lane) & (idcol[...] == idrow[:1, :])
    age = jnp.where(seen, (t - lane).astype(jnp.float32), NEVER)
    for j in range(width // LANES):
        columns = slice(j * LANES, (j + 1) * LANES)
        q = q_ref[:, columns]
        zero = jnp.zeros_like(q)
        stacked = jnp.concatenate([jnp.where(lane < HD, q, zero), jnp.where(lane < HD, zero, q)], 0)
        scores = jnp.dot(
            stacked, turned[columns, :], preferred_element_type=jnp.float32
        )
        rates = [rate_of(facts, 2 * j + one, here) for one in (0, 1)]
        weight = jnp.concatenate([jnp.exp(-rate * age) for rate in rates], 0)
        probs = (scores * weight)[:, :tokens].astype(jnp.bfloat16)
        got = jnp.dot(probs, v_ref[:, columns], preferred_element_type=jnp.float32)
        out_ref[:, columns] = jnp.where(lane < HD, got[:tokens], got[tokens:])
        rates_ref[:, columns] = jnp.where(lane[:1] < HD, rates[0], rates[1])


def pass_kernel(facts, after, out_ref):
    out_ref[...] = facts[...]


def few(count):
    return count if count <= 8 else 1


def link_kernel(here, tokens, chunks, facts, *refs):
    others, (linked, through, one, half, before, last) = refs[:-6], refs[-6:]
    members, slices = facts.shape[0], len(others) + 1
    ctx, uly = lax.axis_index("ctx"), lax.axis_index("uly")
    for back, tile in enumerate((facts, *others)):
        at = lax.rem(ctx + slices - back, slices) * members
        last[pl.ds(pl.multiple_of(at, members), members), :] = jnp.broadcast_to(
            tile[:, LANES - 1 :], (members, LANES)
        )
    me = ctx * members + uly
    now = last[...]
    then = jnp.concatenate([now[:1], now[:-1]], 0)
    end = jnp.concatenate([now[chunks - 1 :], now[: chunks - 1]], 0)
    linked[...] = jnp.where(now == then, 1.0, 0.0)
    through[...] = jnp.where(end == then, 1.0, 0.0)
    before[...] = jnp.where(me > 0, last[pl.ds(jnp.maximum(me - 1, 0), 1), :], -1.0)
    rows = one.shape[0]
    share = min(rows, HD)
    owner = lax.rem(ctx, slices // 2) * chunks + lax.rem(uly, chunks)
    for at in range(0, rows, share):
        rate = pair_rate(facts, lax.div(owner * rows + at, HD), here)
        for ref, length in ((one, tokens), (half, tokens * chunks)):
            ref[at : at + share, :] = jnp.broadcast_to(
                jnp.exp(-rate * float(length)), (share, LANES)
            )


def half_kernel(chunks, linked, through, one, half, in_ref, early_ref, final_ref, sum_ref):
    span = early_ref.shape[0] + 1
    later = lax.axis_index("uly") >= chunks
    offset = jnp.where(later, chunks, 0)
    base = jnp.where(lax.axis_index("ctx") >= span, span, 0) * 2 * chunks

    def slice_end(c, total):
        start = base + c * 2 * chunks

        def step(j, state):
            keep = linked[pl.ds(start + offset + j, 1), :] * one[...]
            return in_ref[c * chunks + j].astype(jnp.float32) + keep * state

        begin = in_ref[c * chunks].astype(jnp.float32)
        state = lax.fori_loop(1, chunks, step, begin, unroll=few(chunks - 1))
        low = through[pl.ds(start, 1), :] * half[...]
        high = through[pl.ds(start + chunks, 1), :] * half[...]
        total = jnp.where(later, 1.0, high) * state + low * high * total
        return state.astype(early_ref.dtype), total

    def early(c, total):
        early_ref[c], total = slice_end(c, total)
        return total

    total = jnp.zeros(in_ref.shape[1:], jnp.float32)
    total = lax.fori_loop(0, span - 1, early, total, unroll=few(span - 1))
    final_ref[0], total = slice_end(span - 1, total)
    sum_ref[...] = total.astype(sum_ref.dtype)


def scan_kernel(
    chunks, linked, through, one, half, in_ref, early, final, straight, across, after, out_ref
):
    span = early.shape[0] + 1
    later = lax.axis_index("uly") >= chunks
    offset = jnp.where(later, chunks, 0)
    base = jnp.where(lax.axis_index("ctx") >= span, span, 0) * 2 * chunks

    def over_other(state, c, piece, wanted):
        keep = through[pl.ds(base + c * 2 * chunks + chunks - offset, 1), :] * half[...]
        return jnp.where(wanted, piece.astype(jnp.float32) + keep * state, state)

    def over_own(state, c):
        def step(j, state):
            at = c * chunks + j
            out_ref[at] = state.astype(out_ref.dtype)
            keep = linked[pl.ds(base + c * 2 * chunks + offset + j, 1), :] * one[...]
            return in_ref[at].astype(jnp.float32) + keep * state

        return lax.fori_loop(0, chunks, step, state, unroll=few(chunks))

    def over_slice(c, state):
        state = over_own(over_other(state, c, early[c], later), c)
        return over_other(state, c, early[c], jnp.logical_not(later))

    state = straight[...].astype(jnp.float32) + across[...].astype(jnp.float32)
    state = lax.fori_loop(0, span - 1, over_slice, state, unroll=few(span - 1))
    over_own(over_other(state, span - 1, final[0], later), span - 1)


def norm_kernel(idcol, before, rates, q_ref, s_ref, inner_ref, gain, out_ref, raw, done, sems):
    tokens, width = q_ref.shape
    lane = lax.broadcasted_iota(jnp.int32, (HD, LANES), 1)
    place = lax.broadcasted_iota(jnp.int32, (tokens, LANES), 0)
    age = jnp.where(idcol[...] == before[...], (place + 1).astype(jnp.float32), NEVER)
    zero = jnp.zeros((HD, LANES), s_ref.dtype)
    total = jnp.zeros((tokens, LANES), jnp.float32)
    for j in range(0, width // LANES, 2):
        square = []
        for one in (0, 1):
            state = s_ref[(j + one) * HD : (j + one + 1) * HD, :]
            for half in (jnp.where(lane < HD, state, zero), jnp.where(lane < HD, zero, state)):
                square.append(jnp.concatenate([zero, half] if one else [half, zero], 1))
        columns = slice(j * LANES, (j + 2) * LANES)
        outer = jnp.dot(
            q_ref[:, columns], jnp.concatenate(square, 0), preferred_element_type=jnp.float32
        )
        for one in (0, 1):
            columns = slice((j + one) * LANES, (j + one + 1) * LANES)
            fade = jnp.exp(-rates[:, columns] * age)
            value = inner_ref[:, columns] + outer[:, one * LANES : (one + 1) * LANES] * fade
            total += value * value
            raw[:, columns] = value
    mean = jnp.sum(total, axis=1, keepdims=True) / float(width)
    scale = jnp.broadcast_to(lax.rsqrt(mean + 1e-06), (tokens, LANES))
    parts = sems.shape[0]
    share = width // parts
    copies = []
    for part in range(parts):
        for at in range(part * share, (part + 1) * share, LANES):
            columns = slice(at, at + LANES)
            done[:, columns] = (raw[:, columns] * scale * gain[:, columns]).astype(jnp.bfloat16)
        columns = slice(part * share, (part + 1) * share)
        copies.append(
            pltpu.make_async_copy(done.at[:, columns], out_ref.at[:, columns], sems.at[part])
        )
        copies[-1].start()
    for copy in copies:
        copy.wait()


def local(queries, keys, values, doc_ids, decay_rate, norm_gain):
    tokens, width = queries.shape
    here = decay_rate.shape[0]
    axes = ("ctx", "uly")
    slices, members = lax.axis_size("ctx"), lax.axis_size("uly")
    count = slices * members
    all_pairs = width // LANES
    chunks = members // 2
    span = slices // 2
    group = span * chunks
    rows = all_pairs * HD // group
    device = lambda c, u: c * members + u
    groups = [
        [device(first + c, half + u) for c in range(span) for u in range(chunks)]
        for first in (0, span)
        for half in (0, chunks)
    ]
    opposite = lambda u: (u + chunks) % members
    every = [(c, u) for c in range(slices) for u in range(members)]
    swap = [(device(c, u), device(c, opposite(u))) for c, u in every]
    upward = [(device(c, u), device(c, opposite(u))) for c, u in every if u < chunks]
    onward = [(device(c, u), device(c + span, u)) for c, u in every if c < span]
    onward_across = [(device(c, u), device(c + span, opposite(u))) for c, u in every if c < span]

    vmem = pl.BlockSpec(memory_space=pltpu.VMEM)
    params = pltpu.CompilerParams(vmem_limit_bytes=32 * 1024 * 1024)
    shape = jax.ShapeDtypeStruct
    tile = shape((members, LANES), jnp.float32)

    own = jnp.pad(decay_rate, (0, LANES - here)) + jnp.pad(
        doc_ids, (LANES - tokens, 0)
    ).astype(jnp.float32)
    facts = lax.all_to_all(
        jnp.broadcast_to(own[None, :], tile.shape), "uly", split_axis=0, concat_axis=0, tiled=True
    )
    turned, filled, idrow, idcol = pl.pallas_call(
        turn_kernel,
        in_specs=[vmem] * 3,
        out_specs=[vmem] * 4,
        out_shape=[
            shape((width, LANES), jnp.bfloat16),
            shape((LANES, width), jnp.bfloat16),
            shape((8, LANES), jnp.float32),
            shape((tokens, LANES), jnp.float32),
        ],
        compiler_params=params,
        cost_estimate=pl.CostEstimate(flops=0, bytes_accessed=12_000_000, transcendentals=0),
        name="turn",
    )(own[None, :], keys, values)
    ends = pl.pallas_call(
        functools.partial(ends_kernel, here, tokens),
        in_specs=[vmem] * 4,
        out_specs=pl.BlockSpec(memory_space=pl.ANY),
        out_shape=shape((all_pairs * HD, LANES), jnp.bfloat16),
        scratch_shapes=[
            pltpu.VMEM((all_pairs * HD, LANES), jnp.bfloat16),
            pltpu.SemaphoreType.DMA((8,)),
        ],
        compiler_params=params,
        name="ends",
    )(facts, idrow, turned, filled)
    pieces = lax.all_to_all(
        ends.reshape(group, rows, LANES),
        axes, split_axis=0, concat_axis=0, axis_index_groups=groups, tiled=True,
    )
    slice_facts = pl.pallas_call(
        pass_kernel,
        in_specs=[vmem, pl.BlockSpec(memory_space=pl.ANY)],
        out_specs=vmem,
        out_shape=tile,
        compiler_params=params,
        name="pass",
    )(facts, ends)
    others = [
        lax.ppermute(slice_facts, "ctx", [(c, (c + ahead) % slices) for c in range(slices)])
        for ahead in range(1, slices)
    ]
    linked, through, one, half, before = pl.pallas_call(
        functools.partial(link_kernel, here, tokens, chunks),
        in_specs=[vmem] * slices,
        out_specs=[vmem] * 5,
        out_shape=[shape((count, LANES), jnp.float32)] * 2
        + [shape((rows, LANES), jnp.float32)] * 2
        + [shape((1, LANES), jnp.float32)],
        scratch_shapes=[pltpu.VMEM((count, LANES), jnp.float32)],
        compiler_params=params,
        name="link",
    )(slice_facts, *others)
    block = shape((rows, LANES), jnp.bfloat16)
    early_ends, final_end, left = pl.pallas_call(
        functools.partial(half_kernel, chunks),
        in_specs=[vmem] * 5,
        out_specs=[vmem] * 3,
        out_shape=[
            shape((span - 1, rows, LANES), jnp.bfloat16),
            shape((1, rows, LANES), jnp.bfloat16),
            block,
        ],
        compiler_params=params,
        name="half",
    )(linked, through, one, half, pieces)
    early = lax.ppermute(early_ends, axes, swap)
    final = lax.ppermute(final_end, axes, upward)
    straight = lax.ppermute(left, axes, onward)
    across = lax.ppermute(left, axes, onward_across)
    inner, rates = pl.pallas_call(
        functools.partial(inner_kernel, here),
        in_specs=[vmem] * 6 + [pl.BlockSpec(memory_space=pl.ANY)],
        out_specs=[vmem] * 2,
        out_shape=[shape((tokens, width), jnp.float32), shape((1, width), jnp.float32)],
        compiler_params=params,
        cost_estimate=pl.CostEstimate(
            flops=8_000_000_000, bytes_accessed=4_000_000, transcendentals=600_000
        ),
        name="inner",
    )(facts, idcol, idrow, queries, turned, values, early_ends)
    moved = pl.pallas_call(
        functools.partial(scan_kernel, chunks),
        in_specs=[vmem] * 9 + [pl.BlockSpec(memory_space=pl.ANY)],
        out_specs=vmem,
        out_shape=shape((group, rows, LANES), jnp.bfloat16),
        compiler_params=params,
        name="scan",
    )(linked, through, one, half, pieces, early, final, straight, across, rates)
    states = lax.all_to_all(
        moved, axes, split_axis=0, concat_axis=0, axis_index_groups=groups, tiled=True
    )
    return pl.pallas_call(
        norm_kernel,
        in_specs=[vmem] * 7,
        out_specs=pl.BlockSpec(memory_space=pl.ANY),
        out_shape=shape((tokens, width), jnp.bfloat16),
        scratch_shapes=[
            pltpu.VMEM((tokens, width), jnp.float32),
            pltpu.VMEM((tokens, width), jnp.bfloat16),
            pltpu.SemaphoreType.DMA((16,)),
        ],
        compiler_params=params,
        name="norm",
    )(idcol, before, rates, queries, states.reshape(all_pairs * HD, LANES), inner, norm_gain[None, :])


def solution(mesh):
    in_specs = (
        P(("ctx", "uly"), None),
        P(("ctx", "uly"), None),
        P(("ctx", "uly"), None),
        P(("ctx", "uly")),
        P("uly"),
        P(),
    )
    out_specs = P(("ctx", "uly"), None)
    return jax.shard_map(local, mesh=mesh, in_specs=in_specs, out_specs=out_specs, check_vma=False)
```

```python
import functools

import jax
import jax.numpy as jnp
from jax import lax
from jax.experimental import pallas as pl
from jax.experimental.pallas import tpu as pltpu
from jax.sharding import PartitionSpec as P

HD = 64
LANES = 2 * HD
NEVER = 1e9


def rate_of(facts, head, here):
    return facts[head // here : head // here + 1, head % here : head % here + 1]


def pair_rate(facts, pair, here):
    lane = lax.broadcasted_iota(jnp.int32, (1, LANES), 1)
    rates = []
    for head in (2 * pair, 2 * pair + 1):
        row = facts[pl.ds(lax.div(head, here), 1), :]
        rates.append(
            jnp.sum(jnp.where(lane == lax.rem(head, here), row, 0.0), axis=1, keepdims=True)
        )
    return jnp.where(lane < HD, rates[0], rates[1])


def turn_kernel(row_ref, k_ref, v_ref, turned, filled, idrow, idcol):
    tokens, width = k_ref.shape
    fill = jnp.full((1, LANES - tokens), -1.0, jnp.float32)
    row = jnp.concatenate([row_ref[:1, LANES - tokens :], fill], 1)
    idrow[...] = jnp.broadcast_to(row, idrow.shape)
    idcol[...] = jnp.transpose(jnp.broadcast_to(row, (LANES, LANES)))[:tokens]
    filled[:tokens, :] = v_ref[...]
    filled[tokens:, :] = jnp.zeros((LANES - tokens, width), filled.dtype)
    blank = jnp.zeros((LANES - tokens, LANES), jnp.float32)
    for j in range(width // LANES):
        columns = slice(j * LANES, (j + 1) * LANES)
        block = jnp.concatenate([k_ref[:, columns].astype(jnp.float32), blank], 0)
        turned[columns, :] = jnp.transpose(block).astype(turned.dtype)


def ends_kernel(here, tokens, stored, idrow, turned, v_ref, out_ref, facts, made, sems):
    width = v_ref.shape[1]
    members = facts.shape[0]
    for u in range(members):
        facts[u : u + 1, :] = stored[members - 1 - u : members - u, :]
    lane = lax.broadcasted_iota(jnp.int32, (HD, LANES), 1)
    place = lax.broadcasted_iota(jnp.int32, idrow.shape, 1)
    ids = idrow[...]
    last = ids[:, tokens - 1 : tokens]
    age = jnp.where(ids == last, (tokens - 1 - place).astype(jnp.float32), NEVER)
    parts = sems.shape[0]
    share = made.shape[0] // parts
    copies = []
    for j in range(0, width // LANES, 2):
        weighted = []
        for head in range(2 * j, 2 * j + 4):
            weight = jnp.exp(-rate_of(stored, (members - 1) * here + 2 * (head % here) - head, here) * age)
            keys = turned[head * HD : (head + 1) * HD, :].astype(jnp.float32)
            keys = keys.reshape(HD // 8, 8, LANES) * weight[None]
            weighted.append(keys.reshape(HD, LANES))
        weighted = jnp.concatenate(weighted, 0)
        high = weighted.astype(jnp.bfloat16)
        low = (weighted - high.astype(jnp.float32)).astype(jnp.bfloat16)
        v = v_ref[:, j * LANES : (j + 2) * LANES]
        both = jnp.dot(
            jnp.concatenate([high, low], 1),
            jnp.concatenate([v, v], 0),
            preferred_element_type=jnp.float32,
        )
        for one in (0, 1):
            pair = both[one * LANES : (one + 1) * LANES, one * LANES : (one + 1) * LANES]
            made[(j + one) * HD : (j + one + 1) * HD, :] = jnp.where(
                lane < HD, pair[:HD], pair[HD:]
            ).astype(jnp.bfloat16)
        if (j + 2) * HD % share == 0:
            part = (j + 2) * HD // share - 1
            rows = slice(part * share, (part + 1) * share)
            copies.append(pltpu.make_async_copy(made.at[rows], out_ref.at[rows], sems.at[part]))
            copies[-1].start()
    for copy in copies:
        copy.wait()


def inner_kernel(
    here, facts, idcol, idrow, q_ref, turned, v_ref, after, out_ref, rates_ref
):
    tokens, width = q_ref.shape
    lane = lax.broadcasted_iota(jnp.int32, (tokens, LANES), 1)
    t = lax.broadcasted_iota(jnp.int32, (tokens, LANES), 0)
    seen = (t >= lane) & (idcol[...] == idrow[:1, :])
    age = jnp.where(seen, (t - lane).astype(jnp.float32), NEVER)
    for j in range(width // LANES):
        columns = slice(j * LANES, (j + 1) * LANES)
        q = q_ref[:, columns]
        zero = jnp.zeros_like(q)
        stacked = jnp.concatenate([jnp.where(lane < HD, q, zero), jnp.where(lane < HD, zero, q)], 0)
        scores = jnp.dot(
            stacked, turned[columns, :], preferred_element_type=jnp.float32
        )
        rates = [rate_of(facts, 2 * j + one, here) for one in (0, 1)]
        weight = jnp.concatenate([jnp.exp(-rate * age) for rate in rates], 0)
        probs = (scores * weight)[:, :tokens].astype(jnp.bfloat16)
        got = jnp.dot(probs, v_ref[:, columns], preferred_element_type=jnp.float32)
        out_ref[:, columns] = jnp.where(lane < HD, got[:tokens], got[tokens:])
        rates_ref[:, columns] = jnp.where(lane[:1] < HD, rates[0], rates[1])


def pass_kernel(facts, after, out_ref):
    out_ref[...] = facts[...]


def few(count):
    return count if count <= 8 else 1


def link_kernel(here, tokens, chunks, facts, *refs):
    others, (linked, through, one, half, before, last) = refs[:-6], refs[-6:]
    members, slices = facts.shape[0], len(others) + 1
    ctx, uly = lax.axis_index("ctx"), lax.axis_index("uly")
    for back, tile in enumerate((facts, *others)):
        at = lax.rem(ctx + slices - back, slices) * members
        last[pl.ds(pl.multiple_of(at, members), members), :] = jnp.broadcast_to(
            tile[:, LANES - 1 :], (members, LANES)
        )
    me = ctx * members + uly
    now = last[...]
    then = jnp.concatenate([now[:1], now[:-1]], 0)
    end = jnp.concatenate([now[chunks - 1 :], now[: chunks - 1]], 0)
    linked[...] = jnp.where(now == then, 1.0, 0.0)
    through[...] = jnp.where(end == then, 1.0, 0.0)
    before[...] = jnp.where(me > 0, last[pl.ds(jnp.maximum(me - 1, 0), 1), :], -1.0)
    rows = one.shape[0]
    share = min(rows, HD)
    owner = ctx * chunks + lax.rem(uly, chunks)
    for at in range(0, rows, share):
        rate = pair_rate(facts, lax.div(owner * rows + at, HD), here)
        for ref, length in ((one, tokens), (half, tokens * chunks)):
            ref[at : at + share, :] = jnp.broadcast_to(
                jnp.exp(-rate * float(length)), (share, LANES)
            )


def half_kernel(chunks, linked, one, in_ref, early_ref, final_ref):
    slices = early_ref.shape[0] + 1
    offset = jnp.where(lax.axis_index("uly") >= chunks, chunks, 0)

    def slice_end(c):
        def step(j, state):
            keep = linked[pl.ds(c * 2 * chunks + offset + j, 1), :] * one[...]
            return in_ref[c * chunks + j].astype(jnp.float32) + keep * state

        begin = in_ref[c * chunks].astype(jnp.float32)
        state = lax.fori_loop(1, chunks, step, begin, unroll=few(chunks - 1))
        return state.astype(early_ref.dtype)

    def early(c, _):
        early_ref[c] = slice_end(c)
        return 0

    lax.fori_loop(0, slices - 1, early, 0, unroll=few(slices - 1))
    final_ref[0] = slice_end(slices - 1)


def scan_kernel(
    chunks, linked, through, one, half, in_ref, early, final, after, out_ref
):
    slices = early.shape[0] + 1
    later = lax.axis_index("uly") >= chunks
    offset = jnp.where(later, chunks, 0)

    def over_other(state, c, piece, wanted):
        keep = through[pl.ds(c * 2 * chunks + chunks - offset, 1), :] * half[...]
        return jnp.where(wanted, piece.astype(jnp.float32) + keep * state, state)

    def over_own(state, c):
        def step(j, state):
            at = c * chunks + j
            out_ref[at] = state.astype(out_ref.dtype)
            keep = linked[pl.ds(c * 2 * chunks + offset + j, 1), :] * one[...]
            return in_ref[at].astype(jnp.float32) + keep * state

        return lax.fori_loop(0, chunks, step, state, unroll=few(chunks))

    def over_slice(c, state):
        state = over_own(over_other(state, c, early[c], later), c)
        return over_other(state, c, early[c], jnp.logical_not(later))

    begin = jnp.zeros(in_ref.shape[1:], jnp.float32)
    state = lax.fori_loop(0, slices - 1, over_slice, begin, unroll=few(slices - 1))
    over_own(over_other(state, slices - 1, final[0], later), slices - 1)


def norm_kernel(idcol, before, rates, q_ref, s_ref, inner_ref, gain, out_ref, raw, done, sems):
    tokens, width = q_ref.shape
    lane = lax.broadcasted_iota(jnp.int32, (HD, LANES), 1)
    place = lax.broadcasted_iota(jnp.int32, (tokens, LANES), 0)
    age = jnp.where(idcol[...] == before[...], (place + 1).astype(jnp.float32), NEVER)
    zero = jnp.zeros((HD, LANES), s_ref.dtype)
    total = jnp.zeros((tokens, LANES), jnp.float32)
    for j in range(0, width // LANES, 2):
        square = []
        for one in (0, 1):
            state = s_ref[(j + one) * HD : (j + one + 1) * HD, :]
            for half in (jnp.where(lane < HD, state, zero), jnp.where(lane < HD, zero, state)):
                square.append(jnp.concatenate([zero, half] if one else [half, zero], 1))
        columns = slice(j * LANES, (j + 2) * LANES)
        outer = jnp.dot(
            q_ref[:, columns], jnp.concatenate(square, 0), preferred_element_type=jnp.float32
        )
        for one in (0, 1):
            columns = slice((j + one) * LANES, (j + one + 1) * LANES)
            fade = jnp.exp(-rates[:, columns] * age)
            value = inner_ref[:, columns] + outer[:, one * LANES : (one + 1) * LANES] * fade
            total += value * value
            raw[:, columns] = value
    mean = jnp.sum(total, axis=1, keepdims=True) / float(width)
    scale = jnp.broadcast_to(lax.rsqrt(mean + 1e-06), (tokens, LANES))
    parts = sems.shape[0]
    share = width // parts
    copies = []
    for part in range(parts):
        for at in range(part * share, (part + 1) * share, LANES):
            columns = slice(at, at + LANES)
            done[:, columns] = (raw[:, columns] * scale * gain[:, columns]).astype(jnp.bfloat16)
        columns = slice(part * share, (part + 1) * share)
        copies.append(
            pltpu.make_async_copy(done.at[:, columns], out_ref.at[:, columns], sems.at[part])
        )
        copies[-1].start()
    for copy in copies:
        copy.wait()


def local(queries, keys, values, doc_ids, decay_rate, norm_gain):
    tokens, width = queries.shape
    here = decay_rate.shape[0]
    axes = ("ctx", "uly")
    slices, members = lax.axis_size("ctx"), lax.axis_size("uly")
    count = slices * members
    all_pairs = width // LANES
    chunks = members // 2
    group = slices * chunks
    rows = all_pairs * HD // group
    groups = [
        [c * members + half * chunks + u for c in range(slices) for u in range(chunks)]
        for half in (0, 1)
    ]
    swap = [
        (c * members + u, c * members + (u + chunks) % members)
        for c in range(slices)
        for u in range(members)
    ]

    vmem = pl.BlockSpec(memory_space=pltpu.VMEM)
    params = pltpu.CompilerParams(vmem_limit_bytes=32 * 1024 * 1024)
    shape = jax.ShapeDtypeStruct
    tile = shape((members, LANES), jnp.float32)

    own = jnp.pad(decay_rate, (0, LANES - here)) + jnp.pad(
        doc_ids, (LANES - tokens, 0)
    ).astype(jnp.float32)
    backward = [list(range(members))[::-1]]
    stored = lax.all_to_all(
        jnp.broadcast_to(own[None, :], tile.shape),
        "uly", split_axis=0, concat_axis=0, axis_index_groups=backward, tiled=True,
    )
    turned, filled, idrow, idcol = pl.pallas_call(
        turn_kernel,
        in_specs=[vmem] * 3,
        out_specs=[vmem] * 4,
        out_shape=[
            shape((width, LANES), jnp.bfloat16),
            shape((LANES, width), jnp.bfloat16),
            shape((8, LANES), jnp.float32),
            shape((tokens, LANES), jnp.float32),
        ],
        compiler_params=params,
        cost_estimate=pl.CostEstimate(flops=0, bytes_accessed=12_000_000, transcendentals=0),
        name="turn",
    )(own[None, :], keys, values)
    ends, facts = pl.pallas_call(
        functools.partial(ends_kernel, here, tokens),
        in_specs=[vmem] * 4,
        out_specs=[pl.BlockSpec(memory_space=pl.ANY), vmem],
        out_shape=[shape((all_pairs * HD, LANES), jnp.bfloat16), tile],
        scratch_shapes=[
            pltpu.VMEM((all_pairs * HD, LANES), jnp.bfloat16),
            pltpu.SemaphoreType.DMA((8,)),
        ],
        compiler_params=params,
        name="ends",
    )(stored, idrow, turned, filled)
    pieces = lax.all_to_all(
        ends.reshape(group, rows, LANES),
        axes, split_axis=0, concat_axis=0, axis_index_groups=groups, tiled=True,
    )
    slice_facts = pl.pallas_call(
        pass_kernel,
        in_specs=[vmem, pl.BlockSpec(memory_space=pl.ANY)],
        out_specs=vmem,
        out_shape=tile,
        compiler_params=params,
        name="pass",
    )(facts, ends)
    others = [
        lax.ppermute(slice_facts, "ctx", [(c, (c + ahead) % slices) for c in range(slices)])
        for ahead in range(1, slices)
    ]
    linked, through, one, half, before = pl.pallas_call(
        functools.partial(link_kernel, here, tokens, chunks),
        in_specs=[vmem] * slices,
        out_specs=[vmem] * 5,
        out_shape=[shape((count, LANES), jnp.float32)] * 2
        + [shape((rows, LANES), jnp.float32)] * 2
        + [shape((1, LANES), jnp.float32)],
        scratch_shapes=[pltpu.VMEM((count, LANES), jnp.float32)],
        compiler_params=params,
        name="link",
    )(slice_facts, *others)
    early_ends, final_end = pl.pallas_call(
        functools.partial(half_kernel, chunks),
        in_specs=[vmem] * 3,
        out_specs=[vmem] * 2,
        out_shape=[
            shape((slices - 1, rows, LANES), jnp.bfloat16),
            shape((1, rows, LANES), jnp.bfloat16),
        ],
        compiler_params=params,
        name="half",
    )(linked, one, pieces)
    early = lax.ppermute(early_ends, axes, swap)
    final = lax.ppermute(final_end, axes, [(low, high) for low, high in swap if low < high])
    inner, rates = pl.pallas_call(
        functools.partial(inner_kernel, here),
        in_specs=[vmem] * 6 + [pl.BlockSpec(memory_space=pl.ANY)],
        out_specs=[vmem] * 2,
        out_shape=[shape((tokens, width), jnp.float32), shape((1, width), jnp.float32)],
        compiler_params=params,
        cost_estimate=pl.CostEstimate(
            flops=8_000_000_000, bytes_accessed=4_000_000, transcendentals=600_000
        ),
        name="inner",
    )(facts, idcol, idrow, queries, turned, values, early_ends)
    moved = pl.pallas_call(
        functools.partial(scan_kernel, chunks),
        in_specs=[vmem] * 7 + [pl.BlockSpec(memory_space=pl.ANY)],
        out_specs=vmem,
        out_shape=shape((group, rows, LANES), jnp.bfloat16),
        compiler_params=params,
        name="scan",
    )(linked, through, one, half, pieces, early, final, rates)
    states = lax.all_to_all(
        moved, axes, split_axis=0, concat_axis=0, axis_index_groups=groups, tiled=True
    )
    return pl.pallas_call(
        norm_kernel,
        in_specs=[vmem] * 7,
        out_specs=pl.BlockSpec(memory_space=pl.ANY),
        out_shape=shape((tokens, width), jnp.bfloat16),
        scratch_shapes=[
            pltpu.VMEM((tokens, width), jnp.float32),
            pltpu.VMEM((tokens, width), jnp.bfloat16),
            pltpu.SemaphoreType.DMA((16,)),
        ],
        compiler_params=params,
        name="norm",
    )(idcol, before, rates, queries, states.reshape(all_pairs * HD, LANES), inner, norm_gain[None, :])


def solution(mesh):
    in_specs = (
        P(("ctx", "uly"), None),
        P(("ctx", "uly"), None),
        P(("ctx", "uly"), None),
        P(("ctx", "uly")),
        P("uly"),
        P(),
    )
    out_specs = P(("ctx", "uly"), None)
    return jax.shard_map(local, mesh=mesh, in_specs=in_specs, out_specs=out_specs, check_vma=False)
```

```python
import functools

import jax
import jax.numpy as jnp
from jax import lax
from jax.experimental import pallas as pl
from jax.experimental.pallas import tpu as pltpu
from jax.sharding import PartitionSpec as P

HD = 64
LANES = 2 * HD
NEVER = 1e9


def rate_of(facts, head, here):
    return facts[head // here : head // here + 1, head % here : head % here + 1]


def pair_rate(facts, pair, here):
    lane = lax.broadcasted_iota(jnp.int32, (1, LANES), 1)
    rates = []
    for head in (2 * pair, 2 * pair + 1):
        row = facts[pl.ds(lax.div(head, here), 1), :]
        rates.append(
            jnp.sum(jnp.where(lane == lax.rem(head, here), row, 0.0), axis=1, keepdims=True)
        )
    return jnp.where(lane < HD, rates[0], rates[1])


def turn_kernel(k_ref, v_ref, turned, filled):
    tokens, width = k_ref.shape
    filled[:tokens, :] = v_ref[...]
    filled[tokens:, :] = jnp.zeros((LANES - tokens, width), filled.dtype)
    blank = jnp.zeros((LANES - tokens, LANES), jnp.float32)
    for j in range(width // LANES):
        columns = slice(j * LANES, (j + 1) * LANES)
        block = jnp.concatenate([k_ref[:, columns].astype(jnp.float32), blank], 0)
        turned[columns, :] = jnp.transpose(block).astype(turned.dtype)


def own_ids(stored, tokens):
    at = stored.shape[0] - 1 - lax.axis_index("uly")
    row = stored[pl.ds(at, 1), :]
    fill = jnp.full((1, LANES - tokens), -1.0, jnp.float32)
    return jnp.concatenate([row[:, LANES - tokens :], fill], 1)


def ends_kernel(here, tokens, group, stored, turned, v_ref, out_ref, made, sems):
    width = v_ref.shape[1]
    members = stored.shape[0]
    lane = lax.broadcasted_iota(jnp.int32, (HD, LANES), 1)
    ids = jnp.broadcast_to(own_ids(stored, tokens), (8, LANES))
    place = lax.broadcasted_iota(jnp.int32, ids.shape, 1)
    last = ids[:, tokens - 1 : tokens]
    age = jnp.where(ids == last, (tokens - 1 - place).astype(jnp.float32), NEVER)
    rows_each = made.shape[0] // group
    parts = sems.shape[0]
    share = made.shape[0] // parts
    copies = []
    for j in range(0, width // LANES, 2):
        weighted = []
        for head in range(2 * j, 2 * j + 4):
            weight = jnp.exp(-rate_of(stored, (members - 1) * here + 2 * (head % here) - head, here) * age)
            keys = turned[head * HD : (head + 1) * HD, :].astype(jnp.float32)
            keys = keys.reshape(HD // 8, 8, LANES) * weight[None]
            weighted.append(keys.reshape(HD, LANES))
        weighted = jnp.concatenate(weighted, 0)
        high = weighted.astype(jnp.bfloat16)
        low = (weighted - high.astype(jnp.float32)).astype(jnp.bfloat16)
        v = v_ref[:, j * LANES : (j + 2) * LANES]
        both = jnp.dot(
            jnp.concatenate([high, low], 1),
            jnp.concatenate([v, v], 0),
            preferred_element_type=jnp.float32,
        )
        for one in (0, 1):
            pair = both[one * LANES : (one + 1) * LANES, one * LANES : (one + 1) * LANES]
            state = jnp.where(lane < HD, pair[:HD], pair[HD:])
            size = min(rows_each, HD)
            for at in range(0, HD, size):
                owner, start = divmod((j + one) * HD + at, rows_each)
                start += (group - 1 - owner) * rows_each
                made[start : start + size, :] = state[at : at + size].astype(jnp.bfloat16)
        if (j + 2) * HD % share == 0:
            part = parts - (j + 2) * HD // share
            rows = slice(part * share, (part + 1) * share)
            copies.append(pltpu.make_async_copy(made.at[rows], out_ref.at[rows], sems.at[part]))
            copies[-1].start()
    for copy in copies:
        copy.wait()


def inner_kernel(
    here, facts, idcol, idrow, q_ref, turned, v_ref, after, out_ref, rates_ref
):
    tokens, width = q_ref.shape
    lane = lax.broadcasted_iota(jnp.int32, (tokens, LANES), 1)
    t = lax.broadcasted_iota(jnp.int32, (tokens, LANES), 0)
    seen = (t >= lane) & (idcol[...] == idrow[:1, :])
    age = jnp.where(seen, (t - lane).astype(jnp.float32), NEVER)
    for j in range(width // LANES):
        columns = slice(j * LANES, (j + 1) * LANES)
        q = q_ref[:, columns]
        zero = jnp.zeros_like(q)
        stacked = jnp.concatenate([jnp.where(lane < HD, q, zero), jnp.where(lane < HD, zero, q)], 0)
        scores = jnp.dot(
            stacked, turned[columns, :], preferred_element_type=jnp.float32
        )
        rates = [rate_of(facts, 2 * j + one, here) for one in (0, 1)]
        weight = jnp.concatenate([jnp.exp(-rate * age) for rate in rates], 0)
        probs = (scores * weight)[:, :tokens].astype(jnp.bfloat16)
        got = jnp.dot(probs, v_ref[:, columns], preferred_element_type=jnp.float32)
        out_ref[:, columns] = jnp.where(lane < HD, got[:tokens], got[tokens:])
        rates_ref[:, columns] = jnp.where(lane[:1] < HD, rates[0], rates[1])


def pass_kernel(stored, after, facts, idrow, idcol):
    members, tokens = stored.shape[0], idcol.shape[0]
    for u in range(members):
        facts[u : u + 1, :] = stored[members - 1 - u : members - u, :]
    row = own_ids(stored, tokens)
    idrow[...] = jnp.broadcast_to(row, idrow.shape)
    idcol[...] = jnp.transpose(jnp.broadcast_to(row, (LANES, LANES)))[:tokens]


def few(count):
    return count if count <= 8 else 1


def link_kernel(here, tokens, chunks, facts, *refs):
    others, (linked, through, one, half, before, last) = refs[:-6], refs[-6:]
    members, slices = facts.shape[0], len(others) + 1
    ctx, uly = lax.axis_index("ctx"), lax.axis_index("uly")
    for back, tile in enumerate((facts, *others)):
        at = lax.rem(ctx + slices - back, slices) * members
        last[pl.ds(pl.multiple_of(at, members), members), :] = jnp.broadcast_to(
            tile[:, LANES - 1 :], (members, LANES)
        )
    me = ctx * members + uly
    now = last[...]
    then = jnp.concatenate([now[:1], now[:-1]], 0)
    end = jnp.concatenate([now[chunks - 1 :], now[: chunks - 1]], 0)
    linked[...] = jnp.where(now == then, 1.0, 0.0)
    through[...] = jnp.where(end == then, 1.0, 0.0)
    before[...] = jnp.where(me > 0, last[pl.ds(jnp.maximum(me - 1, 0), 1), :], -1.0)
    rows = one.shape[0]
    share = min(rows, HD)
    owner = ctx * chunks + lax.rem(uly, chunks)
    for at in range(0, rows, share):
        rate = pair_rate(facts, lax.div(owner * rows + at, HD), here)
        for ref, length in ((one, tokens), (half, tokens * chunks)):
            ref[at : at + share, :] = jnp.broadcast_to(
                jnp.exp(-rate * float(length)), (share, LANES)
            )


def half_kernel(chunks, linked, one, in_ref, early_ref, final_ref):
    slices, newest = early_ref.shape[0] + 1, in_ref.shape[0] - 1
    offset = jnp.where(lax.axis_index("uly") >= chunks, chunks, 0)

    def slice_end(c):
        def step(j, state):
            keep = linked[pl.ds(c * 2 * chunks + offset + j, 1), :] * one[...]
            return in_ref[newest - c * chunks - j].astype(jnp.float32) + keep * state

        begin = in_ref[newest - c * chunks].astype(jnp.float32)
        state = lax.fori_loop(1, chunks, step, begin, unroll=few(chunks - 1))
        return state.astype(early_ref.dtype)

    def early(c, _):
        early_ref[c] = slice_end(c)
        return 0

    lax.fori_loop(0, slices - 1, early, 0, unroll=few(slices - 1))
    final_ref[0] = slice_end(slices - 1)


def scan_kernel(
    chunks, linked, through, one, half, in_ref, early, final, after, out_ref
):
    slices, newest = early.shape[0] + 1, in_ref.shape[0] - 1
    later = lax.axis_index("uly") >= chunks
    offset = jnp.where(later, chunks, 0)

    def over_other(state, c, piece, wanted):
        keep = through[pl.ds(c * 2 * chunks + chunks - offset, 1), :] * half[...]
        return jnp.where(wanted, piece.astype(jnp.float32) + keep * state, state)

    def over_own(state, c):
        def step(j, state):
            at = c * chunks + j
            out_ref[at] = state.astype(out_ref.dtype)
            keep = linked[pl.ds(c * 2 * chunks + offset + j, 1), :] * one[...]
            return in_ref[newest - at].astype(jnp.float32) + keep * state

        return lax.fori_loop(0, chunks, step, state, unroll=few(chunks))

    def over_slice(c, state):
        state = over_own(over_other(state, c, early[c], later), c)
        return over_other(state, c, early[c], jnp.logical_not(later))

    begin = jnp.zeros(in_ref.shape[1:], jnp.float32)
    state = lax.fori_loop(0, slices - 1, over_slice, begin, unroll=few(slices - 1))
    over_own(over_other(state, slices - 1, final[0], later), slices - 1)


def norm_kernel(idcol, before, rates, q_ref, s_ref, inner_ref, gain, out_ref, raw, done, sems):
    tokens, width = q_ref.shape
    lane = lax.broadcasted_iota(jnp.int32, (HD, LANES), 1)
    place = lax.broadcasted_iota(jnp.int32, (tokens, LANES), 0)
    age = jnp.where(idcol[...] == before[...], (place + 1).astype(jnp.float32), NEVER)
    zero = jnp.zeros((HD, LANES), s_ref.dtype)
    total = jnp.zeros((tokens, LANES), jnp.float32)
    for j in range(0, width // LANES, 2):
        square = []
        for one in (0, 1):
            state = s_ref[(j + one) * HD : (j + one + 1) * HD, :]
            for half in (jnp.where(lane < HD, state, zero), jnp.where(lane < HD, zero, state)):
                square.append(jnp.concatenate([zero, half] if one else [half, zero], 1))
        columns = slice(j * LANES, (j + 2) * LANES)
        outer = jnp.dot(
            q_ref[:, columns], jnp.concatenate(square, 0), preferred_element_type=jnp.float32
        )
        for one in (0, 1):
            columns = slice((j + one) * LANES, (j + one + 1) * LANES)
            fade = jnp.exp(-rates[:, columns] * age)
            value = inner_ref[:, columns] + outer[:, one * LANES : (one + 1) * LANES] * fade
            total += value * value
            raw[:, columns] = value
    mean = jnp.sum(total, axis=1, keepdims=True) / float(width)
    scale = jnp.broadcast_to(lax.rsqrt(mean + 1e-06), (tokens, LANES))
    parts = sems.shape[0]
    share = width // parts
    copies = []
    for part in range(parts):
        for at in range(part * share, (part + 1) * share, LANES):
            columns = slice(at, at + LANES)
            done[:, columns] = (raw[:, columns] * scale * gain[:, columns]).astype(jnp.bfloat16)
        columns = slice(part * share, (part + 1) * share)
        copies.append(
            pltpu.make_async_copy(done.at[:, columns], out_ref.at[:, columns], sems.at[part])
        )
        copies[-1].start()
    for copy in copies:
        copy.wait()


def local(queries, keys, values, doc_ids, decay_rate, norm_gain):
    tokens, width = queries.shape
    here = decay_rate.shape[0]
    axes = ("ctx", "uly")
    slices, members = lax.axis_size("ctx"), lax.axis_size("uly")
    count = slices * members
    all_pairs = width // LANES
    chunks = members // 2
    group = slices * chunks
    rows = all_pairs * HD // group
    groups = [
        [c * members + half * chunks + u for c in range(slices) for u in range(chunks)]
        for half in (0, 1)
    ]
    swap = [
        (c * members + u, c * members + (u + chunks) % members)
        for c in range(slices)
        for u in range(members)
    ]

    vmem = pl.BlockSpec(memory_space=pltpu.VMEM)
    params = pltpu.CompilerParams(vmem_limit_bytes=32 * 1024 * 1024)
    shape = jax.ShapeDtypeStruct
    tile = shape((members, LANES), jnp.float32)

    own = jnp.pad(decay_rate, (0, LANES - here)) + jnp.pad(
        doc_ids, (LANES - tokens, 0)
    ).astype(jnp.float32)
    backward = [list(range(members))[::-1]]
    stored = lax.all_to_all(
        jnp.broadcast_to(own[None, :], tile.shape),
        "uly", split_axis=0, concat_axis=0, axis_index_groups=backward, tiled=True,
    )
    turned, filled = pl.pallas_call(
        turn_kernel,
        in_specs=[vmem] * 2,
        out_specs=[vmem] * 2,
        out_shape=[shape((width, LANES), jnp.bfloat16), shape((LANES, width), jnp.bfloat16)],
        compiler_params=params,
        cost_estimate=pl.CostEstimate(flops=0, bytes_accessed=12_000_000, transcendentals=0),
        name="turn",
    )(keys, values)
    ends = pl.pallas_call(
        functools.partial(ends_kernel, here, tokens, group),
        in_specs=[vmem] * 3,
        out_specs=pl.BlockSpec(memory_space=pl.ANY),
        out_shape=shape((all_pairs * HD, LANES), jnp.bfloat16),
        scratch_shapes=[
            pltpu.VMEM((all_pairs * HD, LANES), jnp.bfloat16),
            pltpu.SemaphoreType.DMA((8,)),
        ],
        compiler_params=params,
        name="ends",
    )(stored, turned, filled)
    pieces = lax.all_to_all(
        ends.reshape(group, rows, LANES),
        axes, split_axis=0, concat_axis=0, tiled=True,
        axis_index_groups=[members_of[::-1] for members_of in groups],
    )
    facts, idrow, idcol = pl.pallas_call(
        pass_kernel,
        in_specs=[vmem, pl.BlockSpec(memory_space=pl.ANY)],
        out_specs=[vmem] * 3,
        out_shape=[tile, shape((8, LANES), jnp.float32), shape((tokens, LANES), jnp.float32)],
        compiler_params=params,
        name="pass",
    )(stored, ends)
    others = [
        lax.ppermute(facts, "ctx", [(c, (c + ahead) % slices) for c in range(slices)])
        for ahead in range(1, slices)
    ]
    linked, through, one, half, before = pl.pallas_call(
        functools.partial(link_kernel, here, tokens, chunks),
        in_specs=[vmem] * slices,
        out_specs=[vmem] * 5,
        out_shape=[shape((count, LANES), jnp.float32)] * 2
        + [shape((rows, LANES), jnp.float32)] * 2
        + [shape((1, LANES), jnp.float32)],
        scratch_shapes=[pltpu.VMEM((count, LANES), jnp.float32)],
        compiler_params=params,
        name="link",
    )(facts, *others)
    early_ends, final_end = pl.pallas_call(
        functools.partial(half_kernel, chunks),
        in_specs=[vmem] * 3,
        out_specs=[vmem] * 2,
        out_shape=[
            shape((slices - 1, rows, LANES), jnp.bfloat16),
            shape((1, rows, LANES), jnp.bfloat16),
        ],
        compiler_params=params,
        name="half",
    )(linked, one, pieces)
    early = lax.ppermute(early_ends, axes, swap)
    final = lax.ppermute(final_end, axes, [(low, high) for low, high in swap if low < high])
    inner, rates = pl.pallas_call(
        functools.partial(inner_kernel, here),
        in_specs=[vmem] * 6 + [pl.BlockSpec(memory_space=pl.ANY)],
        out_specs=[vmem] * 2,
        out_shape=[shape((tokens, width), jnp.float32), shape((1, width), jnp.float32)],
        compiler_params=params,
        cost_estimate=pl.CostEstimate(
            flops=8_000_000_000, bytes_accessed=4_000_000, transcendentals=600_000
        ),
        name="inner",
    )(facts, idcol, idrow, queries, turned, values, early_ends)
    moved = pl.pallas_call(
        functools.partial(scan_kernel, chunks),
        in_specs=[vmem] * 7 + [pl.BlockSpec(memory_space=pl.ANY)],
        out_specs=vmem,
        out_shape=shape((group, rows, LANES), jnp.bfloat16),
        compiler_params=params,
        name="scan",
    )(linked, through, one, half, pieces, early, final, rates)
    states = lax.all_to_all(
        moved, axes, split_axis=0, concat_axis=0, axis_index_groups=groups, tiled=True
    )
    return pl.pallas_call(
        norm_kernel,
        in_specs=[vmem] * 7,
        out_specs=pl.BlockSpec(memory_space=pl.ANY),
        out_shape=shape((tokens, width), jnp.bfloat16),
        scratch_shapes=[
            pltpu.VMEM((tokens, width), jnp.float32),
            pltpu.VMEM((tokens, width), jnp.bfloat16),
            pltpu.SemaphoreType.DMA((16,)),
        ],
        compiler_params=params,
        name="norm",
    )(idcol, before, rates, queries, states.reshape(all_pairs * HD, LANES), inner, norm_gain[None, :])


def solution(mesh):
    in_specs = (
        P(("ctx", "uly"), None),
        P(("ctx", "uly"), None),
        P(("ctx", "uly"), None),
        P(("ctx", "uly")),
        P("uly"),
        P(),
    )
    out_specs = P(("ctx", "uly"), None)
    return jax.shard_map(local, mesh=mesh, in_specs=in_specs, out_specs=out_specs, check_vma=False)
```

```python
import functools

import jax
import jax.numpy as jnp
from jax import lax
from jax.experimental import pallas as pl
from jax.experimental.pallas import tpu as pltpu
from jax.sharding import PartitionSpec as P

HD = 64
LANES = 2 * HD
NEVER = 1e9


def rate_of(facts, head, here):
    return facts[head // here : head // here + 1, head % here : head % here + 1]


def pair_rate(facts, pair, here):
    lane = lax.broadcasted_iota(jnp.int32, (1, LANES), 1)
    rates = []
    for head in (2 * pair, 2 * pair + 1):
        row = facts[pl.ds(lax.div(head, here), 1), :]
        rates.append(
            jnp.sum(jnp.where(lane == lax.rem(head, here), row, 0.0), axis=1, keepdims=True)
        )
    return jnp.where(lane < HD, rates[0], rates[1])


def turn_kernel(k_ref, v_ref, turned, filled):
    tokens, width = k_ref.shape
    filled[:tokens, :] = v_ref[...]
    filled[tokens:, :] = jnp.zeros((LANES - tokens, width), filled.dtype)
    blank = jnp.zeros((LANES - tokens, LANES), jnp.float32)
    for j in range(width // LANES):
        columns = slice(j * LANES, (j + 1) * LANES)
        block = jnp.concatenate([k_ref[:, columns].astype(jnp.float32), blank], 0)
        turned[columns, :] = jnp.transpose(block).astype(turned.dtype)


def own_ids(stored, tokens):
    members = stored.shape[0]
    at = lax.rem(lax.axis_index("uly") + members // 2, members)
    row = stored[pl.ds(at, 1), :]
    fill = jnp.full((1, LANES - tokens), -1.0, jnp.float32)
    return jnp.concatenate([row[:, LANES - tokens :], fill], 1)


def ends_kernel(here, tokens, group, stored, turned, v_ref, out_ref, made, sems):
    width = v_ref.shape[1]
    members = stored.shape[0]
    lane = lax.broadcasted_iota(jnp.int32, (HD, LANES), 1)
    ids = jnp.broadcast_to(own_ids(stored, tokens), (8, LANES))
    place = lax.broadcasted_iota(jnp.int32, ids.shape, 1)
    last = ids[:, tokens - 1 : tokens]
    age = jnp.where(ids == last, (tokens - 1 - place).astype(jnp.float32), NEVER)
    rows_each = made.shape[0] // group
    parts = sems.shape[0]
    share = made.shape[0] // parts
    copies = []
    for j in range(0, width // LANES, 2):
        weighted = []
        for head in range(2 * j, 2 * j + 4):
            weight = jnp.exp(-rate_of(stored, (head + members // 2 * here) % (members * here), here) * age)
            keys = turned[head * HD : (head + 1) * HD, :].astype(jnp.float32)
            keys = keys.reshape(HD // 8, 8, LANES) * weight[None]
            weighted.append(keys.reshape(HD, LANES))
        weighted = jnp.concatenate(weighted, 0)
        high = weighted.astype(jnp.bfloat16)
        low = (weighted - high.astype(jnp.float32)).astype(jnp.bfloat16)
        v = v_ref[:, j * LANES : (j + 2) * LANES]
        both = jnp.dot(
            jnp.concatenate([high, low], 1),
            jnp.concatenate([v, v], 0),
            preferred_element_type=jnp.float32,
        )
        for one in (0, 1):
            pair = both[one * LANES : (one + 1) * LANES, one * LANES : (one + 1) * LANES]
            state = jnp.where(lane < HD, pair[:HD], pair[HD:])
            size = min(rows_each, HD)
            for at in range(0, HD, size):
                owner, start = divmod((j + one) * HD + at, rows_each)
                start += (group - 1 - owner) * rows_each
                made[start : start + size, :] = state[at : at + size].astype(jnp.bfloat16)
        if (j + 2) * HD % share == 0:
            part = parts - (j + 2) * HD // share
            rows = slice(part * share, (part + 1) * share)
            copies.append(pltpu.make_async_copy(made.at[rows], out_ref.at[rows], sems.at[part]))
            copies[-1].start()
    for copy in copies:
        copy.wait()


def inner_kernel(
    here, facts, idcol, idrow, q_ref, turned, v_ref, after, out_ref, rates_ref
):
    tokens, width = q_ref.shape
    lane = lax.broadcasted_iota(jnp.int32, (tokens, LANES), 1)
    t = lax.broadcasted_iota(jnp.int32, (tokens, LANES), 0)
    seen = (t >= lane) & (idcol[...] == idrow[:1, :])
    age = jnp.where(seen, (t - lane).astype(jnp.float32), NEVER)
    for j in range(width // LANES):
        columns = slice(j * LANES, (j + 1) * LANES)
        q = q_ref[:, columns]
        zero = jnp.zeros_like(q)
        stacked = jnp.concatenate([jnp.where(lane < HD, q, zero), jnp.where(lane < HD, zero, q)], 0)
        scores = jnp.dot(
            stacked, turned[columns, :], preferred_element_type=jnp.float32
        )
        rates = [rate_of(facts, 2 * j + one, here) for one in (0, 1)]
        weight = jnp.concatenate([jnp.exp(-rate * age) for rate in rates], 0)
        probs = (scores * weight)[:, :tokens].astype(jnp.bfloat16)
        got = jnp.dot(probs, v_ref[:, columns], preferred_element_type=jnp.float32)
        out_ref[:, columns] = jnp.where(lane < HD, got[:tokens], got[tokens:])
        rates_ref[:, columns] = jnp.where(lane[:1] < HD, rates[0], rates[1])


def pass_kernel(stored, after, facts, idrow, idcol):
    members, tokens = stored.shape[0], idcol.shape[0]
    for u in range(members):
        at = (u + members // 2) % members
        facts[u : u + 1, :] = stored[at : at + 1, :]
    row = own_ids(stored, tokens)
    idrow[...] = jnp.broadcast_to(row, idrow.shape)
    idcol[...] = jnp.transpose(jnp.broadcast_to(row, (LANES, LANES)))[:tokens]


def few(count):
    return count if count <= 8 else 1


def link_kernel(here, tokens, chunks, facts, *refs):
    others, (linked, through, one, half, before, last) = refs[:-6], refs[-6:]
    members, slices = facts.shape[0], len(others) + 1
    ctx, uly = lax.axis_index("ctx"), lax.axis_index("uly")
    for back, tile in enumerate((facts, *others)):
        at = lax.rem(ctx + slices - back, slices) * members
        last[pl.ds(pl.multiple_of(at, members), members), :] = jnp.broadcast_to(
            tile[:, LANES - 1 :], (members, LANES)
        )
    me = ctx * members + uly
    now = last[...]
    then = jnp.concatenate([now[:1], now[:-1]], 0)
    end = jnp.concatenate([now[chunks - 1 :], now[: chunks - 1]], 0)
    linked[...] = jnp.where(now == then, 1.0, 0.0)
    through[...] = jnp.where(end == then, 1.0, 0.0)
    before[...] = jnp.where(me > 0, last[pl.ds(jnp.maximum(me - 1, 0), 1), :], -1.0)
    rows = one.shape[0]
    share = min(rows, HD)
    owner = ctx * chunks + lax.rem(uly, chunks)
    for at in range(0, rows, share):
        rate = pair_rate(facts, lax.div(owner * rows + at, HD), here)
        for ref, length in ((one, tokens), (half, tokens * chunks)):
            ref[at : at + share, :] = jnp.broadcast_to(
                jnp.exp(-rate * float(length)), (share, LANES)
            )


def half_kernel(chunks, linked, one, in_ref, early_ref, final_ref):
    slices, newest = early_ref.shape[0] + 1, in_ref.shape[0] - 1
    offset = jnp.where(lax.axis_index("uly") >= chunks, chunks, 0)

    def slice_end(c):
        def step(j, state):
            keep = linked[pl.ds(c * 2 * chunks + offset + j, 1), :] * one[...]
            return in_ref[newest - c * chunks - j].astype(jnp.float32) + keep * state

        begin = in_ref[newest - c * chunks].astype(jnp.float32)
        state = lax.fori_loop(1, chunks, step, begin, unroll=few(chunks - 1))
        return state.astype(early_ref.dtype)

    def early(c, _):
        early_ref[c] = slice_end(c)
        return 0

    lax.fori_loop(0, slices - 1, early, 0, unroll=few(slices - 1))
    final_ref[0] = slice_end(slices - 1)


def scan_kernel(
    chunks, linked, through, one, half, in_ref, early, final, after, out_ref
):
    slices, newest = early.shape[0] + 1, in_ref.shape[0] - 1
    later = lax.axis_index("uly") >= chunks
    offset = jnp.where(later, chunks, 0)

    def over_other(state, c, piece, wanted):
        keep = through[pl.ds(c * 2 * chunks + chunks - offset, 1), :] * half[...]
        return jnp.where(wanted, piece.astype(jnp.float32) + keep * state, state)

    def over_own(state, c):
        def step(j, state):
            at = c * chunks + j
            out_ref[at] = state.astype(out_ref.dtype)
            keep = linked[pl.ds(c * 2 * chunks + offset + j, 1), :] * one[...]
            return in_ref[newest - at].astype(jnp.float32) + keep * state

        return lax.fori_loop(0, chunks, step, state, unroll=few(chunks))

    def over_slice(c, state):
        state = over_own(over_other(state, c, early[c], later), c)
        return over_other(state, c, early[c], jnp.logical_not(later))

    begin = jnp.zeros(in_ref.shape[1:], jnp.float32)
    state = lax.fori_loop(0, slices - 1, over_slice, begin, unroll=few(slices - 1))
    over_own(over_other(state, slices - 1, final[0], later), slices - 1)


def norm_kernel(idcol, before, rates, q_ref, s_ref, inner_ref, gain, out_ref, raw, done, sems):
    tokens, width = q_ref.shape
    lane = lax.broadcasted_iota(jnp.int32, (HD, LANES), 1)
    place = lax.broadcasted_iota(jnp.int32, (tokens, LANES), 0)
    age = jnp.where(idcol[...] == before[...], (place + 1).astype(jnp.float32), NEVER)
    zero = jnp.zeros((HD, LANES), s_ref.dtype)
    total = jnp.zeros((tokens, LANES), jnp.float32)
    for j in range(0, width // LANES, 2):
        square = []
        for one in (0, 1):
            state = s_ref[(j + one) * HD : (j + one + 1) * HD, :]
            for half in (jnp.where(lane < HD, state, zero), jnp.where(lane < HD, zero, state)):
                square.append(jnp.concatenate([zero, half] if one else [half, zero], 1))
        columns = slice(j * LANES, (j + 2) * LANES)
        outer = jnp.dot(
            q_ref[:, columns], jnp.concatenate(square, 0), preferred_element_type=jnp.float32
        )
        for one in (0, 1):
            columns = slice((j + one) * LANES, (j + one + 1) * LANES)
            fade = jnp.exp(-rates[:, columns] * age)
            value = inner_ref[:, columns] + outer[:, one * LANES : (one + 1) * LANES] * fade
            total += value * value
            raw[:, columns] = value
    mean = jnp.sum(total, axis=1, keepdims=True) / float(width)
    scale = jnp.broadcast_to(lax.rsqrt(mean + 1e-06), (tokens, LANES))
    parts = sems.shape[0]
    share = width // parts
    copies = []
    for part in range(parts):
        for at in range(part * share, (part + 1) * share, LANES):
            columns = slice(at, at + LANES)
            done[:, columns] = (raw[:, columns] * scale * gain[:, columns]).astype(jnp.bfloat16)
        columns = slice(part * share, (part + 1) * share)
        copies.append(
            pltpu.make_async_copy(done.at[:, columns], out_ref.at[:, columns], sems.at[part])
        )
        copies[-1].start()
    for copy in copies:
        copy.wait()


def local(queries, keys, values, doc_ids, decay_rate, norm_gain):
    tokens, width = queries.shape
    here = decay_rate.shape[0]
    axes = ("ctx", "uly")
    slices, members = lax.axis_size("ctx"), lax.axis_size("uly")
    count = slices * members
    all_pairs = width // LANES
    chunks = members // 2
    group = slices * chunks
    rows = all_pairs * HD // group
    groups = [
        [c * members + half * chunks + u for c in range(slices) for u in range(chunks)]
        for half in (0, 1)
    ]
    swap = [
        (c * members + u, c * members + (u + chunks) % members)
        for c in range(slices)
        for u in range(members)
    ]

    vmem = pl.BlockSpec(memory_space=pltpu.VMEM)
    params = pltpu.CompilerParams(vmem_limit_bytes=32 * 1024 * 1024)
    shape = jax.ShapeDtypeStruct
    tile = shape((members, LANES), jnp.float32)

    own = jnp.pad(decay_rate, (0, LANES - here)) + jnp.pad(
        doc_ids, (LANES - tokens, 0)
    ).astype(jnp.float32)
    turned_round = [[(u + members // 2) % members for u in range(members)]]
    stored = lax.all_to_all(
        jnp.broadcast_to(own[None, :], tile.shape),
        "uly", split_axis=0, concat_axis=0, axis_index_groups=turned_round, tiled=True,
    )
    turned, filled = pl.pallas_call(
        turn_kernel,
        in_specs=[vmem] * 2,
        out_specs=[vmem] * 2,
        out_shape=[shape((width, LANES), jnp.bfloat16), shape((LANES, width), jnp.bfloat16)],
        compiler_params=params,
        cost_estimate=pl.CostEstimate(flops=0, bytes_accessed=12_000_000, transcendentals=0),
        name="turn",
    )(keys, values)
    ends = pl.pallas_call(
        functools.partial(ends_kernel, here, tokens, group),
        in_specs=[vmem] * 3,
        out_specs=pl.BlockSpec(memory_space=pl.ANY),
        out_shape=shape((all_pairs * HD, LANES), jnp.bfloat16),
        scratch_shapes=[
            pltpu.VMEM((all_pairs * HD, LANES), jnp.bfloat16),
            pltpu.SemaphoreType.DMA((8,)),
        ],
        compiler_params=params,
        name="ends",
    )(stored, turned, filled)
    pieces = lax.all_to_all(
        ends.reshape(group, rows, LANES),
        axes, split_axis=0, concat_axis=0, tiled=True,
        axis_index_groups=[members_of[::-1] for members_of in groups],
    )
    facts, idrow, idcol = pl.pallas_call(
        pass_kernel,
        in_specs=[vmem, pl.BlockSpec(memory_space=pl.ANY)],
        out_specs=[vmem] * 3,
        out_shape=[tile, shape((8, LANES), jnp.float32), shape((tokens, LANES), jnp.float32)],
        compiler_params=params,
        name="pass",
    )(stored, ends)
    others = [
        lax.ppermute(facts, "ctx", [(c, (c + ahead) % slices) for c in range(slices)])
        for ahead in range(1, slices)
    ]
    linked, through, one, half, before = pl.pallas_call(
        functools.partial(link_kernel, here, tokens, chunks),
        in_specs=[vmem] * slices,
        out_specs=[vmem] * 5,
        out_shape=[shape((count, LANES), jnp.float32)] * 2
        + [shape((rows, LANES), jnp.float32)] * 2
        + [shape((1, LANES), jnp.float32)],
        scratch_shapes=[pltpu.VMEM((count, LANES), jnp.float32)],
        compiler_params=params,
        name="link",
    )(facts, *others)
    early_ends, final_end = pl.pallas_call(
        functools.partial(half_kernel, chunks),
        in_specs=[vmem] * 3,
        out_specs=[vmem] * 2,
        out_shape=[
            shape((slices - 1, rows, LANES), jnp.bfloat16),
            shape((1, rows, LANES), jnp.bfloat16),
        ],
        compiler_params=params,
        name="half",
    )(linked, one, pieces)
    early = lax.ppermute(early_ends, axes, swap)
    final = lax.ppermute(final_end, axes, [(low, high) for low, high in swap if low < high])
    inner, rates = pl.pallas_call(
        functools.partial(inner_kernel, here),
        in_specs=[vmem] * 6 + [pl.BlockSpec(memory_space=pl.ANY)],
        out_specs=[vmem] * 2,
        out_shape=[shape((tokens, width), jnp.float32), shape((1, width), jnp.float32)],
        compiler_params=params,
        cost_estimate=pl.CostEstimate(
            flops=8_000_000_000, bytes_accessed=4_000_000, transcendentals=600_000
        ),
        name="inner",
    )(facts, idcol, idrow, queries, turned, values, early_ends)
    moved = pl.pallas_call(
        functools.partial(scan_kernel, chunks),
        in_specs=[vmem] * 7 + [pl.BlockSpec(memory_space=pl.ANY)],
        out_specs=vmem,
        out_shape=shape((group, rows, LANES), jnp.bfloat16),
        compiler_params=params,
        name="scan",
    )(linked, through, one, half, pieces, early, final, rates)
    states = lax.all_to_all(
        moved, axes, split_axis=0, concat_axis=0, axis_index_groups=groups, tiled=True
    )
    return pl.pallas_call(
        norm_kernel,
        in_specs=[vmem] * 7,
        out_specs=pl.BlockSpec(memory_space=pl.ANY),
        out_shape=shape((tokens, width), jnp.bfloat16),
        scratch_shapes=[
            pltpu.VMEM((tokens, width), jnp.float32),
            pltpu.VMEM((tokens, width), jnp.bfloat16),
            pltpu.SemaphoreType.DMA((16,)),
        ],
        compiler_params=params,
        name="norm",
    )(idcol, before, rates, queries, states.reshape(all_pairs * HD, LANES), inner, norm_gain[None, :])


def solution(mesh):
    in_specs = (
        P(("ctx", "uly"), None),
        P(("ctx", "uly"), None),
        P(("ctx", "uly"), None),
        P(("ctx", "uly")),
        P("uly"),
        P(),
    )
    out_specs = P(("ctx", "uly"), None)
    return jax.shard_map(local, mesh=mesh, in_specs=in_specs, out_specs=out_specs, check_vma=False)
```

```python
import functools

import jax
import jax.numpy as jnp
from jax import lax
from jax.experimental import pallas as pl
from jax.experimental.pallas import tpu as pltpu
from jax.sharding import PartitionSpec as P

HD = 64
LANES = 2 * HD
NEVER = 1e9


def rate_of(facts, head, here):
    return facts[head // here : head // here + 1, head % here : head % here + 1]


def pair_rate(facts, pair, here):
    lane = lax.broadcasted_iota(jnp.int32, (1, LANES), 1)
    rates = []
    for head in (2 * pair, 2 * pair + 1):
        row = facts[pl.ds(lax.div(head, here), 1), :]
        rates.append(
            jnp.sum(jnp.where(lane == lax.rem(head, here), row, 0.0), axis=1, keepdims=True)
        )
    return jnp.where(lane < HD, rates[0], rates[1])


def turn_kernel(k_ref, v_ref, turned, filled):
    tokens, width = k_ref.shape
    filled[:tokens, :] = v_ref[...]
    filled[tokens:, :] = jnp.zeros((LANES - tokens, width), filled.dtype)
    blank = jnp.zeros((LANES - tokens, LANES), jnp.float32)
    for j in range(width // LANES):
        columns = slice(j * LANES, (j + 1) * LANES)
        block = jnp.concatenate([k_ref[:, columns].astype(jnp.float32), blank], 0)
        turned[columns, :] = jnp.transpose(block).astype(turned.dtype)


def own_ids(stored, tokens):
    members = stored.shape[0]
    at = lax.rem(lax.axis_index("uly") + members // 2, members)
    row = stored[pl.ds(at, 1), :]
    fill = jnp.full((1, LANES - tokens), -1.0, jnp.float32)
    return jnp.concatenate([row[:, LANES - tokens :], fill], 1)


def ends_kernel(here, tokens, group, stored, turned, v_ref, out_ref, made, sems):
    width = v_ref.shape[1]
    members = stored.shape[0]
    lane = lax.broadcasted_iota(jnp.int32, (HD, LANES), 1)
    ids = jnp.broadcast_to(own_ids(stored, tokens), (8, LANES))
    place = lax.broadcasted_iota(jnp.int32, ids.shape, 1)
    last = ids[:, tokens - 1 : tokens]
    age = jnp.where(ids == last, (tokens - 1 - place).astype(jnp.float32), NEVER)
    rows_each = made.shape[0] // group
    parts = sems.shape[0]
    share = made.shape[0] // parts
    copies = []
    for j in range(0, width // LANES, 2):
        weighted = []
        for head in range(2 * j, 2 * j + 4):
            weight = jnp.exp(-rate_of(stored, (head + members // 2 * here) % (members * here), here) * age)
            keys = turned[head * HD : (head + 1) * HD, :].astype(jnp.float32)
            keys = keys.reshape(HD // 8, 8, LANES) * weight[None]
            weighted.append(keys.reshape(HD, LANES))
        weighted = jnp.concatenate(weighted, 0)
        high = weighted.astype(jnp.bfloat16)
        low = (weighted - high.astype(jnp.float32)).astype(jnp.bfloat16)
        v = v_ref[:, j * LANES : (j + 2) * LANES]
        both = jnp.dot(
            jnp.concatenate([high, low], 1),
            jnp.concatenate([v, v], 0),
            preferred_element_type=jnp.float32,
        )
        for one in (0, 1):
            pair = both[one * LANES : (one + 1) * LANES, one * LANES : (one + 1) * LANES]
            state = jnp.where(lane < HD, pair[:HD], pair[HD:])
            size = min(rows_each, HD)
            for at in range(0, HD, size):
                owner, start = divmod((j + one) * HD + at, rows_each)
                start += (group - 1 - owner) * rows_each
                made[start : start + size, :] = state[at : at + size].astype(jnp.bfloat16)
        if (j + 2) * HD % share == 0:
            part = parts - (j + 2) * HD // share
            rows = slice(part * share, (part + 1) * share)
            copies.append(pltpu.make_async_copy(made.at[rows], out_ref.at[rows], sems.at[part]))
            copies[-1].start()
    for copy in copies:
        copy.wait()


def inner_kernel(
    here, facts, idcol, idrow, q_ref, turned, v_ref, after, out_ref, rates_ref
):
    tokens, width = q_ref.shape
    lane = lax.broadcasted_iota(jnp.int32, (tokens, LANES), 1)
    t = lax.broadcasted_iota(jnp.int32, (tokens, LANES), 0)
    seen = (t >= lane) & (idcol[...] == idrow[:1, :])
    age = jnp.where(seen, (t - lane).astype(jnp.float32), NEVER)
    for j in range(width // LANES):
        columns = slice(j * LANES, (j + 1) * LANES)
        q = q_ref[:, columns]
        zero = jnp.zeros_like(q)
        stacked = jnp.concatenate([jnp.where(lane < HD, q, zero), jnp.where(lane < HD, zero, q)], 0)
        scores = jnp.dot(
            stacked, turned[columns, :], preferred_element_type=jnp.float32
        )
        rates = [rate_of(facts, 2 * j + one, here) for one in (0, 1)]
        weight = jnp.concatenate([jnp.exp(-rate * age) for rate in rates], 0)
        probs = (scores * weight)[:, :tokens].astype(jnp.bfloat16)
        got = jnp.dot(probs, v_ref[:, columns], preferred_element_type=jnp.float32)
        out_ref[:, columns] = jnp.where(lane < HD, got[:tokens], got[tokens:])
        rates_ref[:, columns] = jnp.where(lane[:1] < HD, rates[0], rates[1])


def pass_kernel(stored, after, facts, idrow, idcol):
    members, tokens = stored.shape[0], idcol.shape[0]
    for u in range(members):
        at = (u + members // 2) % members
        facts[u : u + 1, :] = stored[at : at + 1, :]
    row = own_ids(stored, tokens)
    idrow[...] = jnp.broadcast_to(row, idrow.shape)
    idcol[...] = jnp.transpose(jnp.broadcast_to(row, (LANES, LANES)))[:tokens]


def few(count):
    return count if count <= 8 else 1


def link_kernel(here, tokens, chunks, facts, *refs):
    others, (linked, through, one, half, before, last) = refs[:-6], refs[-6:]
    members, slices = facts.shape[0], len(others) + 1
    ctx, uly = lax.axis_index("ctx"), lax.axis_index("uly")
    for back, tile in enumerate((facts, *others)):
        at = lax.rem(ctx + slices - back, slices) * members
        last[pl.ds(pl.multiple_of(at, members), members), :] = jnp.broadcast_to(
            tile[:, LANES - 1 :], (members, LANES)
        )
    me = ctx * members + uly
    now = last[...]
    then = jnp.concatenate([now[:1], now[:-1]], 0)
    end = jnp.concatenate([now[chunks - 1 :], now[: chunks - 1]], 0)
    linked[...] = jnp.where(now == then, 1.0, 0.0)
    through[...] = jnp.where(end == then, 1.0, 0.0)
    before[...] = jnp.where(me > 0, last[pl.ds(jnp.maximum(me - 1, 0), 1), :], -1.0)
    rows = one.shape[0]
    share = min(rows, HD)
    owner = ctx * chunks + lax.rem(uly, chunks)
    for at in range(0, rows, share):
        rate = pair_rate(facts, lax.div(owner * rows + at, HD), here)
        for ref, length in ((one, tokens), (half, tokens * chunks)):
            ref[at : at + share, :] = jnp.broadcast_to(
                jnp.exp(-rate * float(length)), (share, LANES)
            )


def half_kernel(chunks, linked, one, in_ref, early_ref, final_ref):
    slices, newest = early_ref.shape[0] + 1, in_ref.shape[0] - 1
    offset = jnp.where(lax.axis_index("uly") >= chunks, chunks, 0)

    def slice_end(c):
        def step(j, state):
            keep = linked[pl.ds(c * 2 * chunks + offset + j, 1), :] * one[...]
            return in_ref[newest - c * chunks - j].astype(jnp.float32) + keep * state

        begin = in_ref[newest - c * chunks].astype(jnp.float32)
        state = lax.fori_loop(1, chunks, step, begin, unroll=few(chunks - 1))
        return state.astype(early_ref.dtype)

    def early(c, _):
        early_ref[c] = slice_end(c)
        return 0

    lax.fori_loop(0, slices - 1, early, 0, unroll=few(slices - 1))
    final_ref[0] = slice_end(slices - 1)


def scan_kernel(
    chunks, linked, through, one, half, in_ref, early, final, after, out_ref
):
    slices, newest = early.shape[0] + 1, in_ref.shape[0] - 1
    later = lax.axis_index("uly") >= chunks
    offset = jnp.where(later, chunks, 0)

    def over_other(state, c, piece, wanted):
        keep = through[pl.ds(c * 2 * chunks + chunks - offset, 1), :] * half[...]
        return jnp.where(wanted, piece.astype(jnp.float32) + keep * state, state)

    def over_own(state, c):
        def step(j, state):
            at = c * chunks + j
            out_ref[lax.rem(at + out_ref.shape[0] // 2, out_ref.shape[0])] = state.astype(out_ref.dtype)
            keep = linked[pl.ds(c * 2 * chunks + offset + j, 1), :] * one[...]
            return in_ref[newest - at].astype(jnp.float32) + keep * state

        return lax.fori_loop(0, chunks, step, state, unroll=few(chunks))

    def over_slice(c, state):
        state = over_own(over_other(state, c, early[c], later), c)
        return over_other(state, c, early[c], jnp.logical_not(later))

    begin = jnp.zeros(in_ref.shape[1:], jnp.float32)
    state = lax.fori_loop(0, slices - 1, over_slice, begin, unroll=few(slices - 1))
    over_own(over_other(state, slices - 1, final[0], later), slices - 1)


def norm_kernel(idcol, before, rates, q_ref, s_ref, inner_ref, gain, out_ref, raw, done, sems):
    tokens, width = q_ref.shape
    lane = lax.broadcasted_iota(jnp.int32, (HD, LANES), 1)
    place = lax.broadcasted_iota(jnp.int32, (tokens, LANES), 0)
    age = jnp.where(idcol[...] == before[...], (place + 1).astype(jnp.float32), NEVER)
    zero = jnp.zeros((HD, LANES), s_ref.dtype)
    total = jnp.zeros((tokens, LANES), jnp.float32)
    for j in range(0, width // LANES, 2):
        square = []
        for one in (0, 1):
            at = ((j + one) * HD + s_ref.shape[0] // 2) % s_ref.shape[0]
            state = s_ref[at : at + HD, :]
            for half in (jnp.where(lane < HD, state, zero), jnp.where(lane < HD, zero, state)):
                square.append(jnp.concatenate([zero, half] if one else [half, zero], 1))
        columns = slice(j * LANES, (j + 2) * LANES)
        outer = jnp.dot(
            q_ref[:, columns], jnp.concatenate(square, 0), preferred_element_type=jnp.float32
        )
        for one in (0, 1):
            columns = slice((j + one) * LANES, (j + one + 1) * LANES)
            fade = jnp.exp(-rates[:, columns] * age)
            value = inner_ref[:, columns] + outer[:, one * LANES : (one + 1) * LANES] * fade
            total += value * value
            raw[:, columns] = value
    mean = jnp.sum(total, axis=1, keepdims=True) / float(width)
    scale = jnp.broadcast_to(lax.rsqrt(mean + 1e-06), (tokens, LANES))
    parts = sems.shape[0]
    share = width // parts
    copies = []
    for part in range(parts):
        for at in range(part * share, (part + 1) * share, LANES):
            columns = slice(at, at + LANES)
            done[:, columns] = (raw[:, columns] * scale * gain[:, columns]).astype(jnp.bfloat16)
        columns = slice(part * share, (part + 1) * share)
        copies.append(
            pltpu.make_async_copy(done.at[:, columns], out_ref.at[:, columns], sems.at[part])
        )
        copies[-1].start()
    for copy in copies:
        copy.wait()


def local(queries, keys, values, doc_ids, decay_rate, norm_gain):
    tokens, width = queries.shape
    here = decay_rate.shape[0]
    axes = ("ctx", "uly")
    slices, members = lax.axis_size("ctx"), lax.axis_size("uly")
    count = slices * members
    all_pairs = width // LANES
    chunks = members // 2
    group = slices * chunks
    rows = all_pairs * HD // group
    groups = [
        [c * members + half * chunks + u for c in range(slices) for u in range(chunks)]
        for half in (0, 1)
    ]
    swap = [
        (c * members + u, c * members + (u + chunks) % members)
        for c in range(slices)
        for u in range(members)
    ]

    vmem = pl.BlockSpec(memory_space=pltpu.VMEM)
    params = pltpu.CompilerParams(vmem_limit_bytes=32 * 1024 * 1024)
    shape = jax.ShapeDtypeStruct
    tile = shape((members, LANES), jnp.float32)

    own = jnp.pad(decay_rate, (0, LANES - here)) + jnp.pad(
        doc_ids, (LANES - tokens, 0)
    ).astype(jnp.float32)
    turned_round = [[(u + members // 2) % members for u in range(members)]]
    stored = lax.all_to_all(
        jnp.broadcast_to(own[None, :], tile.shape),
        "uly", split_axis=0, concat_axis=0, axis_index_groups=turned_round, tiled=True,
    )
    turned, filled = pl.pallas_call(
        turn_kernel,
        in_specs=[vmem] * 2,
        out_specs=[vmem] * 2,
        out_shape=[shape((width, LANES), jnp.bfloat16), shape((LANES, width), jnp.bfloat16)],
        compiler_params=params,
        cost_estimate=pl.CostEstimate(flops=0, bytes_accessed=12_000_000, transcendentals=0),
        name="turn",
    )(keys, values)
    ends = pl.pallas_call(
        functools.partial(ends_kernel, here, tokens, group),
        in_specs=[vmem] * 3,
        out_specs=pl.BlockSpec(memory_space=pl.ANY),
        out_shape=shape((all_pairs * HD, LANES), jnp.bfloat16),
        scratch_shapes=[
            pltpu.VMEM((all_pairs * HD, LANES), jnp.bfloat16),
            pltpu.SemaphoreType.DMA((8,)),
        ],
        compiler_params=params,
        name="ends",
    )(stored, turned, filled)
    pieces = lax.all_to_all(
        ends.reshape(group, rows, LANES),
        axes, split_axis=0, concat_axis=0, tiled=True,
        axis_index_groups=[members_of[::-1] for members_of in groups],
    )
    facts, idrow, idcol = pl.pallas_call(
        pass_kernel,
        in_specs=[vmem, pl.BlockSpec(memory_space=pl.ANY)],
        out_specs=[vmem] * 3,
        out_shape=[tile, shape((8, LANES), jnp.float32), shape((tokens, LANES), jnp.float32)],
        compiler_params=params,
        name="pass",
    )(stored, ends)
    others = [
        lax.ppermute(facts, "ctx", [(c, (c + ahead) % slices) for c in range(slices)])
        for ahead in range(1, slices)
    ]
    linked, through, one, half, before = pl.pallas_call(
        functools.partial(link_kernel, here, tokens, chunks),
        in_specs=[vmem] * slices,
        out_specs=[vmem] * 5,
        out_shape=[shape((count, LANES), jnp.float32)] * 2
        + [shape((rows, LANES), jnp.float32)] * 2
        + [shape((1, LANES), jnp.float32)],
        scratch_shapes=[pltpu.VMEM((count, LANES), jnp.float32)],
        compiler_params=params,
        name="link",
    )(facts, *others)
    early_ends, final_end = pl.pallas_call(
        functools.partial(half_kernel, chunks),
        in_specs=[vmem] * 3,
        out_specs=[vmem] * 2,
        out_shape=[
            shape((slices - 1, rows, LANES), jnp.bfloat16),
            shape((1, rows, LANES), jnp.bfloat16),
        ],
        compiler_params=params,
        name="half",
    )(linked, one, pieces)
    early = lax.ppermute(early_ends, axes, swap)
    final = lax.ppermute(final_end, axes, [(low, high) for low, high in swap if low < high])
    inner, rates = pl.pallas_call(
        functools.partial(inner_kernel, here),
        in_specs=[vmem] * 6 + [pl.BlockSpec(memory_space=pl.ANY)],
        out_specs=[vmem] * 2,
        out_shape=[shape((tokens, width), jnp.float32), shape((1, width), jnp.float32)],
        compiler_params=params,
        cost_estimate=pl.CostEstimate(
            flops=8_000_000_000, bytes_accessed=4_000_000, transcendentals=600_000
        ),
        name="inner",
    )(facts, idcol, idrow, queries, turned, values, early_ends)
    moved = pl.pallas_call(
        functools.partial(scan_kernel, chunks),
        in_specs=[vmem] * 7 + [pl.BlockSpec(memory_space=pl.ANY)],
        out_specs=vmem,
        out_shape=shape((group, rows, LANES), jnp.bfloat16),
        compiler_params=params,
        name="scan",
    )(linked, through, one, half, pieces, early, final, rates)
    states = lax.all_to_all(
        moved,
        axes, split_axis=0, concat_axis=0, tiled=True,
        axis_index_groups=[members_of[group // 2 :] + members_of[: group // 2] for members_of in groups],
    )
    return pl.pallas_call(
        norm_kernel,
        in_specs=[vmem] * 7,
        out_specs=pl.BlockSpec(memory_space=pl.ANY),
        out_shape=shape((tokens, width), jnp.bfloat16),
        scratch_shapes=[
            pltpu.VMEM((tokens, width), jnp.float32),
            pltpu.VMEM((tokens, width), jnp.bfloat16),
            pltpu.SemaphoreType.DMA((16,)),
        ],
        compiler_params=params,
        name="norm",
    )(idcol, before, rates, queries, states.reshape(all_pairs * HD, LANES), inner, norm_gain[None, :])


def solution(mesh):
    in_specs = (
        P(("ctx", "uly"), None),
        P(("ctx", "uly"), None),
        P(("ctx", "uly"), None),
        P(("ctx", "uly")),
        P("uly"),
        P(),
    )
    out_specs = P(("ctx", "uly"), None)
    return jax.shard_map(local, mesh=mesh, in_specs=in_specs, out_specs=out_specs, check_vma=False)
```

```python
import functools

import jax
import jax.numpy as jnp
from jax import lax
from jax.experimental import pallas as pl
from jax.experimental.pallas import tpu as pltpu
from jax.sharding import PartitionSpec as P

HD = 64
LANES = 2 * HD
NEVER = 1e9


def rate_of(facts, head, here):
    return facts[head // here : head // here + 1, head % here : head % here + 1]


def pair_rate(facts, pair, here):
    lane = lax.broadcasted_iota(jnp.int32, (1, LANES), 1)
    rates = []
    for head in (2 * pair, 2 * pair + 1):
        row = facts[pl.ds(lax.div(head, here), 1), :]
        rates.append(
            jnp.sum(jnp.where(lane == lax.rem(head, here), row, 0.0), axis=1, keepdims=True)
        )
    return jnp.where(lane < HD, rates[0], rates[1])


def turn_kernel(k_ref, v_ref, turned, filled):
    tokens, width = k_ref.shape
    filled[:tokens, :] = v_ref[...]
    filled[tokens:, :] = jnp.zeros((LANES - tokens, width), filled.dtype)
    blank = jnp.zeros((LANES - tokens, LANES), jnp.float32)
    for j in range(width // LANES):
        columns = slice(j * LANES, (j + 1) * LANES)
        block = jnp.concatenate([k_ref[:, columns].astype(jnp.float32), blank], 0)
        turned[columns, :] = jnp.transpose(block).astype(turned.dtype)


def own_ids(stored, tokens):
    members = stored.shape[0]
    at = lax.rem(lax.axis_index("uly") + members // 2, members)
    row = stored[pl.ds(at, 1), :]
    fill = jnp.full((1, LANES - tokens), -1.0, jnp.float32)
    return jnp.concatenate([row[:, LANES - tokens :], fill], 1)


def ends_kernel(here, tokens, group, stored, turned, v_ref, out_ref, made, sems):
    width = v_ref.shape[1]
    members = stored.shape[0]
    lane = lax.broadcasted_iota(jnp.int32, (HD, LANES), 1)
    ids = jnp.broadcast_to(own_ids(stored, tokens), (8, LANES))
    place = lax.broadcasted_iota(jnp.int32, ids.shape, 1)
    last = ids[:, tokens - 1 : tokens]
    age = jnp.where(ids == last, (tokens - 1 - place).astype(jnp.float32), NEVER)
    rows_each = made.shape[0] // group
    parts = sems.shape[0]
    share = made.shape[0] // parts
    copies = []
    for j in range(0, width // LANES, 2):
        weighted = []
        for head in range(2 * j, 2 * j + 4):
            weight = jnp.exp(-rate_of(stored, (head + members // 2 * here) % (members * here), here) * age)
            keys = turned[head * HD : (head + 1) * HD, :].astype(jnp.float32)
            keys = keys.reshape(HD // 8, 8, LANES) * weight[None]
            weighted.append(keys.reshape(HD, LANES))
        weighted = jnp.concatenate(weighted, 0)
        high = weighted.astype(jnp.bfloat16)
        low = (weighted - high.astype(jnp.float32)).astype(jnp.bfloat16)
        v = v_ref[:, j * LANES : (j + 2) * LANES]
        both = jnp.dot(
            jnp.concatenate([high, low], 1),
            jnp.concatenate([v, v], 0),
            preferred_element_type=jnp.float32,
        )
        for one in (0, 1):
            pair = both[one * LANES : (one + 1) * LANES, one * LANES : (one + 1) * LANES]
            state = jnp.where(lane < HD, pair[:HD], pair[HD:])
            size = min(rows_each, HD)
            for at in range(0, HD, size):
                owner, start = divmod((j + one) * HD + at, rows_each)
                start += (group - 1 - owner) * rows_each
                made[start : start + size, :] = state[at : at + size].astype(jnp.bfloat16)
        if (j + 2) * HD % share == 0:
            part = parts - (j + 2) * HD // share
            rows = slice(part * share, (part + 1) * share)
            copies.append(pltpu.make_async_copy(made.at[rows], out_ref.at[rows], sems.at[part]))
            copies[-1].start()
    for copy in copies:
        copy.wait()


def inner_kernel(
    here, facts, idcol, idrow, q_ref, turned, v_ref, after, out_ref, rates_ref
):
    tokens, width = q_ref.shape
    lane = lax.broadcasted_iota(jnp.int32, (tokens, LANES), 1)
    t = lax.broadcasted_iota(jnp.int32, (tokens, LANES), 0)
    seen = (t >= lane) & (idcol[...] == idrow[:1, :])
    age = jnp.where(seen, (t - lane).astype(jnp.float32), NEVER)
    for j in range(width // LANES):
        columns = slice(j * LANES, (j + 1) * LANES)
        q = q_ref[:, columns]
        zero = jnp.zeros_like(q)
        stacked = jnp.concatenate([jnp.where(lane < HD, q, zero), jnp.where(lane < HD, zero, q)], 0)
        scores = jnp.dot(
            stacked, turned[columns, :], preferred_element_type=jnp.float32
        )
        rates = [rate_of(facts, 2 * j + one, here) for one in (0, 1)]
        weight = jnp.concatenate([jnp.exp(-rate * age) for rate in rates], 0)
        probs = (scores * weight)[:, :tokens].astype(jnp.bfloat16)
        got = jnp.dot(probs, v_ref[:, columns], preferred_element_type=jnp.float32)
        out_ref[:, columns] = jnp.where(lane < HD, got[:tokens], got[tokens:])
        rates_ref[:, columns] = jnp.where(lane[:1] < HD, rates[0], rates[1])


def pass_kernel(stored, after, facts, idrow, idcol):
    members, tokens = stored.shape[0], idcol.shape[0]
    for u in range(members):
        at = (u + members // 2) % members
        facts[u : u + 1, :] = stored[at : at + 1, :]
    row = own_ids(stored, tokens)
    idrow[...] = jnp.broadcast_to(row, idrow.shape)
    idcol[...] = jnp.transpose(jnp.broadcast_to(row, (LANES, LANES)))[:tokens]


def few(count):
    return count if count <= 8 else 1


def link_kernel(here, tokens, chunks, facts, *refs):
    others, (linked, through, one, half, before, last) = refs[:-6], refs[-6:]
    members, slices = facts.shape[0], len(others) + 1
    ctx, uly = lax.axis_index("ctx"), lax.axis_index("uly")
    for back, tile in enumerate((facts, *others)):
        at = lax.rem(ctx + slices - back, slices) * members
        last[pl.ds(pl.multiple_of(at, members), members), :] = jnp.broadcast_to(
            tile[:, LANES - 1 :], (members, LANES)
        )
    me = ctx * members + uly
    now = last[...]
    then = jnp.concatenate([now[:1], now[:-1]], 0)
    end = jnp.concatenate([now[chunks - 1 :], now[: chunks - 1]], 0)
    linked[...] = jnp.where(now == then, 1.0, 0.0)
    through[...] = jnp.where(end == then, 1.0, 0.0)
    before[...] = jnp.where(me > 0, last[pl.ds(jnp.maximum(me - 1, 0), 1), :], -1.0)
    rows = one.shape[0]
    share = min(rows, HD)
    owner = ctx * chunks + lax.rem(uly, chunks)
    for at in range(0, rows, share):
        rate = pair_rate(facts, lax.div(owner * rows + at, HD), here)
        for ref, length in ((one, tokens), (half, tokens * chunks)):
            ref[at : at + share, :] = jnp.broadcast_to(
                jnp.exp(-rate * float(length)), (share, LANES)
            )


def half_kernel(chunks, linked, one, in_ref, early_ref, final_ref):
    slices, newest = early_ref.shape[0] + 1, in_ref.shape[0] - 1
    offset = jnp.where(lax.axis_index("uly") >= chunks, chunks, 0)

    def slice_end(c):
        def step(j, state):
            keep = linked[pl.ds(c * 2 * chunks + offset + j, 1), :] * one[...]
            return in_ref[newest - c * chunks - j].astype(jnp.float32) + keep * state

        begin = in_ref[newest - c * chunks].astype(jnp.float32)
        state = lax.fori_loop(1, chunks, step, begin, unroll=few(chunks - 1))
        return state.astype(early_ref.dtype)

    def early(c, _):
        early_ref[c] = slice_end(c)
        return 0

    lax.fori_loop(0, slices - 1, early, 0, unroll=few(slices - 1))
    final_ref[0] = slice_end(slices - 1)


def scan_kernel(
    chunks, linked, through, one, half, in_ref, early, final, after, out_ref
):
    slices, newest = early.shape[0] + 1, in_ref.shape[0] - 1
    later = lax.axis_index("uly") >= chunks
    offset = jnp.where(later, chunks, 0)

    def over_other(state, c, piece, wanted):
        keep = through[pl.ds(c * 2 * chunks + chunks - offset, 1), :] * half[...]
        return jnp.where(wanted, piece.astype(jnp.float32) + keep * state, state)

    def over_own(state, c):
        def step(j, state):
            at = c * chunks + j
            out_ref[at] = state.astype(out_ref.dtype)
            keep = linked[pl.ds(c * 2 * chunks + offset + j, 1), :] * one[...]
            return in_ref[newest - at].astype(jnp.float32) + keep * state

        return lax.fori_loop(0, chunks, step, state, unroll=few(chunks))

    def over_slice(c, state):
        state = over_own(over_other(state, c, early[c], later), c)
        return over_other(state, c, early[c], jnp.logical_not(later))

    begin = jnp.zeros(in_ref.shape[1:], jnp.float32)
    state = lax.fori_loop(0, slices - 1, over_slice, begin, unroll=few(slices - 1))
    over_own(over_other(state, slices - 1, final[0], later), slices - 1)


def norm_kernel(idcol, before, rates, q_ref, s_ref, inner_ref, gain, out_ref, raw, done, sems):
    tokens, width = q_ref.shape
    lane = lax.broadcasted_iota(jnp.int32, (HD, LANES), 1)
    place = lax.broadcasted_iota(jnp.int32, (tokens, LANES), 0)
    age = jnp.where(idcol[...] == before[...], (place + 1).astype(jnp.float32), NEVER)
    zero = jnp.zeros((HD, LANES), s_ref.dtype)
    total = jnp.zeros((tokens, LANES), jnp.float32)
    for j in range(0, width // LANES, 2):
        square = []
        for one in (0, 1):
            state = s_ref[(j + one) * HD : (j + one + 1) * HD, :]
            for half in (jnp.where(lane < HD, state, zero), jnp.where(lane < HD, zero, state)):
                square.append(jnp.concatenate([zero, half] if one else [half, zero], 1))
        columns = slice(j * LANES, (j + 2) * LANES)
        outer = jnp.dot(
            q_ref[:, columns], jnp.concatenate(square, 0), preferred_element_type=jnp.float32
        )
        for one in (0, 1):
            columns = slice((j + one) * LANES, (j + one + 1) * LANES)
            fade = jnp.exp(-rates[:, columns] * age)
            value = inner_ref[:, columns] + outer[:, one * LANES : (one + 1) * LANES] * fade
            total += value * value
            raw[:, columns] = value
    mean = jnp.sum(total, axis=1, keepdims=True) / float(width)
    scale = jnp.broadcast_to(lax.rsqrt(mean + 1e-06), (tokens, LANES))
    parts = sems.shape[0]
    share = tokens // parts
    copies = []
    for part in range(parts):
        rows = slice(part * share, (part + 1) * share)
        for at in range(0, width, LANES):
            columns = slice(at, at + LANES)
            done[rows, columns] = (raw[rows, columns] * scale[rows] * gain[:, columns]).astype(
                jnp.bfloat16
            )
        copies.append(pltpu.make_async_copy(done.at[rows], out_ref.at[rows], sems.at[part]))
        copies[-1].start()
    for copy in copies:
        copy.wait()


def local(queries, keys, values, doc_ids, decay_rate, norm_gain):
    tokens, width = queries.shape
    here = decay_rate.shape[0]
    axes = ("ctx", "uly")
    slices, members = lax.axis_size("ctx"), lax.axis_size("uly")
    count = slices * members
    all_pairs = width // LANES
    chunks = members // 2
    group = slices * chunks
    rows = all_pairs * HD // group
    groups = [
        [c * members + half * chunks + u for c in range(slices) for u in range(chunks)]
        for half in (0, 1)
    ]
    swap = [
        (c * members + u, c * members + (u + chunks) % members)
        for c in range(slices)
        for u in range(members)
    ]

    vmem = pl.BlockSpec(memory_space=pltpu.VMEM)
    params = pltpu.CompilerParams(vmem_limit_bytes=32 * 1024 * 1024)
    shape = jax.ShapeDtypeStruct
    tile = shape((members, LANES), jnp.float32)

    own = jnp.pad(decay_rate, (0, LANES - here)) + jnp.pad(
        doc_ids, (LANES - tokens, 0)
    ).astype(jnp.float32)
    turned_round = [[(u + members // 2) % members for u in range(members)]]
    stored = lax.all_to_all(
        jnp.broadcast_to(own[None, :], tile.shape),
        "uly", split_axis=0, concat_axis=0, axis_index_groups=turned_round, tiled=True,
    )
    turned, filled = pl.pallas_call(
        turn_kernel,
        in_specs=[vmem] * 2,
        out_specs=[vmem] * 2,
        out_shape=[shape((width, LANES), jnp.bfloat16), shape((LANES, width), jnp.bfloat16)],
        compiler_params=params,
        cost_estimate=pl.CostEstimate(flops=0, bytes_accessed=12_000_000, transcendentals=0),
        name="turn",
    )(keys, values)
    ends = pl.pallas_call(
        functools.partial(ends_kernel, here, tokens, group),
        in_specs=[vmem] * 3,
        out_specs=pl.BlockSpec(memory_space=pl.ANY),
        out_shape=shape((all_pairs * HD, LANES), jnp.bfloat16),
        scratch_shapes=[
            pltpu.VMEM((all_pairs * HD, LANES), jnp.bfloat16),
            pltpu.SemaphoreType.DMA((8,)),
        ],
        compiler_params=params,
        name="ends",
    )(stored, turned, filled)
    pieces = lax.all_to_all(
        ends.reshape(group, rows, LANES),
        axes, split_axis=0, concat_axis=0, tiled=True,
        axis_index_groups=[members_of[::-1] for members_of in groups],
    )
    facts, idrow, idcol = pl.pallas_call(
        pass_kernel,
        in_specs=[vmem, pl.BlockSpec(memory_space=pl.ANY)],
        out_specs=[vmem] * 3,
        out_shape=[tile, shape((8, LANES), jnp.float32), shape((tokens, LANES), jnp.float32)],
        compiler_params=params,
        name="pass",
    )(stored, ends)
    others = [
        lax.ppermute(facts, "ctx", [(c, (c + ahead) % slices) for c in range(slices)])
        for ahead in range(1, slices)
    ]
    linked, through, one, half, before = pl.pallas_call(
        functools.partial(link_kernel, here, tokens, chunks),
        in_specs=[vmem] * slices,
        out_specs=[vmem] * 5,
        out_shape=[shape((count, LANES), jnp.float32)] * 2
        + [shape((rows, LANES), jnp.float32)] * 2
        + [shape((1, LANES), jnp.float32)],
        scratch_shapes=[pltpu.VMEM((count, LANES), jnp.float32)],
        compiler_params=params,
        name="link",
    )(facts, *others)
    early_ends, final_end = pl.pallas_call(
        functools.partial(half_kernel, chunks),
        in_specs=[vmem] * 3,
        out_specs=[vmem] * 2,
        out_shape=[
            shape((slices - 1, rows, LANES), jnp.bfloat16),
            shape((1, rows, LANES), jnp.bfloat16),
        ],
        compiler_params=params,
        name="half",
    )(linked, one, pieces)
    early = lax.ppermute(early_ends, axes, swap)
    final = lax.ppermute(final_end, axes, [(low, high) for low, high in swap if low < high])
    inner, rates = pl.pallas_call(
        functools.partial(inner_kernel, here),
        in_specs=[vmem] * 6 + [pl.BlockSpec(memory_space=pl.ANY)],
        out_specs=[vmem] * 2,
        out_shape=[shape((tokens, width), jnp.float32), shape((1, width), jnp.float32)],
        compiler_params=params,
        cost_estimate=pl.CostEstimate(
            flops=8_000_000_000, bytes_accessed=4_000_000, transcendentals=600_000
        ),
        name="inner",
    )(facts, idcol, idrow, queries, turned, values, early_ends)
    moved = pl.pallas_call(
        functools.partial(scan_kernel, chunks),
        in_specs=[vmem] * 7 + [pl.BlockSpec(memory_space=pl.ANY)],
        out_specs=vmem,
        out_shape=shape((group, rows, LANES), jnp.bfloat16),
        compiler_params=params,
        name="scan",
    )(linked, through, one, half, pieces, early, final, rates)
    states = lax.all_to_all(
        moved, axes, split_axis=0, concat_axis=0, axis_index_groups=groups, tiled=True
    )
    return pl.pallas_call(
        norm_kernel,
        in_specs=[vmem] * 7,
        out_specs=pl.BlockSpec(memory_space=pl.ANY),
        out_shape=shape((tokens, width), jnp.bfloat16),
        scratch_shapes=[
            pltpu.VMEM((tokens, width), jnp.float32),
            pltpu.VMEM((tokens, width), jnp.bfloat16),
            pltpu.SemaphoreType.DMA((tokens // 16,)),
        ],
        compiler_params=params,
        name="norm",
    )(idcol, before, rates, queries, states.reshape(all_pairs * HD, LANES), inner, norm_gain[None, :])


def solution(mesh):
    in_specs = (
        P(("ctx", "uly"), None),
        P(("ctx", "uly"), None),
        P(("ctx", "uly"), None),
        P(("ctx", "uly")),
        P("uly"),
        P(),
    )
    out_specs = P(("ctx", "uly"), None)
    return jax.shard_map(local, mesh=mesh, in_specs=in_specs, out_specs=out_specs, check_vma=False)
```

```python
import functools

import jax
import jax.numpy as jnp
from jax import lax
from jax.experimental import pallas as pl
from jax.experimental.pallas import tpu as pltpu
from jax.sharding import PartitionSpec as P

HD = 64
LANES = 2 * HD
NEVER = 1e9


def rate_of(facts, head, here):
    return facts[head // here : head // here + 1, head % here : head % here + 1]


def pair_rate(facts, pair, here):
    lane = lax.broadcasted_iota(jnp.int32, (1, LANES), 1)
    rates = []
    for head in (2 * pair, 2 * pair + 1):
        row = facts[pl.ds(lax.div(head, here), 1), :]
        rates.append(
            jnp.sum(jnp.where(lane == lax.rem(head, here), row, 0.0), axis=1, keepdims=True)
        )
    return jnp.where(lane < HD, rates[0], rates[1])


def own_kernel(rates, ids, out_ref, rates_here, ids_here, rows, sems):
    here, tokens = rates.shape[1], ids.shape[1]
    copies = [
        pltpu.make_async_copy(rates, rates_here, sems.at[0]),
        pltpu.make_async_copy(ids, ids_here, sems.at[1]),
    ]
    for copy in copies:
        copy.start()
    for copy in copies:
        copy.wait()
    blank = jnp.zeros((1, LANES - tokens - here), jnp.float32)
    row = jnp.concatenate([rates_here[...], blank, ids_here[...].astype(jnp.float32)], 1)
    rows[...] = jnp.broadcast_to(row, rows.shape)
    done = pltpu.make_async_copy(rows, out_ref, sems.at[2])
    done.start()
    done.wait()


def turn_kernel(k_ref, v_ref, turned, filled):
    tokens, width = k_ref.shape
    filled[:tokens, :] = v_ref[...]
    filled[tokens:, :] = jnp.zeros((LANES - tokens, width), filled.dtype)
    blank = jnp.zeros((LANES - tokens, LANES), jnp.float32)
    for j in range(width // LANES):
        columns = slice(j * LANES, (j + 1) * LANES)
        block = jnp.concatenate([k_ref[:, columns].astype(jnp.float32), blank], 0)
        turned[columns, :] = jnp.transpose(block).astype(turned.dtype)


def own_ids(stored, tokens):
    members = stored.shape[0]
    at = lax.rem(lax.axis_index("uly") + members // 2, members)
    row = stored[pl.ds(at, 1), :]
    fill = jnp.full((1, LANES - tokens), -1.0, jnp.float32)
    return jnp.concatenate([row[:, LANES - tokens :], fill], 1)


def ends_kernel(here, tokens, group, stored, turned, v_ref, out_ref, made, sems):
    width = v_ref.shape[1]
    members = stored.shape[0]
    lane = lax.broadcasted_iota(jnp.int32, (HD, LANES), 1)
    ids = jnp.broadcast_to(own_ids(stored, tokens), (8, LANES))
    place = lax.broadcasted_iota(jnp.int32, ids.shape, 1)
    last = ids[:, tokens - 1 : tokens]
    age = jnp.where(ids == last, (tokens - 1 - place).astype(jnp.float32), NEVER)
    rows_each = made.shape[0] // group
    parts = sems.shape[0]
    share = made.shape[0] // parts
    copies = []
    for j in range(0, width // LANES, 2):
        weighted = []
        for head in range(2 * j, 2 * j + 4):
            weight = jnp.exp(-rate_of(stored, (head + members // 2 * here) % (members * here), here) * age)
            keys = turned[head * HD : (head + 1) * HD, :].astype(jnp.float32)
            keys = keys.reshape(HD // 8, 8, LANES) * weight[None]
            weighted.append(keys.reshape(HD, LANES))
        weighted = jnp.concatenate(weighted, 0)
        high = weighted.astype(jnp.bfloat16)
        low = (weighted - high.astype(jnp.float32)).astype(jnp.bfloat16)
        v = v_ref[:, j * LANES : (j + 2) * LANES]
        both = jnp.dot(
            jnp.concatenate([high, low], 1),
            jnp.concatenate([v, v], 0),
            preferred_element_type=jnp.float32,
        )
        for one in (0, 1):
            pair = both[one * LANES : (one + 1) * LANES, one * LANES : (one + 1) * LANES]
            state = jnp.where(lane < HD, pair[:HD], pair[HD:])
            size = min(rows_each, HD)
            for at in range(0, HD, size):
                owner, start = divmod((j + one) * HD + at, rows_each)
                start += (group - 1 - owner) * rows_each
                made[start : start + size, :] = state[at : at + size].astype(jnp.bfloat16)
        if (j + 2) * HD % share == 0:
            part = parts - (j + 2) * HD // share
            rows = slice(part * share, (part + 1) * share)
            copies.append(pltpu.make_async_copy(made.at[rows], out_ref.at[rows], sems.at[part]))
            copies[-1].start()
    for copy in copies:
        copy.wait()


def inner_kernel(
    here, facts, idcol, idrow, q_ref, turned, v_ref, after, out_ref, rates_ref
):
    tokens, width = q_ref.shape
    lane = lax.broadcasted_iota(jnp.int32, (tokens, LANES), 1)
    t = lax.broadcasted_iota(jnp.int32, (tokens, LANES), 0)
    seen = (t >= lane) & (idcol[...] == idrow[:1, :])
    age = jnp.where(seen, (t - lane).astype(jnp.float32), NEVER)
    for j in range(width // LANES):
        columns = slice(j * LANES, (j + 1) * LANES)
        q = q_ref[:, columns]
        zero = jnp.zeros_like(q)
        stacked = jnp.concatenate([jnp.where(lane < HD, q, zero), jnp.where(lane < HD, zero, q)], 0)
        scores = jnp.dot(
            stacked, turned[columns, :], preferred_element_type=jnp.float32
        )
        rates = [rate_of(facts, 2 * j + one, here) for one in (0, 1)]
        weight = jnp.concatenate([jnp.exp(-rate * age) for rate in rates], 0)
        probs = (scores * weight)[:, :tokens].astype(jnp.bfloat16)
        got = jnp.dot(probs, v_ref[:, columns], preferred_element_type=jnp.float32)
        out_ref[:, columns] = jnp.where(lane < HD, got[:tokens], got[tokens:])
        rates_ref[:, columns] = jnp.where(lane[:1] < HD, rates[0], rates[1])


def pass_kernel(stored, after, facts, idrow, idcol):
    members, tokens = stored.shape[0], idcol.shape[0]
    for u in range(members):
        at = (u + members // 2) % members
        facts[u : u + 1, :] = stored[at : at + 1, :]
    row = own_ids(stored, tokens)
    idrow[...] = jnp.broadcast_to(row, idrow.shape)
    idcol[...] = jnp.transpose(jnp.broadcast_to(row, (LANES, LANES)))[:tokens]


def few(count):
    return count if count <= 8 else 1


def link_kernel(here, tokens, chunks, facts, *refs):
    others, (linked, through, one, half, before, last) = refs[:-6], refs[-6:]
    members, slices = facts.shape[0], len(others) + 1
    ctx, uly = lax.axis_index("ctx"), lax.axis_index("uly")
    for back, tile in enumerate((facts, *others)):
        at = lax.rem(ctx + slices - back, slices) * members
        last[pl.ds(pl.multiple_of(at, members), members), :] = jnp.broadcast_to(
            tile[:, LANES - 1 :], (members, LANES)
        )
    me = ctx * members + uly
    now = last[...]
    then = jnp.concatenate([now[:1], now[:-1]], 0)
    end = jnp.concatenate([now[chunks - 1 :], now[: chunks - 1]], 0)
    linked[...] = jnp.where(now == then, 1.0, 0.0)
    through[...] = jnp.where(end == then, 1.0, 0.0)
    before[...] = jnp.where(me > 0, last[pl.ds(jnp.maximum(me - 1, 0), 1), :], -1.0)
    rows = one.shape[0]
    share = min(rows, HD)
    owner = ctx * chunks + lax.rem(uly, chunks)
    for at in range(0, rows, share):
        rate = pair_rate(facts, lax.div(owner * rows + at, HD), here)
        for ref, length in ((one, tokens), (half, tokens * chunks)):
            ref[at : at + share, :] = jnp.broadcast_to(
                jnp.exp(-rate * float(length)), (share, LANES)
            )


def half_kernel(chunks, linked, one, in_ref, early_ref, final_ref):
    slices, newest = early_ref.shape[0] + 1, in_ref.shape[0] - 1
    offset = jnp.where(lax.axis_index("uly") >= chunks, chunks, 0)

    def slice_end(c):
        def step(j, state):
            keep = linked[pl.ds(c * 2 * chunks + offset + j, 1), :] * one[...]
            return in_ref[newest - c * chunks - j].astype(jnp.float32) + keep * state

        begin = in_ref[newest - c * chunks].astype(jnp.float32)
        state = lax.fori_loop(1, chunks, step, begin, unroll=few(chunks - 1))
        return state.astype(early_ref.dtype)

    def early(c, _):
        early_ref[c] = slice_end(c)
        return 0

    lax.fori_loop(0, slices - 1, early, 0, unroll=few(slices - 1))
    final_ref[0] = slice_end(slices - 1)


def scan_kernel(
    chunks, linked, through, one, half, in_ref, early, final, after, out_ref
):
    slices, newest = early.shape[0] + 1, in_ref.shape[0] - 1
    later = lax.axis_index("uly") >= chunks
    offset = jnp.where(later, chunks, 0)

    def over_other(state, c, piece, wanted):
        keep = through[pl.ds(c * 2 * chunks + chunks - offset, 1), :] * half[...]
        return jnp.where(wanted, piece.astype(jnp.float32) + keep * state, state)

    def over_own(state, c):
        def step(j, state):
            at = c * chunks + j
            out_ref[at] = state.astype(out_ref.dtype)
            keep = linked[pl.ds(c * 2 * chunks + offset + j, 1), :] * one[...]
            return in_ref[newest - at].astype(jnp.float32) + keep * state

        return lax.fori_loop(0, chunks, step, state, unroll=few(chunks))

    def over_slice(c, state):
        state = over_own(over_other(state, c, early[c], later), c)
        return over_other(state, c, early[c], jnp.logical_not(later))

    begin = jnp.zeros(in_ref.shape[1:], jnp.float32)
    state = lax.fori_loop(0, slices - 1, over_slice, begin, unroll=few(slices - 1))
    over_own(over_other(state, slices - 1, final[0], later), slices - 1)


def norm_kernel(idcol, before, rates, q_ref, s_ref, inner_ref, gain, out_ref, raw, done, sems):
    tokens, width = q_ref.shape
    lane = lax.broadcasted_iota(jnp.int32, (HD, LANES), 1)
    place = lax.broadcasted_iota(jnp.int32, (tokens, LANES), 0)
    age = jnp.where(idcol[...] == before[...], (place + 1).astype(jnp.float32), NEVER)
    zero = jnp.zeros((HD, LANES), s_ref.dtype)
    total = jnp.zeros((tokens, LANES), jnp.float32)
    for j in range(0, width // LANES, 2):
        square = []
        for one in (0, 1):
            state = s_ref[(j + one) * HD : (j + one + 1) * HD, :]
            for half in (jnp.where(lane < HD, state, zero), jnp.where(lane < HD, zero, state)):
                square.append(jnp.concatenate([zero, half] if one else [half, zero], 1))
        columns = slice(j * LANES, (j + 2) * LANES)
        outer = jnp.dot(
            q_ref[:, columns], jnp.concatenate(square, 0), preferred_element_type=jnp.float32
        )
        for one in (0, 1):
            columns = slice((j + one) * LANES, (j + one + 1) * LANES)
            fade = jnp.exp(-rates[:, columns] * age)
            value = inner_ref[:, columns] + outer[:, one * LANES : (one + 1) * LANES] * fade
            total += value * value
            raw[:, columns] = value
    mean = jnp.sum(total, axis=1, keepdims=True) / float(width)
    scale = jnp.broadcast_to(lax.rsqrt(mean + 1e-06), (tokens, LANES))
    parts = sems.shape[0]
    share = tokens // parts
    copies = []
    for part in range(parts):
        rows = slice(part * share, (part + 1) * share)
        for at in range(0, width, LANES):
            columns = slice(at, at + LANES)
            done[rows, columns] = (raw[rows, columns] * scale[rows] * gain[:, columns]).astype(
                jnp.bfloat16
            )
        copies.append(pltpu.make_async_copy(done.at[rows], out_ref.at[rows], sems.at[part]))
        copies[-1].start()
    for copy in copies:
        copy.wait()


def local(queries, keys, values, doc_ids, decay_rate, norm_gain):
    tokens, width = queries.shape
    here = decay_rate.shape[0]
    axes = ("ctx", "uly")
    slices, members = lax.axis_size("ctx"), lax.axis_size("uly")
    count = slices * members
    all_pairs = width // LANES
    chunks = members // 2
    group = slices * chunks
    rows = all_pairs * HD // group
    groups = [
        [c * members + half * chunks + u for c in range(slices) for u in range(chunks)]
        for half in (0, 1)
    ]
    swap = [
        (c * members + u, c * members + (u + chunks) % members)
        for c in range(slices)
        for u in range(members)
    ]

    vmem = pl.BlockSpec(memory_space=pltpu.VMEM)
    params = pltpu.CompilerParams(vmem_limit_bytes=32 * 1024 * 1024)
    shape = jax.ShapeDtypeStruct
    tile = shape((members, LANES), jnp.float32)

    own = pl.pallas_call(
        own_kernel,
        in_specs=[pl.BlockSpec(memory_space=pl.ANY)] * 2,
        out_specs=pl.BlockSpec(memory_space=pl.ANY),
        out_shape=tile,
        scratch_shapes=[
            pltpu.VMEM((1, here), jnp.float32),
            pltpu.VMEM((1, tokens), jnp.int32),
            pltpu.VMEM(tile.shape, jnp.float32),
            pltpu.SemaphoreType.DMA((3,)),
        ],
        compiler_params=pltpu.CompilerParams(vmem_limit_bytes=62 * 1024 * 1024),
        name="own",
    )(decay_rate[None, :], doc_ids[None, :])
    turned_round = [[(u + members // 2) % members for u in range(members)]]
    stored = lax.all_to_all(
        own,
        "uly", split_axis=0, concat_axis=0, axis_index_groups=turned_round, tiled=True,
    )
    turned, filled = pl.pallas_call(
        turn_kernel,
        in_specs=[vmem] * 2,
        out_specs=[vmem] * 2,
        out_shape=[shape((width, LANES), jnp.bfloat16), shape((LANES, width), jnp.bfloat16)],
        compiler_params=params,
        cost_estimate=pl.CostEstimate(flops=0, bytes_accessed=12_000_000, transcendentals=0),
        name="turn",
    )(keys, values)
    ends = pl.pallas_call(
        functools.partial(ends_kernel, here, tokens, group),
        in_specs=[vmem] * 3,
        out_specs=pl.BlockSpec(memory_space=pl.ANY),
        out_shape=shape((all_pairs * HD, LANES), jnp.bfloat16),
        scratch_shapes=[
            pltpu.VMEM((all_pairs * HD, LANES), jnp.bfloat16),
            pltpu.SemaphoreType.DMA((8,)),
        ],
        compiler_params=params,
        name="ends",
    )(stored, turned, filled)
    pieces = lax.all_to_all(
        ends.reshape(group, rows, LANES),
        axes, split_axis=0, concat_axis=0, tiled=True,
        axis_index_groups=[members_of[::-1] for members_of in groups],
    )
    facts, idrow, idcol = pl.pallas_call(
        pass_kernel,
        in_specs=[vmem, pl.BlockSpec(memory_space=pl.ANY)],
        out_specs=[vmem] * 3,
        out_shape=[tile, shape((8, LANES), jnp.float32), shape((tokens, LANES), jnp.float32)],
        compiler_params=params,
        name="pass",
    )(stored, ends)
    others = [
        lax.ppermute(facts, "ctx", [(c, (c + ahead) % slices) for c in range(slices)])
        for ahead in range(1, slices)
    ]
    linked, through, one, half, before = pl.pallas_call(
        functools.partial(link_kernel, here, tokens, chunks),
        in_specs=[vmem] * slices,
        out_specs=[vmem] * 5,
        out_shape=[shape((count, LANES), jnp.float32)] * 2
        + [shape((rows, LANES), jnp.float32)] * 2
        + [shape((1, LANES), jnp.float32)],
        scratch_shapes=[pltpu.VMEM((count, LANES), jnp.float32)],
        compiler_params=params,
        name="link",
    )(facts, *others)
    early_ends, final_end = pl.pallas_call(
        functools.partial(half_kernel, chunks),
        in_specs=[vmem] * 3,
        out_specs=[vmem] * 2,
        out_shape=[
            shape((slices - 1, rows, LANES), jnp.bfloat16),
            shape((1, rows, LANES), jnp.bfloat16),
        ],
        compiler_params=params,
        name="half",
    )(linked, one, pieces)
    early = lax.ppermute(early_ends, axes, swap)
    final = lax.ppermute(final_end, axes, [(low, high) for low, high in swap if low < high])
    inner, rates = pl.pallas_call(
        functools.partial(inner_kernel, here),
        in_specs=[vmem] * 6 + [pl.BlockSpec(memory_space=pl.ANY)],
        out_specs=[vmem] * 2,
        out_shape=[shape((tokens, width), jnp.float32), shape((1, width), jnp.float32)],
        compiler_params=params,
        cost_estimate=pl.CostEstimate(
            flops=8_000_000_000, bytes_accessed=4_000_000, transcendentals=600_000
        ),
        name="inner",
    )(facts, idcol, idrow, queries, turned, values, early_ends)
    moved = pl.pallas_call(
        functools.partial(scan_kernel, chunks),
        in_specs=[vmem] * 7 + [pl.BlockSpec(memory_space=pl.ANY)],
        out_specs=vmem,
        out_shape=shape((group, rows, LANES), jnp.bfloat16),
        compiler_params=params,
        name="scan",
    )(linked, through, one, half, pieces, early, final, rates)
    states = lax.all_to_all(
        moved, axes, split_axis=0, concat_axis=0, axis_index_groups=groups, tiled=True
    )
    return pl.pallas_call(
        norm_kernel,
        in_specs=[vmem] * 7,
        out_specs=pl.BlockSpec(memory_space=pl.ANY),
        out_shape=shape((tokens, width), jnp.bfloat16),
        scratch_shapes=[
            pltpu.VMEM((tokens, width), jnp.float32),
            pltpu.VMEM((tokens, width), jnp.bfloat16),
            pltpu.SemaphoreType.DMA((tokens // 16,)),
        ],
        compiler_params=params,
        name="norm",
    )(idcol, before, rates, queries, states.reshape(all_pairs * HD, LANES), inner, norm_gain[None, :])


def solution(mesh):
    in_specs = (
        P(("ctx", "uly"), None),
        P(("ctx", "uly"), None),
        P(("ctx", "uly"), None),
        P(("ctx", "uly")),
        P("uly"),
        P(),
    )
    out_specs = P(("ctx", "uly"), None)
    return jax.shard_map(local, mesh=mesh, in_specs=in_specs, out_specs=out_specs, check_vma=False)
```

```python
import functools

import jax
import jax.numpy as jnp
from jax import lax
from jax.experimental import pallas as pl
from jax.experimental.pallas import tpu as pltpu
from jax.sharding import PartitionSpec as P

HD = 64
LANES = 2 * HD
NEVER = 1e9
MARK = 8


def rate_of(facts, head, here):
    return facts[head // here : head // here + 1, head % here : head % here + 1]


def pair_rate(stored, pair, here):
    members = stored.shape[0]
    lane = lax.broadcasted_iota(jnp.int32, (1, LANES), 1)
    rates = []
    for head in (2 * pair, 2 * pair + 1):
        at = lax.rem(lax.div(head, here) + members // 2, members)
        row = stored[pl.ds(at, 1), :]
        rates.append(
            jnp.sum(jnp.where(lane == lax.rem(head, here), row, 0.0), axis=1, keepdims=True)
        )
    return jnp.where(lane < HD, rates[0], rates[1])


def own_ids(stored, tokens):
    members = stored.shape[0]
    at = lax.rem(lax.axis_index("uly") + members // 2, members)
    row = stored[pl.ds(at, 1), :]
    fill = jnp.full((1, LANES - tokens), -1.0, jnp.float32)
    return jnp.concatenate([row[:, LANES - tokens :], fill], 1)


def turn_kernel(k_ref, v_ref, turned, filled):
    tokens, width = k_ref.shape
    filled[:tokens, :] = v_ref[...]
    filled[tokens:, :] = jnp.zeros((LANES - tokens, width), filled.dtype)
    blank = jnp.zeros((LANES - tokens, LANES), jnp.float32)
    for j in range(width // LANES):
        columns = slice(j * LANES, (j + 1) * LANES)
        block = jnp.concatenate([k_ref[:, columns].astype(jnp.float32), blank], 0)
        turned[columns, :] = jnp.transpose(block).astype(turned.dtype)


def ends_kernel(here, tokens, stored, turned, v_ref, out_ref):
    width = v_ref.shape[1]
    members = stored.shape[0]
    group, rows = out_ref.shape[0], out_ref.shape[1] - MARK
    lane = lax.broadcasted_iota(jnp.int32, (HD, LANES), 1)
    ids = jnp.broadcast_to(own_ids(stored, tokens), (8, LANES))
    place = lax.broadcasted_iota(jnp.int32, ids.shape, 1)
    last = ids[:, tokens - 1 : tokens]
    age = jnp.where(ids == last, (tokens - 1 - place).astype(jnp.float32), NEVER)
    mark = jnp.broadcast_to(last[:1], (MARK, LANES)).astype(jnp.bfloat16)
    for owner in range(group):
        out_ref[owner, rows:, :] = mark
    for j in range(0, width // LANES, 2):
        weighted = []
        for head in range(2 * j, 2 * j + 4):
            weight = jnp.exp(-rate_of(stored, (head + members // 2 * here) % (members * here), here) * age)
            keys = turned[head * HD : (head + 1) * HD, :].astype(jnp.float32)
            keys = keys.reshape(HD // 8, 8, LANES) * weight[None]
            weighted.append(keys.reshape(HD, LANES))
        weighted = jnp.concatenate(weighted, 0)
        high = weighted.astype(jnp.bfloat16)
        low = (weighted - high.astype(jnp.float32)).astype(jnp.bfloat16)
        v = v_ref[:, j * LANES : (j + 2) * LANES]
        both = jnp.dot(
            jnp.concatenate([high, low], 1),
            jnp.concatenate([v, v], 0),
            preferred_element_type=jnp.float32,
        )
        for one in (0, 1):
            pair = both[one * LANES : (one + 1) * LANES, one * LANES : (one + 1) * LANES]
            state = jnp.where(lane < HD, pair[:HD], pair[HD:])
            size = min(rows, HD)
            for at in range(0, HD, size):
                owner, start = divmod((j + one) * HD + at, rows)
                out_ref[group - 1 - owner, start : start + size, :] = state[at : at + size].astype(
                    jnp.bfloat16
                )


def inner_kernel(here, stored, q_ref, turned, v_ref, after, out_ref, rates_ref, idcol):
    tokens, width = q_ref.shape
    members = stored.shape[0]
    row = own_ids(stored, tokens)
    column = jnp.transpose(jnp.broadcast_to(row, (LANES, LANES)))[:tokens]
    idcol[...] = column
    lane = lax.broadcasted_iota(jnp.int32, (tokens, LANES), 1)
    t = lax.broadcasted_iota(jnp.int32, (tokens, LANES), 0)
    seen = (t >= lane) & (column == row)
    age = jnp.where(seen, (t - lane).astype(jnp.float32), NEVER)
    for j in range(width // LANES):
        columns = slice(j * LANES, (j + 1) * LANES)
        q = q_ref[:, columns]
        zero = jnp.zeros_like(q)
        stacked = jnp.concatenate([jnp.where(lane < HD, q, zero), jnp.where(lane < HD, zero, q)], 0)
        scores = jnp.dot(
            stacked, turned[columns, :], preferred_element_type=jnp.float32
        )
        rates = [
            rate_of(stored, (2 * j + one + members // 2 * here) % (members * here), here)
            for one in (0, 1)
        ]
        weight = jnp.concatenate([jnp.exp(-rate * age) for rate in rates], 0)
        probs = (scores * weight)[:, :tokens].astype(jnp.bfloat16)
        got = jnp.dot(probs, v_ref[:, columns], preferred_element_type=jnp.float32)
        out_ref[:, columns] = jnp.where(lane < HD, got[:tokens], got[tokens:])
        rates_ref[:, columns] = jnp.where(lane[:1] < HD, rates[0], rates[1])


def few(count):
    return count if count <= 8 else 1


def split(piece, rows):
    return piece[:rows].astype(jnp.float32), piece[rows : rows + 1].astype(jnp.float32)


def half_kernel(here, tokens, chunks, stored, in_ref, early_ref, final_ref, one, half, mine):
    slices, newest = early_ref.shape[0] + 1, in_ref.shape[0] - 1
    rows = one.shape[0]
    owner = lax.axis_index("ctx") * chunks + lax.rem(lax.axis_index("uly"), chunks)
    share = min(rows, HD)
    for at in range(0, rows, share):
        rate = pair_rate(stored, lax.div(owner * rows + at, HD), here)
        for ref, length in ((one, tokens), (half, tokens * chunks)):
            ref[at : at + share, :] = jnp.broadcast_to(
                jnp.exp(-rate * float(length)), (share, LANES)
            )
    last = own_ids(stored, tokens)[:, tokens - 1 : tokens]
    mine[...] = jnp.broadcast_to(last, mine.shape)

    def slice_end(c, ref, at):
        def step(j, carry):
            state, last = carry
            fresh, own = split(in_ref[newest - c * chunks - j], rows)
            return fresh + jnp.where(own == last, one[...], 0.0) * state, own

        begin = split(in_ref[newest - c * chunks], rows)
        state, _ = lax.fori_loop(1, chunks, step, begin, unroll=few(chunks - 1))
        ref[at, :rows, :] = state.astype(ref.dtype)
        ref[at, rows:, :] = in_ref[newest - c * chunks - chunks + 1][rows:]

    def early(c, _):
        slice_end(c, early_ref, c)
        return 0

    lax.fori_loop(0, slices - 1, early, 0, unroll=few(slices - 1))
    slice_end(slices - 1, final_ref, 0)


def scan_kernel(chunks, one, half, in_ref, early, final, after, out_ref):
    slices, newest = early.shape[0] + 1, in_ref.shape[0] - 1
    rows = one.shape[0]
    later = lax.axis_index("uly") >= chunks

    def over_other(carry, piece, wanted):
        state, last = carry
        fresh, own = split(piece, rows)
        moved = fresh + jnp.where(own == last, half[...], 0.0) * state
        return jnp.where(wanted, moved, state), jnp.where(wanted, own, last)

    def over_own(carry, c):
        def step(j, carry):
            state, last = carry
            at = c * chunks + j
            out_ref[at] = state.astype(out_ref.dtype)
            fresh, own = split(in_ref[newest - at], rows)
            return fresh + jnp.where(own == last, one[...], 0.0) * state, own

        return lax.fori_loop(0, chunks, step, carry, unroll=few(chunks))

    def over_slice(c, carry):
        carry = over_own(over_other(carry, early[c], later), c)
        return over_other(carry, early[c], jnp.logical_not(later))

    begin = (jnp.zeros((rows, LANES), jnp.float32), jnp.full((1, LANES), -1.0, jnp.float32))
    carry = lax.fori_loop(0, slices - 1, over_slice, begin, unroll=few(slices - 1))
    over_own(over_other(carry, final[0], later), slices - 1)


def norm_kernel(idcol, stored, earlier, rates, q_ref, s_ref, inner_ref, gain, out_ref, raw, done, sems):
    tokens, width = q_ref.shape
    lane = lax.broadcasted_iota(jnp.int32, (HD, LANES), 1)
    place = lax.broadcasted_iota(jnp.int32, (tokens, LANES), 0)
    ctx, uly = lax.axis_index("ctx"), lax.axis_index("uly")
    members = stored.shape[0]
    at = lax.rem(uly + members - 1 + members // 2, members)
    before = jnp.where(uly > 0, stored[pl.ds(at, 1), LANES - 1 :], earlier[:1, :1])
    before = jnp.where(ctx + uly > 0, before, -1.0)
    age = jnp.where(idcol[...] == before, (place + 1).astype(jnp.float32), NEVER)
    zero = jnp.zeros((HD, LANES), s_ref.dtype)
    total = jnp.zeros((tokens, LANES), jnp.float32)
    for j in range(0, width // LANES, 2):
        square = []
        for one in (0, 1):
            state = s_ref[(j + one) * HD : (j + one + 1) * HD, :]
            for half in (jnp.where(lane < HD, state, zero), jnp.where(lane < HD, zero, state)):
                square.append(jnp.concatenate([zero, half] if one else [half, zero], 1))
        columns = slice(j * LANES, (j + 2) * LANES)
        outer = jnp.dot(
            q_ref[:, columns], jnp.concatenate(square, 0), preferred_element_type=jnp.float32
        )
        for one in (0, 1):
            columns = slice((j + one) * LANES, (j + one + 1) * LANES)
            fade = jnp.exp(-rates[:, columns] * age)
            value = inner_ref[:, columns] + outer[:, one * LANES : (one + 1) * LANES] * fade
            total += value * value
            raw[:, columns] = value
    mean = jnp.sum(total, axis=1, keepdims=True) / float(width)
    scale = jnp.broadcast_to(lax.rsqrt(mean + 1e-06), (tokens, LANES))
    parts = sems.shape[0]
    share = tokens // parts
    copies = []
    for part in range(parts):
        rows = slice(part * share, (part + 1) * share)
        for at in range(0, width, LANES):
            columns = slice(at, at + LANES)
            done[rows, columns] = (raw[rows, columns] * scale[rows] * gain[:, columns]).astype(
                jnp.bfloat16
            )
        copies.append(pltpu.make_async_copy(done.at[rows], out_ref.at[rows], sems.at[part]))
        copies[-1].start()
    for copy in copies:
        copy.wait()


def local(queries, keys, values, doc_ids, decay_rate, norm_gain):
    tokens, width = queries.shape
    here = decay_rate.shape[0]
    axes = ("ctx", "uly")
    slices, members = lax.axis_size("ctx"), lax.axis_size("uly")
    count = slices * members
    all_pairs = width // LANES
    chunks = members // 2
    group = slices * chunks
    rows = all_pairs * HD // group
    groups = [
        [c * members + half * chunks + u for c in range(slices) for u in range(chunks)]
        for half in (0, 1)
    ]
    swap = [
        (c * members + u, c * members + (u + chunks) % members)
        for c in range(slices)
        for u in range(members)
    ]

    vmem = pl.BlockSpec(memory_space=pltpu.VMEM)
    params = pltpu.CompilerParams(vmem_limit_bytes=32 * 1024 * 1024)
    shape = jax.ShapeDtypeStruct
    tile = shape((members, LANES), jnp.float32)

    own = jnp.pad(decay_rate, (0, LANES - here)) + jnp.pad(
        doc_ids, (LANES - tokens, 0)
    ).astype(jnp.float32)
    turned_round = [[(u + members // 2) % members for u in range(members)]]
    stored = lax.all_to_all(
        jnp.broadcast_to(own[None, :], tile.shape),
        "uly", split_axis=0, concat_axis=0, axis_index_groups=turned_round, tiled=True,
    )
    turned, filled = pl.pallas_call(
        turn_kernel,
        in_specs=[vmem] * 2,
        out_specs=[vmem] * 2,
        out_shape=[shape((width, LANES), jnp.bfloat16), shape((LANES, width), jnp.bfloat16)],
        compiler_params=params,
        cost_estimate=pl.CostEstimate(flops=0, bytes_accessed=12_000_000, transcendentals=0),
        name="turn",
    )(keys, values)
    ends = pl.pallas_call(
        functools.partial(ends_kernel, here, tokens),
        in_specs=[vmem] * 3,
        out_specs=vmem,
        out_shape=shape((group, rows + MARK, LANES), jnp.bfloat16),
        compiler_params=params,
        name="ends",
    )(stored, turned, filled)
    pieces = lax.all_to_all(
        ends,
        axes, split_axis=0, concat_axis=0, tiled=True,
        axis_index_groups=[members_of[::-1] for members_of in groups],
    )
    early_ends, final_end, one, half, mine = pl.pallas_call(
        functools.partial(half_kernel, here, tokens, chunks),
        in_specs=[vmem] * 2,
        out_specs=[vmem] * 5,
        out_shape=[
            shape((slices - 1, rows + MARK, LANES), jnp.bfloat16),
            shape((1, rows + MARK, LANES), jnp.bfloat16),
            shape((rows, LANES), jnp.float32),
            shape((rows, LANES), jnp.float32),
            shape((8, LANES), jnp.float32),
        ],
        compiler_params=params,
        name="half",
    )(stored, pieces)
    early = lax.ppermute(early_ends, axes, swap)
    final = lax.ppermute(final_end, axes, [(low, high) for low, high in swap if low < high])
    earlier = lax.ppermute(
        mine, axes, [(c * members - 1, c * members) for c in range(1, slices)]
    )
    inner, rates, idcol = pl.pallas_call(
        functools.partial(inner_kernel, here),
        in_specs=[vmem] * 4 + [pl.BlockSpec(memory_space=pl.ANY)],
        out_specs=[vmem] * 3,
        out_shape=[
            shape((tokens, width), jnp.float32),
            shape((1, width), jnp.float32),
            shape((tokens, LANES), jnp.float32),
        ],
        compiler_params=params,
        cost_estimate=pl.CostEstimate(
            flops=8_000_000_000, bytes_accessed=4_000_000, transcendentals=600_000
        ),
        name="inner",
    )(stored, queries, turned, values, early_ends)
    moved = pl.pallas_call(
        functools.partial(scan_kernel, chunks),
        in_specs=[vmem] * 5 + [pl.BlockSpec(memory_space=pl.ANY)],
        out_specs=vmem,
        out_shape=shape((group, rows, LANES), jnp.bfloat16),
        compiler_params=params,
        name="scan",
    )(one, half, pieces, early, final, rates)
    states = lax.all_to_all(
        moved, axes, split_axis=0, concat_axis=0, axis_index_groups=groups, tiled=True
    )
    return pl.pallas_call(
        norm_kernel,
        in_specs=[vmem] * 8,
        out_specs=pl.BlockSpec(memory_space=pl.ANY),
        out_shape=shape((tokens, width), jnp.bfloat16),
        scratch_shapes=[
            pltpu.VMEM((tokens, width), jnp.float32),
            pltpu.VMEM((tokens, width), jnp.bfloat16),
            pltpu.SemaphoreType.DMA((tokens // 16,)),
        ],
        compiler_params=params,
        name="norm",
    )(idcol, stored, earlier, rates, queries, states.reshape(all_pairs * HD, LANES), inner, norm_gain[None, :])


def solution(mesh):
    in_specs = (
        P(("ctx", "uly"), None),
        P(("ctx", "uly"), None),
        P(("ctx", "uly"), None),
        P(("ctx", "uly")),
        P("uly"),
        P(),
    )
    out_specs = P(("ctx", "uly"), None)
    return jax.shard_map(local, mesh=mesh, in_specs=in_specs, out_specs=out_specs, check_vma=False)
```

```python
import functools

import jax
import jax.numpy as jnp
from jax import lax
from jax.experimental import pallas as pl
from jax.experimental.pallas import tpu as pltpu
from jax.sharding import PartitionSpec as P

HD = 64
LANES = 2 * HD
NEVER = 1e9
MARK = 8


def rate_of(facts, head, here):
    return facts[head // here : head // here + 1, head % here : head % here + 1]


def pair_rate(stored, pair, here):
    members = stored.shape[0]
    lane = lax.broadcasted_iota(jnp.int32, (1, LANES), 1)
    rates = []
    for head in (2 * pair, 2 * pair + 1):
        at = lax.rem(lax.div(head, here) + members // 2, members)
        row = stored[pl.ds(at, 1), :]
        rates.append(
            jnp.sum(jnp.where(lane == lax.rem(head, here), row, 0.0), axis=1, keepdims=True)
        )
    return jnp.where(lane < HD, rates[0], rates[1])


def own_ids(stored, tokens):
    members = stored.shape[0]
    at = lax.rem(lax.axis_index("uly") + members // 2, members)
    row = stored[pl.ds(at, 1), :]
    fill = jnp.full((1, LANES - tokens), -1.0, jnp.float32)
    return jnp.concatenate([row[:, LANES - tokens :], fill], 1)


def turn_kernel(k_ref, v_ref, turned, filled):
    tokens, width = k_ref.shape
    filled[:tokens, :] = v_ref[...]
    filled[tokens:, :] = jnp.zeros((LANES - tokens, width), filled.dtype)
    blank = jnp.zeros((LANES - tokens, LANES), jnp.float32)
    for j in range(width // LANES):
        columns = slice(j * LANES, (j + 1) * LANES)
        block = jnp.concatenate([k_ref[:, columns].astype(jnp.float32), blank], 0)
        turned[columns, :] = jnp.transpose(block).astype(turned.dtype)


def ends_kernel(here, tokens, stored, turned, v_ref, out_ref):
    width = v_ref.shape[1]
    members = stored.shape[0]
    group, rows = out_ref.shape[0], out_ref.shape[1] - MARK
    lane = lax.broadcasted_iota(jnp.int32, (HD, LANES), 1)
    ids = jnp.broadcast_to(own_ids(stored, tokens), (8, LANES))
    place = lax.broadcasted_iota(jnp.int32, ids.shape, 1)
    last = ids[:, tokens - 1 : tokens]
    age = jnp.where(ids == last, (tokens - 1 - place).astype(jnp.float32), NEVER)
    mark = jnp.broadcast_to(last[:1], (MARK, LANES)).astype(jnp.bfloat16)
    for owner in range(group):
        out_ref[owner, rows:, :] = mark
    for j in range(0, width // LANES, 2):
        weighted = []
        for head in range(2 * j, 2 * j + 4):
            weight = jnp.exp(-rate_of(stored, (head + members // 2 * here) % (members * here), here) * age)
            keys = turned[head * HD : (head + 1) * HD, :].astype(jnp.float32)
            keys = keys.reshape(HD // 8, 8, LANES) * weight[None]
            weighted.append(keys.reshape(HD, LANES))
        weighted = jnp.concatenate(weighted, 0)
        high = weighted.astype(jnp.bfloat16)
        low = (weighted - high.astype(jnp.float32)).astype(jnp.bfloat16)
        v = v_ref[:, j * LANES : (j + 2) * LANES]
        both = jnp.dot(
            jnp.concatenate([high, low], 1),
            jnp.concatenate([v, v], 0),
            preferred_element_type=jnp.float32,
        )
        for one in (0, 1):
            pair = both[one * LANES : (one + 1) * LANES, one * LANES : (one + 1) * LANES]
            state = jnp.where(lane < HD, pair[:HD], pair[HD:])
            size = min(rows, HD)
            for at in range(0, HD, size):
                owner, start = divmod((j + one) * HD + at, rows)
                out_ref[group - 1 - owner, start : start + size, :] = state[at : at + size].astype(
                    jnp.bfloat16
                )


def inner_kernel(here, stored, q_ref, turned, v_ref, after, out_ref, rates_ref, idcol):
    tokens, width = q_ref.shape
    members = stored.shape[0]
    row = own_ids(stored, tokens)
    column = jnp.transpose(jnp.broadcast_to(row, (LANES, LANES)))[:tokens]
    idcol[...] = column
    lane = lax.broadcasted_iota(jnp.int32, (tokens, LANES), 1)
    t = lax.broadcasted_iota(jnp.int32, (tokens, LANES), 0)
    seen = (t >= lane) & (column == row)
    age = jnp.where(seen, (t - lane).astype(jnp.float32), NEVER)
    for j in range(width // LANES):
        columns = slice(j * LANES, (j + 1) * LANES)
        q = q_ref[:, columns]
        zero = jnp.zeros_like(q)
        stacked = jnp.concatenate([jnp.where(lane < HD, q, zero), jnp.where(lane < HD, zero, q)], 0)
        scores = jnp.dot(
            stacked, turned[columns, :], preferred_element_type=jnp.float32
        )
        rates = [
            rate_of(stored, (2 * j + one + members // 2 * here) % (members * here), here)
            for one in (0, 1)
        ]
        weight = jnp.concatenate([jnp.exp(-rate * age) for rate in rates], 0)
        probs = (scores * weight)[:, :tokens].astype(jnp.bfloat16)
        got = jnp.dot(probs, v_ref[:, columns], preferred_element_type=jnp.float32)
        out_ref[:, columns] = jnp.where(lane < HD, got[:tokens], got[tokens:])
        rates_ref[:, columns] = jnp.where(lane[:1] < HD, rates[0], rates[1])


def few(count):
    return count if count <= 8 else 1


def split(piece, rows):
    return piece[:rows].astype(jnp.float32), piece[rows : rows + 1].astype(jnp.float32)


def half_kernel(here, tokens, chunks, stored, in_ref, early_ref, final_ref, one, half, mine):
    slices, newest = early_ref.shape[0] + 1, in_ref.shape[0] - 1
    rows = one.shape[0]
    owner = lax.axis_index("ctx") * chunks + lax.rem(lax.axis_index("uly"), chunks)
    share = min(rows, HD)
    for at in range(0, rows, share):
        rate = pair_rate(stored, lax.div(owner * rows + at, HD), here)
        for ref, length in ((one, tokens), (half, tokens * chunks)):
            ref[at : at + share, :] = jnp.broadcast_to(
                jnp.exp(-rate * float(length)), (share, LANES)
            )
    last = own_ids(stored, tokens)[:, tokens - 1 : tokens]
    mine[...] = jnp.broadcast_to(last, mine.shape)

    def slice_end(c, ref, at):
        def step(j, carry):
            state, last = carry
            fresh, own = split(in_ref[newest - c * chunks - j], rows)
            return fresh + jnp.where(own == last, one[...], 0.0) * state, own

        begin = split(in_ref[newest - c * chunks], rows)
        state, _ = lax.fori_loop(1, chunks, step, begin, unroll=few(chunks - 1))
        ref[at, :rows, :] = state.astype(ref.dtype)
        ref[at, rows:, :] = in_ref[newest - c * chunks - chunks + 1][rows:]

    def early(c, _):
        slice_end(c, early_ref, c)
        return 0

    lax.fori_loop(0, slices - 1, early, 0, unroll=few(slices - 1))
    slice_end(slices - 1, final_ref, 0)


def scan_kernel(chunks, one, half, in_ref, early, final, after, earlier, out_ref):
    slices, newest = early.shape[0] + 1, in_ref.shape[0] - 1
    rows = one.shape[0]
    later = lax.axis_index("uly") >= chunks

    def over_other(carry, piece, wanted):
        state, last = carry
        fresh, own = split(piece, rows)
        moved = fresh + jnp.where(own == last, half[...], 0.0) * state
        return jnp.where(wanted, moved, state), jnp.where(wanted, own, last)

    def over_own(carry, c):
        def step(j, carry):
            state, last = carry
            at = c * chunks + j
            out_ref[at] = state.astype(out_ref.dtype)
            fresh, own = split(in_ref[newest - at], rows)
            return fresh + jnp.where(own == last, one[...], 0.0) * state, own

        return lax.fori_loop(0, chunks, step, carry, unroll=few(chunks))

    def over_slice(c, carry):
        carry = over_own(over_other(carry, early[c], later), c)
        return over_other(carry, early[c], jnp.logical_not(later))

    begin = (jnp.zeros((rows, LANES), jnp.float32), jnp.full((1, LANES), -1.0, jnp.float32))
    carry = lax.fori_loop(0, slices - 1, over_slice, begin, unroll=few(slices - 1))
    over_own(over_other(carry, final[0], later), slices - 1)


def norm_kernel(idcol, stored, earlier, rates, q_ref, s_ref, inner_ref, gain, out_ref, raw, done, sems):
    tokens, width = q_ref.shape
    lane = lax.broadcasted_iota(jnp.int32, (HD, LANES), 1)
    place = lax.broadcasted_iota(jnp.int32, (tokens, LANES), 0)
    ctx, uly = lax.axis_index("ctx"), lax.axis_index("uly")
    members = stored.shape[0]
    at = lax.rem(uly + members - 1 + members // 2, members)
    before = jnp.where(uly > 0, stored[pl.ds(at, 1), LANES - 1 :], earlier[:1, :1])
    before = jnp.where(ctx + uly > 0, before, -1.0)
    age = jnp.where(idcol[...] == before, (place + 1).astype(jnp.float32), NEVER)
    zero = jnp.zeros((HD, LANES), s_ref.dtype)
    total = jnp.zeros((tokens, LANES), jnp.float32)
    for j in range(0, width // LANES, 2):
        square = []
        for one in (0, 1):
            state = s_ref[(j + one) * HD : (j + one + 1) * HD, :]
            for half in (jnp.where(lane < HD, state, zero), jnp.where(lane < HD, zero, state)):
                square.append(jnp.concatenate([zero, half] if one else [half, zero], 1))
        columns = slice(j * LANES, (j + 2) * LANES)
        outer = jnp.dot(
            q_ref[:, columns], jnp.concatenate(square, 0), preferred_element_type=jnp.float32
        )
        for one in (0, 1):
            columns = slice((j + one) * LANES, (j + one + 1) * LANES)
            fade = jnp.exp(-rates[:, columns] * age)
            value = inner_ref[:, columns] + outer[:, one * LANES : (one + 1) * LANES] * fade
            total += value * value
            raw[:, columns] = value
    mean = jnp.sum(total, axis=1, keepdims=True) / float(width)
    scale = jnp.broadcast_to(lax.rsqrt(mean + 1e-06), (tokens, LANES))
    parts = sems.shape[0]
    share = tokens // parts
    copies = []
    for part in range(parts):
        rows = slice(part * share, (part + 1) * share)
        for at in range(0, width, LANES):
            columns = slice(at, at + LANES)
            done[rows, columns] = (raw[rows, columns] * scale[rows] * gain[:, columns]).astype(
                jnp.bfloat16
            )
        copies.append(pltpu.make_async_copy(done.at[rows], out_ref.at[rows], sems.at[part]))
        copies[-1].start()
    for copy in copies:
        copy.wait()


def local(queries, keys, values, doc_ids, decay_rate, norm_gain):
    tokens, width = queries.shape
    here = decay_rate.shape[0]
    axes = ("ctx", "uly")
    slices, members = lax.axis_size("ctx"), lax.axis_size("uly")
    count = slices * members
    all_pairs = width // LANES
    chunks = members // 2
    group = slices * chunks
    rows = all_pairs * HD // group
    groups = [
        [c * members + half * chunks + u for c in range(slices) for u in range(chunks)]
        for half in (0, 1)
    ]
    swap = [
        (c * members + u, c * members + (u + chunks) % members)
        for c in range(slices)
        for u in range(members)
    ]

    vmem = pl.BlockSpec(memory_space=pltpu.VMEM)
    params = pltpu.CompilerParams(vmem_limit_bytes=32 * 1024 * 1024)
    shape = jax.ShapeDtypeStruct
    tile = shape((members, LANES), jnp.float32)

    own = jnp.pad(decay_rate, (0, LANES - here)) + jnp.pad(
        doc_ids, (LANES - tokens, 0)
    ).astype(jnp.float32)
    turned_round = [[(u + members // 2) % members for u in range(members)]]
    stored = lax.all_to_all(
        jnp.broadcast_to(own[None, :], tile.shape),
        "uly", split_axis=0, concat_axis=0, axis_index_groups=turned_round, tiled=True,
    )
    turned, filled = pl.pallas_call(
        turn_kernel,
        in_specs=[vmem] * 2,
        out_specs=[vmem] * 2,
        out_shape=[shape((width, LANES), jnp.bfloat16), shape((LANES, width), jnp.bfloat16)],
        compiler_params=params,
        cost_estimate=pl.CostEstimate(flops=0, bytes_accessed=12_000_000, transcendentals=0),
        name="turn",
    )(keys, values)
    ends = pl.pallas_call(
        functools.partial(ends_kernel, here, tokens),
        in_specs=[vmem] * 3,
        out_specs=vmem,
        out_shape=shape((group, rows + MARK, LANES), jnp.bfloat16),
        compiler_params=params,
        name="ends",
    )(stored, turned, filled)
    pieces = lax.all_to_all(
        ends,
        axes, split_axis=0, concat_axis=0, tiled=True,
        axis_index_groups=[members_of[::-1] for members_of in groups],
    )
    early_ends, final_end, one, half, mine = pl.pallas_call(
        functools.partial(half_kernel, here, tokens, chunks),
        in_specs=[vmem] * 2,
        out_specs=[vmem] * 5,
        out_shape=[
            shape((slices - 1, rows + MARK, LANES), jnp.bfloat16),
            shape((1, rows + MARK, LANES), jnp.bfloat16),
            shape((rows, LANES), jnp.float32),
            shape((rows, LANES), jnp.float32),
            shape((8, LANES), jnp.float32),
        ],
        compiler_params=params,
        name="half",
    )(stored, pieces)
    early = lax.ppermute(early_ends, axes, swap)
    final = lax.ppermute(final_end, axes, [(low, high) for low, high in swap if low < high])
    earlier = lax.ppermute(
        mine, axes, [(c * members - 1, c * members) for c in range(1, slices)]
    )
    inner, rates, idcol = pl.pallas_call(
        functools.partial(inner_kernel, here),
        in_specs=[vmem] * 4 + [pl.BlockSpec(memory_space=pl.ANY)],
        out_specs=[vmem] * 3,
        out_shape=[
            shape((tokens, width), jnp.float32),
            shape((1, width), jnp.float32),
            shape((tokens, LANES), jnp.float32),
        ],
        compiler_params=params,
        cost_estimate=pl.CostEstimate(
            flops=8_000_000_000, bytes_accessed=4_000_000, transcendentals=600_000
        ),
        name="inner",
    )(stored, queries, turned, values, early_ends)
    moved = pl.pallas_call(
        functools.partial(scan_kernel, chunks),
        in_specs=[vmem] * 5 + [pl.BlockSpec(memory_space=pl.ANY)] * 2,
        out_specs=vmem,
        out_shape=shape((group, rows, LANES), jnp.bfloat16),
        compiler_params=params,
        name="scan",
    )(one, half, pieces, early, final, rates, earlier)
    states = lax.all_to_all(
        moved, axes, split_axis=0, concat_axis=0, axis_index_groups=groups, tiled=True
    )
    return pl.pallas_call(
        norm_kernel,
        in_specs=[vmem] * 8,
        out_specs=pl.BlockSpec(memory_space=pl.ANY),
        out_shape=shape((tokens, width), jnp.bfloat16),
        scratch_shapes=[
            pltpu.VMEM((tokens, width), jnp.float32),
            pltpu.VMEM((tokens, width), jnp.bfloat16),
            pltpu.SemaphoreType.DMA((tokens // 16,)),
        ],
        compiler_params=params,
        name="norm",
    )(idcol, stored, earlier, rates, queries, states.reshape(all_pairs * HD, LANES), inner, norm_gain[None, :])


def solution(mesh):
    in_specs = (
        P(("ctx", "uly"), None),
        P(("ctx", "uly"), None),
        P(("ctx", "uly"), None),
        P(("ctx", "uly")),
        P("uly"),
        P(),
    )
    out_specs = P(("ctx", "uly"), None)
    return jax.shard_map(local, mesh=mesh, in_specs=in_specs, out_specs=out_specs, check_vma=False)
```

```python
import functools

import jax
import jax.numpy as jnp
from jax import lax
from jax.experimental import pallas as pl
from jax.experimental.pallas import tpu as pltpu
from jax.sharding import PartitionSpec as P

HD = 64
LANES = 2 * HD
NEVER = 1e9
MARK = 8


def rate_of(facts, head, here):
    return facts[head // here : head // here + 1, head % here : head % here + 1]


def pair_rate(stored, pair, here):
    members = stored.shape[0]
    lane = lax.broadcasted_iota(jnp.int32, (1, LANES), 1)
    rates = []
    for head in (2 * pair, 2 * pair + 1):
        at = lax.rem(lax.div(head, here) + members // 2, members)
        row = stored[pl.ds(at, 1), :]
        rates.append(
            jnp.sum(jnp.where(lane == lax.rem(head, here), row, 0.0), axis=1, keepdims=True)
        )
    return jnp.where(lane < HD, rates[0], rates[1])


def own_ids(stored, tokens):
    members = stored.shape[0]
    at = lax.rem(lax.axis_index("uly") + members // 2, members)
    row = stored[pl.ds(at, 1), :]
    fill = jnp.full((1, LANES - tokens), -1.0, jnp.float32)
    return jnp.concatenate([row[:, LANES - tokens :], fill], 1)


def turn_kernel(k_ref, v_ref, turned, filled):
    tokens, width = k_ref.shape
    filled[:tokens, :] = v_ref[...]
    filled[tokens:, :] = jnp.zeros((LANES - tokens, width), filled.dtype)
    blank = jnp.zeros((LANES - tokens, LANES), jnp.float32)
    for j in range(width // LANES):
        columns = slice(j * LANES, (j + 1) * LANES)
        block = jnp.concatenate([k_ref[:, columns].astype(jnp.float32), blank], 0)
        turned[columns, :] = jnp.transpose(block).astype(turned.dtype)


def ends_kernel(here, tokens, stored, turned, v_ref, out_ref):
    width = v_ref.shape[1]
    members = stored.shape[0]
    group, rows = out_ref.shape[0], out_ref.shape[1] - MARK
    lane = lax.broadcasted_iota(jnp.int32, (HD, LANES), 1)
    ids = jnp.broadcast_to(own_ids(stored, tokens), (8, LANES))
    place = lax.broadcasted_iota(jnp.int32, ids.shape, 1)
    last = ids[:, tokens - 1 : tokens]
    age = jnp.where(ids == last, (tokens - 1 - place).astype(jnp.float32), NEVER)
    mark = jnp.broadcast_to(last[:1], (MARK, LANES)).astype(jnp.bfloat16)
    for owner in range(group):
        out_ref[owner, rows:, :] = mark
    for j in range(0, width // LANES, 2):
        weighted = []
        for head in range(2 * j, 2 * j + 4):
            weight = jnp.exp(-rate_of(stored, (head + members // 2 * here) % (members * here), here) * age)
            keys = turned[head * HD : (head + 1) * HD, :].astype(jnp.float32)
            keys = keys.reshape(HD // 8, 8, LANES) * weight[None]
            weighted.append(keys.reshape(HD, LANES))
        weighted = jnp.concatenate(weighted, 0)
        high = weighted.astype(jnp.bfloat16)
        low = (weighted - high.astype(jnp.float32)).astype(jnp.bfloat16)
        v = v_ref[:, j * LANES : (j + 2) * LANES]
        both = jnp.dot(
            jnp.concatenate([high, low], 1),
            jnp.concatenate([v, v], 0),
            preferred_element_type=jnp.float32,
        )
        for one in (0, 1):
            pair = both[one * LANES : (one + 1) * LANES, one * LANES : (one + 1) * LANES]
            state = jnp.where(lane < HD, pair[:HD], pair[HD:])
            size = min(rows, HD)
            for at in range(0, HD, size):
                owner, start = divmod((j + one) * HD + at, rows)
                out_ref[group - 1 - owner, start : start + size, :] = state[at : at + size].astype(
                    jnp.bfloat16
                )


def inner_kernel(here, stored, q_ref, turned, v_ref, after, out_ref, rates_ref, idcol):
    tokens, width = q_ref.shape
    members = stored.shape[0]
    row = own_ids(stored, tokens)
    column = jnp.transpose(jnp.broadcast_to(row, (LANES, LANES)))[:tokens]
    idcol[...] = column
    lane = lax.broadcasted_iota(jnp.int32, (tokens, LANES), 1)
    t = lax.broadcasted_iota(jnp.int32, (tokens, LANES), 0)
    seen = (t >= lane) & (column == row)
    age = jnp.where(seen, (t - lane).astype(jnp.float32), NEVER)
    for j in range(width // LANES):
        columns = slice(j * LANES, (j + 1) * LANES)
        q = q_ref[:, columns]
        zero = jnp.zeros_like(q)
        stacked = jnp.concatenate([jnp.where(lane < HD, q, zero), jnp.where(lane < HD, zero, q)], 0)
        scores = jnp.dot(
            stacked, turned[columns, :], preferred_element_type=jnp.float32
        )
        rates = [
            rate_of(stored, (2 * j + one + members // 2 * here) % (members * here), here)
            for one in (0, 1)
        ]
        weight = jnp.concatenate([jnp.exp(-rate * age) for rate in rates], 0)
        probs = (scores * weight)[:, :tokens].astype(jnp.bfloat16)
        got = jnp.dot(probs, v_ref[:, columns], preferred_element_type=jnp.float32)
        out_ref[:, columns] = jnp.where(lane < HD, got[:tokens], got[tokens:])
        rates_ref[:, columns] = jnp.where(lane[:1] < HD, rates[0], rates[1])


def few(count):
    return count if count <= 8 else 1


def split(piece, rows):
    return piece[:rows].astype(jnp.float32), piece[rows : rows + 1].astype(jnp.float32)


def half_kernel(here, tokens, chunks, stored, in_ref, early_ref, final_ref, one, half):
    slices, newest = early_ref.shape[0] + 1, in_ref.shape[0] - 1
    rows = one.shape[0]
    owner = lax.axis_index("ctx") * chunks + lax.rem(lax.axis_index("uly"), chunks)
    share = min(rows, HD)
    for at in range(0, rows, share):
        rate = pair_rate(stored, lax.div(owner * rows + at, HD), here)
        for ref, length in ((one, tokens), (half, tokens * chunks)):
            ref[at : at + share, :] = jnp.broadcast_to(
                jnp.exp(-rate * float(length)), (share, LANES)
            )

    def slice_end(c, ref, at):
        def step(j, carry):
            state, last = carry
            fresh, own = split(in_ref[newest - c * chunks - j], rows)
            return fresh + jnp.where(own == last, one[...], 0.0) * state, own

        begin = split(in_ref[newest - c * chunks], rows)
        state, _ = lax.fori_loop(1, chunks, step, begin, unroll=few(chunks - 1))
        ref[at, :rows, :] = state.astype(ref.dtype)
        ref[at, rows:, :] = in_ref[newest - c * chunks - chunks + 1][rows:]

    def early(c, _):
        slice_end(c, early_ref, c)
        return 0

    lax.fori_loop(0, slices - 1, early, 0, unroll=few(slices - 1))
    slice_end(slices - 1, final_ref, 0)


def scan_kernel(chunks, stored, one, half, in_ref, early, final, after, out_ref, before):
    slices, newest = early.shape[0] + 1, in_ref.shape[0] - 1
    rows = one.shape[0]
    ctx, uly = lax.axis_index("ctx"), lax.axis_index("uly")
    later = uly >= chunks
    members = stored.shape[0]
    at = lax.rem(uly + members - 1 + members // 2, members)
    _, slice_before = split(early[jnp.maximum(ctx - 1, 0)], rows)
    first = jnp.where(ctx > 0, slice_before, -1.0)
    before[...] = jnp.where(uly > 0, stored[pl.ds(at, 1), LANES - 1 :], first)

    def over_other(carry, piece, wanted):
        state, last = carry
        fresh, own = split(piece, rows)
        moved = fresh + jnp.where(own == last, half[...], 0.0) * state
        return jnp.where(wanted, moved, state), jnp.where(wanted, own, last)

    def over_own(carry, c):
        def step(j, carry):
            state, last = carry
            at = c * chunks + j
            out_ref[at] = state.astype(out_ref.dtype)
            fresh, own = split(in_ref[newest - at], rows)
            return fresh + jnp.where(own == last, one[...], 0.0) * state, own

        return lax.fori_loop(0, chunks, step, carry, unroll=few(chunks))

    def over_slice(c, carry):
        carry = over_own(over_other(carry, early[c], later), c)
        return over_other(carry, early[c], jnp.logical_not(later))

    begin = (jnp.zeros((rows, LANES), jnp.float32), jnp.full((1, LANES), -1.0, jnp.float32))
    carry = lax.fori_loop(0, slices - 1, over_slice, begin, unroll=few(slices - 1))
    over_own(over_other(carry, final[0], later), slices - 1)


def norm_kernel(idcol, before, rates, q_ref, s_ref, inner_ref, gain, out_ref, raw, done, sems):
    tokens, width = q_ref.shape
    lane = lax.broadcasted_iota(jnp.int32, (HD, LANES), 1)
    place = lax.broadcasted_iota(jnp.int32, (tokens, LANES), 0)
    age = jnp.where(idcol[...] == before[...], (place + 1).astype(jnp.float32), NEVER)
    zero = jnp.zeros((HD, LANES), s_ref.dtype)
    total = jnp.zeros((tokens, LANES), jnp.float32)
    for j in range(0, width // LANES, 2):
        square = []
        for one in (0, 1):
            state = s_ref[(j + one) * HD : (j + one + 1) * HD, :]
            for half in (jnp.where(lane < HD, state, zero), jnp.where(lane < HD, zero, state)):
                square.append(jnp.concatenate([zero, half] if one else [half, zero], 1))
        columns = slice(j * LANES, (j + 2) * LANES)
        outer = jnp.dot(
            q_ref[:, columns], jnp.concatenate(square, 0), preferred_element_type=jnp.float32
        )
        for one in (0, 1):
            columns = slice((j + one) * LANES, (j + one + 1) * LANES)
            fade = jnp.exp(-rates[:, columns] * age)
            value = inner_ref[:, columns] + outer[:, one * LANES : (one + 1) * LANES] * fade
            total += value * value
            raw[:, columns] = value
    mean = jnp.sum(total, axis=1, keepdims=True) / float(width)
    scale = jnp.broadcast_to(lax.rsqrt(mean + 1e-06), (tokens, LANES))
    parts = sems.shape[0]
    share = tokens // parts
    copies = []
    for part in range(parts):
        rows = slice(part * share, (part + 1) * share)
        for at in range(0, width, LANES):
            columns = slice(at, at + LANES)
            done[rows, columns] = (raw[rows, columns] * scale[rows] * gain[:, columns]).astype(
                jnp.bfloat16
            )
        copies.append(pltpu.make_async_copy(done.at[rows], out_ref.at[rows], sems.at[part]))
        copies[-1].start()
    for copy in copies:
        copy.wait()


def local(queries, keys, values, doc_ids, decay_rate, norm_gain):
    tokens, width = queries.shape
    here = decay_rate.shape[0]
    axes = ("ctx", "uly")
    slices, members = lax.axis_size("ctx"), lax.axis_size("uly")
    count = slices * members
    all_pairs = width // LANES
    chunks = members // 2
    group = slices * chunks
    rows = all_pairs * HD // group
    groups = [
        [c * members + half * chunks + u for c in range(slices) for u in range(chunks)]
        for half in (0, 1)
    ]
    swap = [
        (c * members + u, c * members + (u + chunks) % members)
        for c in range(slices)
        for u in range(members)
    ]

    vmem = pl.BlockSpec(memory_space=pltpu.VMEM)
    params = pltpu.CompilerParams(vmem_limit_bytes=32 * 1024 * 1024)
    shape = jax.ShapeDtypeStruct
    tile = shape((members, LANES), jnp.float32)

    own = jnp.pad(decay_rate, (0, LANES - here)) + jnp.pad(
        doc_ids, (LANES - tokens, 0)
    ).astype(jnp.float32)
    turned_round = [[(u + members // 2) % members for u in range(members)]]
    stored = lax.all_to_all(
        jnp.broadcast_to(own[None, :], tile.shape),
        "uly", split_axis=0, concat_axis=0, axis_index_groups=turned_round, tiled=True,
    )
    turned, filled = pl.pallas_call(
        turn_kernel,
        in_specs=[vmem] * 2,
        out_specs=[vmem] * 2,
        out_shape=[shape((width, LANES), jnp.bfloat16), shape((LANES, width), jnp.bfloat16)],
        compiler_params=params,
        cost_estimate=pl.CostEstimate(flops=0, bytes_accessed=12_000_000, transcendentals=0),
        name="turn",
    )(keys, values)
    ends = pl.pallas_call(
        functools.partial(ends_kernel, here, tokens),
        in_specs=[vmem] * 3,
        out_specs=vmem,
        out_shape=shape((group, rows + MARK, LANES), jnp.bfloat16),
        compiler_params=params,
        name="ends",
    )(stored, turned, filled)
    pieces = lax.all_to_all(
        ends,
        axes, split_axis=0, concat_axis=0, tiled=True,
        axis_index_groups=[members_of[::-1] for members_of in groups],
    )
    early_ends, final_end, one, half = pl.pallas_call(
        functools.partial(half_kernel, here, tokens, chunks),
        in_specs=[vmem] * 2,
        out_specs=[vmem] * 4,
        out_shape=[
            shape((slices - 1, rows + MARK, LANES), jnp.bfloat16),
            shape((1, rows + MARK, LANES), jnp.bfloat16),
            shape((rows, LANES), jnp.float32),
            shape((rows, LANES), jnp.float32),
        ],
        compiler_params=params,
        name="half",
    )(stored, pieces)
    early = lax.ppermute(early_ends, axes, swap)
    final = lax.ppermute(final_end, axes, [(low, high) for low, high in swap if low < high])
    inner, rates, idcol = pl.pallas_call(
        functools.partial(inner_kernel, here),
        in_specs=[vmem] * 4 + [pl.BlockSpec(memory_space=pl.ANY)],
        out_specs=[vmem] * 3,
        out_shape=[
            shape((tokens, width), jnp.float32),
            shape((1, width), jnp.float32),
            shape((tokens, LANES), jnp.float32),
        ],
        compiler_params=params,
        cost_estimate=pl.CostEstimate(
            flops=8_000_000_000, bytes_accessed=4_000_000, transcendentals=600_000
        ),
        name="inner",
    )(stored, queries, turned, values, early_ends)
    moved, before = pl.pallas_call(
        functools.partial(scan_kernel, chunks),
        in_specs=[vmem] * 6 + [pl.BlockSpec(memory_space=pl.ANY)],
        out_specs=[vmem] * 2,
        out_shape=[
            shape((group, rows, LANES), jnp.bfloat16),
            shape((1, LANES), jnp.float32),
        ],
        compiler_params=params,
        name="scan",
    )(stored, one, half, pieces, early, final, rates)
    states = lax.all_to_all(
        moved, axes, split_axis=0, concat_axis=0, axis_index_groups=groups, tiled=True
    )
    return pl.pallas_call(
        norm_kernel,
        in_specs=[vmem] * 7,
        out_specs=pl.BlockSpec(memory_space=pl.ANY),
        out_shape=shape((tokens, width), jnp.bfloat16),
        scratch_shapes=[
            pltpu.VMEM((tokens, width), jnp.float32),
            pltpu.VMEM((tokens, width), jnp.bfloat16),
            pltpu.SemaphoreType.DMA((tokens // 16,)),
        ],
        compiler_params=params,
        name="norm",
    )(idcol, before, rates, queries, states.reshape(all_pairs * HD, LANES), inner, norm_gain[None, :])


def solution(mesh):
    in_specs = (
        P(("ctx", "uly"), None),
        P(("ctx", "uly"), None),
        P(("ctx", "uly"), None),
        P(("ctx", "uly")),
        P("uly"),
        P(),
    )
    out_specs = P(("ctx", "uly"), None)
    return jax.shard_map(local, mesh=mesh, in_specs=in_specs, out_specs=out_specs, check_vma=False)
```

```python
import functools

import jax
import jax.numpy as jnp
from jax import lax
from jax.experimental import pallas as pl
from jax.experimental.pallas import tpu as pltpu
from jax.sharding import PartitionSpec as P

HD = 64
LANES = 2 * HD
NEVER = 1e9
MARK = 8


def rate_of(facts, head, here):
    return facts[head // here : head // here + 1, head % here : head % here + 1]


def pair_rate(stored, pair, here):
    members = stored.shape[0]
    lane = lax.broadcasted_iota(jnp.int32, (1, LANES), 1)
    rates = []
    for head in (2 * pair, 2 * pair + 1):
        at = lax.rem(lax.div(head, here) + members // 2, members)
        row = stored[pl.ds(at, 1), :]
        rates.append(
            jnp.sum(jnp.where(lane == lax.rem(head, here), row, 0.0), axis=1, keepdims=True)
        )
    return jnp.where(lane < HD, rates[0], rates[1])


def own_ids(stored, tokens):
    members = stored.shape[0]
    at = lax.rem(lax.axis_index("uly") + members // 2, members)
    row = stored[pl.ds(at, 1), :]
    fill = jnp.full((1, LANES - tokens), -1.0, jnp.float32)
    return jnp.concatenate([row[:, LANES - tokens :], fill], 1)


def turn_kernel(k_ref, v_ref, turned, filled):
    tokens, width = k_ref.shape
    filled[:tokens, :] = v_ref[...]
    filled[tokens:, :] = jnp.zeros((LANES - tokens, width), filled.dtype)
    blank = jnp.zeros((LANES - tokens, LANES), jnp.float32)
    for j in range(width // LANES):
        columns = slice(j * LANES, (j + 1) * LANES)
        block = jnp.concatenate([k_ref[:, columns].astype(jnp.float32), blank], 0)
        turned[columns, :] = jnp.transpose(block).astype(turned.dtype)


def ends_kernel(here, tokens, stored, turned, v_ref, out_ref):
    width = v_ref.shape[1]
    members = stored.shape[0]
    group, rows = out_ref.shape[0], out_ref.shape[1] - MARK
    lane = lax.broadcasted_iota(jnp.int32, (HD, LANES), 1)
    ids = jnp.broadcast_to(own_ids(stored, tokens), (8, LANES))
    place = lax.broadcasted_iota(jnp.int32, ids.shape, 1)
    last = ids[:, tokens - 1 : tokens]
    age = jnp.where(ids == last, (tokens - 1 - place).astype(jnp.float32), NEVER)
    mark = jnp.broadcast_to(last[:1], (MARK, LANES)).astype(jnp.bfloat16)
    for owner in range(group):
        out_ref[owner, rows:, :] = mark
    for j in range(0, width // LANES, 2):
        weighted = []
        for head in range(2 * j, 2 * j + 4):
            weight = jnp.exp(-rate_of(stored, (head + members // 2 * here) % (members * here), here) * age)
            keys = turned[head * HD : (head + 1) * HD, :].astype(jnp.float32)
            keys = keys.reshape(HD // 8, 8, LANES) * weight[None]
            weighted.append(keys.reshape(HD, LANES))
        weighted = jnp.concatenate(weighted, 0)
        high = weighted.astype(jnp.bfloat16)
        low = (weighted - high.astype(jnp.float32)).astype(jnp.bfloat16)
        v = v_ref[:, j * LANES : (j + 2) * LANES]
        both = jnp.dot(
            jnp.concatenate([high, low], 1),
            jnp.concatenate([v, v], 0),
            preferred_element_type=jnp.float32,
        )
        for one in (0, 1):
            pair = both[one * LANES : (one + 1) * LANES, one * LANES : (one + 1) * LANES]
            state = jnp.where(lane < HD, pair[:HD], pair[HD:])
            size = min(rows, HD)
            for at in range(0, HD, size):
                owner, start = divmod((j + one) * HD + at, rows)
                out_ref[group - 1 - owner, start : start + size, :] = state[at : at + size].astype(
                    jnp.bfloat16
                )


def inner_kernel(here, stored, q_ref, turned, v_ref, after, out_ref, rates_ref, idcol):
    tokens, width = q_ref.shape
    members = stored.shape[0]
    row = own_ids(stored, tokens)
    column = jnp.transpose(jnp.broadcast_to(row, (LANES, LANES)))[:tokens]
    idcol[...] = column
    lane = lax.broadcasted_iota(jnp.int32, (tokens, LANES), 1)
    t = lax.broadcasted_iota(jnp.int32, (tokens, LANES), 0)
    seen = (t >= lane) & (column == row)
    age = jnp.where(seen, (t - lane).astype(jnp.float32), NEVER)
    for j in range(width // LANES):
        columns = slice(j * LANES, (j + 1) * LANES)
        q = q_ref[:, columns]
        zero = jnp.zeros_like(q)
        stacked = jnp.concatenate([jnp.where(lane < HD, q, zero), jnp.where(lane < HD, zero, q)], 0)
        scores = jnp.dot(
            stacked, turned[columns, :], preferred_element_type=jnp.float32
        )
        rates = [
            rate_of(stored, (2 * j + one + members // 2 * here) % (members * here), here)
            for one in (0, 1)
        ]
        weight = jnp.concatenate([jnp.exp(-rate * age) for rate in rates], 0)
        probs = (scores * weight)[:, :tokens].astype(jnp.bfloat16)
        got = jnp.dot(probs, v_ref[:, columns], preferred_element_type=jnp.float32)
        out_ref[:, columns] = jnp.where(lane < HD, got[:tokens], got[tokens:])
        rates_ref[:, columns] = jnp.where(lane[:1] < HD, rates[0], rates[1])


def few(count):
    return count if count <= 8 else 1


def split(piece, rows):
    return piece[:rows].astype(jnp.float32), piece[rows : rows + 1].astype(jnp.float32)


def half_kernel(here, tokens, chunks, stored, in_ref, early_ref, final_ref, one, half):
    slices, newest = early_ref.shape[0] + 1, in_ref.shape[0] - 1
    rows = one.shape[0]
    owner = lax.axis_index("ctx") * chunks + lax.rem(lax.axis_index("uly"), chunks)
    share = min(rows, HD)
    for at in range(0, rows, share):
        rate = pair_rate(stored, lax.div(owner * rows + at, HD), here)
        for ref, length in ((one, tokens), (half, tokens * chunks)):
            ref[at : at + share, :] = jnp.broadcast_to(
                jnp.exp(-rate * float(length)), (share, LANES)
            )

    def slice_end(c, ref, at):
        def step(j, carry):
            state, last = carry
            fresh, own = split(in_ref[newest - c * chunks - j], rows)
            return fresh + jnp.where(own == last, one[...], 0.0) * state, own

        begin = split(in_ref[newest - c * chunks], rows)
        state, _ = lax.fori_loop(1, chunks, step, begin, unroll=few(chunks - 1))
        ref[at, :rows, :] = state.astype(ref.dtype)
        ref[at, rows:, :] = in_ref[newest - c * chunks - chunks + 1][rows:]

    def early(c, _):
        slice_end(c, early_ref, c)
        return 0

    lax.fori_loop(0, slices - 1, early, 0, unroll=few(slices - 1))
    slice_end(slices - 1, final_ref, 0)


def scan_kernel(chunks, stored, one, half, in_ref, early, final, after, out_ref, before):
    slices, newest = early.shape[0] + 1, in_ref.shape[0] - 1
    rows = one.shape[0]
    ctx, uly = lax.axis_index("ctx"), lax.axis_index("uly")
    later = uly >= chunks
    members = stored.shape[0]
    at = lax.rem(uly + members - 1 + members // 2, members)
    _, slice_before = split(early[jnp.maximum(ctx - 1, 0)], rows)
    first = jnp.where(ctx > 0, slice_before, -1.0)
    before[...] = jnp.where(uly > 0, stored[pl.ds(at, 1), LANES - 1 :], first)

    def over_other(carry, piece, wanted):
        state, last = carry
        fresh, own = split(piece, rows)
        moved = fresh + jnp.where(own == last, half[...], 0.0) * state
        return jnp.where(wanted, moved, state), jnp.where(wanted, own, last)

    def over_own(carry, c):
        def step(j, carry):
            state, last = carry
            at = c * chunks + j
            out_ref[newest - at] = state.astype(out_ref.dtype)
            fresh, own = split(in_ref[newest - at], rows)
            return fresh + jnp.where(own == last, one[...], 0.0) * state, own

        return lax.fori_loop(0, chunks, step, carry, unroll=few(chunks))

    def over_slice(c, carry):
        carry = over_own(over_other(carry, early[c], later), c)
        return over_other(carry, early[c], jnp.logical_not(later))

    begin = (jnp.zeros((rows, LANES), jnp.float32), jnp.full((1, LANES), -1.0, jnp.float32))
    carry = lax.fori_loop(0, slices - 1, over_slice, begin, unroll=few(slices - 1))
    over_own(over_other(carry, final[0], later), slices - 1)


def norm_kernel(group, idcol, before, rates, q_ref, s_ref, inner_ref, gain, out_ref, raw, done, sems):
    tokens, width = q_ref.shape
    lane = lax.broadcasted_iota(jnp.int32, (HD, LANES), 1)
    place = lax.broadcasted_iota(jnp.int32, (tokens, LANES), 0)
    age = jnp.where(idcol[...] == before[...], (place + 1).astype(jnp.float32), NEVER)
    zero = jnp.zeros((HD, LANES), s_ref.dtype)
    rows = s_ref.shape[0] // group
    size = min(rows, HD)
    total = jnp.zeros((tokens, LANES), jnp.float32)
    for j in range(0, width // LANES, 2):
        square = []
        for one in (0, 1):
            state = []
            for at in range((j + one) * HD, (j + one + 1) * HD, size):
                owner, start = divmod(at, rows)
                start += (group - 1 - owner) * rows
                state.append(s_ref[start : start + size, :])
            if len(state) > 1:
                state = [jnp.concatenate([s.astype(jnp.float32) for s in state], 0).astype(zero.dtype)]
            state = state[0]
            for half in (jnp.where(lane < HD, state, zero), jnp.where(lane < HD, zero, state)):
                square.append(jnp.concatenate([zero, half] if one else [half, zero], 1))
        columns = slice(j * LANES, (j + 2) * LANES)
        outer = jnp.dot(
            q_ref[:, columns], jnp.concatenate(square, 0), preferred_element_type=jnp.float32
        )
        for one in (0, 1):
            columns = slice((j + one) * LANES, (j + one + 1) * LANES)
            fade = jnp.exp(-rates[:, columns] * age)
            value = inner_ref[:, columns] + outer[:, one * LANES : (one + 1) * LANES] * fade
            total += value * value
            raw[:, columns] = value
    mean = jnp.sum(total, axis=1, keepdims=True) / float(width)
    scale = jnp.broadcast_to(lax.rsqrt(mean + 1e-06), (tokens, LANES))
    parts = sems.shape[0]
    share = tokens // parts
    copies = []
    for part in range(parts):
        rows = slice(part * share, (part + 1) * share)
        for at in range(0, width, LANES):
            columns = slice(at, at + LANES)
            done[rows, columns] = (raw[rows, columns] * scale[rows] * gain[:, columns]).astype(
                jnp.bfloat16
            )
        copies.append(pltpu.make_async_copy(done.at[rows], out_ref.at[rows], sems.at[part]))
        copies[-1].start()
    for copy in copies:
        copy.wait()


def local(queries, keys, values, doc_ids, decay_rate, norm_gain):
    tokens, width = queries.shape
    here = decay_rate.shape[0]
    axes = ("ctx", "uly")
    slices, members = lax.axis_size("ctx"), lax.axis_size("uly")
    count = slices * members
    all_pairs = width // LANES
    chunks = members // 2
    group = slices * chunks
    rows = all_pairs * HD // group
    groups = [
        [c * members + half * chunks + u for c in range(slices) for u in range(chunks)]
        for half in (0, 1)
    ]
    swap = [
        (c * members + u, c * members + (u + chunks) % members)
        for c in range(slices)
        for u in range(members)
    ]

    vmem = pl.BlockSpec(memory_space=pltpu.VMEM)
    params = pltpu.CompilerParams(vmem_limit_bytes=32 * 1024 * 1024)
    shape = jax.ShapeDtypeStruct
    tile = shape((members, LANES), jnp.float32)

    own = jnp.pad(decay_rate, (0, LANES - here)) + jnp.pad(
        doc_ids, (LANES - tokens, 0)
    ).astype(jnp.float32)
    turned_round = [[(u + members // 2) % members for u in range(members)]]
    stored = lax.all_to_all(
        jnp.broadcast_to(own[None, :], tile.shape),
        "uly", split_axis=0, concat_axis=0, axis_index_groups=turned_round, tiled=True,
    )
    turned, filled = pl.pallas_call(
        turn_kernel,
        in_specs=[vmem] * 2,
        out_specs=[vmem] * 2,
        out_shape=[shape((width, LANES), jnp.bfloat16), shape((LANES, width), jnp.bfloat16)],
        compiler_params=params,
        cost_estimate=pl.CostEstimate(flops=0, bytes_accessed=12_000_000, transcendentals=0),
        name="turn",
    )(keys, values)
    ends = pl.pallas_call(
        functools.partial(ends_kernel, here, tokens),
        in_specs=[vmem] * 3,
        out_specs=vmem,
        out_shape=shape((group, rows + MARK, LANES), jnp.bfloat16),
        compiler_params=params,
        name="ends",
    )(stored, turned, filled)
    pieces = lax.all_to_all(
        ends,
        axes, split_axis=0, concat_axis=0, tiled=True,
        axis_index_groups=[members_of[::-1] for members_of in groups],
    )
    early_ends, final_end, one, half = pl.pallas_call(
        functools.partial(half_kernel, here, tokens, chunks),
        in_specs=[vmem] * 2,
        out_specs=[vmem] * 4,
        out_shape=[
            shape((slices - 1, rows + MARK, LANES), jnp.bfloat16),
            shape((1, rows + MARK, LANES), jnp.bfloat16),
            shape((rows, LANES), jnp.float32),
            shape((rows, LANES), jnp.float32),
        ],
        compiler_params=params,
        name="half",
    )(stored, pieces)
    early = lax.ppermute(early_ends, axes, swap)
    final = lax.ppermute(final_end, axes, [(low, high) for low, high in swap if low < high])
    inner, rates, idcol = pl.pallas_call(
        functools.partial(inner_kernel, here),
        in_specs=[vmem] * 4 + [pl.BlockSpec(memory_space=pl.ANY)],
        out_specs=[vmem] * 3,
        out_shape=[
            shape((tokens, width), jnp.float32),
            shape((1, width), jnp.float32),
            shape((tokens, LANES), jnp.float32),
        ],
        compiler_params=params,
        cost_estimate=pl.CostEstimate(
            flops=8_000_000_000, bytes_accessed=4_000_000, transcendentals=600_000
        ),
        name="inner",
    )(stored, queries, turned, values, early_ends)
    moved, before = pl.pallas_call(
        functools.partial(scan_kernel, chunks),
        in_specs=[vmem] * 6 + [pl.BlockSpec(memory_space=pl.ANY)],
        out_specs=[vmem] * 2,
        out_shape=[
            shape((group, rows, LANES), jnp.bfloat16),
            shape((1, LANES), jnp.float32),
        ],
        compiler_params=params,
        name="scan",
    )(stored, one, half, pieces, early, final, rates)
    states = lax.all_to_all(
        moved,
        axes, split_axis=0, concat_axis=0, tiled=True,
        axis_index_groups=[members_of[::-1] for members_of in groups],
    )
    return pl.pallas_call(
        functools.partial(norm_kernel, group),
        in_specs=[vmem] * 7,
        out_specs=pl.BlockSpec(memory_space=pl.ANY),
        out_shape=shape((tokens, width), jnp.bfloat16),
        scratch_shapes=[
            pltpu.VMEM((tokens, width), jnp.float32),
            pltpu.VMEM((tokens, width), jnp.bfloat16),
            pltpu.SemaphoreType.DMA((tokens // 16,)),
        ],
        compiler_params=params,
        name="norm",
    )(idcol, before, rates, queries, states.reshape(all_pairs * HD, LANES), inner, norm_gain[None, :])


def solution(mesh):
    in_specs = (
        P(("ctx", "uly"), None),
        P(("ctx", "uly"), None),
        P(("ctx", "uly"), None),
        P(("ctx", "uly")),
        P("uly"),
        P(),
    )
    out_specs = P(("ctx", "uly"), None)
    return jax.shard_map(local, mesh=mesh, in_specs=in_specs, out_specs=out_specs, check_vma=False)
```

```python
import functools

import jax
import jax.numpy as jnp
from jax import lax
from jax.experimental import pallas as pl
from jax.experimental.pallas import tpu as pltpu
from jax.sharding import PartitionSpec as P

HD = 64
LANES = 2 * HD
NEVER = 1e9
MARK = 8


def rate_of(facts, head, here):
    return facts[head // here : head // here + 1, head % here : head % here + 1]


def pair_rate(stored, pair, here):
    members = stored.shape[0]
    lane = lax.broadcasted_iota(jnp.int32, (1, LANES), 1)
    rates = []
    for head in (2 * pair, 2 * pair + 1):
        at = lax.rem(lax.div(head, here) + members // 2, members)
        row = stored[pl.ds(at, 1), :]
        rates.append(
            jnp.sum(jnp.where(lane == lax.rem(head, here), row, 0.0), axis=1, keepdims=True)
        )
    return jnp.where(lane < HD, rates[0], rates[1])


def own_ids(stored, tokens):
    members = stored.shape[0]
    at = lax.rem(lax.axis_index("uly") + members // 2, members)
    row = stored[pl.ds(at, 1), :]
    fill = jnp.full((1, LANES - tokens), -1.0, jnp.float32)
    return jnp.concatenate([row[:, LANES - tokens :], fill], 1)


def turn_kernel(k_ref, v_ref, turned, filled):
    tokens, width = k_ref.shape
    filled[:tokens, :] = v_ref[...]
    filled[tokens:, :] = jnp.zeros((LANES - tokens, width), filled.dtype)
    blank = jnp.zeros((LANES - tokens, LANES), jnp.float32)
    for j in range(width // LANES):
        columns = slice(j * LANES, (j + 1) * LANES)
        block = jnp.concatenate([k_ref[:, columns].astype(jnp.float32), blank], 0)
        turned[columns, :] = jnp.transpose(block).astype(turned.dtype)


def ends_kernel(here, tokens, stored, turned, v_ref, out_ref):
    width = v_ref.shape[1]
    members = stored.shape[0]
    group, rows = out_ref.shape[0], out_ref.shape[1] - MARK
    lane = lax.broadcasted_iota(jnp.int32, (HD, LANES), 1)
    ids = jnp.broadcast_to(own_ids(stored, tokens), (8, LANES))
    place = lax.broadcasted_iota(jnp.int32, ids.shape, 1)
    last = ids[:, tokens - 1 : tokens]
    age = jnp.where(ids == last, (tokens - 1 - place).astype(jnp.float32), NEVER)
    mark = jnp.broadcast_to(last[:1], (MARK, LANES)).astype(jnp.bfloat16)
    for owner in range(group):
        out_ref[owner, rows:, :] = mark
    for j in range(0, width // LANES, 2):
        weighted = []
        for head in range(2 * j, 2 * j + 4):
            weight = jnp.exp(-rate_of(stored, (head + members // 2 * here) % (members * here), here) * age)
            keys = turned[head * HD : (head + 1) * HD, :].astype(jnp.float32)
            keys = keys.reshape(HD // 8, 8, LANES) * weight[None]
            weighted.append(keys.reshape(HD, LANES))
        weighted = jnp.concatenate(weighted, 0)
        high = weighted.astype(jnp.bfloat16)
        low = (weighted - high.astype(jnp.float32)).astype(jnp.bfloat16)
        v = v_ref[:, j * LANES : (j + 2) * LANES]
        both = jnp.dot(
            jnp.concatenate([high, low], 1),
            jnp.concatenate([v, v], 0),
            preferred_element_type=jnp.float32,
        )
        for one in (0, 1):
            pair = both[one * LANES : (one + 1) * LANES, one * LANES : (one + 1) * LANES]
            state = jnp.where(lane < HD, pair[:HD], pair[HD:])
            size = min(rows, HD)
            for at in range(0, HD, size):
                owner, start = divmod((j + one) * HD + at, rows)
                out_ref[(owner + group // 2) % group, start : start + size, :] = state[at : at + size].astype(
                    jnp.bfloat16
                )


def inner_kernel(here, stored, q_ref, turned, v_ref, after, out_ref, rates_ref, idcol):
    tokens, width = q_ref.shape
    members = stored.shape[0]
    row = own_ids(stored, tokens)
    column = jnp.transpose(jnp.broadcast_to(row, (LANES, LANES)))[:tokens]
    idcol[...] = column
    lane = lax.broadcasted_iota(jnp.int32, (tokens, LANES), 1)
    t = lax.broadcasted_iota(jnp.int32, (tokens, LANES), 0)
    seen = (t >= lane) & (column == row)
    age = jnp.where(seen, (t - lane).astype(jnp.float32), NEVER)
    for j in range(width // LANES):
        columns = slice(j * LANES, (j + 1) * LANES)
        q = q_ref[:, columns]
        zero = jnp.zeros_like(q)
        stacked = jnp.concatenate([jnp.where(lane < HD, q, zero), jnp.where(lane < HD, zero, q)], 0)
        scores = jnp.dot(
            stacked, turned[columns, :], preferred_element_type=jnp.float32
        )
        rates = [
            rate_of(stored, (2 * j + one + members // 2 * here) % (members * here), here)
            for one in (0, 1)
        ]
        weight = jnp.concatenate([jnp.exp(-rate * age) for rate in rates], 0)
        probs = (scores * weight)[:, :tokens].astype(jnp.bfloat16)
        got = jnp.dot(probs, v_ref[:, columns], preferred_element_type=jnp.float32)
        out_ref[:, columns] = jnp.where(lane < HD, got[:tokens], got[tokens:])
        rates_ref[:, columns] = jnp.where(lane[:1] < HD, rates[0], rates[1])


def few(count):
    return count if count <= 8 else 1


def half_way(at, count):
    return lax.rem(at + count // 2, count)


def split(piece, rows):
    return piece[:rows].astype(jnp.float32), piece[rows : rows + 1].astype(jnp.float32)


def half_kernel(here, tokens, chunks, stored, in_ref, early_ref, final_ref, one, half):
    slices, count = early_ref.shape[0] + 1, in_ref.shape[0]
    rows = one.shape[0]
    owner = lax.axis_index("ctx") * chunks + lax.rem(lax.axis_index("uly"), chunks)
    share = min(rows, HD)
    for at in range(0, rows, share):
        rate = pair_rate(stored, lax.div(owner * rows + at, HD), here)
        for ref, length in ((one, tokens), (half, tokens * chunks)):
            ref[at : at + share, :] = jnp.broadcast_to(
                jnp.exp(-rate * float(length)), (share, LANES)
            )

    def slice_end(c, ref, at):
        def step(j, carry):
            state, last = carry
            fresh, own = split(in_ref[half_way(c * chunks + j, count)], rows)
            return fresh + jnp.where(own == last, one[...], 0.0) * state, own

        begin = split(in_ref[half_way(c * chunks, count)], rows)
        state, _ = lax.fori_loop(1, chunks, step, begin, unroll=few(chunks - 1))
        ref[at, :rows, :] = state.astype(ref.dtype)
        ref[at, rows:, :] = in_ref[half_way(c * chunks + chunks - 1, count)][rows:]

    def early(c, _):
        slice_end(c, early_ref, c)
        return 0

    lax.fori_loop(0, slices - 1, early, 0, unroll=few(slices - 1))
    slice_end(slices - 1, final_ref, 0)


def scan_kernel(chunks, stored, one, half, in_ref, early, final, after, out_ref, before):
    slices, count = early.shape[0] + 1, in_ref.shape[0]
    rows = one.shape[0]
    ctx, uly = lax.axis_index("ctx"), lax.axis_index("uly")
    later = uly >= chunks
    members = stored.shape[0]
    at = lax.rem(uly + members - 1 + members // 2, members)
    _, slice_before = split(early[jnp.maximum(ctx - 1, 0)], rows)
    first = jnp.where(ctx > 0, slice_before, -1.0)
    before[...] = jnp.where(uly > 0, stored[pl.ds(at, 1), LANES - 1 :], first)

    def over_other(carry, piece, wanted):
        state, last = carry
        fresh, own = split(piece, rows)
        moved = fresh + jnp.where(own == last, half[...], 0.0) * state
        return jnp.where(wanted, moved, state), jnp.where(wanted, own, last)

    def over_own(carry, c):
        def step(j, carry):
            state, last = carry
            at = c * chunks + j
            out_ref[count - 1 - at] = state.astype(out_ref.dtype)
            fresh, own = split(in_ref[half_way(at, count)], rows)
            return fresh + jnp.where(own == last, one[...], 0.0) * state, own

        return lax.fori_loop(0, chunks, step, carry, unroll=few(chunks))

    def over_slice(c, carry):
        carry = over_own(over_other(carry, early[c], later), c)
        return over_other(carry, early[c], jnp.logical_not(later))

    begin = (jnp.zeros((rows, LANES), jnp.float32), jnp.full((1, LANES), -1.0, jnp.float32))
    carry = lax.fori_loop(0, slices - 1, over_slice, begin, unroll=few(slices - 1))
    over_own(over_other(carry, final[0], later), slices - 1)


def norm_kernel(group, idcol, before, rates, q_ref, s_ref, inner_ref, gain, out_ref, raw, done, sems):
    tokens, width = q_ref.shape
    lane = lax.broadcasted_iota(jnp.int32, (HD, LANES), 1)
    place = lax.broadcasted_iota(jnp.int32, (tokens, LANES), 0)
    age = jnp.where(idcol[...] == before[...], (place + 1).astype(jnp.float32), NEVER)
    zero = jnp.zeros((HD, LANES), s_ref.dtype)
    rows = s_ref.shape[0] // group
    size = min(rows, HD)
    total = jnp.zeros((tokens, LANES), jnp.float32)
    for j in range(0, width // LANES, 2):
        square = []
        for one in (0, 1):
            state = []
            for at in range((j + one) * HD, (j + one + 1) * HD, size):
                owner, start = divmod(at, rows)
                start += (group - 1 - owner) * rows
                state.append(s_ref[start : start + size, :])
            if len(state) > 1:
                state = [jnp.concatenate([s.astype(jnp.float32) for s in state], 0).astype(zero.dtype)]
            state = state[0]
            for half in (jnp.where(lane < HD, state, zero), jnp.where(lane < HD, zero, state)):
                square.append(jnp.concatenate([zero, half] if one else [half, zero], 1))
        columns = slice(j * LANES, (j + 2) * LANES)
        outer = jnp.dot(
            q_ref[:, columns], jnp.concatenate(square, 0), preferred_element_type=jnp.float32
        )
        for one in (0, 1):
            columns = slice((j + one) * LANES, (j + one + 1) * LANES)
            fade = jnp.exp(-rates[:, columns] * age)
            value = inner_ref[:, columns] + outer[:, one * LANES : (one + 1) * LANES] * fade
            total += value * value
            raw[:, columns] = value
    mean = jnp.sum(total, axis=1, keepdims=True) / float(width)
    scale = jnp.broadcast_to(lax.rsqrt(mean + 1e-06), (tokens, LANES))
    parts = sems.shape[0]
    share = tokens // parts
    copies = []
    for part in range(parts):
        rows = slice(part * share, (part + 1) * share)
        for at in range(0, width, LANES):
            columns = slice(at, at + LANES)
            done[rows, columns] = (raw[rows, columns] * scale[rows] * gain[:, columns]).astype(
                jnp.bfloat16
            )
        copies.append(pltpu.make_async_copy(done.at[rows], out_ref.at[rows], sems.at[part]))
        copies[-1].start()
    for copy in copies:
        copy.wait()


def local(queries, keys, values, doc_ids, decay_rate, norm_gain):
    tokens, width = queries.shape
    here = decay_rate.shape[0]
    axes = ("ctx", "uly")
    slices, members = lax.axis_size("ctx"), lax.axis_size("uly")
    count = slices * members
    all_pairs = width // LANES
    chunks = members // 2
    group = slices * chunks
    rows = all_pairs * HD // group
    groups = [
        [c * members + half * chunks + u for c in range(slices) for u in range(chunks)]
        for half in (0, 1)
    ]
    swap = [
        (c * members + u, c * members + (u + chunks) % members)
        for c in range(slices)
        for u in range(members)
    ]

    vmem = pl.BlockSpec(memory_space=pltpu.VMEM)
    params = pltpu.CompilerParams(vmem_limit_bytes=32 * 1024 * 1024)
    shape = jax.ShapeDtypeStruct
    tile = shape((members, LANES), jnp.float32)

    own = jnp.pad(decay_rate, (0, LANES - here)) + jnp.pad(
        doc_ids, (LANES - tokens, 0)
    ).astype(jnp.float32)
    turned_round = [[(u + members // 2) % members for u in range(members)]]
    stored = lax.all_to_all(
        jnp.broadcast_to(own[None, :], tile.shape),
        "uly", split_axis=0, concat_axis=0, axis_index_groups=turned_round, tiled=True,
    )
    turned, filled = pl.pallas_call(
        turn_kernel,
        in_specs=[vmem] * 2,
        out_specs=[vmem] * 2,
        out_shape=[shape((width, LANES), jnp.bfloat16), shape((LANES, width), jnp.bfloat16)],
        compiler_params=params,
        cost_estimate=pl.CostEstimate(flops=0, bytes_accessed=12_000_000, transcendentals=0),
        name="turn",
    )(keys, values)
    ends = pl.pallas_call(
        functools.partial(ends_kernel, here, tokens),
        in_specs=[vmem] * 3,
        out_specs=vmem,
        out_shape=shape((group, rows + MARK, LANES), jnp.bfloat16),
        compiler_params=params,
        name="ends",
    )(stored, turned, filled)
    pieces = lax.all_to_all(
        ends,
        axes, split_axis=0, concat_axis=0, tiled=True,
        axis_index_groups=[members_of[group // 2 :] + members_of[: group // 2] for members_of in groups],
    )
    early_ends, final_end, one, half = pl.pallas_call(
        functools.partial(half_kernel, here, tokens, chunks),
        in_specs=[vmem] * 2,
        out_specs=[vmem] * 4,
        out_shape=[
            shape((slices - 1, rows + MARK, LANES), jnp.bfloat16),
            shape((1, rows + MARK, LANES), jnp.bfloat16),
            shape((rows, LANES), jnp.float32),
            shape((rows, LANES), jnp.float32),
        ],
        compiler_params=params,
        name="half",
    )(stored, pieces)
    early = lax.ppermute(early_ends, axes, swap)
    final = lax.ppermute(final_end, axes, [(low, high) for low, high in swap if low < high])
    inner, rates, idcol = pl.pallas_call(
        functools.partial(inner_kernel, here),
        in_specs=[vmem] * 4 + [pl.BlockSpec(memory_space=pl.ANY)],
        out_specs=[vmem] * 3,
        out_shape=[
            shape((tokens, width), jnp.float32),
            shape((1, width), jnp.float32),
            shape((tokens, LANES), jnp.float32),
        ],
        compiler_params=params,
        cost_estimate=pl.CostEstimate(
            flops=8_000_000_000, bytes_accessed=4_000_000, transcendentals=600_000
        ),
        name="inner",
    )(stored, queries, turned, values, early_ends)
    moved, before = pl.pallas_call(
        functools.partial(scan_kernel, chunks),
        in_specs=[vmem] * 6 + [pl.BlockSpec(memory_space=pl.ANY)],
        out_specs=[vmem] * 2,
        out_shape=[
            shape((group, rows, LANES), jnp.bfloat16),
            shape((1, LANES), jnp.float32),
        ],
        compiler_params=params,
        name="scan",
    )(stored, one, half, pieces, early, final, rates)
    states = lax.all_to_all(
        moved,
        axes, split_axis=0, concat_axis=0, tiled=True,
        axis_index_groups=[members_of[::-1] for members_of in groups],
    )
    return pl.pallas_call(
        functools.partial(norm_kernel, group),
        in_specs=[vmem] * 7,
        out_specs=pl.BlockSpec(memory_space=pl.ANY),
        out_shape=shape((tokens, width), jnp.bfloat16),
        scratch_shapes=[
            pltpu.VMEM((tokens, width), jnp.float32),
            pltpu.VMEM((tokens, width), jnp.bfloat16),
            pltpu.SemaphoreType.DMA((tokens // 16,)),
        ],
        compiler_params=params,
        name="norm",
    )(idcol, before, rates, queries, states.reshape(all_pairs * HD, LANES), inner, norm_gain[None, :])


def solution(mesh):
    in_specs = (
        P(("ctx", "uly"), None),
        P(("ctx", "uly"), None),
        P(("ctx", "uly"), None),
        P(("ctx", "uly")),
        P("uly"),
        P(),
    )
    out_specs = P(("ctx", "uly"), None)
    return jax.shard_map(local, mesh=mesh, in_specs=in_specs, out_specs=out_specs, check_vma=False)
```

```python
import functools

import jax
import jax.numpy as jnp
from jax import lax
from jax.experimental import pallas as pl
from jax.experimental.pallas import tpu as pltpu
from jax.sharding import PartitionSpec as P

HD = 64
LANES = 2 * HD
NEVER = 1e9
MARK = 8


def rate_of(facts, head, here):
    return facts[head // here : head // here + 1, head % here : head % here + 1]


def pair_rate(stored, pair, here):
    members = stored.shape[0]
    lane = lax.broadcasted_iota(jnp.int32, (1, LANES), 1)
    rates = []
    for head in (2 * pair, 2 * pair + 1):
        at = lax.rem(lax.div(head, here) + members - members // 4, members)
        row = stored[pl.ds(at, 1), :]
        rates.append(
            jnp.sum(jnp.where(lane == lax.rem(head, here), row, 0.0), axis=1, keepdims=True)
        )
    return jnp.where(lane < HD, rates[0], rates[1])


def own_ids(stored, tokens):
    members = stored.shape[0]
    at = lax.rem(lax.axis_index("uly") + members - members // 4, members)
    row = stored[pl.ds(at, 1), :]
    fill = jnp.full((1, LANES - tokens), -1.0, jnp.float32)
    return jnp.concatenate([row[:, LANES - tokens :], fill], 1)


def turn_kernel(k_ref, v_ref, turned, filled):
    tokens, width = k_ref.shape
    filled[:tokens, :] = v_ref[...]
    filled[tokens:, :] = jnp.zeros((LANES - tokens, width), filled.dtype)
    blank = jnp.zeros((LANES - tokens, LANES), jnp.float32)
    for j in range(width // LANES):
        columns = slice(j * LANES, (j + 1) * LANES)
        block = jnp.concatenate([k_ref[:, columns].astype(jnp.float32), blank], 0)
        turned[columns, :] = jnp.transpose(block).astype(turned.dtype)


def ends_kernel(here, tokens, stored, turned, v_ref, out_ref):
    width = v_ref.shape[1]
    members = stored.shape[0]
    group, rows = out_ref.shape[0], out_ref.shape[1] - MARK
    lane = lax.broadcasted_iota(jnp.int32, (HD, LANES), 1)
    ids = jnp.broadcast_to(own_ids(stored, tokens), (8, LANES))
    place = lax.broadcasted_iota(jnp.int32, ids.shape, 1)
    last = ids[:, tokens - 1 : tokens]
    age = jnp.where(ids == last, (tokens - 1 - place).astype(jnp.float32), NEVER)
    mark = jnp.broadcast_to(last[:1], (MARK, LANES)).astype(jnp.bfloat16)
    for owner in range(group):
        out_ref[owner, rows:, :] = mark
    for j in range(0, width // LANES, 2):
        weighted = []
        for head in range(2 * j, 2 * j + 4):
            weight = jnp.exp(-rate_of(stored, (head - members // 4 * here) % (members * here), here) * age)
            keys = turned[head * HD : (head + 1) * HD, :].astype(jnp.float32)
            keys = keys.reshape(HD // 8, 8, LANES) * weight[None]
            weighted.append(keys.reshape(HD, LANES))
        weighted = jnp.concatenate(weighted, 0)
        high = weighted.astype(jnp.bfloat16)
        low = (weighted - high.astype(jnp.float32)).astype(jnp.bfloat16)
        v = v_ref[:, j * LANES : (j + 2) * LANES]
        both = jnp.dot(
            jnp.concatenate([high, low], 1),
            jnp.concatenate([v, v], 0),
            preferred_element_type=jnp.float32,
        )
        for one in (0, 1):
            pair = both[one * LANES : (one + 1) * LANES, one * LANES : (one + 1) * LANES]
            state = jnp.where(lane < HD, pair[:HD], pair[HD:])
            size = min(rows, HD)
            for at in range(0, HD, size):
                owner, start = divmod((j + one) * HD + at, rows)
                out_ref[group - 1 - owner, start : start + size, :] = state[at : at + size].astype(
                    jnp.bfloat16
                )


def inner_kernel(here, stored, q_ref, turned, v_ref, after, out_ref, rates_ref, idcol):
    tokens, width = q_ref.shape
    members = stored.shape[0]
    row = own_ids(stored, tokens)
    column = jnp.transpose(jnp.broadcast_to(row, (LANES, LANES)))[:tokens]
    idcol[...] = column
    lane = lax.broadcasted_iota(jnp.int32, (tokens, LANES), 1)
    t = lax.broadcasted_iota(jnp.int32, (tokens, LANES), 0)
    seen = (t >= lane) & (column == row)
    age = jnp.where(seen, (t - lane).astype(jnp.float32), NEVER)
    for j in range(width // LANES):
        columns = slice(j * LANES, (j + 1) * LANES)
        q = q_ref[:, columns]
        zero = jnp.zeros_like(q)
        stacked = jnp.concatenate([jnp.where(lane < HD, q, zero), jnp.where(lane < HD, zero, q)], 0)
        scores = jnp.dot(
            stacked, turned[columns, :], preferred_element_type=jnp.float32
        )
        rates = [
            rate_of(stored, (2 * j + one - members // 4 * here) % (members * here), here)
            for one in (0, 1)
        ]
        weight = jnp.concatenate([jnp.exp(-rate * age) for rate in rates], 0)
        probs = (scores * weight)[:, :tokens].astype(jnp.bfloat16)
        got = jnp.dot(probs, v_ref[:, columns], preferred_element_type=jnp.float32)
        out_ref[:, columns] = jnp.where(lane < HD, got[:tokens], got[tokens:])
        rates_ref[:, columns] = jnp.where(lane[:1] < HD, rates[0], rates[1])


def few(count):
    return count if count <= 8 else 1


def split(piece, rows):
    return piece[:rows].astype(jnp.float32), piece[rows : rows + 1].astype(jnp.float32)


def half_kernel(here, tokens, chunks, stored, in_ref, early_ref, final_ref, one, half):
    slices, newest = early_ref.shape[0] + 1, in_ref.shape[0] - 1
    rows = one.shape[0]
    owner = lax.axis_index("ctx") * chunks + lax.rem(lax.axis_index("uly"), chunks)
    share = min(rows, HD)
    for at in range(0, rows, share):
        rate = pair_rate(stored, lax.div(owner * rows + at, HD), here)
        for ref, length in ((one, tokens), (half, tokens * chunks)):
            ref[at : at + share, :] = jnp.broadcast_to(
                jnp.exp(-rate * float(length)), (share, LANES)
            )

    def slice_end(c, ref, at):
        def step(j, carry):
            state, last = carry
            fresh, own = split(in_ref[newest - c * chunks - j], rows)
            return fresh + jnp.where(own == last, one[...], 0.0) * state, own

        begin = split(in_ref[newest - c * chunks], rows)
        state, _ = lax.fori_loop(1, chunks, step, begin, unroll=few(chunks - 1))
        ref[at, :rows, :] = state.astype(ref.dtype)
        ref[at, rows:, :] = in_ref[newest - c * chunks - chunks + 1][rows:]

    def early(c, _):
        slice_end(c, early_ref, c)
        return 0

    lax.fori_loop(0, slices - 1, early, 0, unroll=few(slices - 1))
    slice_end(slices - 1, final_ref, 0)


def scan_kernel(chunks, stored, one, half, in_ref, early, final, after, out_ref, before):
    slices, newest = early.shape[0] + 1, in_ref.shape[0] - 1
    rows = one.shape[0]
    ctx, uly = lax.axis_index("ctx"), lax.axis_index("uly")
    later = uly >= chunks
    members = stored.shape[0]
    at = lax.rem(uly + members - 1 + members - members // 4, members)
    _, slice_before = split(early[jnp.maximum(ctx - 1, 0)], rows)
    first = jnp.where(ctx > 0, slice_before, -1.0)
    before[...] = jnp.where(uly > 0, stored[pl.ds(at, 1), LANES - 1 :], first)

    def over_other(carry, piece, wanted):
        state, last = carry
        fresh, own = split(piece, rows)
        moved = fresh + jnp.where(own == last, half[...], 0.0) * state
        return jnp.where(wanted, moved, state), jnp.where(wanted, own, last)

    def over_own(carry, c):
        def step(j, carry):
            state, last = carry
            at = c * chunks + j
            out_ref[newest - at] = state.astype(out_ref.dtype)
            fresh, own = split(in_ref[newest - at], rows)
            return fresh + jnp.where(own == last, one[...], 0.0) * state, own

        return lax.fori_loop(0, chunks, step, carry, unroll=few(chunks))

    def over_slice(c, carry):
        carry = over_own(over_other(carry, early[c], later), c)
        return over_other(carry, early[c], jnp.logical_not(later))

    begin = (jnp.zeros((rows, LANES), jnp.float32), jnp.full((1, LANES), -1.0, jnp.float32))
    carry = lax.fori_loop(0, slices - 1, over_slice, begin, unroll=few(slices - 1))
    over_own(over_other(carry, final[0], later), slices - 1)


def norm_kernel(group, idcol, before, rates, q_ref, s_ref, inner_ref, gain, out_ref, raw, done, sems):
    tokens, width = q_ref.shape
    lane = lax.broadcasted_iota(jnp.int32, (HD, LANES), 1)
    place = lax.broadcasted_iota(jnp.int32, (tokens, LANES), 0)
    age = jnp.where(idcol[...] == before[...], (place + 1).astype(jnp.float32), NEVER)
    zero = jnp.zeros((HD, LANES), s_ref.dtype)
    rows = s_ref.shape[0] // group
    size = min(rows, HD)
    total = jnp.zeros((tokens, LANES), jnp.float32)
    for j in range(0, width // LANES, 2):
        square = []
        for one in (0, 1):
            state = []
            for at in range((j + one) * HD, (j + one + 1) * HD, size):
                owner, start = divmod(at, rows)
                start += (group - 1 - owner) * rows
                state.append(s_ref[start : start + size, :])
            if len(state) > 1:
                state = [jnp.concatenate([s.astype(jnp.float32) for s in state], 0).astype(zero.dtype)]
            state = state[0]
            for half in (jnp.where(lane < HD, state, zero), jnp.where(lane < HD, zero, state)):
                square.append(jnp.concatenate([zero, half] if one else [half, zero], 1))
        columns = slice(j * LANES, (j + 2) * LANES)
        outer = jnp.dot(
            q_ref[:, columns], jnp.concatenate(square, 0), preferred_element_type=jnp.float32
        )
        for one in (0, 1):
            columns = slice((j + one) * LANES, (j + one + 1) * LANES)
            fade = jnp.exp(-rates[:, columns] * age)
            value = inner_ref[:, columns] + outer[:, one * LANES : (one + 1) * LANES] * fade
            total += value * value
            raw[:, columns] = value
    mean = jnp.sum(total, axis=1, keepdims=True) / float(width)
    scale = jnp.broadcast_to(lax.rsqrt(mean + 1e-06), (tokens, LANES))
    parts = sems.shape[0]
    share = tokens // parts
    copies = []
    for part in range(parts):
        rows = slice(part * share, (part + 1) * share)
        for at in range(0, width, LANES):
            columns = slice(at, at + LANES)
            done[rows, columns] = (raw[rows, columns] * scale[rows] * gain[:, columns]).astype(
                jnp.bfloat16
            )
        copies.append(pltpu.make_async_copy(done.at[rows], out_ref.at[rows], sems.at[part]))
        copies[-1].start()
    for copy in copies:
        copy.wait()


def local(queries, keys, values, doc_ids, decay_rate, norm_gain):
    tokens, width = queries.shape
    here = decay_rate.shape[0]
    axes = ("ctx", "uly")
    slices, members = lax.axis_size("ctx"), lax.axis_size("uly")
    count = slices * members
    all_pairs = width // LANES
    chunks = members // 2
    group = slices * chunks
    rows = all_pairs * HD // group
    groups = [
        [c * members + half * chunks + u for c in range(slices) for u in range(chunks)]
        for half in (0, 1)
    ]
    swap = [
        (c * members + u, c * members + (u + chunks) % members)
        for c in range(slices)
        for u in range(members)
    ]

    vmem = pl.BlockSpec(memory_space=pltpu.VMEM)
    params = pltpu.CompilerParams(vmem_limit_bytes=32 * 1024 * 1024)
    shape = jax.ShapeDtypeStruct
    tile = shape((members, LANES), jnp.float32)

    own = jnp.pad(decay_rate, (0, LANES - here)) + jnp.pad(
        doc_ids, (LANES - tokens, 0)
    ).astype(jnp.float32)
    turned_round = [[(u + members // 4) % members for u in range(members)]]
    stored = lax.all_to_all(
        jnp.broadcast_to(own[None, :], tile.shape),
        "uly", split_axis=0, concat_axis=0, axis_index_groups=turned_round, tiled=True,
    )
    turned, filled = pl.pallas_call(
        turn_kernel,
        in_specs=[vmem] * 2,
        out_specs=[vmem] * 2,
        out_shape=[shape((width, LANES), jnp.bfloat16), shape((LANES, width), jnp.bfloat16)],
        compiler_params=params,
        cost_estimate=pl.CostEstimate(flops=0, bytes_accessed=12_000_000, transcendentals=0),
        name="turn",
    )(keys, values)
    ends = pl.pallas_call(
        functools.partial(ends_kernel, here, tokens),
        in_specs=[vmem] * 3,
        out_specs=vmem,
        out_shape=shape((group, rows + MARK, LANES), jnp.bfloat16),
        compiler_params=params,
        name="ends",
    )(stored, turned, filled)
    pieces = lax.all_to_all(
        ends,
        axes, split_axis=0, concat_axis=0, tiled=True,
        axis_index_groups=[members_of[::-1] for members_of in groups],
    )
    early_ends, final_end, one, half = pl.pallas_call(
        functools.partial(half_kernel, here, tokens, chunks),
        in_specs=[vmem] * 2,
        out_specs=[vmem] * 4,
        out_shape=[
            shape((slices - 1, rows + MARK, LANES), jnp.bfloat16),
            shape((1, rows + MARK, LANES), jnp.bfloat16),
            shape((rows, LANES), jnp.float32),
            shape((rows, LANES), jnp.float32),
        ],
        compiler_params=params,
        name="half",
    )(stored, pieces)
    early = lax.ppermute(early_ends, axes, swap)
    final = lax.ppermute(final_end, axes, [(low, high) for low, high in swap if low < high])
    inner, rates, idcol = pl.pallas_call(
        functools.partial(inner_kernel, here),
        in_specs=[vmem] * 4 + [pl.BlockSpec(memory_space=pl.ANY)],
        out_specs=[vmem] * 3,
        out_shape=[
            shape((tokens, width), jnp.float32),
            shape((1, width), jnp.float32),
            shape((tokens, LANES), jnp.float32),
        ],
        compiler_params=params,
        cost_estimate=pl.CostEstimate(
            flops=8_000_000_000, bytes_accessed=4_000_000, transcendentals=600_000
        ),
        name="inner",
    )(stored, queries, turned, values, early_ends)
    moved, before = pl.pallas_call(
        functools.partial(scan_kernel, chunks),
        in_specs=[vmem] * 6 + [pl.BlockSpec(memory_space=pl.ANY)],
        out_specs=[vmem] * 2,
        out_shape=[
            shape((group, rows, LANES), jnp.bfloat16),
            shape((1, LANES), jnp.float32),
        ],
        compiler_params=params,
        name="scan",
    )(stored, one, half, pieces, early, final, rates)
    states = lax.all_to_all(
        moved,
        axes, split_axis=0, concat_axis=0, tiled=True,
        axis_index_groups=[members_of[::-1] for members_of in groups],
    )
    return pl.pallas_call(
        functools.partial(norm_kernel, group),
        in_specs=[vmem] * 7,
        out_specs=pl.BlockSpec(memory_space=pl.ANY),
        out_shape=shape((tokens, width), jnp.bfloat16),
        scratch_shapes=[
            pltpu.VMEM((tokens, width), jnp.float32),
            pltpu.VMEM((tokens, width), jnp.bfloat16),
            pltpu.SemaphoreType.DMA((tokens // 16,)),
        ],
        compiler_params=params,
        name="norm",
    )(idcol, before, rates, queries, states.reshape(all_pairs * HD, LANES), inner, norm_gain[None, :])


def solution(mesh):
    in_specs = (
        P(("ctx", "uly"), None),
        P(("ctx", "uly"), None),
        P(("ctx", "uly"), None),
        P(("ctx", "uly")),
        P("uly"),
        P(),
    )
    out_specs = P(("ctx", "uly"), None)
    return jax.shard_map(local, mesh=mesh, in_specs=in_specs, out_specs=out_specs, check_vma=False)
```

```python
import functools

import jax
import jax.numpy as jnp
from jax import lax
from jax.experimental import pallas as pl
from jax.experimental.pallas import tpu as pltpu
from jax.sharding import PartitionSpec as P

HD = 64
LANES = 2 * HD
NEVER = 1e9
MARK = 8


def rate_of(facts, head, here):
    return facts[head // here : head // here + 1, head % here : head % here + 1]


def pair_rate(stored, pair, here):
    members = stored.shape[0]
    lane = lax.broadcasted_iota(jnp.int32, (1, LANES), 1)
    rates = []
    for head in (2 * pair, 2 * pair + 1):
        at = lax.rem(lax.div(head, here) + members // 2 - 1, members)
        row = stored[pl.ds(at, 1), :]
        rates.append(
            jnp.sum(jnp.where(lane == lax.rem(head, here), row, 0.0), axis=1, keepdims=True)
        )
    return jnp.where(lane < HD, rates[0], rates[1])


def own_ids(stored, tokens):
    members = stored.shape[0]
    at = lax.rem(lax.axis_index("uly") + members // 2 - 1, members)
    row = stored[pl.ds(at, 1), :]
    fill = jnp.full((1, LANES - tokens), -1.0, jnp.float32)
    return jnp.concatenate([row[:, LANES - tokens :], fill], 1)


def turn_kernel(k_ref, v_ref, turned, filled):
    tokens, width = k_ref.shape
    filled[:tokens, :] = v_ref[...]
    filled[tokens:, :] = jnp.zeros((LANES - tokens, width), filled.dtype)
    blank = jnp.zeros((LANES - tokens, LANES), jnp.float32)
    for j in range(width // LANES):
        columns = slice(j * LANES, (j + 1) * LANES)
        block = jnp.concatenate([k_ref[:, columns].astype(jnp.float32), blank], 0)
        turned[columns, :] = jnp.transpose(block).astype(turned.dtype)


def ends_kernel(here, tokens, stored, turned, v_ref, out_ref):
    width = v_ref.shape[1]
    members = stored.shape[0]
    group, rows = out_ref.shape[0], out_ref.shape[1] - MARK
    lane = lax.broadcasted_iota(jnp.int32, (HD, LANES), 1)
    ids = jnp.broadcast_to(own_ids(stored, tokens), (8, LANES))
    place = lax.broadcasted_iota(jnp.int32, ids.shape, 1)
    last = ids[:, tokens - 1 : tokens]
    age = jnp.where(ids == last, (tokens - 1 - place).astype(jnp.float32), NEVER)
    mark = jnp.broadcast_to(last[:1], (MARK, LANES)).astype(jnp.bfloat16)
    for owner in range(group):
        out_ref[owner, rows:, :] = mark
    for j in range(0, width // LANES, 2):
        weighted = []
        for head in range(2 * j, 2 * j + 4):
            weight = jnp.exp(-rate_of(stored, (head + (members // 2 - 1) * here) % (members * here), here) * age)
            keys = turned[head * HD : (head + 1) * HD, :].astype(jnp.float32)
            keys = keys.reshape(HD // 8, 8, LANES) * weight[None]
            weighted.append(keys.reshape(HD, LANES))
        weighted = jnp.concatenate(weighted, 0)
        high = weighted.astype(jnp.bfloat16)
        low = (weighted - high.astype(jnp.float32)).astype(jnp.bfloat16)
        v = v_ref[:, j * LANES : (j + 2) * LANES]
        both = jnp.dot(
            jnp.concatenate([high, low], 1),
            jnp.concatenate([v, v], 0),
            preferred_element_type=jnp.float32,
        )
        for one in (0, 1):
            pair = both[one * LANES : (one + 1) * LANES, one * LANES : (one + 1) * LANES]
            state = jnp.where(lane < HD, pair[:HD], pair[HD:])
            size = min(rows, HD)
            for at in range(0, HD, size):
                owner, start = divmod((j + one) * HD + at, rows)
                out_ref[group - 1 - owner, start : start + size, :] = state[at : at + size].astype(
                    jnp.bfloat16
                )


def inner_kernel(here, stored, q_ref, turned, v_ref, after, out_ref, rates_ref, idcol):
    tokens, width = q_ref.shape
    members = stored.shape[0]
    row = own_ids(stored, tokens)
    column = jnp.transpose(jnp.broadcast_to(row, (LANES, LANES)))[:tokens]
    idcol[...] = column
    lane = lax.broadcasted_iota(jnp.int32, (tokens, LANES), 1)
    t = lax.broadcasted_iota(jnp.int32, (tokens, LANES), 0)
    seen = (t >= lane) & (column == row)
    age = jnp.where(seen, (t - lane).astype(jnp.float32), NEVER)
    for j in range(width // LANES):
        columns = slice(j * LANES, (j + 1) * LANES)
        q = q_ref[:, columns]
        zero = jnp.zeros_like(q)
        stacked = jnp.concatenate([jnp.where(lane < HD, q, zero), jnp.where(lane < HD, zero, q)], 0)
        scores = jnp.dot(
            stacked, turned[columns, :], preferred_element_type=jnp.float32
        )
        rates = [
            rate_of(stored, (2 * j + one + (members // 2 - 1) * here) % (members * here), here)
            for one in (0, 1)
        ]
        weight = jnp.concatenate([jnp.exp(-rate * age) for rate in rates], 0)
        probs = (scores * weight)[:, :tokens].astype(jnp.bfloat16)
        got = jnp.dot(probs, v_ref[:, columns], preferred_element_type=jnp.float32)
        out_ref[:, columns] = jnp.where(lane < HD, got[:tokens], got[tokens:])
        rates_ref[:, columns] = jnp.where(lane[:1] < HD, rates[0], rates[1])


def few(count):
    return count if count <= 8 else 1


def split(piece, rows):
    return piece[:rows].astype(jnp.float32), piece[rows : rows + 1].astype(jnp.float32)


def half_kernel(here, tokens, chunks, stored, in_ref, early_ref, final_ref, one, half):
    slices, newest = early_ref.shape[0] + 1, in_ref.shape[0] - 1
    rows = one.shape[0]
    owner = lax.axis_index("ctx") * chunks + lax.rem(lax.axis_index("uly"), chunks)
    share = min(rows, HD)
    for at in range(0, rows, share):
        rate = pair_rate(stored, lax.div(owner * rows + at, HD), here)
        for ref, length in ((one, tokens), (half, tokens * chunks)):
            ref[at : at + share, :] = jnp.broadcast_to(
                jnp.exp(-rate * float(length)), (share, LANES)
            )

    def slice_end(c, ref, at):
        def step(j, carry):
            state, last = carry
            fresh, own = split(in_ref[newest - c * chunks - j], rows)
            return fresh + jnp.where(own == last, one[...], 0.0) * state, own

        begin = split(in_ref[newest - c * chunks], rows)
        state, _ = lax.fori_loop(1, chunks, step, begin, unroll=few(chunks - 1))
        ref[at, :rows, :] = state.astype(ref.dtype)
        ref[at, rows:, :] = in_ref[newest - c * chunks - chunks + 1][rows:]

    def early(c, _):
        slice_end(c, early_ref, c)
        return 0

    lax.fori_loop(0, slices - 1, early, 0, unroll=few(slices - 1))
    slice_end(slices - 1, final_ref, 0)


def scan_kernel(chunks, stored, one, half, in_ref, early, final, after, out_ref, before):
    slices, newest = early.shape[0] + 1, in_ref.shape[0] - 1
    rows = one.shape[0]
    ctx, uly = lax.axis_index("ctx"), lax.axis_index("uly")
    later = uly >= chunks
    members = stored.shape[0]
    at = lax.rem(uly + members - 1 + members // 2 - 1, members)
    _, slice_before = split(early[jnp.maximum(ctx - 1, 0)], rows)
    first = jnp.where(ctx > 0, slice_before, -1.0)
    before[...] = jnp.where(uly > 0, stored[pl.ds(at, 1), LANES - 1 :], first)

    def over_other(carry, piece, wanted):
        state, last = carry
        fresh, own = split(piece, rows)
        moved = fresh + jnp.where(own == last, half[...], 0.0) * state
        return jnp.where(wanted, moved, state), jnp.where(wanted, own, last)

    def over_own(carry, c):
        def step(j, carry):
            state, last = carry
            at = c * chunks + j
            out_ref[newest - at] = state.astype(out_ref.dtype)
            fresh, own = split(in_ref[newest - at], rows)
            return fresh + jnp.where(own == last, one[...], 0.0) * state, own

        return lax.fori_loop(0, chunks, step, carry, unroll=few(chunks))

    def over_slice(c, carry):
        carry = over_own(over_other(carry, early[c], later), c)
        return over_other(carry, early[c], jnp.logical_not(later))

    begin = (jnp.zeros((rows, LANES), jnp.float32), jnp.full((1, LANES), -1.0, jnp.float32))
    carry = lax.fori_loop(0, slices - 1, over_slice, begin, unroll=few(slices - 1))
    over_own(over_other(carry, final[0], later), slices - 1)


def norm_kernel(group, idcol, before, rates, q_ref, s_ref, inner_ref, gain, out_ref, raw, done, sems):
    tokens, width = q_ref.shape
    lane = lax.broadcasted_iota(jnp.int32, (HD, LANES), 1)
    place = lax.broadcasted_iota(jnp.int32, (tokens, LANES), 0)
    age = jnp.where(idcol[...] == before[...], (place + 1).astype(jnp.float32), NEVER)
    zero = jnp.zeros((HD, LANES), s_ref.dtype)
    rows = s_ref.shape[0] // group
    size = min(rows, HD)
    total = jnp.zeros((tokens, LANES), jnp.float32)
    for j in range(0, width // LANES, 2):
        square = []
        for one in (0, 1):
            state = []
            for at in range((j + one) * HD, (j + one + 1) * HD, size):
                owner, start = divmod(at, rows)
                start += (group - 1 - owner) * rows
                state.append(s_ref[start : start + size, :])
            if len(state) > 1:
                state = [jnp.concatenate([s.astype(jnp.float32) for s in state], 0).astype(zero.dtype)]
            state = state[0]
            for half in (jnp.where(lane < HD, state, zero), jnp.where(lane < HD, zero, state)):
                square.append(jnp.concatenate([zero, half] if one else [half, zero], 1))
        columns = slice(j * LANES, (j + 2) * LANES)
        outer = jnp.dot(
            q_ref[:, columns], jnp.concatenate(square, 0), preferred_element_type=jnp.float32
        )
        for one in (0, 1):
            columns = slice((j + one) * LANES, (j + one + 1) * LANES)
            fade = jnp.exp(-rates[:, columns] * age)
            value = inner_ref[:, columns] + outer[:, one * LANES : (one + 1) * LANES] * fade
            total += value * value
            raw[:, columns] = value
    mean = jnp.sum(total, axis=1, keepdims=True) / float(width)
    scale = jnp.broadcast_to(lax.rsqrt(mean + 1e-06), (tokens, LANES))
    parts = sems.shape[0]
    share = tokens // parts
    copies = []
    for part in range(parts):
        rows = slice(part * share, (part + 1) * share)
        for at in range(0, width, LANES):
            columns = slice(at, at + LANES)
            done[rows, columns] = (raw[rows, columns] * scale[rows] * gain[:, columns]).astype(
                jnp.bfloat16
            )
        copies.append(pltpu.make_async_copy(done.at[rows], out_ref.at[rows], sems.at[part]))
        copies[-1].start()
    for copy in copies:
        copy.wait()


def local(queries, keys, values, doc_ids, decay_rate, norm_gain):
    tokens, width = queries.shape
    here = decay_rate.shape[0]
    axes = ("ctx", "uly")
    slices, members = lax.axis_size("ctx"), lax.axis_size("uly")
    count = slices * members
    all_pairs = width // LANES
    chunks = members // 2
    group = slices * chunks
    rows = all_pairs * HD // group
    groups = [
        [c * members + half * chunks + u for c in range(slices) for u in range(chunks)]
        for half in (0, 1)
    ]
    swap = [
        (c * members + u, c * members + (u + chunks) % members)
        for c in range(slices)
        for u in range(members)
    ]

    vmem = pl.BlockSpec(memory_space=pltpu.VMEM)
    params = pltpu.CompilerParams(vmem_limit_bytes=32 * 1024 * 1024)
    shape = jax.ShapeDtypeStruct
    tile = shape((members, LANES), jnp.float32)

    own = jnp.pad(decay_rate, (0, LANES - here)) + jnp.pad(
        doc_ids, (LANES - tokens, 0)
    ).astype(jnp.float32)
    turned_round = [[(u + members // 2 + 1) % members for u in range(members)]]
    stored = lax.all_to_all(
        jnp.broadcast_to(own[None, :], tile.shape),
        "uly", split_axis=0, concat_axis=0, axis_index_groups=turned_round, tiled=True,
    )
    turned, filled = pl.pallas_call(
        turn_kernel,
        in_specs=[vmem] * 2,
        out_specs=[vmem] * 2,
        out_shape=[shape((width, LANES), jnp.bfloat16), shape((LANES, width), jnp.bfloat16)],
        compiler_params=params,
        cost_estimate=pl.CostEstimate(flops=0, bytes_accessed=12_000_000, transcendentals=0),
        name="turn",
    )(keys, values)
    ends = pl.pallas_call(
        functools.partial(ends_kernel, here, tokens),
        in_specs=[vmem] * 3,
        out_specs=vmem,
        out_shape=shape((group, rows + MARK, LANES), jnp.bfloat16),
        compiler_params=params,
        name="ends",
    )(stored, turned, filled)
    pieces = lax.all_to_all(
        ends,
        axes, split_axis=0, concat_axis=0, tiled=True,
        axis_index_groups=[members_of[::-1] for members_of in groups],
    )
    early_ends, final_end, one, half = pl.pallas_call(
        functools.partial(half_kernel, here, tokens, chunks),
        in_specs=[vmem] * 2,
        out_specs=[vmem] * 4,
        out_shape=[
            shape((slices - 1, rows + MARK, LANES), jnp.bfloat16),
            shape((1, rows + MARK, LANES), jnp.bfloat16),
            shape((rows, LANES), jnp.float32),
            shape((rows, LANES), jnp.float32),
        ],
        compiler_params=params,
        name="half",
    )(stored, pieces)
    early = lax.ppermute(early_ends, axes, swap)
    final = lax.ppermute(final_end, axes, [(low, high) for low, high in swap if low < high])
    inner, rates, idcol = pl.pallas_call(
        functools.partial(inner_kernel, here),
        in_specs=[vmem] * 4 + [pl.BlockSpec(memory_space=pl.ANY)],
        out_specs=[vmem] * 3,
        out_shape=[
            shape((tokens, width), jnp.float32),
            shape((1, width), jnp.float32),
            shape((tokens, LANES), jnp.float32),
        ],
        compiler_params=params,
        cost_estimate=pl.CostEstimate(
            flops=8_000_000_000, bytes_accessed=4_000_000, transcendentals=600_000
        ),
        name="inner",
    )(stored, queries, turned, values, early_ends)
    moved, before = pl.pallas_call(
        functools.partial(scan_kernel, chunks),
        in_specs=[vmem] * 6 + [pl.BlockSpec(memory_space=pl.ANY)],
        out_specs=[vmem] * 2,
        out_shape=[
            shape((group, rows, LANES), jnp.bfloat16),
            shape((1, LANES), jnp.float32),
        ],
        compiler_params=params,
        name="scan",
    )(stored, one, half, pieces, early, final, rates)
    states = lax.all_to_all(
        moved,
        axes, split_axis=0, concat_axis=0, tiled=True,
        axis_index_groups=[members_of[::-1] for members_of in groups],
    )
    return pl.pallas_call(
        functools.partial(norm_kernel, group),
        in_specs=[vmem] * 7,
        out_specs=pl.BlockSpec(memory_space=pl.ANY),
        out_shape=shape((tokens, width), jnp.bfloat16),
        scratch_shapes=[
            pltpu.VMEM((tokens, width), jnp.float32),
            pltpu.VMEM((tokens, width), jnp.bfloat16),
            pltpu.SemaphoreType.DMA((tokens // 16,)),
        ],
        compiler_params=params,
        name="norm",
    )(idcol, before, rates, queries, states.reshape(all_pairs * HD, LANES), inner, norm_gain[None, :])


def solution(mesh):
    in_specs = (
        P(("ctx", "uly"), None),
        P(("ctx", "uly"), None),
        P(("ctx", "uly"), None),
        P(("ctx", "uly")),
        P("uly"),
        P(),
    )
    out_specs = P(("ctx", "uly"), None)
    return jax.shard_map(local, mesh=mesh, in_specs=in_specs, out_specs=out_specs, check_vma=False)
```

```python
import functools

import jax
import jax.numpy as jnp
from jax import lax
from jax.experimental import pallas as pl
from jax.experimental.pallas import tpu as pltpu
from jax.sharding import PartitionSpec as P

HD = 64
LANES = 2 * HD
NEVER = 1e9
MARK = 8


def rate_of(facts, head, here):
    return facts[head // here : head // here + 1, head % here : head % here + 1]


def pair_rate(stored, pair, here):
    members = stored.shape[0]
    lane = lax.broadcasted_iota(jnp.int32, (1, LANES), 1)
    rates = []
    for head in (2 * pair, 2 * pair + 1):
        at = lax.rem(lax.div(head, here) + members // 2 - 2, members)
        row = stored[pl.ds(at, 1), :]
        rates.append(
            jnp.sum(jnp.where(lane == lax.rem(head, here), row, 0.0), axis=1, keepdims=True)
        )
    return jnp.where(lane < HD, rates[0], rates[1])


def own_ids(stored, tokens):
    members = stored.shape[0]
    at = lax.rem(lax.axis_index("uly") + members // 2 - 2, members)
    row = stored[pl.ds(at, 1), :]
    fill = jnp.full((1, LANES - tokens), -1.0, jnp.float32)
    return jnp.concatenate([row[:, LANES - tokens :], fill], 1)


def turn_kernel(k_ref, v_ref, turned, filled):
    tokens, width = k_ref.shape
    filled[:tokens, :] = v_ref[...]
    filled[tokens:, :] = jnp.zeros((LANES - tokens, width), filled.dtype)
    blank = jnp.zeros((LANES - tokens, LANES), jnp.float32)
    for j in range(width // LANES):
        columns = slice(j * LANES, (j + 1) * LANES)
        block = jnp.concatenate([k_ref[:, columns].astype(jnp.float32), blank], 0)
        turned[columns, :] = jnp.transpose(block).astype(turned.dtype)


def ends_kernel(here, tokens, stored, turned, v_ref, out_ref):
    width = v_ref.shape[1]
    members = stored.shape[0]
    group, rows = out_ref.shape[0], out_ref.shape[1] - MARK
    lane = lax.broadcasted_iota(jnp.int32, (HD, LANES), 1)
    ids = jnp.broadcast_to(own_ids(stored, tokens), (8, LANES))
    place = lax.broadcasted_iota(jnp.int32, ids.shape, 1)
    last = ids[:, tokens - 1 : tokens]
    age = jnp.where(ids == last, (tokens - 1 - place).astype(jnp.float32), NEVER)
    mark = jnp.broadcast_to(last[:1], (MARK, LANES)).astype(jnp.bfloat16)
    for owner in range(group):
        out_ref[owner, rows:, :] = mark
    for j in range(0, width // LANES, 2):
        weighted = []
        for head in range(2 * j, 2 * j + 4):
            weight = jnp.exp(-rate_of(stored, (head + (members // 2 - 2) * here) % (members * here), here) * age)
            keys = turned[head * HD : (head + 1) * HD, :].astype(jnp.float32)
            keys = keys.reshape(HD // 8, 8, LANES) * weight[None]
            weighted.append(keys.reshape(HD, LANES))
        weighted = jnp.concatenate(weighted, 0)
        high = weighted.astype(jnp.bfloat16)
        low = (weighted - high.astype(jnp.float32)).astype(jnp.bfloat16)
        v = v_ref[:, j * LANES : (j + 2) * LANES]
        both = jnp.dot(
            jnp.concatenate([high, low], 1),
            jnp.concatenate([v, v], 0),
            preferred_element_type=jnp.float32,
        )
        for one in (0, 1):
            pair = both[one * LANES : (one + 1) * LANES, one * LANES : (one + 1) * LANES]
            state = jnp.where(lane < HD, pair[:HD], pair[HD:])
            size = min(rows, HD)
            for at in range(0, HD, size):
                owner, start = divmod((j + one) * HD + at, rows)
                out_ref[group - 1 - owner, start : start + size, :] = state[at : at + size].astype(
                    jnp.bfloat16
                )


def inner_kernel(here, stored, q_ref, turned, v_ref, after, out_ref, rates_ref, idcol):
    tokens, width = q_ref.shape
    members = stored.shape[0]
    row = own_ids(stored, tokens)
    column = jnp.transpose(jnp.broadcast_to(row, (LANES, LANES)))[:tokens]
    idcol[...] = column
    lane = lax.broadcasted_iota(jnp.int32, (tokens, LANES), 1)
    t = lax.broadcasted_iota(jnp.int32, (tokens, LANES), 0)
    seen = (t >= lane) & (column == row)
    age = jnp.where(seen, (t - lane).astype(jnp.float32), NEVER)
    for j in range(width // LANES):
        columns = slice(j * LANES, (j + 1) * LANES)
        q = q_ref[:, columns]
        zero = jnp.zeros_like(q)
        stacked = jnp.concatenate([jnp.where(lane < HD, q, zero), jnp.where(lane < HD, zero, q)], 0)
        scores = jnp.dot(
            stacked, turned[columns, :], preferred_element_type=jnp.float32
        )
        rates = [
            rate_of(stored, (2 * j + one + (members // 2 - 2) * here) % (members * here), here)
            for one in (0, 1)
        ]
        weight = jnp.concatenate([jnp.exp(-rate * age) for rate in rates], 0)
        probs = (scores * weight)[:, :tokens].astype(jnp.bfloat16)
        got = jnp.dot(probs, v_ref[:, columns], preferred_element_type=jnp.float32)
        out_ref[:, columns] = jnp.where(lane < HD, got[:tokens], got[tokens:])
        rates_ref[:, columns] = jnp.where(lane[:1] < HD, rates[0], rates[1])


def few(count):
    return count if count <= 8 else 1


def split(piece, rows):
    return piece[:rows].astype(jnp.float32), piece[rows : rows + 1].astype(jnp.float32)


def half_kernel(here, tokens, chunks, stored, in_ref, early_ref, final_ref, one, half):
    slices, newest = early_ref.shape[0] + 1, in_ref.shape[0] - 1
    rows = one.shape[0]
    owner = lax.axis_index("ctx") * chunks + lax.rem(lax.axis_index("uly"), chunks)
    share = min(rows, HD)
    for at in range(0, rows, share):
        rate = pair_rate(stored, lax.div(owner * rows + at, HD), here)
        for ref, length in ((one, tokens), (half, tokens * chunks)):
            ref[at : at + share, :] = jnp.broadcast_to(
                jnp.exp(-rate * float(length)), (share, LANES)
            )

    def slice_end(c, ref, at):
        def step(j, carry):
            state, last = carry
            fresh, own = split(in_ref[newest - c * chunks - j], rows)
            return fresh + jnp.where(own == last, one[...], 0.0) * state, own

        begin = split(in_ref[newest - c * chunks], rows)
        state, _ = lax.fori_loop(1, chunks, step, begin, unroll=few(chunks - 1))
        ref[at, :rows, :] = state.astype(ref.dtype)
        ref[at, rows:, :] = in_ref[newest - c * chunks - chunks + 1][rows:]

    def early(c, _):
        slice_end(c, early_ref, c)
        return 0

    lax.fori_loop(0, slices - 1, early, 0, unroll=few(slices - 1))
    slice_end(slices - 1, final_ref, 0)


def scan_kernel(chunks, stored, one, half, in_ref, early, final, after, out_ref, before):
    slices, newest = early.shape[0] + 1, in_ref.shape[0] - 1
    rows = one.shape[0]
    ctx, uly = lax.axis_index("ctx"), lax.axis_index("uly")
    later = uly >= chunks
    members = stored.shape[0]
    at = lax.rem(uly + members - 1 + members // 2 - 2, members)
    _, slice_before = split(early[jnp.maximum(ctx - 1, 0)], rows)
    first = jnp.where(ctx > 0, slice_before, -1.0)
    before[...] = jnp.where(uly > 0, stored[pl.ds(at, 1), LANES - 1 :], first)

    def over_other(carry, piece, wanted):
        state, last = carry
        fresh, own = split(piece, rows)
        moved = fresh + jnp.where(own == last, half[...], 0.0) * state
        return jnp.where(wanted, moved, state), jnp.where(wanted, own, last)

    def over_own(carry, c):
        def step(j, carry):
            state, last = carry
            at = c * chunks + j
            out_ref[newest - at] = state.astype(out_ref.dtype)
            fresh, own = split(in_ref[newest - at], rows)
            return fresh + jnp.where(own == last, one[...], 0.0) * state, own

        return lax.fori_loop(0, chunks, step, carry, unroll=few(chunks))

    def over_slice(c, carry):
        carry = over_own(over_other(carry, early[c], later), c)
        return over_other(carry, early[c], jnp.logical_not(later))

    begin = (jnp.zeros((rows, LANES), jnp.float32), jnp.full((1, LANES), -1.0, jnp.float32))
    carry = lax.fori_loop(0, slices - 1, over_slice, begin, unroll=few(slices - 1))
    over_own(over_other(carry, final[0], later), slices - 1)


def norm_kernel(group, idcol, before, rates, q_ref, s_ref, inner_ref, gain, out_ref, raw, done, sems):
    tokens, width = q_ref.shape
    lane = lax.broadcasted_iota(jnp.int32, (HD, LANES), 1)
    place = lax.broadcasted_iota(jnp.int32, (tokens, LANES), 0)
    age = jnp.where(idcol[...] == before[...], (place + 1).astype(jnp.float32), NEVER)
    zero = jnp.zeros((HD, LANES), s_ref.dtype)
    rows = s_ref.shape[0] // group
    size = min(rows, HD)
    total = jnp.zeros((tokens, LANES), jnp.float32)
    for j in range(0, width // LANES, 2):
        square = []
        for one in (0, 1):
            state = []
            for at in range((j + one) * HD, (j + one + 1) * HD, size):
                owner, start = divmod(at, rows)
                start += (group - 1 - owner) * rows
                state.append(s_ref[start : start + size, :])
            if len(state) > 1:
                state = [jnp.concatenate([s.astype(jnp.float32) for s in state], 0).astype(zero.dtype)]
            state = state[0]
            for half in (jnp.where(lane < HD, state, zero), jnp.where(lane < HD, zero, state)):
                square.append(jnp.concatenate([zero, half] if one else [half, zero], 1))
        columns = slice(j * LANES, (j + 2) * LANES)
        outer = jnp.dot(
            q_ref[:, columns], jnp.concatenate(square, 0), preferred_element_type=jnp.float32
        )
        for one in (0, 1):
            columns = slice((j + one) * LANES, (j + one + 1) * LANES)
            fade = jnp.exp(-rates[:, columns] * age)
            value = inner_ref[:, columns] + outer[:, one * LANES : (one + 1) * LANES] * fade
            total += value * value
            raw[:, columns] = value
    mean = jnp.sum(total, axis=1, keepdims=True) / float(width)
    scale = jnp.broadcast_to(lax.rsqrt(mean + 1e-06), (tokens, LANES))
    parts = sems.shape[0]
    share = tokens // parts
    copies = []
    for part in range(parts):
        rows = slice(part * share, (part + 1) * share)
        for at in range(0, width, LANES):
            columns = slice(at, at + LANES)
            done[rows, columns] = (raw[rows, columns] * scale[rows] * gain[:, columns]).astype(
                jnp.bfloat16
            )
        copies.append(pltpu.make_async_copy(done.at[rows], out_ref.at[rows], sems.at[part]))
        copies[-1].start()
    for copy in copies:
        copy.wait()


def local(queries, keys, values, doc_ids, decay_rate, norm_gain):
    tokens, width = queries.shape
    here = decay_rate.shape[0]
    axes = ("ctx", "uly")
    slices, members = lax.axis_size("ctx"), lax.axis_size("uly")
    count = slices * members
    all_pairs = width // LANES
    chunks = members // 2
    group = slices * chunks
    rows = all_pairs * HD // group
    groups = [
        [c * members + half * chunks + u for c in range(slices) for u in range(chunks)]
        for half in (0, 1)
    ]
    swap = [
        (c * members + u, c * members + (u + chunks) % members)
        for c in range(slices)
        for u in range(members)
    ]

    vmem = pl.BlockSpec(memory_space=pltpu.VMEM)
    params = pltpu.CompilerParams(vmem_limit_bytes=32 * 1024 * 1024)
    shape = jax.ShapeDtypeStruct
    tile = shape((members, LANES), jnp.float32)

    own = jnp.pad(decay_rate, (0, LANES - here)) + jnp.pad(
        doc_ids, (LANES - tokens, 0)
    ).astype(jnp.float32)
    turned_round = [[(u + members // 2 + 2) % members for u in range(members)]]
    stored = lax.all_to_all(
        jnp.broadcast_to(own[None, :], tile.shape),
        "uly", split_axis=0, concat_axis=0, axis_index_groups=turned_round, tiled=True,
    )
    turned, filled = pl.pallas_call(
        turn_kernel,
        in_specs=[vmem] * 2,
        out_specs=[vmem] * 2,
        out_shape=[shape((width, LANES), jnp.bfloat16), shape((LANES, width), jnp.bfloat16)],
        compiler_params=params,
        cost_estimate=pl.CostEstimate(flops=0, bytes_accessed=12_000_000, transcendentals=0),
        name="turn",
    )(keys, values)
    ends = pl.pallas_call(
        functools.partial(ends_kernel, here, tokens),
        in_specs=[vmem] * 3,
        out_specs=vmem,
        out_shape=shape((group, rows + MARK, LANES), jnp.bfloat16),
        compiler_params=params,
        name="ends",
    )(stored, turned, filled)
    pieces = lax.all_to_all(
        ends,
        axes, split_axis=0, concat_axis=0, tiled=True,
        axis_index_groups=[members_of[::-1] for members_of in groups],
    )
    early_ends, final_end, one, half = pl.pallas_call(
        functools.partial(half_kernel, here, tokens, chunks),
        in_specs=[vmem] * 2,
        out_specs=[vmem] * 4,
        out_shape=[
            shape((slices - 1, rows + MARK, LANES), jnp.bfloat16),
            shape((1, rows + MARK, LANES), jnp.bfloat16),
            shape((rows, LANES), jnp.float32),
            shape((rows, LANES), jnp.float32),
        ],
        compiler_params=params,
        name="half",
    )(stored, pieces)
    early = lax.ppermute(early_ends, axes, swap)
    final = lax.ppermute(final_end, axes, [(low, high) for low, high in swap if low < high])
    inner, rates, idcol = pl.pallas_call(
        functools.partial(inner_kernel, here),
        in_specs=[vmem] * 4 + [pl.BlockSpec(memory_space=pl.ANY)],
        out_specs=[vmem] * 3,
        out_shape=[
            shape((tokens, width), jnp.float32),
            shape((1, width), jnp.float32),
            shape((tokens, LANES), jnp.float32),
        ],
        compiler_params=params,
        cost_estimate=pl.CostEstimate(
            flops=8_000_000_000, bytes_accessed=4_000_000, transcendentals=600_000
        ),
        name="inner",
    )(stored, queries, turned, values, early_ends)
    moved, before = pl.pallas_call(
        functools.partial(scan_kernel, chunks),
        in_specs=[vmem] * 6 + [pl.BlockSpec(memory_space=pl.ANY)],
        out_specs=[vmem] * 2,
        out_shape=[
            shape((group, rows, LANES), jnp.bfloat16),
            shape((1, LANES), jnp.float32),
        ],
        compiler_params=params,
        name="scan",
    )(stored, one, half, pieces, early, final, rates)
    states = lax.all_to_all(
        moved,
        axes, split_axis=0, concat_axis=0, tiled=True,
        axis_index_groups=[members_of[::-1] for members_of in groups],
    )
    return pl.pallas_call(
        functools.partial(norm_kernel, group),
        in_specs=[vmem] * 7,
        out_specs=pl.BlockSpec(memory_space=pl.ANY),
        out_shape=shape((tokens, width), jnp.bfloat16),
        scratch_shapes=[
            pltpu.VMEM((tokens, width), jnp.float32),
            pltpu.VMEM((tokens, width), jnp.bfloat16),
            pltpu.SemaphoreType.DMA((tokens // 16,)),
        ],
        compiler_params=params,
        name="norm",
    )(idcol, before, rates, queries, states.reshape(all_pairs * HD, LANES), inner, norm_gain[None, :])


def solution(mesh):
    in_specs = (
        P(("ctx", "uly"), None),
        P(("ctx", "uly"), None),
        P(("ctx", "uly"), None),
        P(("ctx", "uly")),
        P("uly"),
        P(),
    )
    out_specs = P(("ctx", "uly"), None)
    return jax.shard_map(local, mesh=mesh, in_specs=in_specs, out_specs=out_specs, check_vma=False)
```

```python
import functools

import jax
import jax.numpy as jnp
from jax import lax
from jax.experimental import pallas as pl
from jax.experimental.pallas import tpu as pltpu
from jax.sharding import PartitionSpec as P

HD = 64
LANES = 2 * HD
NEVER = 1e9
MARK = 8


def rate_of(facts, head, here):
    return facts[head // here : head // here + 1, head % here : head % here + 1]


def pair_rate(stored, pair, here):
    members = stored.shape[0]
    lane = lax.broadcasted_iota(jnp.int32, (1, LANES), 1)
    rates = []
    for head in (2 * pair, 2 * pair + 1):
        at = lax.rem(lax.div(head, here) + members // 2 - 1, members)
        row = stored[pl.ds(at, 1), :]
        rates.append(
            jnp.sum(jnp.where(lane == lax.rem(head, here), row, 0.0), axis=1, keepdims=True)
        )
    return jnp.where(lane < HD, rates[0], rates[1])


def own_ids(stored, tokens):
    members = stored.shape[0]
    at = lax.rem(lax.axis_index("uly") + members // 2 - 1, members)
    row = stored[pl.ds(at, 1), :]
    fill = jnp.full((1, LANES - tokens), -1.0, jnp.float32)
    return jnp.concatenate([row[:, LANES - tokens :], fill], 1)


def turn_kernel(k_ref, v_ref, turned, filled):
    tokens, width = k_ref.shape
    filled[:tokens, :] = v_ref[...]
    filled[tokens:, :] = jnp.zeros((LANES - tokens, width), filled.dtype)
    blank = jnp.zeros((LANES - tokens, LANES), jnp.float32)
    for j in range(width // LANES):
        columns = slice(j * LANES, (j + 1) * LANES)
        block = jnp.concatenate([k_ref[:, columns].astype(jnp.float32), blank], 0)
        turned[columns, :] = jnp.transpose(block).astype(turned.dtype)


def ends_kernel(here, tokens, chunks, stored, turned, v_ref, out_ref):
    width = v_ref.shape[1]
    members = stored.shape[0]
    group, rows = out_ref.shape[0], out_ref.shape[1] - MARK
    lane = lax.broadcasted_iota(jnp.int32, (HD, LANES), 1)
    ids = jnp.broadcast_to(own_ids(stored, tokens), (8, LANES))
    place = lax.broadcasted_iota(jnp.int32, ids.shape, 1)
    last = ids[:, tokens - 1 : tokens]
    age = jnp.where(ids == last, (tokens - 1 - place).astype(jnp.float32), NEVER)
    mark = jnp.broadcast_to(last[:1], (MARK, LANES)).astype(jnp.bfloat16)
    for owner in range(group):
        out_ref[owner, rows:, :] = mark
    for j in range(0, width // LANES, 2):
        weighted = []
        for head in range(2 * j, 2 * j + 4):
            weight = jnp.exp(-rate_of(stored, (head + (members // 2 - 1) * here) % (members * here), here) * age)
            keys = turned[head * HD : (head + 1) * HD, :].astype(jnp.float32)
            keys = keys.reshape(HD // 8, 8, LANES) * weight[None]
            weighted.append(keys.reshape(HD, LANES))
        weighted = jnp.concatenate(weighted, 0)
        high = weighted.astype(jnp.bfloat16)
        low = (weighted - high.astype(jnp.float32)).astype(jnp.bfloat16)
        v = v_ref[:, j * LANES : (j + 2) * LANES]
        both = jnp.dot(
            jnp.concatenate([high, low], 1),
            jnp.concatenate([v, v], 0),
            preferred_element_type=jnp.float32,
        )
        for one in (0, 1):
            pair = both[one * LANES : (one + 1) * LANES, one * LANES : (one + 1) * LANES]
            state = jnp.where(lane < HD, pair[:HD], pair[HD:])
            size = min(rows, HD)
            for at in range(0, HD, size):
                owner, start = divmod((j + one) * HD + at, rows)
                out_ref[(2 * group - 1 - owner - chunks) % group, start : start + size, :] = state[at : at + size].astype(
                    jnp.bfloat16
                )


def inner_kernel(here, stored, q_ref, turned, v_ref, after, out_ref, rates_ref, idcol):
    tokens, width = q_ref.shape
    members = stored.shape[0]
    row = own_ids(stored, tokens)
    column = jnp.transpose(jnp.broadcast_to(row, (LANES, LANES)))[:tokens]
    idcol[...] = column
    lane = lax.broadcasted_iota(jnp.int32, (tokens, LANES), 1)
    t = lax.broadcasted_iota(jnp.int32, (tokens, LANES), 0)
    seen = (t >= lane) & (column == row)
    age = jnp.where(seen, (t - lane).astype(jnp.float32), NEVER)
    for j in range(width // LANES):
        columns = slice(j * LANES, (j + 1) * LANES)
        q = q_ref[:, columns]
        zero = jnp.zeros_like(q)
        stacked = jnp.concatenate([jnp.where(lane < HD, q, zero), jnp.where(lane < HD, zero, q)], 0)
        scores = jnp.dot(
            stacked, turned[columns, :], preferred_element_type=jnp.float32
        )
        rates = [
            rate_of(stored, (2 * j + one + (members // 2 - 1) * here) % (members * here), here)
            for one in (0, 1)
        ]
        weight = jnp.concatenate([jnp.exp(-rate * age) for rate in rates], 0)
        probs = (scores * weight)[:, :tokens].astype(jnp.bfloat16)
        got = jnp.dot(probs, v_ref[:, columns], preferred_element_type=jnp.float32)
        out_ref[:, columns] = jnp.where(lane < HD, got[:tokens], got[tokens:])
        rates_ref[:, columns] = jnp.where(lane[:1] < HD, rates[0], rates[1])


def few(count):
    return count if count <= 8 else 1


def split(piece, rows):
    return piece[:rows].astype(jnp.float32), piece[rows : rows + 1].astype(jnp.float32)


def half_kernel(here, tokens, chunks, stored, in_ref, early_ref, final_ref, one, half):
    slices, newest = early_ref.shape[0] + 1, in_ref.shape[0] - 1
    rows = one.shape[0]
    owner = lax.axis_index("ctx") * chunks + lax.rem(lax.axis_index("uly"), chunks)
    share = min(rows, HD)
    for at in range(0, rows, share):
        rate = pair_rate(stored, lax.div(owner * rows + at, HD), here)
        for ref, length in ((one, tokens), (half, tokens * chunks)):
            ref[at : at + share, :] = jnp.broadcast_to(
                jnp.exp(-rate * float(length)), (share, LANES)
            )

    def slice_end(c, ref, at):
        def step(j, carry):
            state, last = carry
            fresh, own = split(in_ref[lax.rem(2 * newest + 1 - chunks - (c * chunks + j), newest + 1)], rows)
            return fresh + jnp.where(own == last, one[...], 0.0) * state, own

        begin = split(in_ref[lax.rem(2 * newest + 1 - chunks - (c * chunks), newest + 1)], rows)
        state, _ = lax.fori_loop(1, chunks, step, begin, unroll=few(chunks - 1))
        ref[at, :rows, :] = state.astype(ref.dtype)
        ref[at, rows:, :] = in_ref[lax.rem(2 * newest + 1 - chunks - (c * chunks + chunks - 1), newest + 1)][rows:]

    def early(c, _):
        slice_end(c, early_ref, c)
        return 0

    lax.fori_loop(0, slices - 1, early, 0, unroll=few(slices - 1))
    slice_end(slices - 1, final_ref, 0)


def scan_kernel(chunks, stored, one, half, in_ref, early, final, after, out_ref, before):
    slices, newest = early.shape[0] + 1, in_ref.shape[0] - 1
    rows = one.shape[0]
    ctx, uly = lax.axis_index("ctx"), lax.axis_index("uly")
    later = uly >= chunks
    members = stored.shape[0]
    at = lax.rem(uly + members - 1 + members // 2 - 1, members)
    _, slice_before = split(early[jnp.maximum(ctx - 1, 0)], rows)
    first = jnp.where(ctx > 0, slice_before, -1.0)
    before[...] = jnp.where(uly > 0, stored[pl.ds(at, 1), LANES - 1 :], first)

    def over_other(carry, piece, wanted):
        state, last = carry
        fresh, own = split(piece, rows)
        moved = fresh + jnp.where(own == last, half[...], 0.0) * state
        return jnp.where(wanted, moved, state), jnp.where(wanted, own, last)

    def over_own(carry, c):
        def step(j, carry):
            state, last = carry
            at = c * chunks + j
            out_ref[newest - at] = state.astype(out_ref.dtype)
            fresh, own = split(in_ref[lax.rem(2 * newest + 1 - chunks - (at), newest + 1)], rows)
            return fresh + jnp.where(own == last, one[...], 0.0) * state, own

        return lax.fori_loop(0, chunks, step, carry, unroll=few(chunks))

    def over_slice(c, carry):
        carry = over_own(over_other(carry, early[c], later), c)
        return over_other(carry, early[c], jnp.logical_not(later))

    begin = (jnp.zeros((rows, LANES), jnp.float32), jnp.full((1, LANES), -1.0, jnp.float32))
    carry = lax.fori_loop(0, slices - 1, over_slice, begin, unroll=few(slices - 1))
    over_own(over_other(carry, final[0], later), slices - 1)


def norm_kernel(group, idcol, before, rates, q_ref, s_ref, inner_ref, gain, out_ref, raw, done, sems):
    tokens, width = q_ref.shape
    lane = lax.broadcasted_iota(jnp.int32, (HD, LANES), 1)
    place = lax.broadcasted_iota(jnp.int32, (tokens, LANES), 0)
    age = jnp.where(idcol[...] == before[...], (place + 1).astype(jnp.float32), NEVER)
    zero = jnp.zeros((HD, LANES), s_ref.dtype)
    rows = s_ref.shape[0] // group
    size = min(rows, HD)
    total = jnp.zeros((tokens, LANES), jnp.float32)
    for j in range(0, width // LANES, 2):
        square = []
        for one in (0, 1):
            state = []
            for at in range((j + one) * HD, (j + one + 1) * HD, size):
                owner, start = divmod(at, rows)
                start += (group - 1 - owner) * rows
                state.append(s_ref[start : start + size, :])
            if len(state) > 1:
                state = [jnp.concatenate([s.astype(jnp.float32) for s in state], 0).astype(zero.dtype)]
            state = state[0]
            for half in (jnp.where(lane < HD, state, zero), jnp.where(lane < HD, zero, state)):
                square.append(jnp.concatenate([zero, half] if one else [half, zero], 1))
        columns = slice(j * LANES, (j + 2) * LANES)
        outer = jnp.dot(
            q_ref[:, columns], jnp.concatenate(square, 0), preferred_element_type=jnp.float32
        )
        for one in (0, 1):
            columns = slice((j + one) * LANES, (j + one + 1) * LANES)
            fade = jnp.exp(-rates[:, columns] * age)
            value = inner_ref[:, columns] + outer[:, one * LANES : (one + 1) * LANES] * fade
            total += value * value
            raw[:, columns] = value
    mean = jnp.sum(total, axis=1, keepdims=True) / float(width)
    scale = jnp.broadcast_to(lax.rsqrt(mean + 1e-06), (tokens, LANES))
    parts = sems.shape[0]
    share = tokens // parts
    copies = []
    for part in range(parts):
        rows = slice(part * share, (part + 1) * share)
        for at in range(0, width, LANES):
            columns = slice(at, at + LANES)
            done[rows, columns] = (raw[rows, columns] * scale[rows] * gain[:, columns]).astype(
                jnp.bfloat16
            )
        copies.append(pltpu.make_async_copy(done.at[rows], out_ref.at[rows], sems.at[part]))
        copies[-1].start()
    for copy in copies:
        copy.wait()


def local(queries, keys, values, doc_ids, decay_rate, norm_gain):
    tokens, width = queries.shape
    here = decay_rate.shape[0]
    axes = ("ctx", "uly")
    slices, members = lax.axis_size("ctx"), lax.axis_size("uly")
    count = slices * members
    all_pairs = width // LANES
    chunks = members // 2
    group = slices * chunks
    rows = all_pairs * HD // group
    groups = [
        [c * members + half * chunks + u for c in range(slices) for u in range(chunks)]
        for half in (0, 1)
    ]
    swap = [
        (c * members + u, c * members + (u + chunks) % members)
        for c in range(slices)
        for u in range(members)
    ]

    vmem = pl.BlockSpec(memory_space=pltpu.VMEM)
    params = pltpu.CompilerParams(vmem_limit_bytes=32 * 1024 * 1024)
    shape = jax.ShapeDtypeStruct
    tile = shape((members, LANES), jnp.float32)

    own = jnp.pad(decay_rate, (0, LANES - here)) + jnp.pad(
        doc_ids, (LANES - tokens, 0)
    ).astype(jnp.float32)
    turned_round = [[(u + members // 2 + 1) % members for u in range(members)]]
    stored = lax.all_to_all(
        jnp.broadcast_to(own[None, :], tile.shape),
        "uly", split_axis=0, concat_axis=0, axis_index_groups=turned_round, tiled=True,
    )
    turned, filled = pl.pallas_call(
        turn_kernel,
        in_specs=[vmem] * 2,
        out_specs=[vmem] * 2,
        out_shape=[shape((width, LANES), jnp.bfloat16), shape((LANES, width), jnp.bfloat16)],
        compiler_params=params,
        cost_estimate=pl.CostEstimate(flops=0, bytes_accessed=12_000_000, transcendentals=0),
        name="turn",
    )(keys, values)
    ends = pl.pallas_call(
        functools.partial(ends_kernel, here, tokens, chunks),
        in_specs=[vmem] * 3,
        out_specs=vmem,
        out_shape=shape((group, rows + MARK, LANES), jnp.bfloat16),
        compiler_params=params,
        name="ends",
    )(stored, turned, filled)
    pieces = lax.all_to_all(
        ends,
        axes, split_axis=0, concat_axis=0, tiled=True,
        axis_index_groups=[members_of[::-1][chunks:] + members_of[::-1][:chunks] for members_of in groups],
    )
    early_ends, final_end, one, half = pl.pallas_call(
        functools.partial(half_kernel, here, tokens, chunks),
        in_specs=[vmem] * 2,
        out_specs=[vmem] * 4,
        out_shape=[
            shape((slices - 1, rows + MARK, LANES), jnp.bfloat16),
            shape((1, rows + MARK, LANES), jnp.bfloat16),
            shape((rows, LANES), jnp.float32),
            shape((rows, LANES), jnp.float32),
        ],
        compiler_params=params,
        name="half",
    )(stored, pieces)
    early = lax.ppermute(early_ends, axes, swap)
    final = lax.ppermute(final_end, axes, [(low, high) for low, high in swap if low < high])
    inner, rates, idcol = pl.pallas_call(
        functools.partial(inner_kernel, here),
        in_specs=[vmem] * 4 + [pl.BlockSpec(memory_space=pl.ANY)],
        out_specs=[vmem] * 3,
        out_shape=[
            shape((tokens, width), jnp.float32),
            shape((1, width), jnp.float32),
            shape((tokens, LANES), jnp.float32),
        ],
        compiler_params=params,
        cost_estimate=pl.CostEstimate(
            flops=8_000_000_000, bytes_accessed=4_000_000, transcendentals=600_000
        ),
        name="inner",
    )(stored, queries, turned, values, early_ends)
    moved, before = pl.pallas_call(
        functools.partial(scan_kernel, chunks),
        in_specs=[vmem] * 6 + [pl.BlockSpec(memory_space=pl.ANY)],
        out_specs=[vmem] * 2,
        out_shape=[
            shape((group, rows, LANES), jnp.bfloat16),
            shape((1, LANES), jnp.float32),
        ],
        compiler_params=params,
        name="scan",
    )(stored, one, half, pieces, early, final, rates)
    states = lax.all_to_all(
        moved,
        axes, split_axis=0, concat_axis=0, tiled=True,
        axis_index_groups=[members_of[::-1] for members_of in groups],
    )
    return pl.pallas_call(
        functools.partial(norm_kernel, group),
        in_specs=[vmem] * 7,
        out_specs=pl.BlockSpec(memory_space=pl.ANY),
        out_shape=shape((tokens, width), jnp.bfloat16),
        scratch_shapes=[
            pltpu.VMEM((tokens, width), jnp.float32),
            pltpu.VMEM((tokens, width), jnp.bfloat16),
            pltpu.SemaphoreType.DMA((tokens // 16,)),
        ],
        compiler_params=params,
        name="norm",
    )(idcol, before, rates, queries, states.reshape(all_pairs * HD, LANES), inner, norm_gain[None, :])


def solution(mesh):
    in_specs = (
        P(("ctx", "uly"), None),
        P(("ctx", "uly"), None),
        P(("ctx", "uly"), None),
        P(("ctx", "uly")),
        P("uly"),
        P(),
    )
    out_specs = P(("ctx", "uly"), None)
    return jax.shard_map(local, mesh=mesh, in_specs=in_specs, out_specs=out_specs, check_vma=False)
```

```python
import functools

import jax
import jax.numpy as jnp
from jax import lax
from jax.experimental import pallas as pl
from jax.experimental.pallas import tpu as pltpu
from jax.sharding import PartitionSpec as P

HD = 64
LANES = 2 * HD
NEVER = 1e9
MARK = 8


def rate_of(facts, head, here):
    return facts[head // here : head // here + 1, head % here : head % here + 1]


def pair_rate(stored, pair, here):
    members = stored.shape[0]
    lane = lax.broadcasted_iota(jnp.int32, (1, LANES), 1)
    rates = []
    for head in (2 * pair, 2 * pair + 1):
        at = lax.rem(lax.div(head, here) + members // 2 - 1, members)
        row = stored[pl.ds(at, 1), :]
        rates.append(
            jnp.sum(jnp.where(lane == lax.rem(head, here), row, 0.0), axis=1, keepdims=True)
        )
    return jnp.where(lane < HD, rates[0], rates[1])


def own_ids(stored, tokens):
    members = stored.shape[0]
    at = lax.rem(lax.axis_index("uly") + members // 2 - 1, members)
    row = stored[pl.ds(at, 1), :]
    fill = jnp.full((1, LANES - tokens), -1.0, jnp.float32)
    return jnp.concatenate([row[:, LANES - tokens :], fill], 1)


def turn_kernel(k_ref, v_ref, turned, filled):
    tokens, width = k_ref.shape
    filled[:tokens, :] = v_ref[...]
    filled[tokens:, :] = jnp.zeros((LANES - tokens, width), filled.dtype)
    blank = jnp.zeros((LANES - tokens, LANES), jnp.float32)
    for j in range(width // LANES):
        columns = slice(j * LANES, (j + 1) * LANES)
        block = jnp.concatenate([k_ref[:, columns].astype(jnp.float32), blank], 0)
        turned[columns, :] = jnp.transpose(block).astype(turned.dtype)


def ends_kernel(here, tokens, stored, turned, v_ref, out_ref):
    width = v_ref.shape[1]
    members = stored.shape[0]
    group, rows = out_ref.shape[0], out_ref.shape[1] - MARK
    lane = lax.broadcasted_iota(jnp.int32, (HD, LANES), 1)
    ids = jnp.broadcast_to(own_ids(stored, tokens), (8, LANES))
    place = lax.broadcasted_iota(jnp.int32, ids.shape, 1)
    last = ids[:, tokens - 1 : tokens]
    age = jnp.where(ids == last, (tokens - 1 - place).astype(jnp.float32), NEVER)
    mark = jnp.broadcast_to(last[:1], (MARK, LANES)).astype(jnp.bfloat16)
    for owner in range(group):
        out_ref[owner, rows:, :] = mark
    for j in range(0, width // LANES, 2):
        weighted = []
        for head in range(2 * j, 2 * j + 4):
            weight = jnp.exp(-rate_of(stored, (head + (members // 2 - 1) * here) % (members * here), here) * age)
            keys = turned[head * HD : (head + 1) * HD, :].astype(jnp.float32)
            keys = keys.reshape(HD // 8, 8, LANES) * weight[None]
            weighted.append(keys.reshape(HD, LANES))
        weighted = jnp.concatenate(weighted, 0)
        high = weighted.astype(jnp.bfloat16)
        low = (weighted - high.astype(jnp.float32)).astype(jnp.bfloat16)
        v = v_ref[:, j * LANES : (j + 2) * LANES]
        both = jnp.dot(
            jnp.concatenate([high, low], 1),
            jnp.concatenate([v, v], 0),
            preferred_element_type=jnp.float32,
        )
        for one in (0, 1):
            pair = both[one * LANES : (one + 1) * LANES, one * LANES : (one + 1) * LANES]
            state = jnp.where(lane < HD, pair[:HD], pair[HD:])
            size = min(rows, HD)
            for at in range(0, HD, size):
                owner, start = divmod((j + one) * HD + at, rows)
                out_ref[group - 1 - owner, start : start + size, :] = state[at : at + size].astype(
                    jnp.bfloat16
                )


def inner_kernel(here, stored, q_ref, turned, v_ref, after, out_ref, rates_ref, idcol):
    tokens, width = q_ref.shape
    members = stored.shape[0]
    row = own_ids(stored, tokens)
    column = jnp.transpose(jnp.broadcast_to(row, (LANES, LANES)))[:tokens]
    idcol[...] = column
    lane = lax.broadcasted_iota(jnp.int32, (tokens, LANES), 1)
    t = lax.broadcasted_iota(jnp.int32, (tokens, LANES), 0)
    seen = (t >= lane) & (column == row)
    age = jnp.where(seen, (t - lane).astype(jnp.float32), NEVER)
    for j in range(width // LANES):
        columns = slice(j * LANES, (j + 1) * LANES)
        q = q_ref[:, columns]
        zero = jnp.zeros_like(q)
        stacked = jnp.concatenate([jnp.where(lane < HD, q, zero), jnp.where(lane < HD, zero, q)], 0)
        scores = jnp.dot(
            stacked, turned[columns, :], preferred_element_type=jnp.float32
        )
        rates = [
            rate_of(stored, (2 * j + one + (members // 2 - 1) * here) % (members * here), here)
            for one in (0, 1)
        ]
        weight = jnp.concatenate([jnp.exp(-rate * age) for rate in rates], 0)
        probs = (scores * weight)[:, :tokens].astype(jnp.bfloat16)
        got = jnp.dot(probs, v_ref[:, columns], preferred_element_type=jnp.float32)
        out_ref[:, columns] = jnp.where(lane < HD, got[:tokens], got[tokens:])
        rates_ref[:, columns] = jnp.where(lane[:1] < HD, rates[0], rates[1])


def few(count):
    return count if count <= 8 else 1


def split(piece, rows):
    return piece[:rows].astype(jnp.float32), piece[rows : rows + 1].astype(jnp.float32)


def half_kernel(here, tokens, chunks, stored, in_ref, early_ref, final_ref, one, half):
    slices, newest = early_ref.shape[0] + 1, in_ref.shape[0] - 1
    rows = one.shape[0]
    owner = lax.axis_index("ctx") * chunks + lax.rem(lax.axis_index("uly"), chunks)
    share = min(rows, HD)
    for at in range(0, rows, share):
        rate = pair_rate(stored, lax.div(owner * rows + at, HD), here)
        for ref, length in ((one, tokens), (half, tokens * chunks)):
            ref[at : at + share, :] = jnp.broadcast_to(
                jnp.exp(-rate * float(length)), (share, LANES)
            )

    def slice_end(c, ref, at):
        def step(j, carry):
            state, last = carry
            fresh, own = split(in_ref[newest - c * chunks - j], rows)
            return fresh + jnp.where(own == last, one[...], 0.0) * state, own

        begin = split(in_ref[newest - c * chunks], rows)
        state, _ = lax.fori_loop(1, chunks, step, begin, unroll=few(chunks - 1))
        ref[at, :rows, :] = state.astype(ref.dtype)
        ref[at, rows:, :] = in_ref[newest - c * chunks - chunks + 1][rows:]

    def early(c, _):
        slice_end(c, early_ref, c)
        return 0

    lax.fori_loop(0, slices - 1, early, 0, unroll=few(slices - 1))
    slice_end(slices - 1, final_ref, 0)


def scan_kernel(chunks, stored, one, half, in_ref, early, final, after, out_ref, before):
    slices, newest = early.shape[0] + 1, in_ref.shape[0] - 1
    rows = one.shape[0]
    ctx, uly = lax.axis_index("ctx"), lax.axis_index("uly")
    later = uly >= chunks
    members = stored.shape[0]
    at = lax.rem(uly + members - 1 + members // 2 - 1, members)
    _, slice_before = split(early[jnp.maximum(ctx - 1, 0)], rows)
    first = jnp.where(ctx > 0, slice_before, -1.0)
    before[...] = jnp.where(uly > 0, stored[pl.ds(at, 1), LANES - 1 :], first)

    def over_other(carry, piece, wanted):
        state, last = carry
        fresh, own = split(piece, rows)
        moved = fresh + jnp.where(own == last, half[...], 0.0) * state
        return jnp.where(wanted, moved, state), jnp.where(wanted, own, last)

    def over_own(carry, c):
        def step(j, carry):
            state, last = carry
            at = c * chunks + j
            out_ref[lax.rem(2 * newest + 1 - chunks - at, newest + 1)] = state.astype(out_ref.dtype)
            fresh, own = split(in_ref[newest - at], rows)
            return fresh + jnp.where(own == last, one[...], 0.0) * state, own

        return lax.fori_loop(0, chunks, step, carry, unroll=few(chunks))

    def over_slice(c, carry):
        carry = over_own(over_other(carry, early[c], later), c)
        return over_other(carry, early[c], jnp.logical_not(later))

    begin = (jnp.zeros((rows, LANES), jnp.float32), jnp.full((1, LANES), -1.0, jnp.float32))
    carry = lax.fori_loop(0, slices - 1, over_slice, begin, unroll=few(slices - 1))
    over_own(over_other(carry, final[0], later), slices - 1)


def norm_kernel(group, chunks, idcol, before, rates, q_ref, s_ref, inner_ref, gain, out_ref, raw, done, sems):
    tokens, width = q_ref.shape
    lane = lax.broadcasted_iota(jnp.int32, (HD, LANES), 1)
    place = lax.broadcasted_iota(jnp.int32, (tokens, LANES), 0)
    age = jnp.where(idcol[...] == before[...], (place + 1).astype(jnp.float32), NEVER)
    zero = jnp.zeros((HD, LANES), s_ref.dtype)
    rows = s_ref.shape[0] // group
    size = min(rows, HD)
    total = jnp.zeros((tokens, LANES), jnp.float32)
    for j in range(0, width // LANES, 2):
        square = []
        for one in (0, 1):
            state = []
            for at in range((j + one) * HD, (j + one + 1) * HD, size):
                owner, start = divmod(at, rows)
                start += (2 * group - 1 - owner - chunks) % group * rows
                state.append(s_ref[start : start + size, :])
            if len(state) > 1:
                state = [jnp.concatenate([s.astype(jnp.float32) for s in state], 0).astype(zero.dtype)]
            state = state[0]
            for half in (jnp.where(lane < HD, state, zero), jnp.where(lane < HD, zero, state)):
                square.append(jnp.concatenate([zero, half] if one else [half, zero], 1))
        columns = slice(j * LANES, (j + 2) * LANES)
        outer = jnp.dot(
            q_ref[:, columns], jnp.concatenate(square, 0), preferred_element_type=jnp.float32
        )
        for one in (0, 1):
            columns = slice((j + one) * LANES, (j + one + 1) * LANES)
            fade = jnp.exp(-rates[:, columns] * age)
            value = inner_ref[:, columns] + outer[:, one * LANES : (one + 1) * LANES] * fade
            total += value * value
            raw[:, columns] = value
    mean = jnp.sum(total, axis=1, keepdims=True) / float(width)
    scale = jnp.broadcast_to(lax.rsqrt(mean + 1e-06), (tokens, LANES))
    parts = sems.shape[0]
    share = tokens // parts
    copies = []
    for part in range(parts):
        rows = slice(part * share, (part + 1) * share)
        for at in range(0, width, LANES):
            columns = slice(at, at + LANES)
            done[rows, columns] = (raw[rows, columns] * scale[rows] * gain[:, columns]).astype(
                jnp.bfloat16
            )
        copies.append(pltpu.make_async_copy(done.at[rows], out_ref.at[rows], sems.at[part]))
        copies[-1].start()
    for copy in copies:
        copy.wait()


def local(queries, keys, values, doc_ids, decay_rate, norm_gain):
    tokens, width = queries.shape
    here = decay_rate.shape[0]
    axes = ("ctx", "uly")
    slices, members = lax.axis_size("ctx"), lax.axis_size("uly")
    count = slices * members
    all_pairs = width // LANES
    chunks = members // 2
    group = slices * chunks
    rows = all_pairs * HD // group
    groups = [
        [c * members + half * chunks + u for c in range(slices) for u in range(chunks)]
        for half in (0, 1)
    ]
    swap = [
        (c * members + u, c * members + (u + chunks) % members)
        for c in range(slices)
        for u in range(members)
    ]

    vmem = pl.BlockSpec(memory_space=pltpu.VMEM)
    params = pltpu.CompilerParams(vmem_limit_bytes=32 * 1024 * 1024)
    shape = jax.ShapeDtypeStruct
    tile = shape((members, LANES), jnp.float32)

    own = jnp.pad(decay_rate, (0, LANES - here)) + jnp.pad(
        doc_ids, (LANES - tokens, 0)
    ).astype(jnp.float32)
    turned_round = [[(u + members // 2 + 1) % members for u in range(members)]]
    stored = lax.all_to_all(
        jnp.broadcast_to(own[None, :], tile.shape),
        "uly", split_axis=0, concat_axis=0, axis_index_groups=turned_round, tiled=True,
    )
    turned, filled = pl.pallas_call(
        turn_kernel,
        in_specs=[vmem] * 2,
        out_specs=[vmem] * 2,
        out_shape=[shape((width, LANES), jnp.bfloat16), shape((LANES, width), jnp.bfloat16)],
        compiler_params=params,
        cost_estimate=pl.CostEstimate(flops=0, bytes_accessed=12_000_000, transcendentals=0),
        name="turn",
    )(keys, values)
    ends = pl.pallas_call(
        functools.partial(ends_kernel, here, tokens),
        in_specs=[vmem] * 3,
        out_specs=vmem,
        out_shape=shape((group, rows + MARK, LANES), jnp.bfloat16),
        compiler_params=params,
        name="ends",
    )(stored, turned, filled)
    pieces = lax.all_to_all(
        ends,
        axes, split_axis=0, concat_axis=0, tiled=True,
        axis_index_groups=[members_of[::-1] for members_of in groups],
    )
    early_ends, final_end, one, half = pl.pallas_call(
        functools.partial(half_kernel, here, tokens, chunks),
        in_specs=[vmem] * 2,
        out_specs=[vmem] * 4,
        out_shape=[
            shape((slices - 1, rows + MARK, LANES), jnp.bfloat16),
            shape((1, rows + MARK, LANES), jnp.bfloat16),
            shape((rows, LANES), jnp.float32),
            shape((rows, LANES), jnp.float32),
        ],
        compiler_params=params,
        name="half",
    )(stored, pieces)
    early = lax.ppermute(early_ends, axes, swap)
    final = lax.ppermute(final_end, axes, [(low, high) for low, high in swap if low < high])
    inner, rates, idcol = pl.pallas_call(
        functools.partial(inner_kernel, here),
        in_specs=[vmem] * 4 + [pl.BlockSpec(memory_space=pl.ANY)],
        out_specs=[vmem] * 3,
        out_shape=[
            shape((tokens, width), jnp.float32),
            shape((1, width), jnp.float32),
            shape((tokens, LANES), jnp.float32),
        ],
        compiler_params=params,
        cost_estimate=pl.CostEstimate(
            flops=8_000_000_000, bytes_accessed=4_000_000, transcendentals=600_000
        ),
        name="inner",
    )(stored, queries, turned, values, early_ends)
    moved, before = pl.pallas_call(
        functools.partial(scan_kernel, chunks),
        in_specs=[vmem] * 6 + [pl.BlockSpec(memory_space=pl.ANY)],
        out_specs=[vmem] * 2,
        out_shape=[
            shape((group, rows, LANES), jnp.bfloat16),
            shape((1, LANES), jnp.float32),
        ],
        compiler_params=params,
        name="scan",
    )(stored, one, half, pieces, early, final, rates)
    states = lax.all_to_all(
        moved,
        axes, split_axis=0, concat_axis=0, tiled=True,
        axis_index_groups=[members_of[::-1][chunks:] + members_of[::-1][:chunks] for members_of in groups],
    )
    return pl.pallas_call(
        functools.partial(norm_kernel, group, chunks),
        in_specs=[vmem] * 7,
        out_specs=pl.BlockSpec(memory_space=pl.ANY),
        out_shape=shape((tokens, width), jnp.bfloat16),
        scratch_shapes=[
            pltpu.VMEM((tokens, width), jnp.float32),
            pltpu.VMEM((tokens, width), jnp.bfloat16),
            pltpu.SemaphoreType.DMA((tokens // 16,)),
        ],
        compiler_params=params,
        name="norm",
    )(idcol, before, rates, queries, states.reshape(all_pairs * HD, LANES), inner, norm_gain[None, :])


def solution(mesh):
    in_specs = (
        P(("ctx", "uly"), None),
        P(("ctx", "uly"), None),
        P(("ctx", "uly"), None),
        P(("ctx", "uly")),
        P("uly"),
        P(),
    )
    out_specs = P(("ctx", "uly"), None)
    return jax.shard_map(local, mesh=mesh, in_specs=in_specs, out_specs=out_specs, check_vma=False)
```
